32 devices in a mesh: ctx: 4 (over y, x), expert: 8 (over z, core).
Axes of the slice: x: 2, y: 2, z: 4, core: 2. Of those that a mesh axis runs over, the one named last changes fastest.
Arguments:
- tokens: bfloat16 [8, 1024, 2048], P('expert', 'ctx'), may hold values from -6 to 6
- query_weight: bfloat16 [2048, 4096], P(('ctx', 'expert')), may hold values from -0.125 to 0.125
- key_weight: bfloat16 [2048, 512], P(('ctx', 'expert')), may hold values from -0.125 to 0.125
- value_weight: bfloat16 [2048, 512], P(('ctx', 'expert')), may hold values from -0.125 to 0.125
- output_weight: bfloat16 [4096, 2048], P(('ctx', 'expert')), may hold values from -1.5 to 1.5
- norm_gains: bfloat16 [2, 2048], P(None, ('ctx', 'expert')), may hold values from 0.5 to 1.5
- head_gains: bfloat16 [2, 128], P(None, ('ctx', 'expert')), may hold values from 0.5 to 1.5
- expert_gate: bfloat16 [32, 2048, 768], P(('ctx', 'expert')), may hold values from -0.125 to 0.125
- expert_up: bfloat16 [32, 2048, 768], P(('ctx', 'expert')), may hold values from -0.125 to 0.125
- expert_down: bfloat16 [32, 768, 2048], P(('ctx', 'expert')), may hold values from -0.625 to 0.625
- routes: int32 [8, 1024, 8], P('expert', 'ctx'), may hold values from 0 to 31, all different within a row; in each aligned block of 256 rows (0 to 255, 256 to 511, ..., all dimensions but the last counted through in order) at most 80 rows name the same one
- route_gates: float32 [8, 1024, 8], P('expert', 'ctx'), may hold values from 0.06 to 0.19
- cotangent: bfloat16 [8, 1024, 2048], P('expert', 'ctx'), may hold values from -6 to 6
Outputs:
- mixed_out: bfloat16 [8, 1024, 2048], P('expert', 'ctx')
- grad_tokens: bfloat16 [8, 1024, 2048], P('expert', 'ctx')
- grad_query_weight: float32 [2048, 4096], P(('ctx', 'expert'))
- grad_key_weight: float32 [2048, 512], P(('ctx', 'expert'))
- grad_value_weight: float32 [2048, 512], P(('ctx', 'expert'))
- grad_output_weight: float32 [4096, 2048], P(('ctx', 'expert'))
- grad_norm_gains: float32 [2, 2048], P(None, ('ctx', 'expert'))
- grad_head_gains: float32 [2, 128], P(None, ('ctx', 'expert'))
- grad_expert_gate: float32 [32, 2048, 768], P(('ctx', 'expert'))
- grad_expert_up: float32 [32, 2048, 768], P(('ctx', 'expert'))
- grad_expert_down: float32 [32, 768, 2048], P(('ctx', 'expert'))
The draws below stay inside these ranges and needn't reach their ends.
Inputs may be any that keep to these rules, and one draw needn't show every extreme that they name: `routes`: each token names 8 different experts; among the 256 rows of one device no expert is named by more than 80 rows, and in some such blocks one is named by exactly 80.
All inputs are finite; a program needn't handle non-finite values.
Results may differ from the reference program's by a relative error of at most 0.02.
Values may be sent and summed in bfloat16 or wider, within the bound.
A program may use at most 320 MiB of HBM per device.

```python
import math
import jax
import jax.numpy as jnp
import numpy as np
from jax import lax

D = 2048
HQ = 32
HK = 4
HD = 128
FF = 768
TOPK = 8
TOK_CTX = 256
LEN = 1024
SEQS = 8
EXPERTS = 32
CAP = 80
N_CTX = 4
N_EXPERT = 8


def shard_levels(rng, extent, cuts, low, high):
    loudness, own = 1.0, jax.random.fold_in(rng, 6)
    for axis_at, blocks in cuts:
        heights = jnp.exp(jax.random.uniform(jax.random.fold_in(own, axis_at), (blocks,), jnp.float32, low / len(cuts), high / len(cuts)))
        loudness = loudness * jnp.repeat(heights, extent[axis_at] // blocks).reshape([-1 if axis == axis_at else 1 for axis in range(len(extent))])
    return loudness


def shared_out(rng, own, number, rows, number_of, top, most, skew):
    sequence = jax.random.permutation(rng, number_of)
    crowded, common = shares(number_of, rows * top, most, skew, True), shares(number_of, rows * top, most, skew, False)
    places = jnp.arange(number_of)

    def named(lengths, turn):
        used = int((lengths > 0).sum())
        fixed = max(1, used // 4)
        passed = fixed + (places - fixed + turn * (used - fixed)) % max(1, number_of - fixed)
        return jnp.zeros((number_of,), jnp.int32).at[sequence[jnp.where(places < fixed, places, passed)]].set(jnp.asarray(lengths, jnp.int32))

    lengths = jnp.where(number % 4 == 0, named(crowded, number // 4), named(common, number - number // 4 - 1))
    mixed = jax.random.permutation(jax.random.fold_in(own, 3), number_of)
    giver, taker = mixed[0:number_of // 2 * 2:2], mixed[1:number_of // 2 * 2:2]
    slack = jnp.minimum(lengths[giver] - 1, most - lengths[taker]) // 2
    slack = jnp.where((giver == sequence[0]) | (taker == sequence[0]) | (lengths[taker] == 0), 0, jnp.maximum(slack, 0))
    passed = jax.random.randint(jax.random.fold_in(own, 4), (number_of // 2,), 0, 1 << 20) % (slack + 1)
    lengths = lengths.at[giver].add(-passed).at[taker].add(passed)
    labels = jnp.searchsorted(jnp.cumsum(lengths), jnp.arange(rows * top), side="right").astype(jnp.int32)
    listing = labels.reshape(top, rows).T
    listing = listing[jax.random.permutation(jax.random.fold_in(own, 1), rows)]
    turn = jax.random.randint(jax.random.fold_in(own, 2), (rows, 1), 0, top)
    return jnp.take_along_axis(listing, (jnp.arange(top)[None, :] + turn) % top, axis=1)


def shares(number_of, total, bound, lean, full):
    portions = [(1 << 20) // math.isqrt(standing ** lean) + 1 for standing in range(1, number_of + 1)]
    largest = bound if full else min(bound, max(-(-total // number_of), total * portions[0] // sum(portions)))
    least = 1 if total - largest >= number_of - 1 else 0
    holding, rest = [largest] + [least] * (number_of - 1), total - largest - least * (number_of - 1)
    while rest > 0:
        movable = [i for i in range(1, number_of) if holding[i] < largest] or [i for i in range(1, number_of) if holding[i] < bound]
        pool, remaining = sum([portions[i] for i in movable]), rest
        for i in movable:
            more = min(bound - holding[i], max(1, remaining * portions[i] // pool), rest)
            holding[i] = holding[i] + more
            rest = rest - more
    return np.array(holding)


def noise(own_key, extent, spread, reach, shards=(), kind=jnp.bfloat16):
    array = spread * jax.random.normal(own_key, extent, jnp.float32)
    if shards:
        array = array * shard_levels(own_key, extent, shards, -0.22, 0.18)
    return jnp.clip(array, -reach, reach).astype(kind)


def setup_inputs(seed: int = 0) -> dict:
    key_of = jax.random.split(jax.random.key(seed), 14)
    tokens = noise(key_of[0], (SEQS, LEN, D), 1.0, 6.0, ((0, 8), (1, 4)))
    query_weight = noise(key_of[1], (D, HQ * HD), D ** -0.5, 0.125, ((0, 32),))
    key_weight = noise(key_of[2], (D, HK * HD), D ** -0.5, 0.125, ((0, 32),))
    value_weight = noise(key_of[3], (D, HK * HD), D ** -0.5, 0.125, ((0, 32),))
    output_weight = noise(key_of[4], (HQ * HD, D), 16 ** -0.5, 1.5, ((0, 32),))
    norm_gains = jnp.clip(1.0 + 0.1 * jax.random.normal(key_of[5], (2, D), jnp.float32), 0.5, 1.5).astype(jnp.bfloat16)
    head_gains = jnp.clip(1.0 + 0.1 * jax.random.normal(key_of[6], (2, HD), jnp.float32), 0.5, 1.5).astype(jnp.bfloat16)
    expert_gate = noise(key_of[7], (EXPERTS, D, FF), D ** -0.5, 0.125, ((0, 32),))
    expert_up = noise(key_of[8], (EXPERTS, D, FF), D ** -0.5, 0.125, ((0, 32),))
    expert_down = noise(key_of[9], (EXPERTS, FF, D), (FF // 8) ** -0.5, 0.625, ((0, 32),))
    routes_keys = jax.random.split(jax.random.fold_in(key_of[10], 1), SEQS * LEN // TOK_CTX)
    routes_turns = jax.random.permutation(jax.random.fold_in(key_of[10], 3), SEQS * LEN // TOK_CTX)
    routes = jax.vmap(lambda own, number: shared_out(jax.random.fold_in(key_of[10], 2), own, number, TOK_CTX, EXPERTS, TOPK, CAP, 1))(routes_keys, routes_turns).reshape((SEQS, LEN, TOPK))
    route_gates = jnp.clip(jnp.exp(math.log(0.19) - 1.15267952 * jax.random.uniform(key_of[11], (SEQS, LEN, TOPK), jnp.float32) ** shard_levels(key_of[11], (SEQS, LEN, TOPK), ((0, 8), (1, 4)), -0.2, 0.2)), 0.06, 0.19)
    cotangent = noise(key_of[12], (SEQS, LEN, D), 1.0, 6.0, ((0, 8), (1, 4)))
    return {"tokens": tokens, "query_weight": query_weight, "key_weight": key_weight, "value_weight": value_weight, "output_weight": output_weight, "norm_gains": norm_gains, "head_gains": head_gains, "expert_gate": expert_gate, "expert_up": expert_up, "expert_down": expert_down, "routes": routes, "route_gates": route_gates, "cotangent": cotangent}


epsilon = 1e-06
rope_base = 1000000.0
highest = lax.Precision.HIGHEST

@jax.custom_vjp
def low(v):
    return lax.optimization_barrier(v.astype(jnp.bfloat16)).astype(jnp.float32)

@jax.custom_vjp
def low_back(v):
    return v

def low_keep(v):
    return (low(v), None)

def low_pass(kept, grad):
    return (grad,)

def back_keep(v):
    return (v, None)

def back_low(kept, grad):
    return (low(grad),)
low.defvjp(low_keep, low_pass)
low_back.defvjp(back_keep, back_low)

def rms_scale(values, scale_gain):
    return values * lax.rsqrt(lax.optimization_barrier(jnp.mean(values * values, axis=-1, keepdims=True)) + epsilon) * scale_gain

def rotate(values, positions):
    half_size = values.shape[-1] // 2
    frequency = rope_base ** (-jnp.arange(half_size, dtype=jnp.float32) / half_size)
    angles = positions.astype(jnp.float32)[:, None] * frequency[None, :]
    cosine = jnp.cos(angles)[:, None, :]
    sine_part = jnp.sin(angles)[:, None, :]
    first_half = values[..., :half_size]
    second_half = values[..., half_size:]
    return jnp.concatenate([first_half * cosine - second_half * sine_part, second_half * cosine + first_half * sine_part], axis=-1)

def attend_block(queries, keys, values, first_row):
    scores = jnp.einsum('qhgd,khd->hgqk', queries, keys, precision=highest) * HD ** (-0.5)
    scores = low_back(scores)
    query_pos = first_row + jnp.arange(queries.shape[0], dtype=jnp.int32)
    key_pos = jnp.arange(keys.shape[0], dtype=jnp.int32)
    allowed = key_pos[None, :] <= query_pos[:, None]
    scores = jnp.where(allowed, scores, -1e+30)
    probs = low(jax.nn.softmax(scores, axis=-1))
    return jnp.einsum('hgqk,khd->qhgd', probs, values, precision=highest)

def one_sequence(element):
    queries, keys, values = element
    grouped = queries.reshape(LEN, HK, HQ // HK, HD)
    span = math.gcd(LEN, 512)

    def block(block_index):
        first_row = block_index * span
        picked = lax.dynamic_slice_in_dim(grouped, first_row, span, 0)
        return attend_block(picked, keys, values, first_row)
    outputs = lax.map(jax.checkpoint(block), jnp.arange(LEN // span, dtype=jnp.int32))
    return outputs.reshape(LEN, HQ * HD)

def reference(tokens, query_weight, key_weight, value_weight, output_weight, norm_gains, head_gains, expert_gate, expert_up, expert_down, routes, route_gates, cotangent):
    count = SEQS * LEN
    route_ids = routes.reshape(count * TOPK).astype(jnp.int32)
    slots_all = N_CTX * N_EXPERT * CAP

    def find(number):
        return jnp.nonzero(route_ids == number, size=slots_all, fill_value=count * TOPK)[0].astype(jnp.int32)
    chosen = lax.map(find, jnp.arange(EXPERTS, dtype=jnp.int32))
    owners = chosen // TOPK
    gate_flat = jnp.concatenate([route_gates.reshape(count * TOPK).astype(jnp.float32), jnp.zeros((1,), jnp.float32)])
    chosen_gates = gate_flat[chosen]
    positions = jnp.arange(LEN, dtype=jnp.int32)

    def forward(inputs, wq_full, wk_full, wv_full, wo_full, gains_full, head_full, gate_full, up_full, down_full):
        rows_in = inputs.reshape(count, D)
        normed = low(rms_scale(rows_in, gains_full[0]))
        query_raw = low_back(jnp.dot(normed, wq_full, precision=highest)).reshape(SEQS, LEN, HQ, HD)
        key_raw = low_back(jnp.dot(normed, wk_full, precision=highest)).reshape(SEQS, LEN, HK, HD)
        value_rows = low(low_back(jnp.dot(normed, wv_full, precision=highest))).reshape(SEQS, LEN, HK, HD)
        queries = low(rotate(rms_scale(query_raw, head_full[0]), positions))
        keys = low(rotate(rms_scale(key_raw, head_full[1]), positions))
        attended = lax.map(jax.checkpoint(one_sequence), (queries, keys, value_rows))
        attended = low(low_back(attended.reshape(count, HQ * HD)))
        hidden = rows_in + low_back(jnp.dot(attended, wo_full, precision=highest))
        normed_mlp = low(rms_scale(hidden, gains_full[1]))
        padded = jnp.concatenate([normed_mlp, jnp.zeros((1, D), jnp.float32)], axis=0)

        def expert(element):
            gate_mat, up_mat, down_mat, owner_ids = element
            picked = low_back(padded[owner_ids])
            gate_pre = low_back(jnp.dot(picked, gate_mat, precision=highest))
            up_pre = low_back(jnp.dot(picked, up_mat, precision=highest))
            activated = low(jax.nn.silu(gate_pre) * up_pre)
            return low(low_back(jnp.dot(activated, down_mat, precision=highest)))
        produced = lax.map(jax.checkpoint(expert), (gate_full, up_full, down_full, owners))
        weighted = (chosen_gates[:, :, None] * produced).reshape(-1, D)
        combined = jnp.zeros((count + 1, D), jnp.float32).at[owners.reshape(-1)].add(weighted)
        return hidden + combined[:count]
    arrays = (tokens.astype(jnp.float32), query_weight.astype(jnp.float32), key_weight.astype(jnp.float32), value_weight.astype(jnp.float32), output_weight.astype(jnp.float32), norm_gains.astype(jnp.float32), head_gains.astype(jnp.float32), expert_gate.astype(jnp.float32), expert_up.astype(jnp.float32), expert_down.astype(jnp.float32))
    mixed, pull = jax.vjp(forward, *arrays)
    grads = pull(cotangent.reshape(count, D).astype(jnp.float32))
    return (mixed.astype(jnp.bfloat16).reshape(SEQS, LEN, D), grads[0].astype(jnp.bfloat16).reshape(SEQS, LEN, D), grads[1], grads[2], grads[3], grads[4], grads[5], grads[6], grads[7], grads[8], grads[9])
```

```python
import functools

import jax
import jax.numpy as jnp
from jax import lax
from jax.experimental import pallas as pl
from jax.experimental.pallas import tpu as pltpu
from jax.sharding import PartitionSpec as P

HQ = 32
HK = 4
HD = 128


epsilon = 1e-06
rope_base = 1000000.0
masked_value = -1e30


def rms_scale(values, scale_gain):
    return (
        values * lax.rsqrt(jnp.mean(values * values, axis=-1, keepdims=True) + epsilon) * scale_gain
    )


def rotate(values, positions):
    half_size = values.shape[-1] // 2
    frequency = rope_base ** (-jnp.arange(half_size, dtype=jnp.float32) / half_size)
    angles = positions.astype(jnp.float32)[:, None] * frequency[None, :]
    cosine = jnp.cos(angles)[:, None, :]
    sine_part = jnp.sin(angles)[:, None, :]
    first_half = values[..., :half_size]
    second_half = values[..., half_size:]
    return jnp.concatenate(
        [
            first_half * cosine - second_half * sine_part,
            second_half * cosine + first_half * sine_part,
        ],
        axis=-1,
    )


def body(
    tokens,
    query_weight,
    key_weight,
    value_weight,
    output_weight,
    norm_gains,
    head_gains,
    expert_gate,
    expert_up,
    expert_down,
    routes,
    route_gates,
    cotangent,
):
    seq_rows = tokens.shape[1]
    width = tokens.shape[2]
    groups = HQ // HK
    kv_width = HK * HD
    scale = HD ** (-0.5)
    positions = lax.axis_index("ctx") * seq_rows + jnp.arange(seq_rows, dtype=jnp.int32)
    last_pos = lax.axis_index("ctx") * seq_rows + seq_rows - 1
    rows_in = tokens.reshape(seq_rows, width).astype(jnp.float32)
    full_q, full_k, full_v, full_o, gains, head_gain = (
        lax.all_gather(query_weight, ("ctx", "expert"), axis=0, tiled=True),
        lax.all_gather(key_weight, ("ctx", "expert"), axis=0, tiled=True),
        lax.all_gather(value_weight, ("ctx", "expert"), axis=0, tiled=True),
        lax.all_gather(output_weight, ("ctx", "expert"), axis=0, tiled=True),
        lax.all_gather(norm_gains, ("ctx", "expert"), axis=1, tiled=True),
        lax.all_gather(head_gains, ("ctx", "expert"), axis=1, tiled=True),
    )

    def head_prep(raw_heads, gain_vec):
        return rotate(rms_scale(raw_heads, gain_vec), positions)

    normed = rms_scale(rows_in, gains[0].astype(jnp.float32)).astype(jnp.bfloat16)
    query_raw = jnp.dot(normed, full_q, preferred_element_type=jnp.float32).reshape(
        seq_rows, HQ, HD
    )
    key_raw = jnp.dot(normed, full_k, preferred_element_type=jnp.float32).reshape(seq_rows, HK, HD)
    value_rows = jnp.dot(normed, full_v, preferred_element_type=jnp.float32).astype(jnp.bfloat16)
    query_gain = head_gain[0].astype(jnp.float32)
    key_gain = head_gain[1].astype(jnp.float32)
    queries = head_prep(query_raw, query_gain).astype(jnp.bfloat16)
    keys_rot = head_prep(key_raw, key_gain).astype(jnp.bfloat16)
    kv_rows = jnp.concatenate([keys_rot.reshape(seq_rows, kv_width), value_rows], axis=1)
    grouped = queries.reshape(seq_rows, HK, groups, HD)

    def scores_for(key_block, base_row):
        scores = (
            jnp.einsum("qhgd,khd->hgqk", grouped, key_block, preferred_element_type=jnp.float32)
            * scale
        )
        key_pos = base_row + jnp.arange(key_block.shape[0], dtype=jnp.int32)
        allowed = key_pos[None, :] <= positions[:, None]
        return (scores, allowed)

    start_state = (
        jnp.full((HK, groups, seq_rows), masked_value, jnp.float32),
        jnp.zeros((HK, groups, seq_rows), jnp.float32),
        jnp.zeros((HK, groups, seq_rows, HD), jnp.float32),
    )
    shard_rows = lax.all_gather(kv_rows, "ctx", axis=0, tiled=True)
    blocks = shard_rows.reshape(shard_rows.shape[0] // seq_rows, seq_rows, 2 * kv_width)

    def step(state_now, element):
        block_index, block_rows = element
        base_row = block_index * seq_rows

        def step_visit(state_in):
            largest, total_sum, accum = state_in
            key_block = block_rows[:, :kv_width].reshape(seq_rows, HK, HD)
            value_block = block_rows[:, kv_width:].reshape(seq_rows, HK, HD)
            scores, allowed = scores_for(key_block, base_row)
            scores = jnp.where(allowed, scores, masked_value)
            new_largest = jnp.maximum(largest, jnp.max(scores, axis=-1))
            weights = jnp.where(allowed, jnp.exp(scores - new_largest[..., None]), 0.0)
            factor = jnp.exp(largest - new_largest)
            total_sum = total_sum * factor + jnp.sum(weights, axis=-1)
            accum = accum * factor[..., None] + jnp.einsum(
                "hgqk,khd->hgqd",
                weights.astype(jnp.bfloat16),
                value_block,
                preferred_element_type=jnp.float32,
            )
            return (new_largest, total_sum, accum)

        def step_skip(state_in):
            return state_in

        return (lax.cond(base_row <= last_pos, step_visit, step_skip, state_now), None)

    final_state, unused = lax.scan(
        step, start_state, (jnp.arange(blocks.shape[0], dtype=jnp.int32), blocks)
    )
    largest, total_sum, accum = final_state
    attended = (accum / total_sum[..., None]).transpose(2, 0, 1, 3).reshape(seq_rows, HQ * HD)
    log_total = largest + jnp.log(total_sum)
    attended_low = attended.astype(jnp.bfloat16)
    hidden = rows_in + jnp.dot(attended_low, full_o, preferred_element_type=jnp.float32)
    normed_mlp = rms_scale(hidden, gains[1].astype(jnp.float32)).astype(jnp.bfloat16)
    devices = lax.axis_size(("ctx", "expert"))
    local_experts = expert_gate.shape[0]
    experts = local_experts * devices
    topk = routes.shape[2]
    capacity = max(2, 5 * seq_rows * topk // (4 * experts))
    route_ids = routes.reshape(seq_rows * topk)
    onehot = (route_ids[:, None] == jnp.arange(experts, dtype=jnp.int32)[None, :]).astype(jnp.int32)
    slots = jnp.sum((jnp.cumsum(onehot, axis=0) - 1) * onehot, axis=1)
    target = route_ids * capacity + slots
    owner_row = jnp.arange(seq_rows * topk, dtype=jnp.int32) // topk
    gate_rows = route_gates.reshape(seq_rows, topk)

    def to_slots(row_block):
        buffer = (
            jnp.zeros((experts * capacity, row_block.shape[1]), row_block.dtype)
            .at[target]
            .set(row_block)
        )
        return buffer.reshape(devices, local_experts * capacity, row_block.shape[1])

    def to_experts(arrived):
        return (
            arrived.reshape(devices, local_experts, capacity, -1)
            .transpose(1, 0, 2, 3)
            .reshape(local_experts, devices * capacity, -1)
        )

    def from_experts(expert_rows):
        return (
            expert_rows.reshape(local_experts, devices, capacity, -1)
            .transpose(1, 0, 2, 3)
            .reshape(devices, local_experts * capacity, -1)
        )

    arrived = to_experts(
        lax.all_to_all(
            to_slots(normed_mlp[owner_row]),
            ("ctx", "expert"),
            split_axis=0,
            concat_axis=0,
            tiled=True,
        )
    )
    gate_pre = jnp.einsum("erd,edf->erf", arrived, expert_gate, preferred_element_type=jnp.float32)
    up_pre = jnp.einsum("erd,edf->erf", arrived, expert_up, preferred_element_type=jnp.float32)
    sigmoid_gate = jax.nn.sigmoid(gate_pre)
    swish_gate = gate_pre * sigmoid_gate
    activated = (swish_gate * up_pre).astype(jnp.bfloat16)
    produced = jnp.einsum(
        "erf,efd->erd", activated, expert_down, preferred_element_type=jnp.float32
    ).astype(jnp.bfloat16)
    returned = lax.all_to_all(
        from_experts(produced), ("ctx", "expert"), split_axis=0, concat_axis=0, tiled=True
    ).reshape(experts * capacity, width)
    expert_out = returned[target].astype(jnp.float32).reshape(seq_rows, topk, width)
    mixed = hidden + jnp.sum(gate_rows[:, :, None] * expert_out, axis=1)
    full_q, full_k, full_v, full_o, gains, head_gain = (
        lax.all_gather(query_weight, ("ctx", "expert"), axis=0, tiled=True),
        lax.all_gather(key_weight, ("ctx", "expert"), axis=0, tiled=True),
        lax.all_gather(value_weight, ("ctx", "expert"), axis=0, tiled=True),
        lax.all_gather(output_weight, ("ctx", "expert"), axis=0, tiled=True),
        lax.all_gather(norm_gains, ("ctx", "expert"), axis=1, tiled=True),
        lax.all_gather(head_gains, ("ctx", "expert"), axis=1, tiled=True),
    )
    grad_out = cotangent.reshape(seq_rows, width).astype(jnp.float32)
    grad_rows = (
        (gate_rows[:, :, None] * grad_out[:, None, :])
        .astype(jnp.bfloat16)
        .reshape(seq_rows * topk, width)
    )
    grad_arrived = to_experts(
        lax.all_to_all(
            to_slots(grad_rows), ("ctx", "expert"), split_axis=0, concat_axis=0, tiled=True
        )
    )
    grad_down = jnp.einsum(
        "erf,erd->efd", activated, grad_arrived, preferred_element_type=jnp.float32
    )
    grad_act = jnp.einsum(
        "erd,efd->erf", grad_arrived, expert_down, preferred_element_type=jnp.float32
    )
    grad_up_pre = (grad_act * swish_gate).astype(jnp.bfloat16)
    grad_gate_pre = (
        grad_act * up_pre * sigmoid_gate * (1.0 + gate_pre * (1.0 - sigmoid_gate))
    ).astype(jnp.bfloat16)
    grad_gate = jnp.einsum(
        "erd,erf->edf", arrived, grad_gate_pre, preferred_element_type=jnp.float32
    )
    grad_up = jnp.einsum("erd,erf->edf", arrived, grad_up_pre, preferred_element_type=jnp.float32)
    grad_inputs = jnp.einsum(
        "erf,edf->erd", grad_gate_pre, expert_gate, preferred_element_type=jnp.float32
    )
    grad_inputs = (
        grad_inputs
        + jnp.einsum("erf,edf->erd", grad_up_pre, expert_up, preferred_element_type=jnp.float32)
    ).astype(jnp.bfloat16)
    grad_back = lax.all_to_all(
        from_experts(grad_inputs), ("ctx", "expert"), split_axis=0, concat_axis=0, tiled=True
    ).reshape(experts * capacity, width)
    grad_normed_mlp = jnp.sum(
        grad_back[target].astype(jnp.float32).reshape(seq_rows, topk, width), axis=1
    )
    unused_norm, norm_pull = jax.vjp(rms_scale, hidden, gains[1].astype(jnp.float32))
    grad_hidden_norm, grad_gain_mlp = norm_pull(grad_normed_mlp)
    grad_hidden = grad_out + grad_hidden_norm
    grad_branch = grad_hidden.astype(jnp.bfloat16)
    grad_wo = jnp.einsum("qa,qd->ad", attended_low, grad_branch, preferred_element_type=jnp.float32)
    grad_attended = jnp.einsum(
        "qd,ad->qa", grad_branch, full_o, preferred_element_type=jnp.float32
    ).astype(jnp.bfloat16)
    all_kv = lax.all_gather(kv_rows, "ctx", axis=0, tiled=True)
    grad_grouped = grad_attended.reshape(seq_rows, HK, groups, HD)
    delta = jnp.einsum(
        "qhgd,qhgd->hgq",
        grad_grouped.astype(jnp.float32),
        attended.reshape(seq_rows, HK, groups, HD),
    )
    kv_blocks = all_kv.reshape(-1, seq_rows, 2 * kv_width)

    def back_step(grad_query, element):
        block_index, block_rows = element
        base_row = block_index * seq_rows

        def back_visit(grad_in):
            key_block = block_rows[:, :kv_width].reshape(seq_rows, HK, HD)
            value_block = block_rows[:, kv_width:].reshape(seq_rows, HK, HD)
            scores, allowed = scores_for(key_block, base_row)
            probs = jnp.where(allowed, jnp.exp(scores - log_total[..., None]), 0.0)
            grad_probs = jnp.einsum(
                "qhgd,khd->hgqk", grad_grouped, value_block, preferred_element_type=jnp.float32
            )
            grad_scores = (probs * (grad_probs - delta[..., None])).astype(jnp.bfloat16)
            grad_next = grad_in + jnp.einsum(
                "hgqk,khd->qhgd", grad_scores, key_block, preferred_element_type=jnp.float32
            )
            grad_keys = (
                jnp.einsum(
                    "hgqk,qhgd->khd", grad_scores, grouped, preferred_element_type=jnp.float32
                )
                * scale
            )
            grad_values = jnp.einsum(
                "hgqk,qhgd->khd",
                probs.astype(jnp.bfloat16),
                grad_grouped,
                preferred_element_type=jnp.float32,
            )
            joined = jnp.concatenate(
                [grad_keys.reshape(seq_rows, kv_width), grad_values.reshape(seq_rows, kv_width)],
                axis=1,
            )
            return (grad_next, joined)

        def back_skip(grad_in):
            return (grad_in, jnp.zeros((seq_rows, 2 * kv_width), jnp.float32))

        return lax.cond(base_row <= last_pos, back_visit, back_skip, grad_query)

    grad_query, grad_kv_terms = lax.scan(
        back_step,
        jnp.zeros((seq_rows, HK, groups, HD), jnp.float32),
        (jnp.arange(kv_blocks.shape[0], dtype=jnp.int32), kv_blocks),
    )
    grad_query = grad_query * scale
    grad_kv = lax.psum_scatter(
        grad_kv_terms.reshape(-1, 2 * kv_width).astype(jnp.bfloat16),
        "ctx",
        scatter_dimension=0,
        tiled=True,
    ).astype(jnp.float32)
    unused_query, pull_query = jax.vjp(head_prep, query_raw, query_gain)
    grad_query_raw, grad_query_gain = pull_query(grad_query.reshape(seq_rows, HQ, HD))
    unused_key, pull_key = jax.vjp(head_prep, key_raw, key_gain)
    grad_key_raw, grad_key_gain = pull_key(grad_kv[:, :kv_width].reshape(seq_rows, HK, HD))
    grad_q_low = grad_query_raw.reshape(seq_rows, HQ * HD).astype(jnp.bfloat16)
    grad_k_low = grad_key_raw.reshape(seq_rows, kv_width).astype(jnp.bfloat16)
    grad_v_low = grad_kv[:, kv_width:].astype(jnp.bfloat16)
    grad_wq = jnp.einsum("qd,qa->da", normed, grad_q_low, preferred_element_type=jnp.float32)
    grad_wk = jnp.einsum("qd,qa->da", normed, grad_k_low, preferred_element_type=jnp.float32)
    grad_wv = jnp.einsum("qd,qa->da", normed, grad_v_low, preferred_element_type=jnp.float32)
    grad_normed = jnp.einsum("qa,da->qd", grad_q_low, full_q, preferred_element_type=jnp.float32)
    grad_normed = grad_normed + jnp.einsum(
        "qa,da->qd", grad_k_low, full_k, preferred_element_type=jnp.float32
    )
    grad_normed = grad_normed + jnp.einsum(
        "qa,da->qd", grad_v_low, full_v, preferred_element_type=jnp.float32
    )
    unused_attn, pull_attn = jax.vjp(rms_scale, rows_in, gains[0].astype(jnp.float32))
    grad_rows_norm, grad_gain_attn = pull_attn(grad_normed)
    grad_input = grad_hidden + grad_rows_norm
    gain_grads = jnp.stack([grad_gain_attn, grad_gain_mlp])
    head_grads = jnp.stack([grad_query_gain, grad_key_gain])
    sum_q, sum_k, sum_v, sum_o, sum_gain, sum_head = (
        lax.psum_scatter(grad_wq, ("ctx", "expert"), scatter_dimension=0, tiled=True),
        lax.psum_scatter(grad_wk, ("ctx", "expert"), scatter_dimension=0, tiled=True),
        lax.psum_scatter(grad_wv, ("ctx", "expert"), scatter_dimension=0, tiled=True),
        lax.psum_scatter(grad_wo, ("ctx", "expert"), scatter_dimension=0, tiled=True),
        lax.psum_scatter(gain_grads, ("ctx", "expert"), scatter_dimension=1, tiled=True),
        lax.psum_scatter(head_grads, ("ctx", "expert"), scatter_dimension=1, tiled=True),
    )
    return (
        mixed.astype(jnp.bfloat16).reshape(tokens.shape),
        grad_input.astype(jnp.bfloat16).reshape(tokens.shape),
        sum_q,
        sum_k,
        sum_v,
        sum_o,
        sum_gain,
        sum_head,
        grad_gate,
        grad_up,
        grad_down,
    )


MESH = pl.DeviceIdType.MESH
VMEM_BYTES = 58 * 2**20
ANY = pl.BlockSpec(memory_space=pl.ANY)
IN_VMEM = pl.BlockSpec(memory_space=pltpu.VMEM)
f32, bf16 = jnp.float32, jnp.bfloat16


class Place:
    def __init__(self):
        self.c = lax.axis_index("ctx")
        self.e = lax.axis_index("expert")
        self.k = lax.rem(self.e, 2)
        self.z = lax.div(self.e, 2)
        self.cx = self.c + 1 - 2 * lax.rem(self.c, 2)
        self.cy = lax.rem(self.c + 2, 4)
        self.cd = lax.rem(self.cx + 2, 4)
        self.dx = (self.cx, self.e)
        self.dy = (self.cy, self.e)
        self.dd = (self.cd, self.e)
        self.pair = (self.c, self.e + 1 - 2 * self.k)
        self.up = (self.c, self.e + 2)
        self.down = (self.c, self.e - 2)


def greet(p, nz, line=True, pair=True, diagonal=False):
    barrier = pltpu.get_barrier_semaphore()

    def tell(device):
        pl.semaphore_signal(barrier, inc=1, device_id=device, device_id_type=MESH)

    friends = [p.dx, p.dy] + [p.pair] * pair + [p.dd] * diagonal
    for device in friends:
        tell(device)
    count = len(friends)
    if line:
        for there, device in ((p.z > 0, p.down), (p.z < nz - 1, p.up)):

            @pl.when(there)
            def _():
                tell(device)

            count = count + there.astype(jnp.int32)
    pl.semaphore_wait(barrier, count)


def remote(src, dst, send, recv, device):
    return pltpu.make_async_remote_copy(
        src_ref=src,
        dst_ref=dst,
        send_sem=send,
        recv_sem=recv,
        device_id=device,
        device_id_type=MESH,
    )


class Spread:
    def __init__(self, p, nz, mine, block, half, send, recv, line=True, side=True, pair=True):
        self.p, self.nz, self.mine, self.block, self.half = p, nz, mine, block, half
        self.send, self.recv = send, recv
        self.line, self.side, self.pair = line, side, pair

    def ref(self, c, z, k, h=None):
        whole = self.block(c, z, k)
        return whole if h is None else whole.at[pl.ds(h * self.half, self.half)]

    def copy(self, kind, z, own=False):
        p = self.p
        at = functools.partial(self.ref, z=z, k=p.k)
        src, i, j, device = {
            "x": lambda: (at(p.c), 0, 1, p.dx),
            "y": lambda: (at(p.c), 1, 2, p.dy),
            "up": lambda: (at(p.c), 2, 0, p.up),
            "down": lambda: (at(p.c), 3, 0, p.down),
            "via_y": lambda: (at(p.cx, h=0), 4, 3, p.dy),
            "via_x": lambda: (at(p.cy, h=1), 5, 4, p.dx),
            "pair0": lambda: (at(p.c), 6, 5, p.pair),
            "pair1": lambda: (at(p.cx), 7, 6, p.pair),
            "pair2": lambda: (at(p.cy), 8, 7, p.pair),
            "pair3": lambda: (at(p.cd, h=0), 9, 8, p.pair),
            "pair4": lambda: (at(p.cd, h=1), 10, 9, p.pair),
        }[kind]()
        return remote(
            self.mine if own else src, src, self.send.at[z, i], self.recv.at[z, j], device
        )

    def got(self, j, z):
        p = self.p
        k = p.k if j < 5 else 1 - p.k
        c, h = ((p.c, None), (p.cx, None), (p.cy, None), (p.cd, 0), (p.cd, 1))[j % 5]
        ref = self.ref(c, z, k, h)
        remote(ref, ref, self.send.at[z, 0], self.recv.at[z, j], p.pair).wait_recv()

    def each(self, far, act):
        if far == 0:
            act(self.p.z, 0)
            return
        for way in (-1, 1):
            z = self.p.z + way * far

            @pl.when((z >= 0) & (z < self.nz))
            def _():
                act(z, way)

    def onward(self, z, way, act):
        if self.line and way >= 0:

            @pl.when(self.p.z > 0)
            def _():
                act(self.copy("down", z, way == 0))

        if self.line and way <= 0:

            @pl.when(self.p.z < self.nz - 1)
            def _():
                act(self.copy("up", z, way == 0))

    def direct(self):
        return ["x", "y"] * self.side + ["pair0"] * self.pair

    def along(self, far):
        def act(z, way):
            if way:
                self.got(0, z)
            self.onward(z, way, lambda copy: copy.start())
            for kind in self.direct():
                self.copy(kind, z, way == 0).start()

        self.each(far, act)

    def beside(self, far):
        def act(z, way):
            for j, kinds in ((1, ["via_y", "pair1"]), (2, ["via_x", "pair2"])):
                self.got(j, z)
                for kind in kinds[: 1 + self.pair]:
                    self.copy(kind, z).start()

        if self.side:
            self.each(far, act)

    def across(self, far):
        def act(z, way):
            for j, kind in ((3, "pair3"), (4, "pair4")):
                self.got(j, z)
                if self.pair:
                    self.copy(kind, z).start()

        if self.side:
            self.each(far, act)

    def step(self, far):
        reach = self.nz if self.line else 1
        if far < reach:
            self.along(far)
        if 1 <= far <= reach:
            self.beside(far - 1)
        if 2 <= far <= reach + 1:
            self.across(far - 2)

    def finish(self):
        def act(z, way):
            if self.pair:
                for j in range(5, 10 if self.side else 6):
                    self.got(j, z)
            self.onward(z, way, lambda copy: copy.wait_send())
            for kind in self.direct():
                self.copy(kind, z, way == 0).wait_send()
            if self.side:
                for kind in ["via_y", "via_x"] + ["pair1", "pair2", "pair3", "pair4"] * self.pair:
                    self.copy(kind, z).wait_send()

        for far in range(self.nz if self.line else 1):
            self.each(far, act)


def by_device(ref, nz):
    return lambda c, z, k: ref.at[c * (2 * nz) + z * 2 + k]


def spread_sems(nz):
    return [pltpu.SemaphoreType.DMA((nz, 11)), pltpu.SemaphoreType.DMA((nz, 10))]


def first_kernel(nz, pack, wo, tok, cot, meta, packs, wos, toks, cots, metas, *sems):
    pair_sems, (a_send, a_recv, local) = sems[:10], sems[10:]
    p = Place()
    greet(p, nz, diagonal=True)
    own = [
        pltpu.make_async_copy(src, dst, local.at[i])
        for i, (src, dst) in enumerate(
            (
                (pack.at[p.c], packs.at[p.c, p.e]),
                (wo, wos.at[p.e]),
                (tok, toks.at[p.c]),
                (cot, cots.at[p.c * (2 * nz) + p.e]),
                (meta, metas.at[p.c * (2 * nz) + p.e]),
            )
        )
    ]
    for copy in own:
        copy.start()
    swaps = [
        remote(pack.at[c], packs.at[p.c, p.e], a_send.at[i], a_recv.at[i], device)
        for i, (c, device) in enumerate(((p.cx, p.dx), (p.cy, p.dy), (p.cd, p.dd)))
    ]
    for copy in swaps:
        copy.start()
    s = lambda i: (pair_sems[2 * i], pair_sems[2 * i + 1])
    j_tok = Spread(p, nz, tok, lambda c, z, k: toks.at[c], tok.shape[0] // 2, *s(0), False, True, False)
    j_meta = Spread(p, nz, meta, by_device(metas, nz), meta.shape[0] // 2, *s(1))
    j_cot = Spread(p, nz, cot, by_device(cots, nz), cot.shape[0] // 2, *s(2))
    j_wo = Spread(p, nz, wo, lambda c, z, k: wos.at[z * 2 + k], 0, *s(3), True, False, True)
    own_pack = packs.at[:, p.e]
    j_pack = Spread(
        p, nz, own_pack, lambda c, z, k: packs.at[:, z * 2 + k], 0, *s(4), True, False, True
    )
    j_tok.step(0)
    j_meta.step(0)
    for i, c in enumerate((p.cx, p.cy, p.cd)):
        ref = packs.at[c, p.e]
        remote(ref, ref, a_send.at[i], a_recv.at[i], p.dx).wait_recv()
    own[0].wait()
    j_pack.step(0)
    j_wo.step(0)
    j_cot.step(0)
    for far in range(1, nz + 2):
        for job in (j_tok, j_meta, j_pack, j_wo, j_cot):
            job.step(far)
    for copy in own[1:]:
        copy.wait()
    for copy in swaps:
        copy.wait_send()
    for job in (j_tok, j_meta, j_pack, j_wo, j_cot):
        job.finish()


def gather_first(nz, pack, wo, tok, cot, meta):
    blocks = 8 * nz
    shape = jax.ShapeDtypeStruct
    return pl.pallas_call(
        functools.partial(first_kernel, nz),
        out_shape=[
            shape((4, 2 * nz) + pack.shape[1:], pack.dtype),
            shape((2 * nz,) + wo.shape, wo.dtype),
            shape((4,) + tok.shape, tok.dtype),
            shape((blocks,) + cot.shape, cot.dtype),
            shape((blocks,) + meta.shape, meta.dtype),
        ],
        in_specs=[ANY] * 5,
        out_specs=[ANY] * 5,
        scratch_shapes=spread_sems(nz) * 5 + [pltpu.SemaphoreType.DMA((n,)) for n in (3, 3, 5)],
        compiler_params=pltpu.CompilerParams(collective_id=1, has_side_effects=True),
    )(pack, wo, tok, cot, meta)


def spread_kernel(nz, everywhere, mine, out, send, recv, local):
    p = Place()
    greet(p, nz, line=everywhere, pair=everywhere)
    block = by_device(out, nz) if everywhere else (lambda c, z, k: out.at[c])
    keep = pltpu.make_async_copy(mine, block(p.c, p.z, p.k), local)
    keep.start()
    job = Spread(
        p, nz, mine, block, mine.shape[0] // 2, send, recv, everywhere, True, everywhere
    )
    for far in range(nz + 2 if everywhere else 3):
        job.step(far)
    keep.wait()
    job.finish()


def gather_rows(nz, everywhere, mine, collective_id):
    blocks = 8 * nz if everywhere else 4
    return pl.pallas_call(
        functools.partial(spread_kernel, nz, everywhere),
        out_shape=jax.ShapeDtypeStruct((blocks,) + mine.shape, mine.dtype),
        in_specs=[ANY],
        out_specs=ANY,
        scratch_shapes=spread_sems(nz) + [pltpu.SemaphoreType.DMA],
        compiler_params=pltpu.CompilerParams(collective_id=collective_id, has_side_effects=True),
    )(mine)


def far_first(nz):
    return [sorted(range(nz), key=lambda to: (-abs(to - z), to)) for z in range(nz)]


def pick_order(p, nz):
    table = far_first(nz)
    return [
        sum(jnp.where(p.z == z, table[z][i], 0) for z in range(nz)) for i in range(nz)
    ]


def combine_kernel(nz, cap, rows, w, out, rbuf, sd, sx, sy, sz, h0, h1, bx, by, bz, *sems):
    pair_send, pair_recv, load, s_h0, s_h1, s_x, s_y, s_z, r_h0, r_h1, r_x, r_y, r_z = sems
    p = Place()
    order = pick_order(p, nz)
    seq = w.shape[2]
    half = seq // 2
    width = rbuf.shape[3]
    tile = min(512, width)

    @pl.when(p.z == 0)
    def _():
        bz[pl.ds(0, nz)] = jnp.zeros((nz,) + bz.shape[1:], bz.dtype)

    @pl.when(p.z == nz - 1)
    def _():
        bz[pl.ds(0, nz - 1)] = jnp.zeros((nz - 1,) + bz.shape[1:], bz.dtype)
        bz[nz] = jnp.zeros(bz.shape[1:], bz.dtype)

    greet(p, nz)
    rel = (p.cd, p.cx, p.cy, p.c)

    def pair_copy(c, z):
        other = c * (2 * nz) + z * 2 + 1 - p.k
        return remote(
            rows.at[other],
            rbuf.at[c, z, pl.ds(cap, cap)],
            pair_send.at[c, z],
            pair_recv.at[c, z],
            p.pair,
        )

    def load_copy(c, z):
        return pltpu.make_async_copy(
            rows.at[c * (2 * nz) + z * 2 + p.k], rbuf.at[c, z, pl.ds(0, cap)], load.at[c, z]
        )

    for z in order:
        for c in rel:
            load_copy(c, z).start()
            pair_copy(c, z).start()

    def ready(c, z):
        load_copy(c, z).wait()
        pair_copy(c, z).wait_recv()

    def fill(c, z, low, high, store):
        for first, adds in ((0, low), (half, high)):

            @pl.loop(0, width // tile)
            def _(t):
                cols = pl.ds(pl.multiple_of(t * tile, tile), tile)
                total = jnp.dot(
                    w[c, z, pl.ds(first, half)],
                    rbuf[c, z, :, cols],
                    preferred_element_type=f32,
                )
                for ref, start in adds:
                    total = total + ref[pl.ds(start, half), cols].astype(f32)
                store(pl.ds(first, half), cols, total)

    def into(buf, z):
        def store(lines, cols, total):
            buf[z, lines, cols] = total.astype(buf.dtype)

        return store

    def copy_h0(z):
        return remote(sd.at[z, pl.ds(0, half)], h0.at[z], s_h0.at[z], r_h0.at[z], p.dx)

    def copy_h1(z):
        return remote(sd.at[z, pl.ds(half, half)], h1.at[z], s_h1.at[z], r_h1.at[z], p.dy)

    def copy_x(z):
        return remote(sx.at[z], bx.at[z], s_x.at[z], r_x.at[z], p.dx)

    def copy_y(z):
        return remote(sy.at[z], by.at[z], s_y.at[z], r_y.at[z], p.dy)

    def copy_up(z):
        return remote(sz.at[z], bz.at[z], s_z.at[z], r_z.at[z], p.up)

    def copy_down(z):
        slot = jnp.where(z == p.z - 1, nz, z)
        return remote(sz.at[z], bz.at[slot], s_z.at[z], r_z.at[slot], p.down)

    def line_recv(slot):
        remote(bz.at[slot], bz.at[slot], s_z.at[0], r_z.at[slot], p.pair).wait_recv()

    def diagonal(z):
        ready(p.cd, z)
        fill(p.cd, z, [], [], into(sd, z))
        copy_h0(z).start()
        copy_h1(z).start()

    def sides(z):
        ready(p.cx, z)
        copy_h1(z).wait_recv()
        fill(p.cx, z, [], [(h1.at[z], 0)], into(sx, z))
        copy_x(z).start()
        ready(p.cy, z)
        copy_h0(z).wait_recv()
        fill(p.cy, z, [(h0.at[z], 0)], [], into(sy, z))
        copy_y(z).start()

    def mine(z, last):
        ready(p.c, z)
        copy_x(z).wait_recv()
        copy_y(z).wait_recv()
        arrived = [bx.at[z], by.at[z], bz.at[z]]
        if last:

            @pl.when(p.z > 0)
            def _():
                line_recv(z)

            @pl.when(p.z < nz - 1)
            def _():
                line_recv(nz)

            def store(lines, cols, total):
                out[lines, cols] = total

            arrived.append(bz.at[nz])
        else:

            @pl.when(((z > p.z) & (p.z > 0)) | ((z < p.z) & (p.z < nz - 1)))
            def _():
                line_recv(z)

            store = into(sz, z)
        fill(
            p.c, z, [(ref, 0) for ref in arrived], [(ref, half) for ref in arrived], store
        )
        if not last:

            @pl.when(z > p.z)
            def _():
                copy_up(z).start()

            @pl.when(z < p.z)
            def _():
                copy_down(z).start()

    diagonal(order[0])
    if nz > 1:
        diagonal(order[1])
    for i in range(nz):
        sides(order[i])
        if i + 2 < nz:
            diagonal(order[i + 2])
        if i > 0:
            mine(order[i - 1], False)
    mine(order[nz - 1], True)

    for i, z in enumerate(order):
        for c in rel:
            pair_copy(c, z).wait_send()
        for copy in (copy_h0(z), copy_h1(z), copy_x(z), copy_y(z)):
            copy.wait_send()
        if i < nz - 1:
            copy_up(z).wait_send()


def combine(nz, rows, w, collective_id):
    blocks, cap, width = rows.shape
    seq = w.shape[2]
    dma = pltpu.SemaphoreType.DMA
    buf = lambda n, r: pltpu.VMEM((n, r, width), bf16)
    return pl.pallas_call(
        functools.partial(combine_kernel, nz, cap),
        out_shape=jax.ShapeDtypeStruct((seq, width), f32),
        in_specs=[ANY, IN_VMEM],
        out_specs=IN_VMEM,
        scratch_shapes=[pltpu.VMEM((4, nz, 2 * cap, width), bf16)]
        + [buf(nz, seq)] * 4
        + [buf(nz, seq // 2)] * 2
        + [buf(nz, seq)] * 2
        + [buf(nz + 1, seq)]
        + [dma((4, nz))] * 3
        + [dma((nz,))] * 9
        + [dma((nz + 1,))],
        compiler_params=pltpu.CompilerParams(
            collective_id=collective_id, has_side_effects=True, vmem_limit_bytes=VMEM_BYTES
        ),
    )(rows, w)


def fold_kernel(parts, out, sx, sy, h0, h1, bx, by, send, recv):
    p = Place()
    greet(p, 1, line=False, pair=False)
    half = out.shape[0] // 2
    low, high = pl.ds(0, half), pl.ds(half, half)
    to_x = remote(parts.at[p.cd, low], h0, send.at[0], recv.at[0], p.dx)
    to_y = remote(parts.at[p.cd, high], h1, send.at[1], recv.at[1], p.dy)
    x_low = remote(parts.at[p.cx, low], bx.at[low], send.at[2], recv.at[2], p.dx)
    y_high = remote(parts.at[p.cy, high], by.at[high], send.at[3], recv.at[3], p.dy)
    x_high = remote(sx, bx.at[high], send.at[4], recv.at[4], p.dx)
    y_low = remote(sy, by.at[low], send.at[5], recv.at[5], p.dy)
    copies = (to_x, to_y, x_low, y_high, x_high, y_low)
    for copy in copies[:4]:
        copy.start()
    to_y.wait_recv()
    sx[...] = (parts[p.cx, high].astype(f32) + h1[...].astype(f32)).astype(sx.dtype)
    x_high.start()
    to_x.wait_recv()
    sy[...] = (parts[p.cy, low].astype(f32) + h0[...].astype(f32)).astype(sy.dtype)
    y_low.start()
    x_low.wait_recv()
    y_low.wait_recv()
    out[low] = parts[p.c, low].astype(f32) + bx[low].astype(f32) + by[low].astype(f32)
    y_high.wait_recv()
    x_high.wait_recv()
    out[high] = parts[p.c, high].astype(f32) + bx[high].astype(f32) + by[high].astype(f32)
    for copy in copies:
        copy.wait_send()


def fold(parts, collective_id):
    _, seq, width = parts.shape
    buf = lambda r: pltpu.VMEM((r, width), parts.dtype)
    return pl.pallas_call(
        fold_kernel,
        out_shape=jax.ShapeDtypeStruct((seq, width), f32),
        in_specs=[IN_VMEM],
        out_specs=IN_VMEM,
        scratch_shapes=[buf(seq // 2)] * 4
        + [buf(seq)] * 2
        + [pltpu.SemaphoreType.DMA((6,))] * 2,
        compiler_params=pltpu.CompilerParams(
            collective_id=collective_id, has_side_effects=True, vmem_limit_bytes=VMEM_BYTES
        ),
    )(parts)


def last_kernel(nz, gq, go, gains, oq, ok, ov, oo, all_gains, *scratch):
    own_q, own_o, sib_q, sib_o, s_q, s_o, b_q, b_o, swap_s, swap_r, scratch = (
        *scratch[:10],
        scratch[10:],
    )
    load, pair_s, pair_r, line_s, line_r, a_send, a_recv, g_send, g_recv, local = scratch
    p = Place()
    order = pick_order(p, nz)

    @pl.when(p.z == 0)
    def _():
        for ref in (b_q, b_o):
            ref[pl.ds(0, nz)] = jnp.zeros((nz,) + ref.shape[1:], ref.dtype)

    @pl.when(p.z == nz - 1)
    def _():
        for ref in (b_q, b_o):
            ref[pl.ds(0, nz - 1)] = jnp.zeros((nz - 1,) + ref.shape[1:], ref.dtype)
            ref[nz] = jnp.zeros(ref.shape[1:], ref.dtype)

    greet(p, nz, diagonal=True)
    keep = pltpu.make_async_copy(gains, all_gains.at[p.c * (2 * nz) + p.e], local)
    keep.start()
    job = Spread(p, nz, gains, by_device(all_gains, nz), gains.shape[0] // 2, g_send, g_recv)
    arrays = (
        (0, lambda z, k: gq.at[:, z * 2 + k], own_q, sib_q, s_q, b_q),
        (1, lambda z, k: go.at[z * 2 + k], own_o, sib_o, s_o, b_o),
    )

    def load_copy(i, z):
        _, part, own, _, _, _ = arrays[i]
        return pltpu.make_async_copy(part(z, p.k), own.at[z], load.at[i, z])

    def pair_copy(i, z):
        _, part, _, sib, _, _ = arrays[i]
        return remote(part(z, 1 - p.k), sib.at[z], pair_s.at[i, z], pair_r.at[i, z], p.pair)

    def copy_up(i, z):
        _, _, _, _, s, b = arrays[i]
        return remote(s.at[z], b.at[z], line_s.at[i, z], line_r.at[i, z], p.up)

    def copy_down(i, z):
        _, _, _, _, s, b = arrays[i]
        slot = jnp.where(z == p.z - 1, nz, z)
        return remote(s.at[z], b.at[slot], line_s.at[i, z], line_r.at[i, slot], p.down)

    def line_recv(i, slot):
        b = arrays[i][5]
        remote(b.at[slot], b.at[slot], line_s.at[i, 0], line_r.at[i, slot], p.pair).wait_recv()

    for z in order:
        for i in (0, 1):
            pair_copy(i, z).start()
            load_copy(i, z).start()
    for far in range(nz + 2):
        job.step(far)
        if far >= nz:
            continue
        z, last = order[far], far == nz - 1
        for i in (0, 1):
            _, _, own, sib, s, b = arrays[i]
            load_copy(i, z).wait()
            pair_copy(i, z).wait_recv()
            if last:

                @pl.when(p.z > 0)
                def _():
                    line_recv(i, z)

                @pl.when(p.z < nz - 1)
                def _():
                    line_recv(i, nz)

                total = own[z].astype(f32) + sib[z].astype(f32) + b[z].astype(f32)
                total = total + b[nz].astype(f32)
                if i:
                    oo[...] = total
                else:
                    swap_s[...] = total.astype(swap_s.dtype)
            else:

                @pl.when(((z > p.z) & (p.z > 0)) | ((z < p.z) & (p.z < nz - 1)))
                def _():
                    line_recv(i, z)

                total = own[z].astype(f32) + sib[z].astype(f32) + b[z].astype(f32)
                s[z] = total.astype(s.dtype)

                @pl.when(z > p.z)
                def _():
                    copy_up(i, z).start()

                @pl.when(z < p.z)
                def _():
                    copy_down(i, z).start()

            if last and i == 0:
                swaps = [
                    remote(
                        swap_s.at[c], swap_r.at[p.c], a_send.at[n], a_recv.at[n], device
                    )
                    for n, (c, device) in enumerate(((p.cx, p.dx), (p.cy, p.dy), (p.cd, p.dd)))
                ]
                for copy in swaps:
                    copy.start()
                swap_r[p.c] = swap_s[p.c]
    for n, c in enumerate((p.cx, p.cy, p.cd)):
        ref = swap_r.at[c]
        remote(ref, ref, a_send.at[n], a_recv.at[n], p.dx).wait_recv()
    heads = oq.shape[1] // 4
    kv = ok.shape[1] // 4
    for c in range(4):
        oq[:, pl.ds(c * heads, heads)] = swap_r[c, :, pl.ds(0, heads)].astype(f32)
        ok[:, pl.ds(c * kv, kv)] = swap_r[c, :, pl.ds(heads, kv)].astype(f32)
        ov[:, pl.ds(c * kv, kv)] = swap_r[c, :, pl.ds(heads + kv, kv)].astype(f32)
    for copy in swaps:
        copy.wait_send()
    for n, z in enumerate(order):
        for i in (0, 1):
            pair_copy(i, z).wait_send()
            if n < nz - 1:
                copy_up(i, z).wait_send()
    keep.wait()
    job.finish()


def reduce_last(nz, gq, go, gains):
    _, _, rows_q, wide = gq.shape
    _, rows_o, width = go.shape
    kv = HD
    heads = wide - 2 * kv
    dma = pltpu.SemaphoreType.DMA
    shape = jax.ShapeDtypeStruct
    q = lambda *n: pltpu.VMEM(n + (4, rows_q, wide), bf16)
    o = lambda *n: pltpu.VMEM(n + (rows_o, width), bf16)
    return pl.pallas_call(
        functools.partial(last_kernel, nz),
        out_shape=[
            shape((rows_q, 4 * heads), f32),
            shape((rows_q, 4 * kv), f32),
            shape((rows_q, 4 * kv), f32),
            shape((rows_o, width), f32),
            shape((8 * nz,) + gains.shape, f32),
        ],
        in_specs=[ANY] * 3,
        out_specs=[IN_VMEM] * 4 + [ANY],
        scratch_shapes=[q(nz), o(nz), q(nz), o(nz), q(nz), o(nz), q(nz + 1), o(nz + 1), q(), q()]
        + [dma((2, nz))] * 4
        + [dma((2, nz + 1))]
        + [dma((3,))] * 2
        + spread_sems(nz)
        + [dma],
        compiler_params=pltpu.CompilerParams(
            collective_id=9, has_side_effects=True, vmem_limit_bytes=VMEM_BYTES
        ),
    )(gq, go, gains)


def attend_kernel(scale, span, q, k, vt, ot, lse):
    for i in range(q.shape[1] // span):
        keys = (i + 1) * span
        here = pl.ds(i * span, span)
        s = lax.dot_general(
            k[pl.ds(0, keys)], q[0, here], (((1,), (1,)), ((), ())), preferred_element_type=f32
        )
        s = s * scale
        key_pos = lax.broadcasted_iota(jnp.int32, s.shape, 0)
        query_pos = lax.broadcasted_iota(jnp.int32, s.shape, 1) + i * span
        s = jnp.where(key_pos <= query_pos, s, masked_value)
        largest = jnp.max(s, axis=0, keepdims=True)
        weights = jnp.exp(s - largest)
        total = jnp.sum(weights, axis=0, keepdims=True)
        o = jnp.dot(vt[:, pl.ds(0, keys)], weights.astype(bf16), preferred_element_type=f32)
        ot[0, :, here] = (o / total).astype(bf16)
        lse[0, :, here] = largest + jnp.log(total)


def attend(q, k, vt, scale):
    heads, length, hd = q.shape
    shape = jax.ShapeDtypeStruct
    return pl.pallas_call(
        functools.partial(attend_kernel, scale, length // 4),
        grid=(heads,),
        out_shape=[shape((heads, hd, length), bf16), shape((heads, 1, length), f32)],
        in_specs=[
            pl.BlockSpec((1, length, hd), lambda h: (h, 0, 0)),
            pl.BlockSpec((length, hd), lambda h: (0, 0)),
            pl.BlockSpec((hd, length), lambda h: (0, 0)),
        ],
        out_specs=[
            pl.BlockSpec((1, hd, length), lambda h: (h, 0, 0)),
            pl.BlockSpec((1, 1, length), lambda h: (h, 0, 0)),
        ],
        compiler_params=pltpu.CompilerParams(vmem_limit_bytes=32 * 2**20),
    )(q, k, vt)


def attend_back_kernel(scale, span, q, k, kt, v, do, lse, dq, dk, dv):
    @pl.when(pl.program_id(0) == 0)
    def _():
        dk[...] = jnp.zeros(dk.shape, f32)
        dv[...] = jnp.zeros(dv.shape, f32)

    for i in range(q.shape[1] // span):
        keys = pl.ds(0, (i + 1) * span)
        here = pl.ds(i * span, span)
        nt = (((1,), (1,)), ((), ()))
        s = lax.dot_general(k[keys], q[0, here], nt, preferred_element_type=f32) * scale
        key_pos = lax.broadcasted_iota(jnp.int32, s.shape, 0)
        query_pos = lax.broadcasted_iota(jnp.int32, s.shape, 1) + i * span
        probs = jnp.where(key_pos <= query_pos, jnp.exp(s - lse[0, :, here]), 0.0)
        dp = lax.dot_general(v[keys], do[here], nt, preferred_element_type=f32)
        delta = jnp.sum(probs * dp, axis=0, keepdims=True)
        ds = (probs * (dp - delta)).astype(bf16)
        dk[keys] += jnp.dot(ds, q[0, here], preferred_element_type=f32) * scale
        dv[keys] += jnp.dot(probs.astype(bf16), do[here], preferred_element_type=f32)
        part = jnp.dot(kt[:, keys], ds, preferred_element_type=f32) * scale
        dq[here] = part.T


def attend_back(q, k, v, do, lse, scale):
    heads, length, hd = q.shape
    shape = jax.ShapeDtypeStruct
    whole = pl.BlockSpec((length, hd), lambda h: (0, 0))
    column = pl.BlockSpec((length, hd), lambda h: (0, h))
    return pl.pallas_call(
        functools.partial(attend_back_kernel, scale, length // 4),
        grid=(heads,),
        out_shape=[
            shape((length, heads * hd), f32),
            shape((length, hd), f32),
            shape((length, hd), f32),
        ],
        in_specs=[
            pl.BlockSpec((1, length, hd), lambda h: (h, 0, 0)),
            whole,
            pl.BlockSpec((hd, length), lambda h: (0, 0)),
            whole,
            column,
            pl.BlockSpec((1, 1, length), lambda h: (h, 0, 0)),
        ],
        out_specs=[column, whole, whole],
        compiler_params=pltpu.CompilerParams(vmem_limit_bytes=32 * 2**20),
    )(q, k, k.T, v, do, lse)


def mm(a, b, contract, kind=f32):
    return lax.dot_general(a, b, ((contract[:1], contract[1:]), ((), ())), preferred_element_type=f32).astype(kind)


def fast_body(
    tokens,
    query_weight,
    key_weight,
    value_weight,
    output_weight,
    norm_gains,
    head_gains,
    expert_gate,
    expert_up,
    expert_down,
    routes,
    route_gates,
    cotangent,
):
    seq, width = tokens.shape[1:]
    nz = lax.axis_size("expert") // 2
    devices = lax.axis_size(("ctx", "expert"))
    length = 4 * seq
    topk = routes.shape[2]
    cap = max(2, 5 * seq * topk // (4 * devices))
    heads = HQ // 4
    wq = heads * HD
    scale = HD ** (-0.5)
    c = lax.axis_index("ctx")
    e = lax.axis_index("expert")
    k = lax.rem(e, 2)
    me = c * (2 * nz) + e
    rows_in = tokens.reshape(seq, width).astype(f32)
    rows_q = query_weight.shape[0]

    def cols(weight):
        return weight.reshape(rows_q, 4, -1).transpose(1, 0, 2)

    pack = jnp.concatenate([cols(query_weight), cols(key_weight), cols(value_weight)], axis=2)
    share = norm_gains.shape[1]
    head_share = head_gains.shape[1]
    parts = [
        routes.astype(f32).reshape(-1),
        route_gates.reshape(-1),
        norm_gains.astype(f32).reshape(-1),
        head_gains.astype(f32).reshape(-1),
    ]
    flat = jnp.concatenate(parts)
    lines = -(-flat.shape[0] // (128 * 16)) * 16
    meta = jnp.pad(flat, (0, lines * 128 - flat.shape[0])).reshape(lines, 128)
    weight, wo, toks, cots, metas = gather_first(
        nz,
        pack,
        output_weight,
        tokens.reshape(seq, width),
        cotangent.reshape(seq, width),
        meta,
    )
    weight = weight.reshape(width, -1)
    wo = wo.reshape(-1, width)
    metas = metas.reshape(devices, -1)
    n = seq * topk
    all_routes = metas[:, :n].reshape(devices, seq, topk)
    all_gates = metas[:, n : 2 * n].reshape(devices, seq, topk)
    at = 2 * n
    gains = metas[:, at : at + 2 * share].reshape(devices, 2, share).transpose(1, 0, 2)
    gains = gains.reshape(2, width)
    at += 2 * share
    head_gain = metas[:, at : at + 2 * head_share].reshape(devices, 2, head_share)
    head_gain = head_gain.transpose(1, 0, 2).reshape(2, HD)

    positions = jnp.arange(length, dtype=jnp.int32)
    normed = rms_scale(toks.reshape(length, width).astype(f32), gains[0]).astype(bf16)
    raw = mm(normed, weight, (1, 0))
    query_raw = raw[:, :wq].reshape(length, heads, HD)
    key_raw = raw[:, wq : wq + HD].reshape(length, 1, HD)
    values = raw[:, wq + HD :].astype(bf16)

    def head_prep(raw_heads, gain_vec):
        return rotate(rms_scale(raw_heads, gain_vec), positions)

    queries = head_prep(query_raw, head_gain[0]).astype(bf16).transpose(1, 0, 2)
    keys = head_prep(key_raw, head_gain[1]).astype(bf16).reshape(length, HD)
    attended, lse = attend(queries, keys, values.T, scale)
    attended = attended.reshape(wq, length)
    hidden = rows_in + fold(mm(attended, wo, (0, 0), bf16).reshape(4, seq, width), 2)
    normed_mlp = rms_scale(hidden, gains[1]).astype(bf16)

    all_rows = gather_rows(nz, True, normed_mlp, 3)

    def picks(expert):
        named = all_routes == expert.astype(f32)
        member = jnp.any(named, axis=2)
        weight_of = jnp.sum(jnp.where(named, all_gates, 0.0), axis=2)
        upto = jnp.arange(seq)[:, None] <= jnp.arange(seq)[None, :]
        rank = jnp.dot(member.astype(bf16), upto.astype(bf16), preferred_element_type=f32)
        slot = jnp.where(member, rank.astype(jnp.int32) - 1, -1)
        return slot, weight_of

    slot, weight_of = picks(me)
    slot_pair, weight_pair = picks(me + 1 - 2 * k)
    chosen = (slot[:, None, :] == jnp.arange(cap, dtype=jnp.int32)[None, :, None])
    row_gate = jnp.sum(jnp.where(chosen, weight_of[:, None, :], 0.0), axis=2)
    chosen = chosen.astype(bf16)

    def plane(a):
        a = a.reshape(4, nz, 2, seq)
        return jnp.where(k == 0, a[:, :, 0], a[:, :, 1])

    slots2 = jnp.stack([plane(slot), plane(slot_pair)], axis=-1)
    back = slots2[..., None] == jnp.arange(cap, dtype=jnp.int32)
    gate2 = jnp.stack([plane(weight_of), plane(weight_pair)], axis=-1)
    back_gate = jnp.where(back, gate2[..., None], 0.0).astype(bf16).reshape(4, nz, seq, 2 * cap)
    back_one = back.astype(bf16).reshape(4, nz, seq, 2 * cap)

    def pick(rows):
        return lax.dot_general(
            chosen, rows, (((2,), (1,)), ((0,), (0,))), preferred_element_type=f32
        ).reshape(devices * cap, width)

    gate_w, up_w, down_w = expert_gate[0], expert_up[0], expert_down[0]
    arrived = pick(all_rows).astype(bf16)
    grad_arrived = (row_gate.reshape(-1, 1) * pick(cots).astype(bf16).astype(f32)).astype(bf16)
    gate_pre = mm(arrived, gate_w, (1, 0))
    up_pre = mm(arrived, up_w, (1, 0))
    sigmoid_gate = jax.nn.sigmoid(gate_pre)
    swish_gate = gate_pre * sigmoid_gate
    activated = (swish_gate * up_pre).astype(bf16)
    produced = mm(activated, down_w, (1, 0), bf16)
    grad_act = mm(grad_arrived, down_w, (1, 1))
    grad_up_pre = (grad_act * swish_gate).astype(bf16)
    grad_gate_pre = (
        grad_act * up_pre * sigmoid_gate * (1.0 + gate_pre * (1.0 - sigmoid_gate))
    ).astype(bf16)
    grad_inputs = (mm(grad_gate_pre, gate_w, (1, 1)) + mm(grad_up_pre, up_w, (1, 1))).astype(bf16)
    grad_normed_mlp = combine(nz, grad_inputs.reshape(devices, cap, width), back_one, 4)
    mixed = hidden + combine(nz, produced.reshape(devices, cap, width), back_gate, 5)
    grad_down = mm(activated, grad_arrived, (0, 0))
    grad_gate = mm(arrived, grad_gate_pre, (0, 0))
    grad_up = mm(arrived, grad_up_pre, (0, 0))

    grad_out = cotangent.reshape(seq, width).astype(f32)
    _, norm_pull = jax.vjp(rms_scale, hidden, gains[1])
    grad_hidden_norm, grad_gain_mlp = norm_pull(grad_normed_mlp)
    grad_hidden = grad_out + grad_hidden_norm
    branch = gather_rows(nz, False, grad_hidden.astype(bf16), 6).reshape(length, width)
    grad_wo = mm(attended, branch, (1, 0), bf16)
    grad_attended = mm(branch, wo, (1, 1), bf16)
    grad_query, grad_key, grad_value = attend_back(
        queries, keys, values, grad_attended, lse, scale
    )
    _, pull_query = jax.vjp(head_prep, query_raw, head_gain[0])
    grad_query_raw, grad_query_gain = pull_query(grad_query.reshape(length, heads, HD))
    _, pull_key = jax.vjp(head_prep, key_raw, head_gain[1])
    grad_key_raw, grad_key_gain = pull_key(grad_key.reshape(length, 1, HD))
    low = jnp.concatenate(
        [
            grad_query_raw.reshape(length, wq).astype(bf16),
            grad_key_raw.reshape(length, HD).astype(bf16),
            grad_value.astype(bf16),
        ],
        axis=1,
    )
    grad_weight = mm(normed, low, (0, 0), bf16)
    grad_normed = fold(mm(low, weight, (1, 1), bf16).reshape(4, seq, width), 7)
    _, pull_attn = jax.vjp(rms_scale, rows_in, gains[0])
    grad_rows_norm, grad_gain_attn = pull_attn(grad_normed)
    grad_input = grad_hidden + grad_rows_norm
    gain_parts = jnp.concatenate(
        [grad_gain_attn, grad_gain_mlp, grad_query_gain, grad_key_gain]
    ).reshape(-1, 128)
    extra = -gain_parts.shape[0] % 16
    gain_parts = jnp.pad(gain_parts, ((0, extra), (0, 0)))
    sum_q, sum_k, sum_v, sum_o, all_gain_parts = reduce_last(
        nz,
        grad_weight.reshape(4, 2 * nz, rows_q, -1),
        grad_wo.reshape(2 * nz, -1, width),
        gain_parts,
    )
    gain_sums = jnp.sum(all_gain_parts, axis=0).reshape(-1)
    norm_sums = gain_sums[: 2 * width].reshape(2, width)
    head_sums = gain_sums[2 * width : 2 * width + 2 * HD].reshape(2, HD)
    return (
        mixed.astype(bf16).reshape(tokens.shape),
        grad_input.astype(bf16).reshape(tokens.shape),
        sum_q,
        sum_k,
        sum_v,
        sum_o,
        lax.dynamic_slice_in_dim(norm_sums, me * share, share, 1),
        lax.dynamic_slice_in_dim(head_sums, me * head_share, head_share, 1),
        grad_gate[None],
        grad_up[None],
        grad_down[None],
    )


def solution(mesh):
    small = mesh.shape["ctx"] == HK and mesh.shape["expert"] % 2 == 0 and mesh.size <= 32
    return jax.shard_map(
        fast_body if small else body,
        mesh=mesh,
        in_specs=(
            P("expert", "ctx", None),
            P(("ctx", "expert"), None),
            P(("ctx", "expert"), None),
            P(("ctx", "expert"), None),
            P(("ctx", "expert"), None),
            P(None, ("ctx", "expert")),
            P(None, ("ctx", "expert")),
            P(("ctx", "expert"), None, None),
            P(("ctx", "expert"), None, None),
            P(("ctx", "expert"), None, None),
            P("expert", "ctx", None),
            P("expert", "ctx", None),
            P("expert", "ctx", None),
        ),
        out_specs=(
            P("expert", "ctx", None),
            P("expert", "ctx", None),
            P(("ctx", "expert"), None),
            P(("ctx", "expert"), None),
            P(("ctx", "expert"), None),
            P(("ctx", "expert"), None),
            P(None, ("ctx", "expert")),
            P(None, ("ctx", "expert")),
            P(("ctx", "expert"), None, None),
            P(("ctx", "expert"), None, None),
            P(("ctx", "expert"), None, None),
        ),
        check_vma=False,
    )
```

```python
import functools

import jax
import jax.numpy as jnp
from jax import lax
from jax.experimental import pallas as pl
from jax.experimental.pallas import tpu as pltpu
from jax.sharding import PartitionSpec as P

HQ = 32
HK = 4
HD = 128


epsilon = 1e-06
rope_base = 1000000.0
masked_value = -1e30


def rms_scale(values, scale_gain):
    return (
        values * lax.rsqrt(jnp.mean(values * values, axis=-1, keepdims=True) + epsilon) * scale_gain
    )


def rotate(values, positions):
    half_size = values.shape[-1] // 2
    frequency = rope_base ** (-jnp.arange(half_size, dtype=jnp.float32) / half_size)
    angles = positions.astype(jnp.float32)[:, None] * frequency[None, :]
    cosine = jnp.cos(angles)[:, None, :]
    sine_part = jnp.sin(angles)[:, None, :]
    first_half = values[..., :half_size]
    second_half = values[..., half_size:]
    return jnp.concatenate(
        [
            first_half * cosine - second_half * sine_part,
            second_half * cosine + first_half * sine_part,
        ],
        axis=-1,
    )


def body(
    tokens,
    query_weight,
    key_weight,
    value_weight,
    output_weight,
    norm_gains,
    head_gains,
    expert_gate,
    expert_up,
    expert_down,
    routes,
    route_gates,
    cotangent,
):
    seq_rows = tokens.shape[1]
    width = tokens.shape[2]
    groups = HQ // HK
    kv_width = HK * HD
    scale = HD ** (-0.5)
    positions = lax.axis_index("ctx") * seq_rows + jnp.arange(seq_rows, dtype=jnp.int32)
    last_pos = lax.axis_index("ctx") * seq_rows + seq_rows - 1
    rows_in = tokens.reshape(seq_rows, width).astype(jnp.float32)
    full_q, full_k, full_v, full_o, gains, head_gain = (
        lax.all_gather(query_weight, ("ctx", "expert"), axis=0, tiled=True),
        lax.all_gather(key_weight, ("ctx", "expert"), axis=0, tiled=True),
        lax.all_gather(value_weight, ("ctx", "expert"), axis=0, tiled=True),
        lax.all_gather(output_weight, ("ctx", "expert"), axis=0, tiled=True),
        lax.all_gather(norm_gains, ("ctx", "expert"), axis=1, tiled=True),
        lax.all_gather(head_gains, ("ctx", "expert"), axis=1, tiled=True),
    )

    def head_prep(raw_heads, gain_vec):
        return rotate(rms_scale(raw_heads, gain_vec), positions)

    normed = rms_scale(rows_in, gains[0].astype(jnp.float32)).astype(jnp.bfloat16)
    query_raw = jnp.dot(normed, full_q, preferred_element_type=jnp.float32).reshape(
        seq_rows, HQ, HD
    )
    key_raw = jnp.dot(normed, full_k, preferred_element_type=jnp.float32).reshape(seq_rows, HK, HD)
    value_rows = jnp.dot(normed, full_v, preferred_element_type=jnp.float32).astype(jnp.bfloat16)
    query_gain = head_gain[0].astype(jnp.float32)
    key_gain = head_gain[1].astype(jnp.float32)
    queries = head_prep(query_raw, query_gain).astype(jnp.bfloat16)
    keys_rot = head_prep(key_raw, key_gain).astype(jnp.bfloat16)
    kv_rows = jnp.concatenate([keys_rot.reshape(seq_rows, kv_width), value_rows], axis=1)
    grouped = queries.reshape(seq_rows, HK, groups, HD)

    def scores_for(key_block, base_row):
        scores = (
            jnp.einsum("qhgd,khd->hgqk", grouped, key_block, preferred_element_type=jnp.float32)
            * scale
        )
        key_pos = base_row + jnp.arange(key_block.shape[0], dtype=jnp.int32)
        allowed = key_pos[None, :] <= positions[:, None]
        return (scores, allowed)

    start_state = (
        jnp.full((HK, groups, seq_rows), masked_value, jnp.float32),
        jnp.zeros((HK, groups, seq_rows), jnp.float32),
        jnp.zeros((HK, groups, seq_rows, HD), jnp.float32),
    )
    shard_rows = lax.all_gather(kv_rows, "ctx", axis=0, tiled=True)
    blocks = shard_rows.reshape(shard_rows.shape[0] // seq_rows, seq_rows, 2 * kv_width)

    def step(state_now, element):
        block_index, block_rows = element
        base_row = block_index * seq_rows

        def step_visit(state_in):
            largest, total_sum, accum = state_in
            key_block = block_rows[:, :kv_width].reshape(seq_rows, HK, HD)
            value_block = block_rows[:, kv_width:].reshape(seq_rows, HK, HD)
            scores, allowed = scores_for(key_block, base_row)
            scores = jnp.where(allowed, scores, masked_value)
            new_largest = jnp.maximum(largest, jnp.max(scores, axis=-1))
            weights = jnp.where(allowed, jnp.exp(scores - new_largest[..., None]), 0.0)
            factor = jnp.exp(largest - new_largest)
            total_sum = total_sum * factor + jnp.sum(weights, axis=-1)
            accum = accum * factor[..., None] + jnp.einsum(
                "hgqk,khd->hgqd",
                weights.astype(jnp.bfloat16),
                value_block,
                preferred_element_type=jnp.float32,
            )
            return (new_largest, total_sum, accum)

        def step_skip(state_in):
            return state_in

        return (lax.cond(base_row <= last_pos, step_visit, step_skip, state_now), None)

    final_state, unused = lax.scan(
        step, start_state, (jnp.arange(blocks.shape[0], dtype=jnp.int32), blocks)
    )
    largest, total_sum, accum = final_state
    attended = (accum / total_sum[..., None]).transpose(2, 0, 1, 3).reshape(seq_rows, HQ * HD)
    log_total = largest + jnp.log(total_sum)
    attended_low = attended.astype(jnp.bfloat16)
    hidden = rows_in + jnp.dot(attended_low, full_o, preferred_element_type=jnp.float32)
    normed_mlp = rms_scale(hidden, gains[1].astype(jnp.float32)).astype(jnp.bfloat16)
    devices = lax.axis_size(("ctx", "expert"))
    local_experts = expert_gate.shape[0]
    experts = local_experts * devices
    topk = routes.shape[2]
    capacity = max(2, 5 * seq_rows * topk // (4 * experts))
    route_ids = routes.reshape(seq_rows * topk)
    onehot = (route_ids[:, None] == jnp.arange(experts, dtype=jnp.int32)[None, :]).astype(jnp.int32)
    slots = jnp.sum((jnp.cumsum(onehot, axis=0) - 1) * onehot, axis=1)
    target = route_ids * capacity + slots
    owner_row = jnp.arange(seq_rows * topk, dtype=jnp.int32) // topk
    gate_rows = route_gates.reshape(seq_rows, topk)

    def to_slots(row_block):
        buffer = (
            jnp.zeros((experts * capacity, row_block.shape[1]), row_block.dtype)
            .at[target]
            .set(row_block)
        )
        return buffer.reshape(devices, local_experts * capacity, row_block.shape[1])

    def to_experts(arrived):
        return (
            arrived.reshape(devices, local_experts, capacity, -1)
            .transpose(1, 0, 2, 3)
            .reshape(local_experts, devices * capacity, -1)
        )

    def from_experts(expert_rows):
        return (
            expert_rows.reshape(local_experts, devices, capacity, -1)
            .transpose(1, 0, 2, 3)
            .reshape(devices, local_experts * capacity, -1)
        )

    arrived = to_experts(
        lax.all_to_all(
            to_slots(normed_mlp[owner_row]),
            ("ctx", "expert"),
            split_axis=0,
            concat_axis=0,
            tiled=True,
        )
    )
    gate_pre = jnp.einsum("erd,edf->erf", arrived, expert_gate, preferred_element_type=jnp.float32)
    up_pre = jnp.einsum("erd,edf->erf", arrived, expert_up, preferred_element_type=jnp.float32)
    sigmoid_gate = jax.nn.sigmoid(gate_pre)
    swish_gate = gate_pre * sigmoid_gate
    activated = (swish_gate * up_pre).astype(jnp.bfloat16)
    produced = jnp.einsum(
        "erf,efd->erd", activated, expert_down, preferred_element_type=jnp.float32
    ).astype(jnp.bfloat16)
    returned = lax.all_to_all(
        from_experts(produced), ("ctx", "expert"), split_axis=0, concat_axis=0, tiled=True
    ).reshape(experts * capacity, width)
    expert_out = returned[target].astype(jnp.float32).reshape(seq_rows, topk, width)
    mixed = hidden + jnp.sum(gate_rows[:, :, None] * expert_out, axis=1)
    full_q, full_k, full_v, full_o, gains, head_gain = (
        lax.all_gather(query_weight, ("ctx", "expert"), axis=0, tiled=True),
        lax.all_gather(key_weight, ("ctx", "expert"), axis=0, tiled=True),
        lax.all_gather(value_weight, ("ctx", "expert"), axis=0, tiled=True),
        lax.all_gather(output_weight, ("ctx", "expert"), axis=0, tiled=True),
        lax.all_gather(norm_gains, ("ctx", "expert"), axis=1, tiled=True),
        lax.all_gather(head_gains, ("ctx", "expert"), axis=1, tiled=True),
    )
    grad_out = cotangent.reshape(seq_rows, width).astype(jnp.float32)
    grad_rows = (
        (gate_rows[:, :, None] * grad_out[:, None, :])
        .astype(jnp.bfloat16)
        .reshape(seq_rows * topk, width)
    )
    grad_arrived = to_experts(
        lax.all_to_all(
            to_slots(grad_rows), ("ctx", "expert"), split_axis=0, concat_axis=0, tiled=True
        )
    )
    grad_down = jnp.einsum(
        "erf,erd->efd", activated, grad_arrived, preferred_element_type=jnp.float32
    )
    grad_act = jnp.einsum(
        "erd,efd->erf", grad_arrived, expert_down, preferred_element_type=jnp.float32
    )
    grad_up_pre = (grad_act * swish_gate).astype(jnp.bfloat16)
    grad_gate_pre = (
        grad_act * up_pre * sigmoid_gate * (1.0 + gate_pre * (1.0 - sigmoid_gate))
    ).astype(jnp.bfloat16)
    grad_gate = jnp.einsum(
        "erd,erf->edf", arrived, grad_gate_pre, preferred_element_type=jnp.float32
    )
    grad_up = jnp.einsum("erd,erf->edf", arrived, grad_up_pre, preferred_element_type=jnp.float32)
    grad_inputs = jnp.einsum(
        "erf,edf->erd", grad_gate_pre, expert_gate, preferred_element_type=jnp.float32
    )
    grad_inputs = (
        grad_inputs
        + jnp.einsum("erf,edf->erd", grad_up_pre, expert_up, preferred_element_type=jnp.float32)
    ).astype(jnp.bfloat16)
    grad_back = lax.all_to_all(
        from_experts(grad_inputs), ("ctx", "expert"), split_axis=0, concat_axis=0, tiled=True
    ).reshape(experts * capacity, width)
    grad_normed_mlp = jnp.sum(
        grad_back[target].astype(jnp.float32).reshape(seq_rows, topk, width), axis=1
    )
    unused_norm, norm_pull = jax.vjp(rms_scale, hidden, gains[1].astype(jnp.float32))
    grad_hidden_norm, grad_gain_mlp = norm_pull(grad_normed_mlp)
    grad_hidden = grad_out + grad_hidden_norm
    grad_branch = grad_hidden.astype(jnp.bfloat16)
    grad_wo = jnp.einsum("qa,qd->ad", attended_low, grad_branch, preferred_element_type=jnp.float32)
    grad_attended = jnp.einsum(
        "qd,ad->qa", grad_branch, full_o, preferred_element_type=jnp.float32
    ).astype(jnp.bfloat16)
    all_kv = lax.all_gather(kv_rows, "ctx", axis=0, tiled=True)
    grad_grouped = grad_attended.reshape(seq_rows, HK, groups, HD)
    delta = jnp.einsum(
        "qhgd,qhgd->hgq",
        grad_grouped.astype(jnp.float32),
        attended.reshape(seq_rows, HK, groups, HD),
    )
    kv_blocks = all_kv.reshape(-1, seq_rows, 2 * kv_width)

    def back_step(grad_query, element):
        block_index, block_rows = element
        base_row = block_index * seq_rows

        def back_visit(grad_in):
            key_block = block_rows[:, :kv_width].reshape(seq_rows, HK, HD)
            value_block = block_rows[:, kv_width:].reshape(seq_rows, HK, HD)
            scores, allowed = scores_for(key_block, base_row)
            probs = jnp.where(allowed, jnp.exp(scores - log_total[..., None]), 0.0)
            grad_probs = jnp.einsum(
                "qhgd,khd->hgqk", grad_grouped, value_block, preferred_element_type=jnp.float32
            )
            grad_scores = (probs * (grad_probs - delta[..., None])).astype(jnp.bfloat16)
            grad_next = grad_in + jnp.einsum(
                "hgqk,khd->qhgd", grad_scores, key_block, preferred_element_type=jnp.float32
            )
            grad_keys = (
                jnp.einsum(
                    "hgqk,qhgd->khd", grad_scores, grouped, preferred_element_type=jnp.float32
                )
                * scale
            )
            grad_values = jnp.einsum(
                "hgqk,qhgd->khd",
                probs.astype(jnp.bfloat16),
                grad_grouped,
                preferred_element_type=jnp.float32,
            )
            joined = jnp.concatenate(
                [grad_keys.reshape(seq_rows, kv_width), grad_values.reshape(seq_rows, kv_width)],
                axis=1,
            )
            return (grad_next, joined)

        def back_skip(grad_in):
            return (grad_in, jnp.zeros((seq_rows, 2 * kv_width), jnp.float32))

        return lax.cond(base_row <= last_pos, back_visit, back_skip, grad_query)

    grad_query, grad_kv_terms = lax.scan(
        back_step,
        jnp.zeros((seq_rows, HK, groups, HD), jnp.float32),
        (jnp.arange(kv_blocks.shape[0], dtype=jnp.int32), kv_blocks),
    )
    grad_query = grad_query * scale
    grad_kv = lax.psum_scatter(
        grad_kv_terms.reshape(-1, 2 * kv_width).astype(jnp.bfloat16),
        "ctx",
        scatter_dimension=0,
        tiled=True,
    ).astype(jnp.float32)
    unused_query, pull_query = jax.vjp(head_prep, query_raw, query_gain)
    grad_query_raw, grad_query_gain = pull_query(grad_query.reshape(seq_rows, HQ, HD))
    unused_key, pull_key = jax.vjp(head_prep, key_raw, key_gain)
    grad_key_raw, grad_key_gain = pull_key(grad_kv[:, :kv_width].reshape(seq_rows, HK, HD))
    grad_q_low = grad_query_raw.reshape(seq_rows, HQ * HD).astype(jnp.bfloat16)
    grad_k_low = grad_key_raw.reshape(seq_rows, kv_width).astype(jnp.bfloat16)
    grad_v_low = grad_kv[:, kv_width:].astype(jnp.bfloat16)
    grad_wq = jnp.einsum("qd,qa->da", normed, grad_q_low, preferred_element_type=jnp.float32)
    grad_wk = jnp.einsum("qd,qa->da", normed, grad_k_low, preferred_element_type=jnp.float32)
    grad_wv = jnp.einsum("qd,qa->da", normed, grad_v_low, preferred_element_type=jnp.float32)
    grad_normed = jnp.einsum("qa,da->qd", grad_q_low, full_q, preferred_element_type=jnp.float32)
    grad_normed = grad_normed + jnp.einsum(
        "qa,da->qd", grad_k_low, full_k, preferred_element_type=jnp.float32
    )
    grad_normed = grad_normed + jnp.einsum(
        "qa,da->qd", grad_v_low, full_v, preferred_element_type=jnp.float32
    )
    unused_attn, pull_attn = jax.vjp(rms_scale, rows_in, gains[0].astype(jnp.float32))
    grad_rows_norm, grad_gain_attn = pull_attn(grad_normed)
    grad_input = grad_hidden + grad_rows_norm
    gain_grads = jnp.stack([grad_gain_attn, grad_gain_mlp])
    head_grads = jnp.stack([grad_query_gain, grad_key_gain])
    sum_q, sum_k, sum_v, sum_o, sum_gain, sum_head = (
        lax.psum_scatter(grad_wq, ("ctx", "expert"), scatter_dimension=0, tiled=True),
        lax.psum_scatter(grad_wk, ("ctx", "expert"), scatter_dimension=0, tiled=True),
        lax.psum_scatter(grad_wv, ("ctx", "expert"), scatter_dimension=0, tiled=True),
        lax.psum_scatter(grad_wo, ("ctx", "expert"), scatter_dimension=0, tiled=True),
        lax.psum_scatter(gain_grads, ("ctx", "expert"), scatter_dimension=1, tiled=True),
        lax.psum_scatter(head_grads, ("ctx", "expert"), scatter_dimension=1, tiled=True),
    )
    return (
        mixed.astype(jnp.bfloat16).reshape(tokens.shape),
        grad_input.astype(jnp.bfloat16).reshape(tokens.shape),
        sum_q,
        sum_k,
        sum_v,
        sum_o,
        sum_gain,
        sum_head,
        grad_gate,
        grad_up,
        grad_down,
    )


MESH = pl.DeviceIdType.MESH
VMEM_BYTES = 58 * 2**20
ANY = pl.BlockSpec(memory_space=pl.ANY)
IN_VMEM = pl.BlockSpec(memory_space=pltpu.VMEM)
f32, bf16 = jnp.float32, jnp.bfloat16


class Place:
    def __init__(self):
        self.c = lax.axis_index("ctx")
        self.e = lax.axis_index("expert")
        self.k = lax.rem(self.e, 2)
        self.z = lax.div(self.e, 2)
        self.cx = self.c + 1 - 2 * lax.rem(self.c, 2)
        self.cy = lax.rem(self.c + 2, 4)
        self.cd = lax.rem(self.cx + 2, 4)
        self.dx = (self.cx, self.e)
        self.dy = (self.cy, self.e)
        self.dd = (self.cd, self.e)
        self.pair = (self.c, self.e + 1 - 2 * self.k)
        self.up = (self.c, self.e + 2)
        self.down = (self.c, self.e - 2)


def greet(p, nz, line=True, pair=True, diagonal=False):
    barrier = pltpu.get_barrier_semaphore()

    def tell(device):
        pl.semaphore_signal(barrier, inc=1, device_id=device, device_id_type=MESH)

    friends = [p.dx, p.dy] + [p.pair] * pair + [p.dd] * diagonal
    for device in friends:
        tell(device)
    count = len(friends)
    if line:
        for there, device in ((p.z > 0, p.down), (p.z < nz - 1, p.up)):

            @pl.when(there)
            def _():
                tell(device)

            count = count + there.astype(jnp.int32)
    pl.semaphore_wait(barrier, count)


def remote(src, dst, send, recv, device):
    return pltpu.make_async_remote_copy(
        src_ref=src,
        dst_ref=dst,
        send_sem=send,
        recv_sem=recv,
        device_id=device,
        device_id_type=MESH,
    )


def far_first(nz, z):
    return sorted(range(nz), key=lambda to: (-abs(to - z), to))


def near_first(nz, z):
    return sorted(range(nz), key=lambda to: (abs(to - z), to))


def pick_order(p, nz, order=far_first):
    tables = [order(nz, z) for z in range(nz)]
    return [sum(jnp.where(p.z == z, tables[z][i], 0) for z in range(nz)) for i in range(nz)]


class Spread:
    def __init__(self, p, nz, mine, block, half, send, recv, line=True, side=True, pair=True):
        self.p, self.nz, self.mine, self.block, self.half = p, nz, mine, block, half
        self.send, self.recv = send, recv
        self.line, self.side, self.pair = line, side, pair
        self.order = pick_order(p, nz, near_first) if line else [p.z]

    def ref(self, c, z, k, h=None):
        whole = self.block(c, z, k)
        return whole if h is None else whole.at[pl.ds(h * self.half, self.half)]

    def copy(self, kind, z, own=False):
        p = self.p
        at = functools.partial(self.ref, z=z, k=p.k)
        src, i, j, device = {
            "x": lambda: (at(p.c), 0, 1, p.dx),
            "y": lambda: (at(p.c), 1, 2, p.dy),
            "up": lambda: (at(p.c), 2, 0, p.up),
            "down": lambda: (at(p.c), 3, 0, p.down),
            "via_y": lambda: (at(p.cx, h=0), 4, 3, p.dy),
            "via_x": lambda: (at(p.cy, h=1), 5, 4, p.dx),
            "pair0": lambda: (at(p.c), 6, 5, p.pair),
            "pair1": lambda: (at(p.cx), 7, 6, p.pair),
            "pair2": lambda: (at(p.cy), 8, 7, p.pair),
            "pair3": lambda: (at(p.cd, h=0), 9, 8, p.pair),
            "pair4": lambda: (at(p.cd, h=1), 10, 9, p.pair),
        }[kind]()
        return remote(
            self.mine if own else src, src, self.send.at[z, i], self.recv.at[z, j], device
        )

    def got(self, j, z):
        p = self.p
        k = p.k if j < 5 else 1 - p.k
        c, h = ((p.c, None), (p.cx, None), (p.cy, None), (p.cd, 0), (p.cd, 1))[j % 5]
        ref = self.ref(c, z, k, h)
        remote(ref, ref, self.send.at[z, 0], self.recv.at[z, j], p.pair).wait_recv()

    def each(self, far, act):
        if far == 0:
            act(self.p.z, 0)
            return
        for way in (-1, 1):
            z = self.p.z + way * far

            @pl.when((z >= 0) & (z < self.nz))
            def _():
                act(z, way)

    def onward(self, z, way, act):
        if self.line and way >= 0:

            @pl.when(self.p.z > 0)
            def _():
                act(self.copy("down", z, way == 0))

        if self.line and way <= 0:

            @pl.when(self.p.z < self.nz - 1)
            def _():
                act(self.copy("up", z, way == 0))

    def direct(self):
        return ["x", "y"] * self.side + ["pair0"] * self.pair

    def along(self, far):
        def act(z, way):
            if way:
                self.got(0, z)
            self.onward(z, way, lambda copy: copy.start())
            for kind in self.direct():
                self.copy(kind, z, way == 0).start()

        self.each(far, act)

    def beside(self, z):
        for j, kinds in ((1, ["via_y", "pair1"]), (2, ["via_x", "pair2"])):
            self.got(j, z)
            for kind in kinds[: 1 + self.pair]:
                self.copy(kind, z).start()

    def across(self, z):
        for j, kind in ((3, "pair3"), (4, "pair4")):
            self.got(j, z)
            if self.pair:
                self.copy(kind, z).start()

    def from_pair(self, z):
        if self.pair:
            for j in range(5, 10 if self.side else 6):
                self.got(j, z)

    def step(self, i):
        reach = self.nz if self.line else 1
        if i < reach:
            self.along(i)
        if self.side and 1 <= i <= reach:
            self.beside(self.order[i - 1])
        if self.side and 2 <= i <= reach + 1:
            self.across(self.order[i - 2])

    def finish(self, pair=True):
        def act(z, way):
            if pair:
                self.from_pair(z)
            self.onward(z, way, lambda copy: copy.wait_send())
            for kind in self.direct():
                self.copy(kind, z, way == 0).wait_send()
            if self.side:
                for kind in ["via_y", "via_x"] + ["pair1", "pair2", "pair3", "pair4"] * self.pair:
                    self.copy(kind, z).wait_send()

        for far in range(self.nz if self.line else 1):
            self.each(far, act)


def by_device(ref, nz):
    return lambda c, z, k: ref.at[c * (2 * nz) + z * 2 + k]


def spread_sems(nz):
    return [pltpu.SemaphoreType.DMA((nz, 11)), pltpu.SemaphoreType.DMA((nz, 10))]


def first_kernel(nz, pack, wo, tok, cot, meta, packs, wos, toks, cots, metas, *sems):
    pair_sems, (a_send, a_recv, local) = sems[:10], sems[10:]
    p = Place()
    greet(p, nz, diagonal=True)
    own = [
        pltpu.make_async_copy(src, dst, local.at[i])
        for i, (src, dst) in enumerate(
            (
                (pack.at[p.c], packs.at[p.c, p.e]),
                (wo, wos.at[p.e]),
                (tok, toks.at[p.c]),
                (cot, cots.at[p.c * (2 * nz) + p.e]),
                (meta, metas.at[p.c * (2 * nz) + p.e]),
            )
        )
    ]
    for copy in own:
        copy.start()
    swaps = [
        remote(pack.at[c], packs.at[p.c, p.e], a_send.at[i], a_recv.at[i], device)
        for i, (c, device) in enumerate(((p.cx, p.dx), (p.cy, p.dy), (p.cd, p.dd)))
    ]
    for copy in swaps:
        copy.start()
    s = lambda i: (pair_sems[2 * i], pair_sems[2 * i + 1])
    j_tok = Spread(p, nz, tok, lambda c, z, k: toks.at[c], tok.shape[0] // 2, *s(0), False, True, False)
    j_meta = Spread(p, nz, meta, by_device(metas, nz), meta.shape[0] // 2, *s(1))
    j_cot = Spread(p, nz, cot, by_device(cots, nz), cot.shape[0] // 2, *s(2))
    j_wo = Spread(p, nz, wo, lambda c, z, k: wos.at[z * 2 + k], 0, *s(3), True, False, True)
    own_pack = packs.at[:, p.e]
    j_pack = Spread(
        p, nz, own_pack, lambda c, z, k: packs.at[:, z * 2 + k], 0, *s(4), True, False, True
    )
    j_tok.step(0)
    j_meta.step(0)
    for i, c in enumerate((p.cx, p.cy, p.cd)):
        ref = packs.at[c, p.e]
        remote(ref, ref, a_send.at[i], a_recv.at[i], p.dx).wait_recv()
    own[0].wait()
    j_pack.step(0)
    j_wo.step(0)
    j_cot.step(0)
    for far in range(1, nz + 2):
        for job in (j_tok, j_meta, j_pack, j_wo, j_cot):
            job.step(far)
    for copy in own[1:]:
        copy.wait()
    for copy in swaps:
        copy.wait_send()
    for job in (j_tok, j_meta, j_pack, j_wo, j_cot):
        job.finish()


def gather_first(nz, pack, wo, tok, cot, meta):
    blocks = 8 * nz
    shape = jax.ShapeDtypeStruct
    return pl.pallas_call(
        functools.partial(first_kernel, nz),
        out_shape=[
            shape((4, 2 * nz) + pack.shape[1:], pack.dtype),
            shape((2 * nz,) + wo.shape, wo.dtype),
            shape((4,) + tok.shape, tok.dtype),
            shape((blocks,) + cot.shape, cot.dtype),
            shape((blocks,) + meta.shape, meta.dtype),
        ],
        in_specs=[ANY] * 5,
        out_specs=[ANY] * 5,
        scratch_shapes=spread_sems(nz) * 5 + [pltpu.SemaphoreType.DMA((n,)) for n in (3, 3, 5)],
        compiler_params=pltpu.CompilerParams(collective_id=1, has_side_effects=True),
    )(pack, wo, tok, cot, meta)


def spread_kernel(nz, everywhere, mine, out, send, recv, local):
    p = Place()
    greet(p, nz, line=everywhere, pair=everywhere)
    block = by_device(out, nz) if everywhere else (lambda c, z, k: out.at[c])
    keep = pltpu.make_async_copy(mine, block(p.c, p.z, p.k), local)
    keep.start()
    job = Spread(
        p, nz, mine, block, mine.shape[0] // 2, send, recv, everywhere, True, everywhere
    )
    for far in range(nz + 2 if everywhere else 3):
        job.step(far)
    keep.wait()
    job.finish()


def gather_rows(nz, everywhere, mine, collective_id):
    blocks = 8 * nz if everywhere else 4
    return pl.pallas_call(
        functools.partial(spread_kernel, nz, everywhere),
        out_shape=jax.ShapeDtypeStruct((blocks,) + mine.shape, mine.dtype),
        in_specs=[ANY],
        out_specs=ANY,
        scratch_shapes=spread_sems(nz) + [pltpu.SemaphoreType.DMA],
        compiler_params=pltpu.CompilerParams(collective_id=collective_id, has_side_effects=True),
    )(mine)


def combine_kernel(nz, cap, rows, slots, gates, out, rbuf, w, sd, sx, sy, sz, h0, h1, bx, by, bz, *sems):
    pair_send, pair_recv, load, s_h0, s_h1, s_x, s_y, s_z, r_h0, r_h1, r_x, r_y, r_z = sems
    p = Place()
    order = pick_order(p, nz)
    seq = w.shape[2]
    half = seq // 2
    width = rbuf.shape[3]
    names = lax.broadcasted_iota(jnp.int32, (cap, seq), 0)
    tile = min(512, width)

    @pl.when(p.z == 0)
    def _():
        bz[pl.ds(0, nz)] = jnp.zeros((nz,) + bz.shape[1:], bz.dtype)

    @pl.when(p.z == nz - 1)
    def _():
        bz[pl.ds(0, nz - 1)] = jnp.zeros((nz - 1,) + bz.shape[1:], bz.dtype)
        bz[nz] = jnp.zeros(bz.shape[1:], bz.dtype)

    greet(p, nz)
    rel = (p.cd, p.cx, p.cy, p.c)

    def pair_copy(c, z):
        other = c * (2 * nz) + z * 2 + 1 - p.k
        return remote(
            rows.at[other],
            rbuf.at[c, z, pl.ds(cap, cap)],
            pair_send.at[c, z],
            pair_recv.at[c, z],
            p.pair,
        )

    def load_copy(c, z):
        return pltpu.make_async_copy(
            rows.at[c * (2 * nz) + z * 2 + p.k], rbuf.at[c, z, pl.ds(0, cap)], load.at[c, z]
        )

    for z in order:
        for c in rel:
            load_copy(c, z).start()
            pair_copy(c, z).start()

    def ready(c, z):
        b = c * (2 * nz) + z * 2 + p.k
        both = [jnp.where(names == slots[n, b], gates[n, b], 0.0) for n in (0, 1)]
        w[c, z] = jnp.concatenate(both, axis=0).T.astype(bf16)
        load_copy(c, z).wait()
        pair_copy(c, z).wait_recv()

    def fill(c, z, low, high, store):
        for t in range(width // tile):
            cols = pl.ds(t * tile, tile)
            total = jnp.dot(w[c, z], rbuf[c, z, :, cols], preferred_element_type=f32)
            for first, adds in ((0, low), (half, high)):
                part = total[first : first + half]
                for ref, start in adds:
                    part = part + ref[pl.ds(start, half), cols].astype(f32)
                store(pl.ds(first, half), cols, part)

    def into(buf, z):
        def store(lines, cols, total):
            buf[z, lines, cols] = total.astype(buf.dtype)

        return store

    def copy_h0(z):
        return remote(sd.at[z, pl.ds(0, half)], h0.at[z], s_h0.at[z], r_h0.at[z], p.dx)

    def copy_h1(z):
        return remote(sd.at[z, pl.ds(half, half)], h1.at[z], s_h1.at[z], r_h1.at[z], p.dy)

    def copy_x(z):
        return remote(sx.at[z], bx.at[z], s_x.at[z], r_x.at[z], p.dx)

    def copy_y(z):
        return remote(sy.at[z], by.at[z], s_y.at[z], r_y.at[z], p.dy)

    def copy_up(z):
        return remote(sz.at[z], bz.at[z], s_z.at[z], r_z.at[z], p.up)

    def copy_down(z):
        slot = jnp.where(z == p.z - 1, nz, z)
        return remote(sz.at[z], bz.at[slot], s_z.at[z], r_z.at[slot], p.down)

    def line_recv(slot):
        remote(bz.at[slot], bz.at[slot], s_z.at[0], r_z.at[slot], p.pair).wait_recv()

    def diagonal(z):
        ready(p.cd, z)
        fill(p.cd, z, [], [], into(sd, z))
        copy_h0(z).start()
        copy_h1(z).start()

    def sides(z):
        ready(p.cx, z)
        copy_h1(z).wait_recv()
        fill(p.cx, z, [], [(h1.at[z], 0)], into(sx, z))
        copy_x(z).start()
        ready(p.cy, z)
        copy_h0(z).wait_recv()
        fill(p.cy, z, [(h0.at[z], 0)], [], into(sy, z))
        copy_y(z).start()

    def mine(z, last):
        ready(p.c, z)
        copy_x(z).wait_recv()
        copy_y(z).wait_recv()
        arrived = [bx.at[z], by.at[z], bz.at[z]]
        if last:

            @pl.when(p.z > 0)
            def _():
                line_recv(z)

            @pl.when(p.z < nz - 1)
            def _():
                line_recv(nz)

            def store(lines, cols, total):
                out[lines, cols] = total

            arrived.append(bz.at[nz])
        else:

            @pl.when(((z > p.z) & (p.z > 0)) | ((z < p.z) & (p.z < nz - 1)))
            def _():
                line_recv(z)

            store = into(sz, z)
        fill(
            p.c, z, [(ref, 0) for ref in arrived], [(ref, half) for ref in arrived], store
        )
        if not last:

            @pl.when(z > p.z)
            def _():
                copy_up(z).start()

            @pl.when(z < p.z)
            def _():
                copy_down(z).start()

    diagonal(order[0])
    if nz > 1:
        diagonal(order[1])
    for i in range(nz):
        sides(order[i])
        if i + 2 < nz:
            diagonal(order[i + 2])
        if i > 0:
            mine(order[i - 1], False)
    mine(order[nz - 1], True)

    for i, z in enumerate(order):
        for c in rel:
            pair_copy(c, z).wait_send()
        for copy in (copy_h0(z), copy_h1(z), copy_x(z), copy_y(z)):
            copy.wait_send()
        if i < nz - 1:
            copy_up(z).wait_send()


def combine(nz, rows, slots, gates, collective_id):
    blocks, cap, width = rows.shape
    seq = slots.shape[3]
    dma = pltpu.SemaphoreType.DMA
    buf = lambda n, r: pltpu.VMEM((n, r, width), bf16)
    return pl.pallas_call(
        functools.partial(combine_kernel, nz, cap),
        out_shape=jax.ShapeDtypeStruct((seq, width), f32),
        in_specs=[ANY, IN_VMEM, IN_VMEM],
        out_specs=IN_VMEM,
        scratch_shapes=[
            pltpu.VMEM((4, nz, 2 * cap, width), bf16),
            pltpu.VMEM((4, nz, seq, 2 * cap), bf16),
        ]
        + [buf(nz, seq)] * 4
        + [buf(nz, seq // 2)] * 2
        + [buf(nz, seq)] * 2
        + [buf(nz + 1, seq)]
        + [dma((4, nz))] * 3
        + [dma((nz,))] * 9
        + [dma((nz + 1,))],
        compiler_params=pltpu.CompilerParams(
            collective_id=collective_id, has_side_effects=True, vmem_limit_bytes=VMEM_BYTES
        ),
    )(rows, slots, gates)


def fold_kernel(parts, out, sx, sy, h0, h1, bx, by, send, recv):
    p = Place()
    greet(p, 1, line=False, pair=False)
    half = out.shape[0] // 2
    low, high = pl.ds(0, half), pl.ds(half, half)
    to_x = remote(parts.at[p.cd, low], h0, send.at[0], recv.at[0], p.dx)
    to_y = remote(parts.at[p.cd, high], h1, send.at[1], recv.at[1], p.dy)
    x_low = remote(parts.at[p.cx, low], bx.at[low], send.at[2], recv.at[2], p.dx)
    y_high = remote(parts.at[p.cy, high], by.at[high], send.at[3], recv.at[3], p.dy)
    x_high = remote(sx, bx.at[high], send.at[4], recv.at[4], p.dx)
    y_low = remote(sy, by.at[low], send.at[5], recv.at[5], p.dy)
    copies = (to_x, to_y, x_low, y_high, x_high, y_low)
    for copy in copies[:4]:
        copy.start()
    to_y.wait_recv()
    sx[...] = (parts[p.cx, high].astype(f32) + h1[...].astype(f32)).astype(sx.dtype)
    x_high.start()
    to_x.wait_recv()
    sy[...] = (parts[p.cy, low].astype(f32) + h0[...].astype(f32)).astype(sy.dtype)
    y_low.start()
    x_low.wait_recv()
    y_low.wait_recv()
    out[low] = parts[p.c, low].astype(f32) + bx[low].astype(f32) + by[low].astype(f32)
    y_high.wait_recv()
    x_high.wait_recv()
    out[high] = parts[p.c, high].astype(f32) + bx[high].astype(f32) + by[high].astype(f32)
    for copy in copies:
        copy.wait_send()


def fold(parts, collective_id):
    _, seq, width = parts.shape
    buf = lambda r: pltpu.VMEM((r, width), parts.dtype)
    return pl.pallas_call(
        fold_kernel,
        out_shape=jax.ShapeDtypeStruct((seq, width), f32),
        in_specs=[IN_VMEM],
        out_specs=IN_VMEM,
        scratch_shapes=[buf(seq // 2)] * 4
        + [buf(seq)] * 2
        + [pltpu.SemaphoreType.DMA((6,))] * 2,
        compiler_params=pltpu.CompilerParams(
            collective_id=collective_id, has_side_effects=True, vmem_limit_bytes=VMEM_BYTES
        ),
    )(parts)


def last_kernel(nz, gq, go, gains, oq, ok, ov, oo, all_gains, *scratch):
    own_q, own_o, sib_q, sib_o, s_q, s_o, b_q, b_o, swap_s, swap_r, scratch = (
        *scratch[:10],
        scratch[10:],
    )
    load, pair_s, pair_r, line_s, line_r, a_send, a_recv, g_send, g_recv, local = scratch
    p = Place()
    order = pick_order(p, nz)

    @pl.when(p.z == 0)
    def _():
        for ref in (b_q, b_o):
            ref[pl.ds(0, nz)] = jnp.zeros((nz,) + ref.shape[1:], ref.dtype)

    @pl.when(p.z == nz - 1)
    def _():
        for ref in (b_q, b_o):
            ref[pl.ds(0, nz - 1)] = jnp.zeros((nz - 1,) + ref.shape[1:], ref.dtype)
            ref[nz] = jnp.zeros(ref.shape[1:], ref.dtype)

    greet(p, nz, diagonal=True)
    keep = pltpu.make_async_copy(gains, all_gains.at[p.c * (2 * nz) + p.e], local)
    keep.start()
    job = Spread(p, nz, gains, by_device(all_gains, nz), gains.shape[0] // 2, g_send, g_recv)
    arrays = (
        (0, lambda z, k: gq.at[:, z * 2 + k], own_q, sib_q, s_q, b_q),
        (1, lambda z, k: go.at[z * 2 + k], own_o, sib_o, s_o, b_o),
    )

    def load_copy(i, z):
        _, part, own, _, _, _ = arrays[i]
        return pltpu.make_async_copy(part(z, p.k), own.at[z], load.at[i, z])

    def pair_copy(i, z):
        _, part, _, sib, _, _ = arrays[i]
        return remote(part(z, 1 - p.k), sib.at[z], pair_s.at[i, z], pair_r.at[i, z], p.pair)

    def copy_up(i, z):
        _, _, _, _, s, b = arrays[i]
        return remote(s.at[z], b.at[z], line_s.at[i, z], line_r.at[i, z], p.up)

    def copy_down(i, z):
        _, _, _, _, s, b = arrays[i]
        slot = jnp.where(z == p.z - 1, nz, z)
        return remote(s.at[z], b.at[slot], line_s.at[i, z], line_r.at[i, slot], p.down)

    def line_recv(i, slot):
        b = arrays[i][5]
        remote(b.at[slot], b.at[slot], line_s.at[i, 0], line_r.at[i, slot], p.pair).wait_recv()

    for z in order:
        for i in (0, 1):
            pair_copy(i, z).start()
            load_copy(i, z).start()
    for far in range(nz + 2):
        job.step(far)
        if far >= nz:
            continue
        z, last = order[far], far == nz - 1
        for i in (0, 1):
            _, _, own, sib, s, b = arrays[i]
            load_copy(i, z).wait()
            pair_copy(i, z).wait_recv()
            if last:

                @pl.when(p.z > 0)
                def _():
                    line_recv(i, z)

                @pl.when(p.z < nz - 1)
                def _():
                    line_recv(i, nz)

                total = own[z].astype(f32) + sib[z].astype(f32) + b[z].astype(f32)
                total = total + b[nz].astype(f32)
                if i:
                    oo[...] = total
                else:
                    swap_s[...] = total.astype(swap_s.dtype)
            else:

                @pl.when(((z > p.z) & (p.z > 0)) | ((z < p.z) & (p.z < nz - 1)))
                def _():
                    line_recv(i, z)

                total = own[z].astype(f32) + sib[z].astype(f32) + b[z].astype(f32)
                s[z] = total.astype(s.dtype)

                @pl.when(z > p.z)
                def _():
                    copy_up(i, z).start()

                @pl.when(z < p.z)
                def _():
                    copy_down(i, z).start()

            if last and i == 0:
                swaps = [
                    remote(
                        swap_s.at[c], swap_r.at[p.c], a_send.at[n], a_recv.at[n], device
                    )
                    for n, (c, device) in enumerate(((p.cx, p.dx), (p.cy, p.dy), (p.cd, p.dd)))
                ]
                for copy in swaps:
                    copy.start()
                swap_r[p.c] = swap_s[p.c]
    for n, c in enumerate((p.cx, p.cy, p.cd)):
        ref = swap_r.at[c]
        remote(ref, ref, a_send.at[n], a_recv.at[n], p.dx).wait_recv()
    heads = oq.shape[1] // 4
    kv = ok.shape[1] // 4
    for c in range(4):
        oq[:, pl.ds(c * heads, heads)] = swap_r[c, :, pl.ds(0, heads)].astype(f32)
        ok[:, pl.ds(c * kv, kv)] = swap_r[c, :, pl.ds(heads, kv)].astype(f32)
        ov[:, pl.ds(c * kv, kv)] = swap_r[c, :, pl.ds(heads + kv, kv)].astype(f32)
    for copy in swaps:
        copy.wait_send()
    for n, z in enumerate(order):
        for i in (0, 1):
            pair_copy(i, z).wait_send()
            if n < nz - 1:
                copy_up(i, z).wait_send()
    keep.wait()
    job.finish()


def reduce_last(nz, gq, go, gains):
    _, _, rows_q, wide = gq.shape
    _, rows_o, width = go.shape
    kv = HD
    heads = wide - 2 * kv
    dma = pltpu.SemaphoreType.DMA
    shape = jax.ShapeDtypeStruct
    q = lambda *n: pltpu.VMEM(n + (4, rows_q, wide), bf16)
    o = lambda *n: pltpu.VMEM(n + (rows_o, width), bf16)
    return pl.pallas_call(
        functools.partial(last_kernel, nz),
        out_shape=[
            shape((rows_q, 4 * heads), f32),
            shape((rows_q, 4 * kv), f32),
            shape((rows_q, 4 * kv), f32),
            shape((rows_o, width), f32),
            shape((8 * nz,) + gains.shape, f32),
        ],
        in_specs=[ANY] * 3,
        out_specs=[IN_VMEM] * 4 + [ANY],
        scratch_shapes=[q(nz), o(nz), q(nz), o(nz), q(nz), o(nz), q(nz + 1), o(nz + 1), q(), q()]
        + [dma((2, nz))] * 4
        + [dma((2, nz + 1))]
        + [dma((3,))] * 2
        + spread_sems(nz)
        + [dma],
        compiler_params=pltpu.CompilerParams(
            collective_id=9, has_side_effects=True, vmem_limit_bytes=VMEM_BYTES
        ),
    )(gq, go, gains)


def attend_kernel(scale, span, q, k, vt, ot, lse):
    for i in range(q.shape[1] // span):
        keys = (i + 1) * span
        here = pl.ds(i * span, span)
        s = lax.dot_general(
            k[pl.ds(0, keys)], q[0, here], (((1,), (1,)), ((), ())), preferred_element_type=f32
        )
        s = s * scale
        key_pos = lax.broadcasted_iota(jnp.int32, s.shape, 0)
        query_pos = lax.broadcasted_iota(jnp.int32, s.shape, 1) + i * span
        s = jnp.where(key_pos <= query_pos, s, masked_value)
        largest = jnp.max(s, axis=0, keepdims=True)
        weights = jnp.exp(s - largest)
        total = jnp.sum(weights, axis=0, keepdims=True)
        o = jnp.dot(vt[:, pl.ds(0, keys)], weights.astype(bf16), preferred_element_type=f32)
        ot[0, :, here] = (o / total).astype(bf16)
        lse[0, :, here] = largest + jnp.log(total)


def attend(q, k, vt, scale):
    heads, length, hd = q.shape
    shape = jax.ShapeDtypeStruct
    return pl.pallas_call(
        functools.partial(attend_kernel, scale, length // 4),
        grid=(heads,),
        out_shape=[shape((heads, hd, length), bf16), shape((heads, 1, length), f32)],
        in_specs=[
            pl.BlockSpec((1, length, hd), lambda h: (h, 0, 0)),
            pl.BlockSpec((length, hd), lambda h: (0, 0)),
            pl.BlockSpec((hd, length), lambda h: (0, 0)),
        ],
        out_specs=[
            pl.BlockSpec((1, hd, length), lambda h: (h, 0, 0)),
            pl.BlockSpec((1, 1, length), lambda h: (h, 0, 0)),
        ],
        compiler_params=pltpu.CompilerParams(vmem_limit_bytes=32 * 2**20),
    )(q, k, vt)


def attend_back_kernel(scale, span, q, k, kt, v, do, lse, dq, dk, dv):
    @pl.when(pl.program_id(0) == 0)
    def _():
        dk[...] = jnp.zeros(dk.shape, f32)
        dv[...] = jnp.zeros(dv.shape, f32)

    for i in range(q.shape[1] // span):
        keys = pl.ds(0, (i + 1) * span)
        here = pl.ds(i * span, span)
        nt = (((1,), (1,)), ((), ()))
        s = lax.dot_general(k[keys], q[0, here], nt, preferred_element_type=f32) * scale
        key_pos = lax.broadcasted_iota(jnp.int32, s.shape, 0)
        query_pos = lax.broadcasted_iota(jnp.int32, s.shape, 1) + i * span
        probs = jnp.where(key_pos <= query_pos, jnp.exp(s - lse[0, :, here]), 0.0)
        dp = lax.dot_general(v[keys], do[here], nt, preferred_element_type=f32)
        delta = jnp.sum(probs * dp, axis=0, keepdims=True)
        ds = (probs * (dp - delta)).astype(bf16)
        dk[keys] += jnp.dot(ds, q[0, here], preferred_element_type=f32) * scale
        dv[keys] += jnp.dot(probs.astype(bf16), do[here], preferred_element_type=f32)
        part = jnp.dot(kt[:, keys], ds, preferred_element_type=f32) * scale
        dq[here] = part.T


def attend_back(q, k, v, do, lse, scale):
    heads, length, hd = q.shape
    shape = jax.ShapeDtypeStruct
    whole = pl.BlockSpec((length, hd), lambda h: (0, 0))
    column = pl.BlockSpec((length, hd), lambda h: (0, h))
    return pl.pallas_call(
        functools.partial(attend_back_kernel, scale, length // 4),
        grid=(heads,),
        out_shape=[
            shape((length, heads * hd), f32),
            shape((length, hd), f32),
            shape((length, hd), f32),
        ],
        in_specs=[
            pl.BlockSpec((1, length, hd), lambda h: (h, 0, 0)),
            whole,
            pl.BlockSpec((hd, length), lambda h: (0, 0)),
            whole,
            column,
            pl.BlockSpec((1, 1, length), lambda h: (h, 0, 0)),
        ],
        out_specs=[column, whole, whole],
        compiler_params=pltpu.CompilerParams(vmem_limit_bytes=32 * 2**20),
    )(q, k, k.T, v, do, lse)


NT = (((1,), (1,)), ((), ()))
TN = (((0,), (0,)), ((), ()))


def experts_kernel(
    nz,
    cap,
    mine,
    cots,
    slots,
    gates,
    wg,
    wu,
    wd,
    all_rows,
    produced,
    grad_inputs,
    x_out,
    dr_out,
    a_out,
    dg_out,
    du_out,
    stage_x,
    stage_d,
    x,
    dr,
    r,
    dx,
    a,
    dg,
    du,
    send,
    recv,
    local,
    load,
    out_sem,
    back_sem,
):
    p = Place()
    greet(p, nz)
    job = Spread(p, nz, mine, by_device(all_rows, nz), mine.shape[0] // 2, send, recv)
    keep = pltpu.make_async_copy(mine, job.block(p.c, p.z, p.k), local)
    keep.start()
    seq, width = mine.shape
    ff = a.shape[2]
    wide = min(512, width)
    narrow = min(256, ff)
    lines = [(p.c, 0), (p.cx, 0), (p.c, 1), (p.cx, 1)], [(p.cy, 0), (p.cd, 0), (p.cy, 1), (p.cd, 1)]
    turns = [(i - j, j) for i in range(1, nz + 2) for j in (1, 2) if 0 <= i - j < nz]
    turns = [(i, j - 1) for i, j in turns]

    def index(h, i, z):
        c, other = lines[h][i]
        return c * (2 * nz) + z * 2 + lax.rem(p.k + other, 2)

    def load_x(h, i, z):
        return pltpu.make_async_copy(all_rows.at[index(h, i, z)], stage_x.at[i], load.at[0, i])

    def load_d(n, i):
        at, h = turns[n]
        src = cots.at[index(h, i, job.order[at])]
        return pltpu.make_async_copy(src, stage_d.at[n % 2, i], load.at[1 + n % 2, i])

    def outs(h, z):
        whole = ((x, x_out), (dr, dr_out), (a, a_out), (dg, dg_out), (du, du_out))
        found = [
            pltpu.make_async_copy(src.at[h], dst.at[z, h], out_sem.at[h, n])
            for n, (src, dst) in enumerate(whole)
        ]
        for n, (src, dst) in enumerate(((r, produced), (dx, grad_inputs))):
            for i in range(4):
                found.append(
                    pltpu.make_async_copy(
                        src.at[h, pl.ds(i * cap, cap)], dst.at[index(h, i, z)], back_sem.at[h, n, i]
                    )
                )
        return found

    def group(n):
        at, h = turns[n]
        z = job.order[at]
        for i in range(4):
            load_x(h, i, z).start()
        if n + 1 < len(turns):
            for i in range(4):
                load_d(n + 1, i).start()
        if at:
            for copy in outs(h, job.order[at - 1]):
                copy.wait()
        for i in range(4):
            names = lax.broadcasted_iota(jnp.int32, (cap, seq), 0) == slots[index(h, i, z)]
            chosen = names.astype(f32).astype(bf16)
            row_gate = jnp.where(names, gates[index(h, i, z)], 0.0)
            row_gate = jnp.sum(row_gate, axis=1, keepdims=True)
            here = pl.ds(i * cap, cap)
            load_d(n, i).wait()
            picked = jnp.dot(chosen, stage_d[n % 2, i], preferred_element_type=f32)
            dr[h, here] = (row_gate * picked).astype(bf16)
            load_x(h, i, z).wait()
            picked = jnp.dot(chosen, stage_x[i], preferred_element_type=f32)
            x[h, here] = picked.astype(bf16)

        @pl.loop(0, ff // narrow)
        def _(t):
            cols = pl.ds(pl.multiple_of(t * narrow, narrow), narrow)
            g = jnp.dot(x[h], wg[:, cols], preferred_element_type=f32)
            u = jnp.dot(x[h], wu[:, cols], preferred_element_type=f32)
            da = lax.dot_general(dr[h], wd[cols, :], NT, preferred_element_type=f32)
            s = jax.nn.sigmoid(g)
            swish = g * s
            a[h, :, cols] = (swish * u).astype(bf16)
            du[h, :, cols] = (da * swish).astype(bf16)
            dg[h, :, cols] = (da * u * s * (1.0 + g * (1.0 - s))).astype(bf16)

        @pl.loop(0, width // wide)
        def _(t):
            cols = pl.ds(pl.multiple_of(t * wide, wide), wide)
            r[h, :, cols] = jnp.dot(a[h], wd[:, cols], preferred_element_type=f32).astype(bf16)
            back = lax.dot_general(dg[h], wg[cols, :], NT, preferred_element_type=f32)
            back = back + lax.dot_general(du[h], wu[cols, :], NT, preferred_element_type=f32)
            dx[h, :, cols] = back.astype(bf16)

        for copy in outs(h, z):
            copy.start()

    for i in range(4):
        load_d(0, i).start()
    done = 0
    for i in range(nz + 2):
        if i < nz:
            job.along(i)
        if 1 <= i <= nz:
            z = job.order[i - 1]
            job.beside(z)
            for j in (5, 6):
                job.got(j, z)
            if i == 1:
                keep.wait()
            group(done)
            done += 1
        if i >= 2:
            z = job.order[i - 2]
            job.across(z)
            for j in (7, 8, 9):
                job.got(j, z)
            group(done)
            done += 1
    for h in (0, 1):
        for copy in outs(h, job.order[nz - 1]):
            copy.wait()
    job.finish(pair=False)


def run_experts(nz, cap, mine, cots, slots, gates, wg, wu, wd):
    seq, width = mine.shape
    ff = wg.shape[1]
    rows = 4 * cap
    blocks = 8 * nz
    shape = lambda *n: jax.ShapeDtypeStruct(n, bf16)
    vmem = lambda *n: pltpu.VMEM(n, bf16)
    dma = pltpu.SemaphoreType.DMA
    return pl.pallas_call(
        functools.partial(experts_kernel, nz, cap),
        out_shape=[shape(blocks, seq, width)]
        + [shape(blocks, cap, width)] * 2
        + [shape(nz, 2, rows, width)] * 2
        + [shape(nz, 2, rows, ff)] * 3,
        in_specs=[ANY] * 2 + [IN_VMEM] * 5,
        out_specs=[ANY] * 8,
        scratch_shapes=[vmem(4, seq, width), vmem(2, 4, seq, width)]
        + [vmem(2, rows, width)] * 4
        + [vmem(2, rows, ff)] * 3
        + spread_sems(nz)
        + [dma, dma((3, 4)), dma((2, 5)), dma((2, 2, 4))],
        compiler_params=pltpu.CompilerParams(
            collective_id=3, has_side_effects=True, vmem_limit_bytes=VMEM_BYTES
        ),
    )(mine, cots, slots, gates, wg, wu, wd)[1:]


def mm(a, b, contract, kind=f32):
    return lax.dot_general(a, b, ((contract[:1], contract[1:]), ((), ())), preferred_element_type=f32).astype(kind)


def fast_body(
    tokens,
    query_weight,
    key_weight,
    value_weight,
    output_weight,
    norm_gains,
    head_gains,
    expert_gate,
    expert_up,
    expert_down,
    routes,
    route_gates,
    cotangent,
):
    seq, width = tokens.shape[1:]
    nz = lax.axis_size("expert") // 2
    devices = lax.axis_size(("ctx", "expert"))
    length = 4 * seq
    topk = routes.shape[2]
    cap = max(2, 5 * seq * topk // (4 * devices))
    heads = HQ // 4
    wq = heads * HD
    scale = HD ** (-0.5)
    c = lax.axis_index("ctx")
    e = lax.axis_index("expert")
    k = lax.rem(e, 2)
    me = c * (2 * nz) + e
    rows_in = tokens.reshape(seq, width).astype(f32)
    rows_q = query_weight.shape[0]

    def cols(weight):
        return weight.reshape(rows_q, 4, -1).transpose(1, 0, 2)

    pack = jnp.concatenate([cols(query_weight), cols(key_weight), cols(value_weight)], axis=2)
    share = norm_gains.shape[1]
    head_share = head_gains.shape[1]
    parts = [
        routes.reshape(seq, topk).T.astype(f32).reshape(-1),
        route_gates.reshape(seq, topk).T.reshape(-1),
        norm_gains.astype(f32).reshape(-1),
        head_gains.astype(f32).reshape(-1),
    ]
    flat = jnp.concatenate(parts)
    lines = -(-flat.shape[0] // (128 * 16)) * 16
    meta = jnp.pad(flat, (0, lines * 128 - flat.shape[0])).reshape(lines, 128)
    weight, wo, toks, cots, metas = gather_first(
        nz,
        pack,
        output_weight,
        tokens.reshape(seq, width),
        cotangent.reshape(seq, width),
        meta,
    )
    weight = weight.reshape(width, -1)
    wo = wo.reshape(-1, width)
    metas = metas.reshape(devices, -1)
    n = seq * topk
    all_routes = metas[:, :n].reshape(devices, topk, seq)
    all_gates = metas[:, n : 2 * n].reshape(devices, topk, seq)
    at = 2 * n
    gains = metas[:, at : at + 2 * share].reshape(devices, 2, share).transpose(1, 0, 2)
    gains = gains.reshape(2, width)
    at += 2 * share
    head_gain = metas[:, at : at + 2 * head_share].reshape(devices, 2, head_share)
    head_gain = head_gain.transpose(1, 0, 2).reshape(2, HD)

    positions = jnp.arange(length, dtype=jnp.int32)
    normed = rms_scale(toks.reshape(length, width).astype(f32), gains[0]).astype(bf16)
    raw = mm(normed, weight, (1, 0))
    query_raw = raw[:, :wq].reshape(length, heads, HD)
    key_raw = raw[:, wq : wq + HD].reshape(length, 1, HD)
    values = raw[:, wq + HD :].astype(bf16)

    def head_prep(raw_heads, gain_vec):
        return rotate(rms_scale(raw_heads, gain_vec), positions)

    queries = head_prep(query_raw, head_gain[0]).astype(bf16).transpose(1, 0, 2)
    keys = head_prep(key_raw, head_gain[1]).astype(bf16).reshape(length, HD)
    attended, lse = attend(queries, keys, values.T, scale)
    attended = attended.reshape(wq, length)
    hidden = rows_in + fold(mm(attended, wo, (0, 0), bf16).reshape(4, seq, width), 2)
    normed_mlp = rms_scale(hidden, gains[1]).astype(bf16)

    def picks(expert):
        named = all_routes == expert.astype(f32)
        member = jnp.any(named, axis=1)
        weight_of = jnp.sum(jnp.where(named, all_gates, 0.0), axis=1)
        upto = jnp.arange(seq)[:, None] <= jnp.arange(seq)[None, :]
        rank = jnp.dot(member.astype(bf16), upto.astype(bf16), preferred_element_type=f32)
        slot = jnp.where(member, rank.astype(jnp.int32) - 1, -1)
        return slot.reshape(devices, 1, seq), weight_of.reshape(devices, 1, seq)

    slot, weight_of = picks(me)
    slot_pair, weight_pair = picks(me + 1 - 2 * k)
    slots2 = jnp.stack([slot, slot_pair])
    gates2 = jnp.stack([weight_of, weight_pair])
    produced, grad_inputs, arrived, grad_arrived, activated, grad_gate_pre, grad_up_pre = run_experts(
        nz, cap, normed_mlp, cots, slot, weight_of, expert_gate[0], expert_up[0], expert_down[0]
    )
    grad_normed_mlp = combine(nz, grad_inputs, slots2, jnp.ones_like(gates2), 4)
    mixed = hidden + combine(nz, produced, slots2, gates2, 5)
    arrived, grad_arrived, activated, grad_gate_pre, grad_up_pre = (
        a.reshape(devices * cap, -1)
        for a in (arrived, grad_arrived, activated, grad_gate_pre, grad_up_pre)
    )
    grad_down = mm(activated, grad_arrived, (0, 0))
    grad_gate = mm(arrived, grad_gate_pre, (0, 0))
    grad_up = mm(arrived, grad_up_pre, (0, 0))

    grad_out = cotangent.reshape(seq, width).astype(f32)
    _, norm_pull = jax.vjp(rms_scale, hidden, gains[1])
    grad_hidden_norm, grad_gain_mlp = norm_pull(grad_normed_mlp)
    grad_hidden = grad_out + grad_hidden_norm
    branch = gather_rows(nz, False, grad_hidden.astype(bf16), 6).reshape(length, width)
    grad_wo = mm(attended, branch, (1, 0), bf16)
    grad_attended = mm(branch, wo, (1, 1), bf16)
    grad_query, grad_key, grad_value = attend_back(
        queries, keys, values, grad_attended, lse, scale
    )
    _, pull_query = jax.vjp(head_prep, query_raw, head_gain[0])
    grad_query_raw, grad_query_gain = pull_query(grad_query.reshape(length, heads, HD))
    _, pull_key = jax.vjp(head_prep, key_raw, head_gain[1])
    grad_key_raw, grad_key_gain = pull_key(grad_key.reshape(length, 1, HD))
    low = jnp.concatenate(
        [
            grad_query_raw.reshape(length, wq).astype(bf16),
            grad_key_raw.reshape(length, HD).astype(bf16),
            grad_value.astype(bf16),
        ],
        axis=1,
    )
    grad_weight = mm(normed, low, (0, 0), bf16)
    grad_normed = fold(mm(low, weight, (1, 1), bf16).reshape(4, seq, width), 7)
    _, pull_attn = jax.vjp(rms_scale, rows_in, gains[0])
    grad_rows_norm, grad_gain_attn = pull_attn(grad_normed)
    grad_input = grad_hidden + grad_rows_norm
    gain_parts = jnp.concatenate(
        [grad_gain_attn, grad_gain_mlp, grad_query_gain, grad_key_gain]
    ).reshape(-1, 128)
    extra = -gain_parts.shape[0] % 16
    gain_parts = jnp.pad(gain_parts, ((0, extra), (0, 0)))
    sum_q, sum_k, sum_v, sum_o, all_gain_parts = reduce_last(
        nz,
        grad_weight.reshape(4, 2 * nz, rows_q, -1),
        grad_wo.reshape(2 * nz, -1, width),
        gain_parts,
    )
    gain_sums = jnp.sum(all_gain_parts, axis=0).reshape(-1)
    norm_sums = gain_sums[: 2 * width].reshape(2, width)
    head_sums = gain_sums[2 * width : 2 * width + 2 * HD].reshape(2, HD)
    return (
        mixed.astype(bf16).reshape(tokens.shape),
        grad_input.astype(bf16).reshape(tokens.shape),
        sum_q,
        sum_k,
        sum_v,
        sum_o,
        lax.dynamic_slice_in_dim(norm_sums, me * share, share, 1),
        lax.dynamic_slice_in_dim(head_sums, me * head_share, head_share, 1),
        grad_gate[None],
        grad_up[None],
        grad_down[None],
    )


def solution(mesh):
    small = mesh.shape["ctx"] == HK and mesh.shape["expert"] % 2 == 0 and mesh.size <= 32
    return jax.shard_map(
        fast_body if small else body,
        mesh=mesh,
        in_specs=(
            P("expert", "ctx", None),
            P(("ctx", "expert"), None),
            P(("ctx", "expert"), None),
            P(("ctx", "expert"), None),
            P(("ctx", "expert"), None),
            P(None, ("ctx", "expert")),
            P(None, ("ctx", "expert")),
            P(("ctx", "expert"), None, None),
            P(("ctx", "expert"), None, None),
            P(("ctx", "expert"), None, None),
            P("expert", "ctx", None),
            P("expert", "ctx", None),
            P("expert", "ctx", None),
        ),
        out_specs=(
            P("expert", "ctx", None),
            P("expert", "ctx", None),
            P(("ctx", "expert"), None),
            P(("ctx", "expert"), None),
            P(("ctx", "expert"), None),
            P(("ctx", "expert"), None),
            P(None, ("ctx", "expert")),
            P(None, ("ctx", "expert")),
            P(("ctx", "expert"), None, None),
            P(("ctx", "expert"), None, None),
            P(("ctx", "expert"), None, None),
        ),
        check_vma=False,
    )
```

```python
import functools

import jax
import jax.numpy as jnp
from jax import lax
from jax.experimental import pallas as pl
from jax.experimental.pallas import tpu as pltpu
from jax.sharding import PartitionSpec as P

HQ = 32
HK = 4
HD = 128


epsilon = 1e-06
rope_base = 1000000.0
masked_value = -1e30


def rms_scale(values, scale_gain):
    return (
        values * lax.rsqrt(jnp.mean(values * values, axis=-1, keepdims=True) + epsilon) * scale_gain
    )


def rotate(values, positions):
    half_size = values.shape[-1] // 2
    frequency = rope_base ** (-jnp.arange(half_size, dtype=jnp.float32) / half_size)
    angles = positions.astype(jnp.float32)[:, None] * frequency[None, :]
    cosine = jnp.cos(angles)[:, None, :]
    sine_part = jnp.sin(angles)[:, None, :]
    first_half = values[..., :half_size]
    second_half = values[..., half_size:]
    return jnp.concatenate(
        [
            first_half * cosine - second_half * sine_part,
            second_half * cosine + first_half * sine_part,
        ],
        axis=-1,
    )


def body(
    tokens,
    query_weight,
    key_weight,
    value_weight,
    output_weight,
    norm_gains,
    head_gains,
    expert_gate,
    expert_up,
    expert_down,
    routes,
    route_gates,
    cotangent,
):
    seq_rows = tokens.shape[1]
    width = tokens.shape[2]
    groups = HQ // HK
    kv_width = HK * HD
    scale = HD ** (-0.5)
    positions = lax.axis_index("ctx") * seq_rows + jnp.arange(seq_rows, dtype=jnp.int32)
    last_pos = lax.axis_index("ctx") * seq_rows + seq_rows - 1
    rows_in = tokens.reshape(seq_rows, width).astype(jnp.float32)
    full_q, full_k, full_v, full_o, gains, head_gain = (
        lax.all_gather(query_weight, ("ctx", "expert"), axis=0, tiled=True),
        lax.all_gather(key_weight, ("ctx", "expert"), axis=0, tiled=True),
        lax.all_gather(value_weight, ("ctx", "expert"), axis=0, tiled=True),
        lax.all_gather(output_weight, ("ctx", "expert"), axis=0, tiled=True),
        lax.all_gather(norm_gains, ("ctx", "expert"), axis=1, tiled=True),
        lax.all_gather(head_gains, ("ctx", "expert"), axis=1, tiled=True),
    )

    def head_prep(raw_heads, gain_vec):
        return rotate(rms_scale(raw_heads, gain_vec), positions)

    normed = rms_scale(rows_in, gains[0].astype(jnp.float32)).astype(jnp.bfloat16)
    query_raw = jnp.dot(normed, full_q, preferred_element_type=jnp.float32).reshape(
        seq_rows, HQ, HD
    )
    key_raw = jnp.dot(normed, full_k, preferred_element_type=jnp.float32).reshape(seq_rows, HK, HD)
    value_rows = jnp.dot(normed, full_v, preferred_element_type=jnp.float32).astype(jnp.bfloat16)
    query_gain = head_gain[0].astype(jnp.float32)
    key_gain = head_gain[1].astype(jnp.float32)
    queries = head_prep(query_raw, query_gain).astype(jnp.bfloat16)
    keys_rot = head_prep(key_raw, key_gain).astype(jnp.bfloat16)
    kv_rows = jnp.concatenate([keys_rot.reshape(seq_rows, kv_width), value_rows], axis=1)
    grouped = queries.reshape(seq_rows, HK, groups, HD)

    def scores_for(key_block, base_row):
        scores = (
            jnp.einsum("qhgd,khd->hgqk", grouped, key_block, preferred_element_type=jnp.float32)
            * scale
        )
        key_pos = base_row + jnp.arange(key_block.shape[0], dtype=jnp.int32)
        allowed = key_pos[None, :] <= positions[:, None]
        return (scores, allowed)

    start_state = (
        jnp.full((HK, groups, seq_rows), masked_value, jnp.float32),
        jnp.zeros((HK, groups, seq_rows), jnp.float32),
        jnp.zeros((HK, groups, seq_rows, HD), jnp.float32),
    )
    shard_rows = lax.all_gather(kv_rows, "ctx", axis=0, tiled=True)
    blocks = shard_rows.reshape(shard_rows.shape[0] // seq_rows, seq_rows, 2 * kv_width)

    def step(state_now, element):
        block_index, block_rows = element
        base_row = block_index * seq_rows

        def step_visit(state_in):
            largest, total_sum, accum = state_in
            key_block = block_rows[:, :kv_width].reshape(seq_rows, HK, HD)
            value_block = block_rows[:, kv_width:].reshape(seq_rows, HK, HD)
            scores, allowed = scores_for(key_block, base_row)
            scores = jnp.where(allowed, scores, masked_value)
            new_largest = jnp.maximum(largest, jnp.max(scores, axis=-1))
            weights = jnp.where(allowed, jnp.exp(scores - new_largest[..., None]), 0.0)
            factor = jnp.exp(largest - new_largest)
            total_sum = total_sum * factor + jnp.sum(weights, axis=-1)
            accum = accum * factor[..., None] + jnp.einsum(
                "hgqk,khd->hgqd",
                weights.astype(jnp.bfloat16),
                value_block,
                preferred_element_type=jnp.float32,
            )
            return (new_largest, total_sum, accum)

        def step_skip(state_in):
            return state_in

        return (lax.cond(base_row <= last_pos, step_visit, step_skip, state_now), None)

    final_state, unused = lax.scan(
        step, start_state, (jnp.arange(blocks.shape[0], dtype=jnp.int32), blocks)
    )
    largest, total_sum, accum = final_state
    attended = (accum / total_sum[..., None]).transpose(2, 0, 1, 3).reshape(seq_rows, HQ * HD)
    log_total = largest + jnp.log(total_sum)
    attended_low = attended.astype(jnp.bfloat16)
    hidden = rows_in + jnp.dot(attended_low, full_o, preferred_element_type=jnp.float32)
    normed_mlp = rms_scale(hidden, gains[1].astype(jnp.float32)).astype(jnp.bfloat16)
    devices = lax.axis_size(("ctx", "expert"))
    local_experts = expert_gate.shape[0]
    experts = local_experts * devices
    topk = routes.shape[2]
    capacity = max(2, 5 * seq_rows * topk // (4 * experts))
    route_ids = routes.reshape(seq_rows * topk)
    onehot = (route_ids[:, None] == jnp.arange(experts, dtype=jnp.int32)[None, :]).astype(jnp.int32)
    slots = jnp.sum((jnp.cumsum(onehot, axis=0) - 1) * onehot, axis=1)
    target = route_ids * capacity + slots
    owner_row = jnp.arange(seq_rows * topk, dtype=jnp.int32) // topk
    gate_rows = route_gates.reshape(seq_rows, topk)

    def to_slots(row_block):
        buffer = (
            jnp.zeros((experts * capacity, row_block.shape[1]), row_block.dtype)
            .at[target]
            .set(row_block)
        )
        return buffer.reshape(devices, local_experts * capacity, row_block.shape[1])

    def to_experts(arrived):
        return (
            arrived.reshape(devices, local_experts, capacity, -1)
            .transpose(1, 0, 2, 3)
            .reshape(local_experts, devices * capacity, -1)
        )

    def from_experts(expert_rows):
        return (
            expert_rows.reshape(local_experts, devices, capacity, -1)
            .transpose(1, 0, 2, 3)
            .reshape(devices, local_experts * capacity, -1)
        )

    arrived = to_experts(
        lax.all_to_all(
            to_slots(normed_mlp[owner_row]),
            ("ctx", "expert"),
            split_axis=0,
            concat_axis=0,
            tiled=True,
        )
    )
    gate_pre = jnp.einsum("erd,edf->erf", arrived, expert_gate, preferred_element_type=jnp.float32)
    up_pre = jnp.einsum("erd,edf->erf", arrived, expert_up, preferred_element_type=jnp.float32)
    sigmoid_gate = jax.nn.sigmoid(gate_pre)
    swish_gate = gate_pre * sigmoid_gate
    activated = (swish_gate * up_pre).astype(jnp.bfloat16)
    produced = jnp.einsum(
        "erf,efd->erd", activated, expert_down, preferred_element_type=jnp.float32
    ).astype(jnp.bfloat16)
    returned = lax.all_to_all(
        from_experts(produced), ("ctx", "expert"), split_axis=0, concat_axis=0, tiled=True
    ).reshape(experts * capacity, width)
    expert_out = returned[target].astype(jnp.float32).reshape(seq_rows, topk, width)
    mixed = hidden + jnp.sum(gate_rows[:, :, None] * expert_out, axis=1)
    full_q, full_k, full_v, full_o, gains, head_gain = (
        lax.all_gather(query_weight, ("ctx", "expert"), axis=0, tiled=True),
        lax.all_gather(key_weight, ("ctx", "expert"), axis=0, tiled=True),
        lax.all_gather(value_weight, ("ctx", "expert"), axis=0, tiled=True),
        lax.all_gather(output_weight, ("ctx", "expert"), axis=0, tiled=True),
        lax.all_gather(norm_gains, ("ctx", "expert"), axis=1, tiled=True),
        lax.all_gather(head_gains, ("ctx", "expert"), axis=1, tiled=True),
    )
    grad_out = cotangent.reshape(seq_rows, width).astype(jnp.float32)
    grad_rows = (
        (gate_rows[:, :, None] * grad_out[:, None, :])
        .astype(jnp.bfloat16)
        .reshape(seq_rows * topk, width)
    )
    grad_arrived = to_experts(
        lax.all_to_all(
            to_slots(grad_rows), ("ctx", "expert"), split_axis=0, concat_axis=0, tiled=True
        )
    )
    grad_down = jnp.einsum(
        "erf,erd->efd", activated, grad_arrived, preferred_element_type=jnp.float32
    )
    grad_act = jnp.einsum(
        "erd,efd->erf", grad_arrived, expert_down, preferred_element_type=jnp.float32
    )
    grad_up_pre = (grad_act * swish_gate).astype(jnp.bfloat16)
    grad_gate_pre = (
        grad_act * up_pre * sigmoid_gate * (1.0 + gate_pre * (1.0 - sigmoid_gate))
    ).astype(jnp.bfloat16)
    grad_gate = jnp.einsum(
        "erd,erf->edf", arrived, grad_gate_pre, preferred_element_type=jnp.float32
    )
    grad_up = jnp.einsum("erd,erf->edf", arrived, grad_up_pre, preferred_element_type=jnp.float32)
    grad_inputs = jnp.einsum(
        "erf,edf->erd", grad_gate_pre, expert_gate, preferred_element_type=jnp.float32
    )
    grad_inputs = (
        grad_inputs
        + jnp.einsum("erf,edf->erd", grad_up_pre, expert_up, preferred_element_type=jnp.float32)
    ).astype(jnp.bfloat16)
    grad_back = lax.all_to_all(
        from_experts(grad_inputs), ("ctx", "expert"), split_axis=0, concat_axis=0, tiled=True
    ).reshape(experts * capacity, width)
    grad_normed_mlp = jnp.sum(
        grad_back[target].astype(jnp.float32).reshape(seq_rows, topk, width), axis=1
    )
    unused_norm, norm_pull = jax.vjp(rms_scale, hidden, gains[1].astype(jnp.float32))
    grad_hidden_norm, grad_gain_mlp = norm_pull(grad_normed_mlp)
    grad_hidden = grad_out + grad_hidden_norm
    grad_branch = grad_hidden.astype(jnp.bfloat16)
    grad_wo = jnp.einsum("qa,qd->ad", attended_low, grad_branch, preferred_element_type=jnp.float32)
    grad_attended = jnp.einsum(
        "qd,ad->qa", grad_branch, full_o, preferred_element_type=jnp.float32
    ).astype(jnp.bfloat16)
    all_kv = lax.all_gather(kv_rows, "ctx", axis=0, tiled=True)
    grad_grouped = grad_attended.reshape(seq_rows, HK, groups, HD)
    delta = jnp.einsum(
        "qhgd,qhgd->hgq",
        grad_grouped.astype(jnp.float32),
        attended.reshape(seq_rows, HK, groups, HD),
    )
    kv_blocks = all_kv.reshape(-1, seq_rows, 2 * kv_width)

    def back_step(grad_query, element):
        block_index, block_rows = element
        base_row = block_index * seq_rows

        def back_visit(grad_in):
            key_block = block_rows[:, :kv_width].reshape(seq_rows, HK, HD)
            value_block = block_rows[:, kv_width:].reshape(seq_rows, HK, HD)
            scores, allowed = scores_for(key_block, base_row)
            probs = jnp.where(allowed, jnp.exp(scores - log_total[..., None]), 0.0)
            grad_probs = jnp.einsum(
                "qhgd,khd->hgqk", grad_grouped, value_block, preferred_element_type=jnp.float32
            )
            grad_scores = (probs * (grad_probs - delta[..., None])).astype(jnp.bfloat16)
            grad_next = grad_in + jnp.einsum(
                "hgqk,khd->qhgd", grad_scores, key_block, preferred_element_type=jnp.float32
            )
            grad_keys = (
                jnp.einsum(
                    "hgqk,qhgd->khd", grad_scores, grouped, preferred_element_type=jnp.float32
                )
                * scale
            )
            grad_values = jnp.einsum(
                "hgqk,qhgd->khd",
                probs.astype(jnp.bfloat16),
                grad_grouped,
                preferred_element_type=jnp.float32,
            )
            joined = jnp.concatenate(
                [grad_keys.reshape(seq_rows, kv_width), grad_values.reshape(seq_rows, kv_width)],
                axis=1,
            )
            return (grad_next, joined)

        def back_skip(grad_in):
            return (grad_in, jnp.zeros((seq_rows, 2 * kv_width), jnp.float32))

        return lax.cond(base_row <= last_pos, back_visit, back_skip, grad_query)

    grad_query, grad_kv_terms = lax.scan(
        back_step,
        jnp.zeros((seq_rows, HK, groups, HD), jnp.float32),
        (jnp.arange(kv_blocks.shape[0], dtype=jnp.int32), kv_blocks),
    )
    grad_query = grad_query * scale
    grad_kv = lax.psum_scatter(
        grad_kv_terms.reshape(-1, 2 * kv_width).astype(jnp.bfloat16),
        "ctx",
        scatter_dimension=0,
        tiled=True,
    ).astype(jnp.float32)
    unused_query, pull_query = jax.vjp(head_prep, query_raw, query_gain)
    grad_query_raw, grad_query_gain = pull_query(grad_query.reshape(seq_rows, HQ, HD))
    unused_key, pull_key = jax.vjp(head_prep, key_raw, key_gain)
    grad_key_raw, grad_key_gain = pull_key(grad_kv[:, :kv_width].reshape(seq_rows, HK, HD))
    grad_q_low = grad_query_raw.reshape(seq_rows, HQ * HD).astype(jnp.bfloat16)
    grad_k_low = grad_key_raw.reshape(seq_rows, kv_width).astype(jnp.bfloat16)
    grad_v_low = grad_kv[:, kv_width:].astype(jnp.bfloat16)
    grad_wq = jnp.einsum("qd,qa->da", normed, grad_q_low, preferred_element_type=jnp.float32)
    grad_wk = jnp.einsum("qd,qa->da", normed, grad_k_low, preferred_element_type=jnp.float32)
    grad_wv = jnp.einsum("qd,qa->da", normed, grad_v_low, preferred_element_type=jnp.float32)
    grad_normed = jnp.einsum("qa,da->qd", grad_q_low, full_q, preferred_element_type=jnp.float32)
    grad_normed = grad_normed + jnp.einsum(
        "qa,da->qd", grad_k_low, full_k, preferred_element_type=jnp.float32
    )
    grad_normed = grad_normed + jnp.einsum(
        "qa,da->qd", grad_v_low, full_v, preferred_element_type=jnp.float32
    )
    unused_attn, pull_attn = jax.vjp(rms_scale, rows_in, gains[0].astype(jnp.float32))
    grad_rows_norm, grad_gain_attn = pull_attn(grad_normed)
    grad_input = grad_hidden + grad_rows_norm
    gain_grads = jnp.stack([grad_gain_attn, grad_gain_mlp])
    head_grads = jnp.stack([grad_query_gain, grad_key_gain])
    sum_q, sum_k, sum_v, sum_o, sum_gain, sum_head = (
        lax.psum_scatter(grad_wq, ("ctx", "expert"), scatter_dimension=0, tiled=True),
        lax.psum_scatter(grad_wk, ("ctx", "expert"), scatter_dimension=0, tiled=True),
        lax.psum_scatter(grad_wv, ("ctx", "expert"), scatter_dimension=0, tiled=True),
        lax.psum_scatter(grad_wo, ("ctx", "expert"), scatter_dimension=0, tiled=True),
        lax.psum_scatter(gain_grads, ("ctx", "expert"), scatter_dimension=1, tiled=True),
        lax.psum_scatter(head_grads, ("ctx", "expert"), scatter_dimension=1, tiled=True),
    )
    return (
        mixed.astype(jnp.bfloat16).reshape(tokens.shape),
        grad_input.astype(jnp.bfloat16).reshape(tokens.shape),
        sum_q,
        sum_k,
        sum_v,
        sum_o,
        sum_gain,
        sum_head,
        grad_gate,
        grad_up,
        grad_down,
    )


MESH = pl.DeviceIdType.MESH
VMEM_BYTES = 58 * 2**20
ANY = pl.BlockSpec(memory_space=pl.ANY)
IN_VMEM = pl.BlockSpec(memory_space=pltpu.VMEM)
f32, bf16 = jnp.float32, jnp.bfloat16
NT = (((1,), (1,)), ((), ()))
TN = (((0,), (0,)), ((), ()))


class Place:
    def __init__(self):
        self.c = lax.axis_index("ctx")
        self.e = lax.axis_index("expert")
        self.k = lax.rem(self.e, 2)
        self.z = lax.div(self.e, 2)
        self.cx = self.c + 1 - 2 * lax.rem(self.c, 2)
        self.cy = lax.rem(self.c + 2, 4)
        self.cd = lax.rem(self.cx + 2, 4)
        self.dx = (self.cx, self.e)
        self.dy = (self.cy, self.e)
        self.dd = (self.cd, self.e)
        self.pair = (self.c, self.e + 1 - 2 * self.k)
        self.up = (self.c, self.e + 2)
        self.down = (self.c, self.e - 2)


def greet(p, nz, line=True, pair=True, diagonal=False):
    barrier = pltpu.get_barrier_semaphore()

    def tell(device):
        pl.semaphore_signal(barrier, inc=1, device_id=device, device_id_type=MESH)

    friends = [p.dx, p.dy] + [p.pair] * pair + [p.dd] * diagonal
    for device in friends:
        tell(device)
    count = len(friends)
    if line:
        for there, device in ((p.z > 0, p.down), (p.z < nz - 1, p.up)):

            @pl.when(there)
            def _():
                tell(device)

            count = count + there.astype(jnp.int32)
    pl.semaphore_wait(barrier, count)


def remote(src, dst, send, recv, device):
    return pltpu.make_async_remote_copy(
        src_ref=src,
        dst_ref=dst,
        send_sem=send,
        recv_sem=recv,
        device_id=device,
        device_id_type=MESH,
    )


def far_first(nz, z):
    return sorted(range(nz), key=lambda to: (-abs(to - z), to))


def near_first(nz, z):
    return sorted(range(nz), key=lambda to: (abs(to - z), to))


def pick_order(p, nz, order=far_first):
    tables = [order(nz, z) for z in range(nz)]
    return [sum(jnp.where(p.z == z, tables[z][i], 0) for z in range(nz)) for i in range(nz)]


class Spread:
    def __init__(self, p, nz, mine, block, half, send, recv, line=True, side=True, pair=True):
        self.p, self.nz, self.mine, self.block, self.half = p, nz, mine, block, half
        self.send, self.recv = send, recv
        self.line, self.side, self.pair = line, side, pair
        self.order = pick_order(p, nz, near_first) if line else [p.z]

    def ref(self, c, z, k, h=None):
        whole = self.block(c, z, k)
        return whole if h is None else whole.at[pl.ds(h * self.half, self.half)]

    def copy(self, kind, z, own=False):
        p = self.p
        at = functools.partial(self.ref, z=z, k=p.k)
        src, i, j, device = {
            "x": lambda: (at(p.c), 0, 1, p.dx),
            "y": lambda: (at(p.c), 1, 2, p.dy),
            "up": lambda: (at(p.c), 2, 0, p.up),
            "down": lambda: (at(p.c), 3, 0, p.down),
            "via_y": lambda: (at(p.cx, h=0), 4, 3, p.dy),
            "via_x": lambda: (at(p.cy, h=1), 5, 4, p.dx),
            "pair0": lambda: (at(p.c), 6, 5, p.pair),
            "pair1": lambda: (at(p.cx), 7, 6, p.pair),
            "pair2": lambda: (at(p.cy), 8, 7, p.pair),
            "pair3": lambda: (at(p.cd, h=0), 9, 8, p.pair),
            "pair4": lambda: (at(p.cd, h=1), 10, 9, p.pair),
        }[kind]()
        return remote(
            self.mine if own else src, src, self.send.at[z, i], self.recv.at[z, j], device
        )

    def got(self, j, z):
        p = self.p
        k = p.k if j < 5 else 1 - p.k
        c, h = ((p.c, None), (p.cx, None), (p.cy, None), (p.cd, 0), (p.cd, 1))[j % 5]
        ref = self.ref(c, z, k, h)
        remote(ref, ref, self.send.at[z, 0], self.recv.at[z, j], p.pair).wait_recv()

    def each(self, far, act):
        if far == 0:
            act(self.p.z, 0)
            return
        for way in (-1, 1):
            z = self.p.z + way * far

            @pl.when((z >= 0) & (z < self.nz))
            def _():
                act(z, way)

    def onward(self, z, way, act):
        if self.line and way >= 0:

            @pl.when(self.p.z > 0)
            def _():
                act(self.copy("down", z, way == 0))

        if self.line and way <= 0:

            @pl.when(self.p.z < self.nz - 1)
            def _():
                act(self.copy("up", z, way == 0))

    def direct(self):
        return ["x", "y"] * self.side + ["pair0"] * self.pair

    def along(self, far):
        def act(z, way):
            if way:
                self.got(0, z)
            self.onward(z, way, lambda copy: copy.start())
            for kind in self.direct():
                self.copy(kind, z, way == 0).start()

        self.each(far, act)

    def beside(self, z):
        for j, kinds in ((1, ["via_y", "pair1"]), (2, ["via_x", "pair2"])):
            self.got(j, z)
            for kind in kinds[: 1 + self.pair]:
                self.copy(kind, z).start()

    def across(self, z):
        for j, kind in ((3, "pair3"), (4, "pair4")):
            self.got(j, z)
            if self.pair:
                self.copy(kind, z).start()

    def from_pair(self, z):
        if self.pair:
            for j in range(5, 10 if self.side else 6):
                self.got(j, z)

    def step(self, i):
        reach = self.nz if self.line else 1
        if i < reach:
            self.along(i)
        if self.side and 1 <= i <= reach:
            self.beside(self.order[i - 1])
        if self.side and 2 <= i <= reach + 1:
            self.across(self.order[i - 2])

    def finish(self, pair=True):
        def act(z, way):
            if pair:
                self.from_pair(z)
            self.onward(z, way, lambda copy: copy.wait_send())
            for kind in self.direct():
                self.copy(kind, z, way == 0).wait_send()
            if self.side:
                for kind in ["via_y", "via_x"] + ["pair1", "pair2", "pair3", "pair4"] * self.pair:
                    self.copy(kind, z).wait_send()

        for far in range(self.nz if self.line else 1):
            self.each(far, act)


def by_device(ref, nz):
    return lambda c, z, k: ref.at[c * (2 * nz) + z * 2 + k]


def spread_sems(nz):
    return [pltpu.SemaphoreType.DMA((nz, 11)), pltpu.SemaphoreType.DMA((nz, 10))]


class Fold:
    def __init__(self, p, parts, sx, sy, h0, h1, bx, by, send, recv):
        half = bx.shape[0] // 2
        self.halves = low, high = pl.ds(0, half), pl.ds(half, half)
        self.p, self.parts, self.sx, self.sy = p, parts, sx, sy
        self.h0, self.h1, self.bx, self.by = h0, h1, bx, by
        copy = lambda i, src, dst, device: remote(src, dst, send.at[i], recv.at[i], device)
        self.to_x = copy(0, parts.at[p.cd, low], h0, p.dx)
        self.to_y = copy(1, parts.at[p.cd, high], h1, p.dy)
        self.x_low = copy(2, parts.at[p.cx, low], bx.at[low], p.dx)
        self.y_high = copy(3, parts.at[p.cy, high], by.at[high], p.dy)
        self.x_high = copy(4, sx, bx.at[high], p.dx)
        self.y_low = copy(5, sy, by.at[low], p.dy)

    def begin(self):
        for copy in (self.to_x, self.to_y, self.x_low, self.y_high):
            copy.start()

    def middle(self):
        p, (low, high), parts = self.p, self.halves, self.parts
        self.to_y.wait_recv()
        total = parts[p.cx, high].astype(f32) + self.h1[...].astype(f32)
        self.sx[...] = total.astype(self.sx.dtype)
        self.x_high.start()
        self.to_x.wait_recv()
        total = parts[p.cy, low].astype(f32) + self.h0[...].astype(f32)
        self.sy[...] = total.astype(self.sy.dtype)
        self.y_low.start()

    def end(self, store):
        p, parts = self.p, self.parts
        low, high = self.halves
        for rows, waits in ((low, (self.x_low, self.y_low)), (high, (self.y_high, self.x_high))):
            for copy in waits:
                copy.wait_recv()
            total = parts[p.c, rows].astype(f32) + self.bx[rows].astype(f32)
            store(rows, total + self.by[rows].astype(f32))
        for copy in (self.to_x, self.to_y, self.x_low, self.y_high, self.x_high, self.y_low):
            copy.wait_send()


def fold_scratch(seq, width):
    buf = lambda r: pltpu.VMEM((r, width), bf16)
    return (
        [buf(seq // 2)] * 4 + [buf(seq)] * 2 + [pltpu.SemaphoreType.DMA((6,))] * 2
    )


def front_kernel(nz, scale, *refs):
    pack, wo, tok, cot, meta, cosine, sine = refs[:7]
    packs, wos, toks, cots, metas = refs[7:12]
    xn, raw, q, k, v, ot, lse, hidden, hn, gain_out, head_out, slots, gates = refs[12:25]
    tok_v, w_v, wo_v, meta_v, vt, ob, part = refs[25:32]
    fold_refs, pair_sems = refs[32:40], refs[40:50]
    a_send, a_recv, local, load = refs[50:]
    p = Place()
    seq, width = tok.shape
    length = 4 * seq
    heads = q.shape[0]
    me = p.c * (2 * nz) + p.e
    greet(p, nz, diagonal=True)
    into = [
        pltpu.make_async_copy(src, dst, local.at[i])
        for i, (src, dst) in enumerate(
            (
                (pack.at[p.c], w_v.at[p.c, p.e]),
                (wo, wo_v.at[p.e]),
                (tok, tok_v.at[p.c]),
                (cot, part.at[0]),
            )
        )
    ]
    own = [
        pltpu.make_async_copy(src, dst, local.at[4 + i])
        for i, (src, dst) in enumerate(
            (
                (w_v.at[p.c, p.e], packs.at[p.c, p.e]),
                (wo_v.at[p.e], wos.at[p.e]),
                (meta, metas.at[me]),
                (part.at[0], cots.at[me]),
            )
        )
    ]
    loads = [
        pltpu.make_async_copy(src, dst, load.at[i])
        for i, (src, dst) in enumerate(
            [(packs, w_v), (wos, wo_v), (metas, meta_v)]
            + [(toks.at[c], tok_v.at[c]) for c in (p.cx, p.cy, p.cd)]
        )
    ]
    for copy in into:
        copy.start()
    own[2].start()
    swaps = [
        remote(pack.at[c], packs.at[p.c, p.e], a_send.at[i], a_recv.at[i], device)
        for i, (c, device) in enumerate(((p.cx, p.dx), (p.cy, p.dy), (p.cd, p.dd)))
    ]
    for copy in swaps:
        copy.start()

    def job(i, src, block, half, *ways):
        return Spread(p, nz, src, block, half, *pair_sems[2 * i : 2 * i + 2], *ways)

    j_tok = job(0, tok, lambda c, z, k: toks.at[c], seq // 2, False, True, False)
    j_meta = job(1, meta, by_device(metas, nz), meta.shape[0] // 2)
    j_cot = job(2, cot, by_device(cots, nz), seq // 2)
    j_wo = job(3, wo, lambda c, z, k: wos.at[z * 2 + k], 0, True, False, True)
    own_pack = packs.at[:, p.e]
    j_pack = job(4, own_pack, lambda c, z, k: packs.at[:, z * 2 + k], 0, True, False, True)
    j_meta.step(0)
    j_tok.step(0)
    for i in (0, 1, 3):
        into[i].wait()
        own[i].start()
    for i, c in enumerate((p.cx, p.cy, p.cd)):
        ref = packs.at[c, p.e]
        remote(ref, ref, a_send.at[i], a_recv.at[i], p.dx).wait_recv()
    own[0].wait()
    j_pack.step(0)
    j_meta.step(1)
    j_pack.step(1)
    j_tok.step(1)
    loads[3].start()
    loads[4].start()
    j_tok.step(2)
    loads[5].start()
    j_meta.step(2)
    j_pack.step(2)
    j_cot.step(0)
    for i in range(3, nz + 2):
        j_meta.step(i)
        j_pack.step(i)
    own[2].wait()
    for z in j_meta.order:
        j_meta.from_pair(z)
    loads[2].start()
    j_wo.step(0)
    for z in j_pack.order:
        j_pack.from_pair(z)
    loads[0].start()

    loads[2].wait()
    n = meta_lines(q.shape[1], width, seq)
    per = 128 * 8 * nz // width

    def gain(line):
        found = [
            sum(meta_v[per * j + i, pl.ds(line, 1)] for i in range(per))
            for j in range(width // 128)
        ]
        return jnp.concatenate(found, axis=1)

    def head_gain(line):
        return sum(meta_v[b, pl.ds(line, 1)] for b in range(8 * nz))

    gain_out[0:1] = gain(n)
    gain_out[1:2] = gain(n + 1)
    head_out[0:1] = head_gain(n + 2)
    head_out[1:2] = head_gain(n + 3)

    def rms(x, g):
        return x * lax.rsqrt(jnp.mean(x * x, axis=-1, keepdims=True) + epsilon) * g

    into[2].wait()
    for copy in loads[3:]:
        copy.wait()

    @pl.loop(0, 8)
    def _(i):
        c, h = lax.div(i, 2), lax.rem(i, 2)
        half = seq // 2
        rows = tok_v[c, pl.ds(pl.multiple_of(h * half, half), half)].astype(f32)
        here = pl.ds(pl.multiple_of(i * half, half), half)
        xn[here] = rms(rows, gain_out[0:1]).astype(bf16)

    loads[0].wait()

    @pl.loop(0, raw.shape[1] // 256)
    def _(t):
        cols = pl.ds(pl.multiple_of(t * 256, 256), 256)
        w = w_v[:, :, :, cols].reshape(width, 256)
        raw[:, cols] = jnp.dot(xn[...], w, preferred_element_type=f32)

    j_cot.step(1)
    j_wo.step(1)

    def prep(x, g):
        y = rms(x, g)
        return (y * cosine[...] + pltpu.roll(y, HD // 2, 1) * sine[...]).astype(bf16)

    k[...] = prep(raw[:, pl.ds(heads * HD, HD)], head_out[1:2])
    values = raw[:, pl.ds((heads + 1) * HD, HD)]
    v[...] = values.astype(bf16)
    vt[...] = values.T.astype(bf16)

    def attend(h):
        cols = pl.ds(pl.multiple_of(h * HD, HD), HD)
        q[h] = prep(raw[:, cols], head_out[0:1])
        for i in range(length // seq):
            keys = (i + 1) * seq
            here = pl.ds(i * seq, seq)
            s = lax.dot_general(k[pl.ds(0, keys)], q[h, here], NT, preferred_element_type=f32)
            s = s * scale
            key_pos = lax.broadcasted_iota(jnp.int32, s.shape, 0)
            query_pos = lax.broadcasted_iota(jnp.int32, s.shape, 1) + i * seq
            s = jnp.where(key_pos <= query_pos, s, masked_value)
            largest = jnp.max(s, axis=0, keepdims=True)
            weights = jnp.exp(s - largest)
            total = jnp.sum(weights, axis=0, keepdims=True)
            o = jnp.dot(vt[:, pl.ds(0, keys)], weights.astype(bf16), preferred_element_type=f32)
            o = o / total
            ot[h, :, here] = o.astype(bf16)
            ob[here, cols] = o.T.astype(bf16)
            lse[h, :, here] = largest + jnp.log(total)

    pl.loop(0, heads // 2)(attend)
    j_wo.step(2)
    j_cot.step(2)
    pl.loop(heads // 2, heads)(attend)
    for i in range(3, nz + 2):
        j_wo.step(i)
    own[1].wait()
    for z in j_wo.order:
        j_wo.from_pair(z)
    loads[1].start()
    own[3].wait()

    upto = lax.broadcasted_iota(jnp.int32, (seq, seq), 0) <= lax.broadcasted_iota(
        jnp.int32, (seq, seq), 1
    )
    upto = upto.astype(f32).astype(bf16)
    lines = seq // 128
    topk = n // lines // 2
    for j, expert in enumerate((me, me + 1 - 2 * p.k)):
        expert = expert.astype(f32)
        member, weight = [], []
        for line in range(lines):
            named = [meta_v[:, i * lines + line] == expert for i in range(topk)]
            gate = [meta_v[:, (topk + i) * lines + line] for i in range(topk)]
            member.append(sum(x.astype(f32) for x in named))
            weight.append(sum(jnp.where(x, y, 0.0) for x, y in zip(named, gate)))
        member = jnp.concatenate(member, axis=1)
        rank = jnp.dot(member.astype(bf16), upto, preferred_element_type=f32)
        slots[j] = jnp.where(member > 0.5, rank.astype(jnp.int32) - 1, -1)
        gates[j] = jnp.concatenate(weight, axis=1)

    loads[1].wait()
    tile = 512

    @pl.loop(0, width // tile)
    def _(t):
        cols = pl.ds(pl.multiple_of(t * tile, tile), tile)
        w = wo_v[:, :, cols].reshape(heads * HD, tile)
        out = jnp.dot(ob[...], w, preferred_element_type=f32)
        part[:, :, cols] = out.astype(bf16).reshape(4, seq, tile)

    fold = Fold(p, part, *fold_refs)
    fold.begin()
    j_cot.step(3)
    fold.middle()

    def store(rows, total):
        h = tok_v[p.c, rows].astype(f32) + total
        hidden[rows] = h
        hn[rows] = rms(h, gain_out[1:2]).astype(bf16)

    fold.end(store)
    for i in range(4, nz + 2):
        j_cot.step(i)
    for copy in swaps:
        copy.wait_send()
    for spread in (j_tok, j_meta, j_cot, j_wo, j_pack):
        spread.finish(pair=spread is j_cot)


def meta_lines(length, width, seq):
    return 2 * 8 * seq // 128


def front(nz, scale, pack, wo, tok, cot, meta, cosine, sine):
    blocks = 8 * nz
    seq, width = tok.shape
    length = 4 * seq
    wide = pack.shape[2]
    heads = wide // HD - 2
    hbm = lambda n, a: jax.ShapeDtypeStruct(n + a.shape, a.dtype)
    out = lambda *n: jax.ShapeDtypeStruct(n[:-1], n[-1])
    vmem = lambda *n: pltpu.VMEM(n, bf16)
    dma = pltpu.SemaphoreType.DMA
    return pl.pallas_call(
        functools.partial(front_kernel, nz, scale),
        out_shape=[
            jax.ShapeDtypeStruct((4, 2 * nz) + pack.shape[1:], bf16),
            hbm((2 * nz,), wo),
            hbm((4,), tok),
            hbm((blocks,), cot),
            hbm((blocks,), meta),
            out(length, width, bf16),
            out(length, wide, f32),
            out(heads, length, HD, bf16),
            out(length, HD, bf16),
            out(length, HD, bf16),
            out(heads, HD, length, bf16),
            out(heads, 1, length, f32),
            out(seq, width, f32),
            out(seq, width, bf16),
            out(2, width, f32),
            out(2, HD, f32),
            out(2, blocks, seq, jnp.int32),
            out(2, blocks, seq, f32),
        ],
        in_specs=[ANY] * 5 + [IN_VMEM] * 2,
        out_specs=[ANY] * 5 + [IN_VMEM] * 13,
        scratch_shapes=[
            vmem(4, seq, width),
            vmem(4, 2 * nz, pack.shape[1], wide),
            vmem(2 * nz, wo.shape[0], width),
            pltpu.VMEM((blocks,) + meta.shape, f32),
            vmem(HD, length),
            vmem(length, heads * HD),
            vmem(4, seq, width),
        ]
        + fold_scratch(seq, width)
        + spread_sems(nz) * 5
        + [dma((n,)) for n in (3, 3, 8, 6)],
        compiler_params=pltpu.CompilerParams(
            collective_id=1, has_side_effects=True, vmem_limit_bytes=VMEM_BYTES
        ),
    )(pack, wo, tok, cot, meta, cosine, sine)


def spread_kernel(nz, everywhere, mine, out, send, recv, local):
    p = Place()
    greet(p, nz, line=everywhere, pair=everywhere)
    block = by_device(out, nz) if everywhere else (lambda c, z, k: out.at[c])
    keep = pltpu.make_async_copy(mine, block(p.c, p.z, p.k), local)
    keep.start()
    job = Spread(
        p, nz, mine, block, mine.shape[0] // 2, send, recv, everywhere, True, everywhere
    )
    for far in range(nz + 2 if everywhere else 3):
        job.step(far)
    keep.wait()
    job.finish()


def gather_rows(nz, everywhere, mine, collective_id):
    blocks = 8 * nz if everywhere else 4
    return pl.pallas_call(
        functools.partial(spread_kernel, nz, everywhere),
        out_shape=jax.ShapeDtypeStruct((blocks,) + mine.shape, mine.dtype),
        in_specs=[IN_VMEM],
        out_specs=ANY,
        scratch_shapes=spread_sems(nz) + [pltpu.SemaphoreType.DMA],
        compiler_params=pltpu.CompilerParams(collective_id=collective_id, has_side_effects=True),
    )(mine)


class Combine:
    def __init__(self, p, nz, cap, col, rows, slots, gates, out, *scratch):
        self.p, self.nz, self.cap, self.rows, self.slots, self.gates = p, nz, cap, rows, slots, gates
        self.out = out
        self.rbuf, self.sd, self.sx, self.sy = scratch[:4]
        self.h0, self.h1, self.bx, self.by, self.bz = scratch[4:9]
        self.pair_send, self.pair_recv, self.load = scratch[9:12]
        self.s_h0, self.s_h1, self.s_x, self.s_y, self.s_z = scratch[12:17]
        self.r_h0, self.r_h1, self.r_x, self.r_y, self.r_z = scratch[17:]
        self.order = pick_order(p, nz)
        self.seq, self.width = self.sx.shape[1:]
        self.half = self.seq // 2
        self.cols = pl.ds(col, self.width)

    def clear(self):
        bz, nz = self.bz, self.nz

        @pl.when(self.p.z == 0)
        def _():
            bz[pl.ds(0, nz)] = jnp.zeros((nz,) + bz.shape[1:], bz.dtype)

        @pl.when(self.p.z == nz - 1)
        def _():
            bz[pl.ds(0, nz - 1)] = jnp.zeros((nz - 1,) + bz.shape[1:], bz.dtype)
            bz[nz] = jnp.zeros(bz.shape[1:], bz.dtype)

    def pair_copy(self, c, z):
        p = self.p
        return remote(
            self.rows.at[c * (2 * self.nz) + z * 2 + 1 - p.k, :, self.cols],
            self.rbuf.at[c, z, pl.ds(self.cap, self.cap)],
            self.pair_send.at[c, z],
            self.pair_recv.at[c, z],
            p.pair,
        )

    def load_copy(self, c, z):
        return pltpu.make_async_copy(
            self.rows.at[c * (2 * self.nz) + z * 2 + self.p.k, :, self.cols],
            self.rbuf.at[c, z, pl.ds(0, self.cap)],
            self.load.at[c, z],
        )

    def begin(self):
        p = self.p
        for z in self.order:
            for c in (p.cd, p.cx, p.cy, p.c):
                self.load_copy(c, z).start()
                self.pair_copy(c, z).start()

    def fill(self, c, z, low, high, store):
        half = self.half
        b = pl.ds(c * (2 * self.nz) + z * 2 + self.p.k, 1)
        names = lax.broadcasted_iota(jnp.int32, (self.cap, self.seq), 0)
        both = [jnp.where(names == self.slots[n, b], self.gates[n, b], 0.0) for n in (0, 1)]
        w = jnp.concatenate(both, axis=0).T.astype(bf16)
        self.load_copy(c, z).wait()
        self.pair_copy(c, z).wait_recv()
        tile = min(512, self.width)
        for t in range(self.width // tile):
            cols = pl.ds(t * tile, tile)
            total = jnp.dot(w, self.rbuf[c, z, :, cols], preferred_element_type=f32)
            for first, adds in ((0, low), (half, high)):
                part = total[first : first + half]
                for ref, start in adds:
                    part = part + ref[pl.ds(start, half), cols].astype(f32)
                store(pl.ds(first, half), cols, part)

    def into(self, buf, z):
        def store(lines, cols, total):
            buf[z, lines, cols] = total.astype(buf.dtype)

        return store

    def copy_h0(self, z):
        src = self.sd.at[z, pl.ds(0, self.half)]
        return remote(src, self.h0.at[z], self.s_h0.at[z], self.r_h0.at[z], self.p.dx)

    def copy_h1(self, z):
        src = self.sd.at[z, pl.ds(self.half, self.half)]
        return remote(src, self.h1.at[z], self.s_h1.at[z], self.r_h1.at[z], self.p.dy)

    def copy_x(self, z):
        return remote(self.sx.at[z], self.bx.at[z], self.s_x.at[z], self.r_x.at[z], self.p.dx)

    def copy_y(self, z):
        return remote(self.sy.at[z], self.by.at[z], self.s_y.at[z], self.r_y.at[z], self.p.dy)

    def copy_up(self, z):
        return remote(self.sx.at[z], self.bz.at[z], self.s_z.at[z], self.r_z.at[z], self.p.up)

    def copy_down(self, z):
        slot = jnp.where(z == self.p.z - 1, self.nz, z)
        return remote(
            self.sx.at[z], self.bz.at[slot], self.s_z.at[z], self.r_z.at[slot], self.p.down
        )

    def line_recv(self, slot):
        ref = self.bz.at[slot]
        remote(ref, ref, self.s_z.at[0], self.r_z.at[slot], self.p.pair).wait_recv()

    def diagonal(self, i):
        z = self.order[i]
        self.fill(self.p.cd, z, [], [], self.into(self.sd, z))
        self.copy_h0(z).start()
        self.copy_h1(z).start()

    def sides(self, i):
        z = self.order[i]
        self.copy_h1(z).wait_recv()
        self.fill(self.p.cx, z, [], [(self.h1.at[z], 0)], self.into(self.sx, z))
        self.copy_x(z).start()
        self.copy_h0(z).wait_recv()
        self.fill(self.p.cy, z, [(self.h0.at[z], 0)], [], self.into(self.sy, z))
        self.copy_y(z).start()

    def mine(self, i):
        p, nz, z, last = self.p, self.nz, self.order[i], i == self.nz - 1
        self.copy_x(z).wait_recv()
        self.copy_y(z).wait_recv()
        self.copy_x(z).wait_send()
        arrived = [self.bx.at[z], self.by.at[z], self.bz.at[z]]
        if last:

            @pl.when(p.z > 0)
            def _():
                self.line_recv(z)

            @pl.when(p.z < nz - 1)
            def _():
                self.line_recv(nz)

            def store(lines, cols, total):
                self.out[lines, cols] = total

            arrived.append(self.bz.at[nz])
        else:

            @pl.when(((z > p.z) & (p.z > 0)) | ((z < p.z) & (p.z < nz - 1)))
            def _():
                self.line_recv(z)

            store = self.into(self.sx, z)
        lower, upper = [(ref, 0) for ref in arrived], [(ref, self.half) for ref in arrived]
        self.fill(p.c, z, lower, upper, store)
        if not last:

            @pl.when(z > p.z)
            def _():
                self.copy_up(z).start()

            @pl.when(z < p.z)
            def _():
                self.copy_down(z).start()

    def steps(self):
        nz = self.nz
        found = [(self.diagonal, 0)] + [(self.diagonal, 1)] * (nz > 1)
        for i in range(nz):
            found.append((self.sides, i))
            if i + 2 < nz:
                found.append((self.diagonal, i + 2))
            if i > 0:
                found.append((self.mine, i - 1))
        found.append((self.mine, nz - 1))
        return [functools.partial(act, i) for act, i in found]

    def finish(self):
        p = self.p
        for i, z in enumerate(self.order):
            for c in (p.cd, p.cx, p.cy, p.c):
                self.pair_copy(c, z).wait_send()
            for copy in (self.copy_h0(z), self.copy_h1(z), self.copy_y(z)):
                copy.wait_send()
            if i < self.nz - 1:
                self.copy_up(z).wait_send()


def combine_scratch(nz, cap, seq, width):
    dma = pltpu.SemaphoreType.DMA
    buf = lambda n, r: pltpu.VMEM((n, r, width), bf16)
    return (
        [pltpu.VMEM((4, nz, 2 * cap, width), bf16)]
        + [buf(nz, seq)] * 3
        + [buf(nz, seq // 2)] * 2
        + [buf(nz, seq)] * 2
        + [buf(nz + 1, seq)]
        + [dma((4, nz))] * 3
        + [dma((nz,))] * 9
        + [dma((nz + 1,))]
    )


def combine_kernel(nz, cap, rows, slots, gates, out, *scratch):
    p = Place()
    job = Combine(p, nz, cap, 0, rows, slots, gates, out, *scratch)
    job.clear()
    greet(p, nz)
    job.begin()
    for step in job.steps():
        step()
    job.finish()


def combine(nz, rows, slots, gates, collective_id):
    _, cap, width = rows.shape
    seq = slots.shape[2]
    return pl.pallas_call(
        functools.partial(combine_kernel, nz, cap),
        out_shape=jax.ShapeDtypeStruct((seq, width), f32),
        in_specs=[ANY, IN_VMEM, IN_VMEM],
        out_specs=IN_VMEM,
        scratch_shapes=combine_scratch(nz, cap, seq, width),
        compiler_params=pltpu.CompilerParams(
            collective_id=collective_id, has_side_effects=True, vmem_limit_bytes=VMEM_BYTES
        ),
    )(rows, slots, gates)


def rms_back(x, gain, grad):
    r = lax.rsqrt(jnp.mean(x * x, axis=-1, keepdims=True) + epsilon)
    scaled = gain * grad
    mean = jnp.mean(x * scaled, axis=-1, keepdims=True)
    by_gain = jnp.sum(x * r * grad, axis=0, keepdims=True)
    return r * scaled - x * (r * r * r * mean), by_gain


def back_kernel(nz, cap, scale, *refs):
    branch, wos, packs, xn, raw, q, ot, rows = refs[:8]
    k, v, lse, cosine, sine, head_gain, slots, gates = refs[8:16]
    gwo, gw, part, head_grad, mixed = refs[16:21]
    rows_v, wo_v, w_v, raw_v, q_v, ot_v, do, kt, low, dq, dk, dv, wo_stage, w_stage = refs[21:35]
    load, wo_sem, w_sem = refs[35:38]
    p = Place()
    combine = Combine(p, nz, cap, 0, rows, slots, gates, mixed, *refs[38:])
    length, wide = raw.shape
    heads = q.shape[0]
    seq = length // 4
    width = part.shape[2]
    loads = [
        pltpu.make_async_copy(src, dst, load.at[i])
        for i, (src, dst) in enumerate(
            ((branch, rows_v), (wos, wo_v), (q, q_v), (ot, ot_v), (packs, w_v))
        )
    ]
    load_xn = pltpu.make_async_copy(xn, rows_v, load.at[5])

    def load_raw(cols):
        return pltpu.make_async_copy(raw.at[:, cols], raw_v, load.at[6])

    for copy in loads:
        copy.start()
    combine.clear()
    greet(p, nz)
    combine.begin()
    steps = combine.steps()
    run = lambda n: [steps.pop(0)() for _ in range(min(n, len(steps)))]
    kt[...] = k[...].astype(f32).T.astype(bf16)
    run(2)
    loads[0].wait()
    loads[1].wait()

    @pl.loop(0, heads * HD // 256)
    def _(t):
        cols = pl.ds(pl.multiple_of(t * 256, 256), 256)
        w = wo_v[pl.ds(t * (256 // wo_v.shape[1]), 256 // wo_v.shape[1])].reshape(256, width)
        out = lax.dot_general(rows_v[...].reshape(length, width), w, NT, preferred_element_type=f32)
        do[:, cols] = out.astype(bf16)

    run(1)
    loads[2].wait()
    loads[3].wait()
    dk[...] = jnp.zeros(dk.shape, f32)
    dv[...] = jnp.zeros(dv.shape, f32)
    head_grad[...] = jnp.zeros(head_grad.shape, f32)

    def unprep(x, gain, grad):
        grad = grad * cosine[...] + pltpu.roll(grad * sine[...], HD // 2, 1)
        return rms_back(x, gain, grad)

    def attend(h):
        cols = pl.ds(pl.multiple_of(h * HD, HD), HD)
        load_raw(cols).start()
        for i in range(length // seq):
            keys = pl.ds(0, (i + 1) * seq)
            here = pl.ds(i * seq, seq)
            s = lax.dot_general(k[keys], q_v[h, here], NT, preferred_element_type=f32) * scale
            key_pos = lax.broadcasted_iota(jnp.int32, s.shape, 0)
            query_pos = lax.broadcasted_iota(jnp.int32, s.shape, 1) + i * seq
            probs = jnp.where(key_pos <= query_pos, jnp.exp(s - lse[h, :, here]), 0.0)
            dp = lax.dot_general(v[keys], do[here, cols], NT, preferred_element_type=f32)
            delta = jnp.sum(probs * dp, axis=0, keepdims=True)
            ds = (probs * (dp - delta)).astype(bf16)
            dk[keys] += jnp.dot(ds, q_v[h, here], preferred_element_type=f32) * scale
            dv[keys] += jnp.dot(probs.astype(bf16), do[here, cols], preferred_element_type=f32)
            dq[here] = (jnp.dot(kt[:, keys], ds, preferred_element_type=f32) * scale).T
        load_raw(cols).wait()
        by_x, by_gain = unprep(raw_v[...], head_gain[0:1], dq[...])
        low[:, cols] = by_x.astype(bf16)
        head_grad[0:1] += by_gain

    for first in range(0, heads, 2):
        pl.loop(first, first + 2)(attend)
        run(1)
    load_raw(pl.ds(heads * HD, HD)).start()
    load_raw(pl.ds(heads * HD, HD)).wait()
    by_x, by_gain = unprep(raw_v[...], head_gain[1:2], dk[...])
    low[:, pl.ds(heads * HD, HD)] = by_x.astype(bf16)
    head_grad[1:2] = by_gain
    low[:, pl.ds((heads + 1) * HD, HD)] = dv[...].astype(bf16)

    tile = wo_stage.shape[3]
    wo_out = lambda t: pltpu.make_async_copy(
        wo_stage.at[t % 2], gwo.at[:, :, pl.ds(t * tile, tile)], wo_sem.at[t % 2]
    )
    for t in range(width // tile):
        if t >= 2:
            wo_out(t - 2).wait()
        out = jnp.dot(
            ot_v[...].reshape(heads * HD, length),
            rows_v[:, :, pl.ds(t * tile, tile)].reshape(length, tile),
            preferred_element_type=f32,
        )
        wo_stage[t % 2] = out.astype(bf16).reshape(wo_stage.shape[1:])
        wo_out(t).start()
        if t % 2:
            run(1)
    load_xn.start()
    loads[4].wait()
    for c in range(4):
        w = w_v[c].reshape(width // 4, wide)
        out = lax.dot_general(low[...], w, NT, preferred_element_type=f32)
        part[:, :, pl.ds(c * (width // 4), width // 4)] = out.astype(bf16).reshape(
            4, seq, width // 4
        )
        if c % 2:
            run(1)
    load_xn.wait()
    lines = w_stage.shape[1] * w_stage.shape[2]

    def w_out(t):
        first = t * w_stage.shape[1]
        c, e = first // (2 * nz), first % (2 * nz)
        return pltpu.make_async_copy(
            w_stage.at[t % 2], gw.at[c, pl.ds(e, w_stage.shape[1])], w_sem.at[t % 2]
        )

    for t in range(width // lines):
        if t >= 2:
            w_out(t - 2).wait()
        x = rows_v[:, :, pl.ds(t * lines, lines)].reshape(length, lines)
        out = lax.dot_general(x, low[...], TN, preferred_element_type=f32)
        w_stage[t % 2] = out.astype(bf16).reshape(w_stage.shape[1:])
        w_out(t).start()
        if t % 3 == 2:
            run(1)
    run(len(steps))
    for t in range(2):
        wo_out(width // tile - 2 + t).wait()
        w_out(width // lines - 2 + t).wait()
    combine.finish()


def back(nz, scale, columns, branch, wos, packs, xn, raw, q, ot, rows, k, v, lse, cosine, sine, head_gain, slots, gates):
    length, wide = raw.shape
    heads = q.shape[0]
    seq = length // 4
    width = xn.shape[1]
    cap = rows.shape[1]
    shape = jax.ShapeDtypeStruct
    vmem = lambda *n: pltpu.VMEM(n, bf16)
    wide_f = lambda *n: pltpu.VMEM(n, f32)
    dma = pltpu.SemaphoreType.DMA
    return pl.pallas_call(
        functools.partial(back_kernel, nz, cap, scale),
        out_shape=[
            shape(wos.shape, bf16),
            shape(packs.shape, bf16),
            shape((4, seq, width), bf16),
            shape((2, HD), f32),
            shape((seq, columns), f32),
        ],
        in_specs=[ANY] * 8 + [IN_VMEM] * 8,
        out_specs=[ANY] * 2 + [IN_VMEM] * 3,
        scratch_shapes=[
            vmem(4, seq, width),
            vmem(*wos.shape),
            vmem(*packs.shape),
            wide_f(length, HD),
            vmem(*q.shape),
            vmem(*ot.shape),
            vmem(length, heads * HD),
            vmem(HD, length),
            vmem(length, wide),
            wide_f(length, HD),
            wide_f(length, HD),
            wide_f(length, HD),
            vmem(2, wos.shape[0], wos.shape[1], 256),
            vmem(2, 4, packs.shape[2], wide),
            dma((7,)),
            dma((2,)),
            dma((2,)),
        ]
        + combine_scratch(nz, cap, seq, columns),
        compiler_params=pltpu.CompilerParams(
            collective_id=5, has_side_effects=True, vmem_limit_bytes=VMEM_BYTES
        ),
    )(branch, wos, packs, xn.reshape(4, seq, width), raw, q, ot, rows, k, v, lse, cosine, sine, head_gain, slots, gates)


def last_kernel(nz, cap, col, *refs):
    gq, go, rows, part, tok, dh, gains, mlp_grad, head_grad, slots, gates = refs[:11]
    oq, ok, ov, oo, all_gains, grad_tokens, mixed = refs[11:18]
    own_q, own_o, sib_q, sib_o, b_q, b_o, swap_s, swap_r, gain_v = refs[18:27]
    load, pair_s, pair_r, line_s, line_r, a_send, a_recv, g_send, g_recv, local = refs[27:37]
    p = Place()
    order = pick_order(p, nz)
    fold = Fold(p, part, *refs[37:45])
    combine = Combine(p, nz, cap, col, rows, slots, gates, mixed, *refs[45:])

    @pl.when(p.z == 0)
    def _():
        for ref in (b_q, b_o):
            ref[pl.ds(0, nz)] = jnp.zeros((nz,) + ref.shape[1:], ref.dtype)

    @pl.when(p.z == nz - 1)
    def _():
        for ref in (b_q, b_o):
            ref[pl.ds(0, nz - 1)] = jnp.zeros((nz - 1,) + ref.shape[1:], ref.dtype)
            ref[nz] = jnp.zeros(ref.shape[1:], ref.dtype)

    combine.clear()
    greet(p, nz, diagonal=True)
    arrays = (
        (0, lambda z, k: gq.at[:, z * 2 + k], own_q, sib_q, b_q),
        (1, lambda z, k: go.at[z * 2 + k], own_o, sib_o, b_o),
    )

    def load_copy(i, z):
        _, part, own, _, _ = arrays[i]
        return pltpu.make_async_copy(part(z, p.k), own.at[z], load.at[i, z])

    def pair_copy(i, z):
        _, part, _, sib, _ = arrays[i]
        return remote(part(z, 1 - p.k), sib.at[z], pair_s.at[i, z], pair_r.at[i, z], p.pair)

    def copy_up(i, z):
        _, _, s, _, b = arrays[i]
        return remote(s.at[z], b.at[z], line_s.at[i, z], line_r.at[i, z], p.up)

    def copy_down(i, z):
        _, _, s, _, b = arrays[i]
        slot = jnp.where(z == p.z - 1, nz, z)
        return remote(s.at[z], b.at[slot], line_s.at[i, z], line_r.at[i, slot], p.down)

    def line_recv(i, slot):
        b = arrays[i][4]
        remote(b.at[slot], b.at[slot], line_s.at[i, 0], line_r.at[i, slot], p.pair).wait_recv()

    def swaps():
        return [
            remote(swap_s.at[c], swap_r.at[p.c], a_send.at[n], a_recv.at[n], device)
            for n, (c, device) in enumerate(((p.cx, p.dx), (p.cy, p.dy), (p.cd, p.dd)))
        ]

    def reduce(i, n):
        z, last = order[n], n == nz - 1
        _, _, own, sib, b = arrays[i]
        load_copy(i, z).wait()
        pair_copy(i, z).wait_recv()
        if last:

            @pl.when(p.z > 0)
            def _():
                line_recv(i, z)

            @pl.when(p.z < nz - 1)
            def _():
                line_recv(i, nz)

            total = own[z].astype(f32) + sib[z].astype(f32) + b[z].astype(f32)
            total = total + b[nz].astype(f32)
            if i:
                oo[...] = total
            else:
                swap_s[...] = total.astype(swap_s.dtype)
                for copy in swaps():
                    copy.start()
                swap_r[p.c] = swap_s[p.c]
            return

        @pl.when(((z > p.z) & (p.z > 0)) | ((z < p.z) & (p.z < nz - 1)))
        def _():
            line_recv(i, z)

        total = own[z].astype(f32) + sib[z].astype(f32) + b[z].astype(f32)
        own[z] = total.astype(own.dtype)

        @pl.when(z > p.z)
        def _():
            copy_up(i, z).start()

        @pl.when(z < p.z)
        def _():
            copy_down(i, z).start()

    fold.begin()
    for z in order:
        for i in (1, 0):
            pair_copy(i, z).start()
            load_copy(i, z).start()
    combine.begin()
    steps = combine.steps()
    run = lambda n: [steps.pop(0)() for _ in range(min(n, len(steps)))]
    reduce(1, 0)
    reduce(0, 0)
    run(1)
    fold.middle()
    run(1)
    reduce(1, 1)
    reduce(0, 1)
    run(1)

    half = tok.shape[0] // 2
    gain_v[...] = jnp.zeros(gain_v.shape, f32)
    width = tok.shape[1]

    def store(lines, total):
        by_x, by_gain = rms_back(tok[lines].astype(f32), gains[0:1], total)
        grad_tokens[lines] = (dh[lines] + by_x).astype(bf16)
        for j in range(width // 128):
            gain_v[pl.ds(j, 1)] += by_gain[:, j * 128 : (j + 1) * 128]

    fold.end(store)
    for j in range(width // 128):
        gain_v[pl.ds(width // 128 + j, 1)] = mlp_grad[:, pl.ds(j * 128, 128)]
    gain_v[pl.ds(2 * width // 128, 2)] = head_grad[...]
    block = by_device(all_gains, nz)
    keep = pltpu.make_async_copy(gain_v, block(p.c, p.z, p.k), local)
    keep.start()
    job = Spread(p, nz, gain_v, block, gain_v.shape[0] // 2, g_send, g_recv)
    job.step(0)
    run(1)
    job.step(1)
    for n in range(2, nz):
        reduce(1, n)
        reduce(0, n)
        run(2)
        job.step(n)
    for i in range(nz, nz + 2):
        job.step(i)
        run(1)
    for n, c in enumerate((p.cx, p.cy, p.cd)):
        ref = swap_r.at[c]
        remote(ref, ref, a_send.at[n], a_recv.at[n], p.dx).wait_recv()
    heads = oq.shape[1] // 4
    kv = ok.shape[1] // 4
    for c in range(4):
        oq[:, pl.ds(c * heads, heads)] = swap_r[c, :, pl.ds(0, heads)].astype(f32)
        ok[:, pl.ds(c * kv, kv)] = swap_r[c, :, pl.ds(heads, kv)].astype(f32)
        ov[:, pl.ds(c * kv, kv)] = swap_r[c, :, pl.ds(heads + kv, kv)].astype(f32)
    run(len(steps))
    for copy in swaps():
        copy.wait_send()
    for n, z in enumerate(order):
        for i in (0, 1):
            pair_copy(i, z).wait_send()
            if n < nz - 1:
                copy_up(i, z).wait_send()
    keep.wait()
    job.finish()
    combine.finish()


def reduce_last(nz, col, gq, go, rows, part, tok, dh, gains, mlp_grad, head_grad, slots, gates):
    _, _, rows_q, wide = gq.shape
    _, rows_o, width = go.shape
    cap = rows.shape[1]
    seq = tok.shape[0]
    kv = HD
    heads = wide - 2 * kv
    lines = -(-(2 * width // 128 + 2) // 16) * 16
    dma = pltpu.SemaphoreType.DMA
    shape = jax.ShapeDtypeStruct
    q = lambda *n: pltpu.VMEM(n + (4, rows_q, wide), bf16)
    o = lambda *n: pltpu.VMEM(n + (rows_o, width), bf16)
    return pl.pallas_call(
        functools.partial(last_kernel, nz, cap, col),
        out_shape=[
            shape((rows_q, 4 * heads), f32),
            shape((rows_q, 4 * kv), f32),
            shape((rows_q, 4 * kv), f32),
            shape((rows_o, width), f32),
            shape((8 * nz, lines, 128), f32),
            shape((seq, width), bf16),
            shape((seq, width - col), f32),
        ],
        in_specs=[ANY] * 3 + [IN_VMEM] * 8,
        out_specs=[IN_VMEM] * 4 + [ANY] + [IN_VMEM] * 2,
        scratch_shapes=[q(nz), o(nz), q(nz), o(nz), q(nz + 1), o(nz + 1), q(), q()]
        + [pltpu.VMEM((lines, 128), f32)]
        + [dma((2, nz))] * 4
        + [dma((2, nz + 1))]
        + [dma((3,))] * 2
        + spread_sems(nz)
        + [dma]
        + fold_scratch(seq, width)
        + combine_scratch(nz, cap, seq, width - col),
        compiler_params=pltpu.CompilerParams(
            collective_id=9, has_side_effects=True, vmem_limit_bytes=VMEM_BYTES
        ),
    )(gq, go, rows, part, tok, dh, gains, mlp_grad, head_grad, slots, gates)


def experts_kernel(
    nz,
    cap,
    mine,
    cots,
    slots,
    gates,
    wg,
    wu,
    wd,
    all_rows,
    produced,
    grad_inputs,
    x_out,
    dr_out,
    a_out,
    dg_out,
    du_out,
    stage_x,
    stage_d,
    x,
    dr,
    r,
    dx,
    a,
    dg,
    du,
    send,
    recv,
    load,
    out_sem,
    back_sem,
):
    p = Place()
    greet(p, nz)
    job = Spread(p, nz, mine, by_device(all_rows, nz), mine.shape[0] // 2, send, recv)
    seq, width = mine.shape
    ff = a.shape[2]
    wide = min(512, width)
    narrow = min(256, ff)
    lines = [(p.c, 0), (p.cx, 0), (p.c, 1), (p.cx, 1)], [(p.cy, 0), (p.cd, 0), (p.cy, 1), (p.cd, 1)]
    turns = [(i - j, j) for i in range(1, nz + 2) for j in (1, 2) if 0 <= i - j < nz]
    turns = [(i, j - 1) for i, j in turns]

    def index(h, i, z):
        c, other = lines[h][i]
        return c * (2 * nz) + z * 2 + lax.rem(p.k + other, 2)

    def load_x(n, i):
        at, h = turns[n]
        src = mine if n == i == 0 else all_rows.at[index(h, i, job.order[at])]
        return pltpu.make_async_copy(src, stage_x.at[i], load.at[0, i])

    def load_d(n, i):
        at, h = turns[n]
        src = cots.at[index(h, i, job.order[at])]
        return pltpu.make_async_copy(src, stage_d.at[n % 2, i], load.at[1 + n % 2, i])

    def outs(h, z):
        whole = ((x, x_out), (dr, dr_out), (a, a_out), (dg, dg_out), (du, du_out))
        found = [
            pltpu.make_async_copy(src.at[h], dst.at[z, h], out_sem.at[h, n])
            for n, (src, dst) in enumerate(whole)
        ]
        for n, (src, dst) in enumerate(((r, produced), (dx, grad_inputs))):
            for i in range(4):
                found.append(
                    pltpu.make_async_copy(
                        src.at[h, pl.ds(i * cap, cap)], dst.at[index(h, i, z)], back_sem.at[h, n, i]
                    )
                )
        return found

    def group(n):
        at, h = turns[n]
        z = job.order[at]
        for i in range(4):
            load_x(n, i).start()
        if n + 1 < len(turns):
            for i in range(4):
                load_d(n + 1, i).start()
        if at:
            for copy in outs(h, job.order[at - 1]):
                copy.wait()
        for i in range(4):
            at_b = pl.ds(index(h, i, z), 1)
            names = lax.broadcasted_iota(jnp.int32, (cap, seq), 0) == slots[0, at_b]
            chosen = names.astype(f32).astype(bf16)
            row_gate = jnp.where(names, gates[0, at_b], 0.0)
            row_gate = jnp.sum(row_gate, axis=1, keepdims=True)
            here = pl.ds(i * cap, cap)
            load_d(n, i).wait()
            picked = jnp.dot(chosen, stage_d[n % 2, i], preferred_element_type=f32)
            dr[h, here] = (row_gate * picked).astype(bf16)
            load_x(n, i).wait()
            picked = jnp.dot(chosen, stage_x[i], preferred_element_type=f32)
            x[h, here] = picked.astype(bf16)

        @pl.loop(0, ff // narrow)
        def _(t):
            cols = pl.ds(pl.multiple_of(t * narrow, narrow), narrow)
            g = jnp.dot(x[h], wg[:, cols], preferred_element_type=f32)
            u = jnp.dot(x[h], wu[:, cols], preferred_element_type=f32)
            da = lax.dot_general(dr[h], wd[cols, :], NT, preferred_element_type=f32)
            s = jax.nn.sigmoid(g)
            swish = g * s
            a[h, :, cols] = (swish * u).astype(bf16)
            du[h, :, cols] = (da * swish).astype(bf16)
            dg[h, :, cols] = (da * u * s * (1.0 + g * (1.0 - s))).astype(bf16)

        @pl.loop(0, width // wide)
        def _(t):
            cols = pl.ds(pl.multiple_of(t * wide, wide), wide)
            r[h, :, cols] = jnp.dot(a[h], wd[:, cols], preferred_element_type=f32).astype(bf16)
            back = lax.dot_general(dg[h], wg[cols, :], NT, preferred_element_type=f32)
            back = back + lax.dot_general(du[h], wu[cols, :], NT, preferred_element_type=f32)
            dx[h, :, cols] = back.astype(bf16)

        for copy in outs(h, z):
            copy.start()

    for i in range(4):
        load_d(0, i).start()
    done = 0
    for i in range(nz + 2):
        if i < nz:
            job.along(i)
        if 1 <= i <= nz:
            z = job.order[i - 1]
            job.beside(z)
            for j in (5, 6):
                job.got(j, z)
            group(done)
            done += 1
        if i >= 2:
            z = job.order[i - 2]
            job.across(z)
            for j in (7, 8, 9):
                job.got(j, z)
            group(done)
            done += 1
    for h in (0, 1):
        for copy in outs(h, job.order[nz - 1]):
            copy.wait()
    job.finish(pair=False)


def run_experts(nz, cap, mine, cots, slots, gates, wg, wu, wd):
    seq, width = mine.shape
    ff = wg.shape[1]
    rows = 4 * cap
    blocks = 8 * nz
    shape = lambda *n: jax.ShapeDtypeStruct(n, bf16)
    vmem = lambda *n: pltpu.VMEM(n, bf16)
    dma = pltpu.SemaphoreType.DMA
    return pl.pallas_call(
        functools.partial(experts_kernel, nz, cap),
        out_shape=[shape(blocks, seq, width)]
        + [shape(blocks, cap, width)] * 2
        + [shape(nz, 2, rows, width)] * 2
        + [shape(nz, 2, rows, ff)] * 3,
        in_specs=[ANY] * 2 + [IN_VMEM] * 5,
        out_specs=[ANY] * 8,
        scratch_shapes=[vmem(4, seq, width), vmem(2, 4, seq, width)]
        + [vmem(2, rows, width)] * 4
        + [vmem(2, rows, ff)] * 3
        + spread_sems(nz)
        + [dma((3, 4)), dma((2, 5)), dma((2, 2, 4))],
        compiler_params=pltpu.CompilerParams(
            collective_id=3, has_side_effects=True, vmem_limit_bytes=VMEM_BYTES
        ),
    )(mine, cots, slots, gates, wg, wu, wd)[1:]


def mm(a, b, contract, kind=f32):
    return lax.dot_general(a, b, ((contract[:1], contract[1:]), ((), ())), preferred_element_type=f32).astype(kind)


def fast_body(
    tokens,
    query_weight,
    key_weight,
    value_weight,
    output_weight,
    norm_gains,
    head_gains,
    expert_gate,
    expert_up,
    expert_down,
    routes,
    route_gates,
    cotangent,
):
    seq, width = tokens.shape[1:]
    nz = lax.axis_size("expert") // 2
    devices = lax.axis_size(("ctx", "expert"))
    length = 4 * seq
    topk = routes.shape[2]
    cap = max(2, 5 * seq * topk // (4 * devices))
    heads = HQ // 4
    wq = heads * HD
    scale = HD ** (-0.5)
    c = lax.axis_index("ctx")
    e = lax.axis_index("expert")
    k = lax.rem(e, 2)
    me = c * (2 * nz) + e
    rows_q = query_weight.shape[0]

    def cols(weight):
        return weight.reshape(rows_q, 4, -1).transpose(1, 0, 2)

    pack = jnp.concatenate([cols(query_weight), cols(key_weight), cols(value_weight)], axis=2)
    share = norm_gains.shape[1]
    head_share = head_gains.shape[1]
    lane = jnp.arange(128)

    def placed(part, size):
        spread = jnp.tile(part.astype(f32), (1, 128 // size))
        return jnp.where(lane[None, :] // size == lax.rem(me, 128 // size), spread, 0.0)

    meta = jnp.concatenate(
        [
            routes.reshape(seq, topk).T.astype(f32).reshape(-1, 128),
            route_gates.reshape(seq, topk).T.reshape(-1, 128),
            placed(norm_gains, share),
            placed(head_gains, head_share),
        ]
    )
    meta = jnp.pad(meta, ((0, -meta.shape[0] % 16), (0, 0)))
    half = HD // 2
    angles = jnp.arange(length, dtype=jnp.int32).astype(f32)[:, None] * (
        rope_base ** (-jnp.arange(half, dtype=f32) / half)
    )
    cosine, sine = jnp.cos(angles), jnp.sin(angles)
    tables = (
        jnp.concatenate([cosine, cosine], axis=1),
        jnp.concatenate([-sine, sine], axis=1),
    )
    found = front(
        nz,
        scale,
        pack,
        output_weight,
        tokens.reshape(seq, width),
        cotangent.reshape(seq, width),
        meta,
        *tables,
    )
    weight, wo, _, cots, _, normed, raw, queries, keys, values, attended, lse = found[:12]
    hidden, normed_mlp, gains, head_gain, slots2, gates2 = found[12:]
    produced, grad_inputs, arrived, grad_arrived, activated, grad_gate_pre, grad_up_pre = run_experts(
        nz, cap, normed_mlp, cots, slots2, gates2, expert_gate[0], expert_up[0], expert_down[0]
    )
    grad_normed_mlp = combine(nz, grad_inputs, slots2, jnp.ones_like(gates2), 4)
    arrived, grad_arrived, activated, grad_gate_pre, grad_up_pre = (
        a.reshape(devices * cap, -1)
        for a in (arrived, grad_arrived, activated, grad_gate_pre, grad_up_pre)
    )
    grad_down = mm(activated, grad_arrived, (0, 0))
    grad_gate = mm(arrived, grad_gate_pre, (0, 0))
    grad_up = mm(arrived, grad_up_pre, (0, 0))

    grad_out = cotangent.reshape(seq, width).astype(f32)
    _, norm_pull = jax.vjp(rms_scale, hidden, gains[1])
    grad_hidden_norm, grad_gain_mlp = norm_pull(grad_normed_mlp)
    grad_hidden = grad_out + grad_hidden_norm
    branch = gather_rows(nz, False, grad_hidden.astype(bf16), 6)
    columns = width // 2
    grad_wo, grad_weight, part, grad_head, mixed_low = back(
        nz,
        scale,
        columns,
        branch,
        wo,
        weight,
        normed,
        raw,
        queries,
        attended,
        produced,
        keys,
        values,
        lse,
        *tables,
        head_gain,
        slots2,
        gates2,
    )
    sum_q, sum_k, sum_v, sum_o, all_gain_parts, grad_input, mixed_high = reduce_last(
        nz,
        columns,
        grad_weight,
        grad_wo,
        produced,
        part,
        tokens.reshape(seq, width),
        grad_hidden,
        gains,
        grad_gain_mlp.reshape(1, width),
        grad_head,
        slots2,
        gates2,
    )
    mixed = hidden + jnp.concatenate([mixed_low, mixed_high], axis=1)
    gain_sums = jnp.sum(all_gain_parts, axis=0).reshape(-1)
    norm_sums = gain_sums[: 2 * width].reshape(2, width)
    head_sums = gain_sums[2 * width : 2 * width + 2 * HD].reshape(2, HD)
    return (
        mixed.astype(bf16).reshape(tokens.shape),
        grad_input.reshape(tokens.shape),
        sum_q,
        sum_k,
        sum_v,
        sum_o,
        lax.dynamic_slice_in_dim(norm_sums, me * share, share, 1),
        lax.dynamic_slice_in_dim(head_sums, me * head_share, head_share, 1),
        grad_gate[None],
        grad_up[None],
        grad_down[None],
    )


def solution(mesh):
    small = mesh.shape["ctx"] == HK and mesh.size == 32
    return jax.shard_map(
        fast_body if small else body,
        mesh=mesh,
        in_specs=(
            P("expert", "ctx", None),
            P(("ctx", "expert"), None),
            P(("ctx", "expert"), None),
            P(("ctx", "expert"), None),
            P(("ctx", "expert"), None),
            P(None, ("ctx", "expert")),
            P(None, ("ctx", "expert")),
            P(("ctx", "expert"), None, None),
            P(("ctx", "expert"), None, None),
            P(("ctx", "expert"), None, None),
            P("expert", "ctx", None),
            P("expert", "ctx", None),
            P("expert", "ctx", None),
        ),
        out_specs=(
            P("expert", "ctx", None),
            P("expert", "ctx", None),
            P(("ctx", "expert"), None),
            P(("ctx", "expert"), None),
            P(("ctx", "expert"), None),
            P(("ctx", "expert"), None),
            P(None, ("ctx", "expert")),
            P(None, ("ctx", "expert")),
            P(("ctx", "expert"), None, None),
            P(("ctx", "expert"), None, None),
            P(("ctx", "expert"), None, None),
        ),
        check_vma=False,
    )
```

```python
import functools

import jax
import jax.numpy as jnp
from jax import lax
from jax.experimental import pallas as pl
from jax.experimental.pallas import tpu as pltpu
from jax.sharding import PartitionSpec as P

HQ = 32
HK = 4
HD = 128


epsilon = 1e-06
rope_base = 1000000.0
masked_value = -1e30


def rms_scale(values, scale_gain):
    return (
        values * lax.rsqrt(jnp.mean(values * values, axis=-1, keepdims=True) + epsilon) * scale_gain
    )


def rotate(values, positions):
    half_size = values.shape[-1] // 2
    frequency = rope_base ** (-jnp.arange(half_size, dtype=jnp.float32) / half_size)
    angles = positions.astype(jnp.float32)[:, None] * frequency[None, :]
    cosine = jnp.cos(angles)[:, None, :]
    sine_part = jnp.sin(angles)[:, None, :]
    first_half = values[..., :half_size]
    second_half = values[..., half_size:]
    return jnp.concatenate(
        [
            first_half * cosine - second_half * sine_part,
            second_half * cosine + first_half * sine_part,
        ],
        axis=-1,
    )


def body(
    tokens,
    query_weight,
    key_weight,
    value_weight,
    output_weight,
    norm_gains,
    head_gains,
    expert_gate,
    expert_up,
    expert_down,
    routes,
    route_gates,
    cotangent,
):
    seq_rows = tokens.shape[1]
    width = tokens.shape[2]
    groups = HQ // HK
    kv_width = HK * HD
    scale = HD ** (-0.5)
    positions = lax.axis_index("ctx") * seq_rows + jnp.arange(seq_rows, dtype=jnp.int32)
    last_pos = lax.axis_index("ctx") * seq_rows + seq_rows - 1
    rows_in = tokens.reshape(seq_rows, width).astype(jnp.float32)
    full_q, full_k, full_v, full_o, gains, head_gain = (
        lax.all_gather(query_weight, ("ctx", "expert"), axis=0, tiled=True),
        lax.all_gather(key_weight, ("ctx", "expert"), axis=0, tiled=True),
        lax.all_gather(value_weight, ("ctx", "expert"), axis=0, tiled=True),
        lax.all_gather(output_weight, ("ctx", "expert"), axis=0, tiled=True),
        lax.all_gather(norm_gains, ("ctx", "expert"), axis=1, tiled=True),
        lax.all_gather(head_gains, ("ctx", "expert"), axis=1, tiled=True),
    )

    def head_prep(raw_heads, gain_vec):
        return rotate(rms_scale(raw_heads, gain_vec), positions)

    normed = rms_scale(rows_in, gains[0].astype(jnp.float32)).astype(jnp.bfloat16)
    query_raw = jnp.dot(normed, full_q, preferred_element_type=jnp.float32).reshape(
        seq_rows, HQ, HD
    )
    key_raw = jnp.dot(normed, full_k, preferred_element_type=jnp.float32).reshape(seq_rows, HK, HD)
    value_rows = jnp.dot(normed, full_v, preferred_element_type=jnp.float32).astype(jnp.bfloat16)
    query_gain = head_gain[0].astype(jnp.float32)
    key_gain = head_gain[1].astype(jnp.float32)
    queries = head_prep(query_raw, query_gain).astype(jnp.bfloat16)
    keys_rot = head_prep(key_raw, key_gain).astype(jnp.bfloat16)
    kv_rows = jnp.concatenate([keys_rot.reshape(seq_rows, kv_width), value_rows], axis=1)
    grouped = queries.reshape(seq_rows, HK, groups, HD)

    def scores_for(key_block, base_row):
        scores = (
            jnp.einsum("qhgd,khd->hgqk", grouped, key_block, preferred_element_type=jnp.float32)
            * scale
        )
        key_pos = base_row + jnp.arange(key_block.shape[0], dtype=jnp.int32)
        allowed = key_pos[None, :] <= positions[:, None]
        return (scores, allowed)

    start_state = (
        jnp.full((HK, groups, seq_rows), masked_value, jnp.float32),
        jnp.zeros((HK, groups, seq_rows), jnp.float32),
        jnp.zeros((HK, groups, seq_rows, HD), jnp.float32),
    )
    shard_rows = lax.all_gather(kv_rows, "ctx", axis=0, tiled=True)
    blocks = shard_rows.reshape(shard_rows.shape[0] // seq_rows, seq_rows, 2 * kv_width)

    def step(state_now, element):
        block_index, block_rows = element
        base_row = block_index * seq_rows

        def step_visit(state_in):
            largest, total_sum, accum = state_in
            key_block = block_rows[:, :kv_width].reshape(seq_rows, HK, HD)
            value_block = block_rows[:, kv_width:].reshape(seq_rows, HK, HD)
            scores, allowed = scores_for(key_block, base_row)
            scores = jnp.where(allowed, scores, masked_value)
            new_largest = jnp.maximum(largest, jnp.max(scores, axis=-1))
            weights = jnp.where(allowed, jnp.exp(scores - new_largest[..., None]), 0.0)
            factor = jnp.exp(largest - new_largest)
            total_sum = total_sum * factor + jnp.sum(weights, axis=-1)
            accum = accum * factor[..., None] + jnp.einsum(
                "hgqk,khd->hgqd",
                weights.astype(jnp.bfloat16),
                value_block,
                preferred_element_type=jnp.float32,
            )
            return (new_largest, total_sum, accum)

        def step_skip(state_in):
            return state_in

        return (lax.cond(base_row <= last_pos, step_visit, step_skip, state_now), None)

    final_state, unused = lax.scan(
        step, start_state, (jnp.arange(blocks.shape[0], dtype=jnp.int32), blocks)
    )
    largest, total_sum, accum = final_state
    attended = (accum / total_sum[..., None]).transpose(2, 0, 1, 3).reshape(seq_rows, HQ * HD)
    log_total = largest + jnp.log(total_sum)
    attended_low = attended.astype(jnp.bfloat16)
    hidden = rows_in + jnp.dot(attended_low, full_o, preferred_element_type=jnp.float32)
    normed_mlp = rms_scale(hidden, gains[1].astype(jnp.float32)).astype(jnp.bfloat16)
    devices = lax.axis_size(("ctx", "expert"))
    local_experts = expert_gate.shape[0]
    experts = local_experts * devices
    topk = routes.shape[2]
    capacity = max(2, 5 * seq_rows * topk // (4 * experts))
    route_ids = routes.reshape(seq_rows * topk)
    onehot = (route_ids[:, None] == jnp.arange(experts, dtype=jnp.int32)[None, :]).astype(jnp.int32)
    slots = jnp.sum((jnp.cumsum(onehot, axis=0) - 1) * onehot, axis=1)
    target = route_ids * capacity + slots
    owner_row = jnp.arange(seq_rows * topk, dtype=jnp.int32) // topk
    gate_rows = route_gates.reshape(seq_rows, topk)

    def to_slots(row_block):
        buffer = (
            jnp.zeros((experts * capacity, row_block.shape[1]), row_block.dtype)
            .at[target]
            .set(row_block)
        )
        return buffer.reshape(devices, local_experts * capacity, row_block.shape[1])

    def to_experts(arrived):
        return (
            arrived.reshape(devices, local_experts, capacity, -1)
            .transpose(1, 0, 2, 3)
            .reshape(local_experts, devices * capacity, -1)
        )

    def from_experts(expert_rows):
        return (
            expert_rows.reshape(local_experts, devices, capacity, -1)
            .transpose(1, 0, 2, 3)
            .reshape(devices, local_experts * capacity, -1)
        )

    arrived = to_experts(
        lax.all_to_all(
            to_slots(normed_mlp[owner_row]),
            ("ctx", "expert"),
            split_axis=0,
            concat_axis=0,
            tiled=True,
        )
    )
    gate_pre = jnp.einsum("erd,edf->erf", arrived, expert_gate, preferred_element_type=jnp.float32)
    up_pre = jnp.einsum("erd,edf->erf", arrived, expert_up, preferred_element_type=jnp.float32)
    sigmoid_gate = jax.nn.sigmoid(gate_pre)
    swish_gate = gate_pre * sigmoid_gate
    activated = (swish_gate * up_pre).astype(jnp.bfloat16)
    produced = jnp.einsum(
        "erf,efd->erd", activated, expert_down, preferred_element_type=jnp.float32
    ).astype(jnp.bfloat16)
    returned = lax.all_to_all(
        from_experts(produced), ("ctx", "expert"), split_axis=0, concat_axis=0, tiled=True
    ).reshape(experts * capacity, width)
    expert_out = returned[target].astype(jnp.float32).reshape(seq_rows, topk, width)
    mixed = hidden + jnp.sum(gate_rows[:, :, None] * expert_out, axis=1)
    full_q, full_k, full_v, full_o, gains, head_gain = (
        lax.all_gather(query_weight, ("ctx", "expert"), axis=0, tiled=True),
        lax.all_gather(key_weight, ("ctx", "expert"), axis=0, tiled=True),
        lax.all_gather(value_weight, ("ctx", "expert"), axis=0, tiled=True),
        lax.all_gather(output_weight, ("ctx", "expert"), axis=0, tiled=True),
        lax.all_gather(norm_gains, ("ctx", "expert"), axis=1, tiled=True),
        lax.all_gather(head_gains, ("ctx", "expert"), axis=1, tiled=True),
    )
    grad_out = cotangent.reshape(seq_rows, width).astype(jnp.float32)
    grad_rows = (
        (gate_rows[:, :, None] * grad_out[:, None, :])
        .astype(jnp.bfloat16)
        .reshape(seq_rows * topk, width)
    )
    grad_arrived = to_experts(
        lax.all_to_all(
            to_slots(grad_rows), ("ctx", "expert"), split_axis=0, concat_axis=0, tiled=True
        )
    )
    grad_down = jnp.einsum(
        "erf,erd->efd", activated, grad_arrived, preferred_element_type=jnp.float32
    )
    grad_act = jnp.einsum(
        "erd,efd->erf", grad_arrived, expert_down, preferred_element_type=jnp.float32
    )
    grad_up_pre = (grad_act * swish_gate).astype(jnp.bfloat16)
    grad_gate_pre = (
        grad_act * up_pre * sigmoid_gate * (1.0 + gate_pre * (1.0 - sigmoid_gate))
    ).astype(jnp.bfloat16)
    grad_gate = jnp.einsum(
        "erd,erf->edf", arrived, grad_gate_pre, preferred_element_type=jnp.float32
    )
    grad_up = jnp.einsum("erd,erf->edf", arrived, grad_up_pre, preferred_element_type=jnp.float32)
    grad_inputs = jnp.einsum(
        "erf,edf->erd", grad_gate_pre, expert_gate, preferred_element_type=jnp.float32
    )
    grad_inputs = (
        grad_inputs
        + jnp.einsum("erf,edf->erd", grad_up_pre, expert_up, preferred_element_type=jnp.float32)
    ).astype(jnp.bfloat16)
    grad_back = lax.all_to_all(
        from_experts(grad_inputs), ("ctx", "expert"), split_axis=0, concat_axis=0, tiled=True
    ).reshape(experts * capacity, width)
    grad_normed_mlp = jnp.sum(
        grad_back[target].astype(jnp.float32).reshape(seq_rows, topk, width), axis=1
    )
    unused_norm, norm_pull = jax.vjp(rms_scale, hidden, gains[1].astype(jnp.float32))
    grad_hidden_norm, grad_gain_mlp = norm_pull(grad_normed_mlp)
    grad_hidden = grad_out + grad_hidden_norm
    grad_branch = grad_hidden.astype(jnp.bfloat16)
    grad_wo = jnp.einsum("qa,qd->ad", attended_low, grad_branch, preferred_element_type=jnp.float32)
    grad_attended = jnp.einsum(
        "qd,ad->qa", grad_branch, full_o, preferred_element_type=jnp.float32
    ).astype(jnp.bfloat16)
    all_kv = lax.all_gather(kv_rows, "ctx", axis=0, tiled=True)
    grad_grouped = grad_attended.reshape(seq_rows, HK, groups, HD)
    delta = jnp.einsum(
        "qhgd,qhgd->hgq",
        grad_grouped.astype(jnp.float32),
        attended.reshape(seq_rows, HK, groups, HD),
    )
    kv_blocks = all_kv.reshape(-1, seq_rows, 2 * kv_width)

    def back_step(grad_query, element):
        block_index, block_rows = element
        base_row = block_index * seq_rows

        def back_visit(grad_in):
            key_block = block_rows[:, :kv_width].reshape(seq_rows, HK, HD)
            value_block = block_rows[:, kv_width:].reshape(seq_rows, HK, HD)
            scores, allowed = scores_for(key_block, base_row)
            probs = jnp.where(allowed, jnp.exp(scores - log_total[..., None]), 0.0)
            grad_probs = jnp.einsum(
                "qhgd,khd->hgqk", grad_grouped, value_block, preferred_element_type=jnp.float32
            )
            grad_scores = (probs * (grad_probs - delta[..., None])).astype(jnp.bfloat16)
            grad_next = grad_in + jnp.einsum(
                "hgqk,khd->qhgd", grad_scores, key_block, preferred_element_type=jnp.float32
            )
            grad_keys = (
                jnp.einsum(
                    "hgqk,qhgd->khd", grad_scores, grouped, preferred_element_type=jnp.float32
                )
                * scale
            )
            grad_values = jnp.einsum(
                "hgqk,qhgd->khd",
                probs.astype(jnp.bfloat16),
                grad_grouped,
                preferred_element_type=jnp.float32,
            )
            joined = jnp.concatenate(
                [grad_keys.reshape(seq_rows, kv_width), grad_values.reshape(seq_rows, kv_width)],
                axis=1,
            )
            return (grad_next, joined)

        def back_skip(grad_in):
            return (grad_in, jnp.zeros((seq_rows, 2 * kv_width), jnp.float32))

        return lax.cond(base_row <= last_pos, back_visit, back_skip, grad_query)

    grad_query, grad_kv_terms = lax.scan(
        back_step,
        jnp.zeros((seq_rows, HK, groups, HD), jnp.float32),
        (jnp.arange(kv_blocks.shape[0], dtype=jnp.int32), kv_blocks),
    )
    grad_query = grad_query * scale
    grad_kv = lax.psum_scatter(
        grad_kv_terms.reshape(-1, 2 * kv_width).astype(jnp.bfloat16),
        "ctx",
        scatter_dimension=0,
        tiled=True,
    ).astype(jnp.float32)
    unused_query, pull_query = jax.vjp(head_prep, query_raw, query_gain)
    grad_query_raw, grad_query_gain = pull_query(grad_query.reshape(seq_rows, HQ, HD))
    unused_key, pull_key = jax.vjp(head_prep, key_raw, key_gain)
    grad_key_raw, grad_key_gain = pull_key(grad_kv[:, :kv_width].reshape(seq_rows, HK, HD))
    grad_q_low = grad_query_raw.reshape(seq_rows, HQ * HD).astype(jnp.bfloat16)
    grad_k_low = grad_key_raw.reshape(seq_rows, kv_width).astype(jnp.bfloat16)
    grad_v_low = grad_kv[:, kv_width:].astype(jnp.bfloat16)
    grad_wq = jnp.einsum("qd,qa->da", normed, grad_q_low, preferred_element_type=jnp.float32)
    grad_wk = jnp.einsum("qd,qa->da", normed, grad_k_low, preferred_element_type=jnp.float32)
    grad_wv = jnp.einsum("qd,qa->da", normed, grad_v_low, preferred_element_type=jnp.float32)
    grad_normed = jnp.einsum("qa,da->qd", grad_q_low, full_q, preferred_element_type=jnp.float32)
    grad_normed = grad_normed + jnp.einsum(
        "qa,da->qd", grad_k_low, full_k, preferred_element_type=jnp.float32
    )
    grad_normed = grad_normed + jnp.einsum(
        "qa,da->qd", grad_v_low, full_v, preferred_element_type=jnp.float32
    )
    unused_attn, pull_attn = jax.vjp(rms_scale, rows_in, gains[0].astype(jnp.float32))
    grad_rows_norm, grad_gain_attn = pull_attn(grad_normed)
    grad_input = grad_hidden + grad_rows_norm
    gain_grads = jnp.stack([grad_gain_attn, grad_gain_mlp])
    head_grads = jnp.stack([grad_query_gain, grad_key_gain])
    sum_q, sum_k, sum_v, sum_o, sum_gain, sum_head = (
        lax.psum_scatter(grad_wq, ("ctx", "expert"), scatter_dimension=0, tiled=True),
        lax.psum_scatter(grad_wk, ("ctx", "expert"), scatter_dimension=0, tiled=True),
        lax.psum_scatter(grad_wv, ("ctx", "expert"), scatter_dimension=0, tiled=True),
        lax.psum_scatter(grad_wo, ("ctx", "expert"), scatter_dimension=0, tiled=True),
        lax.psum_scatter(gain_grads, ("ctx", "expert"), scatter_dimension=1, tiled=True),
        lax.psum_scatter(head_grads, ("ctx", "expert"), scatter_dimension=1, tiled=True),
    )
    return (
        mixed.astype(jnp.bfloat16).reshape(tokens.shape),
        grad_input.astype(jnp.bfloat16).reshape(tokens.shape),
        sum_q,
        sum_k,
        sum_v,
        sum_o,
        sum_gain,
        sum_head,
        grad_gate,
        grad_up,
        grad_down,
    )


MESH = pl.DeviceIdType.MESH
VMEM_BYTES = 58 * 2**20
LAST_DEEP = 0
DEEP = 32
ANY = pl.BlockSpec(memory_space=pl.ANY)
IN_VMEM = pl.BlockSpec(memory_space=pltpu.VMEM)
f32, bf16 = jnp.float32, jnp.bfloat16
NT = (((1,), (1,)), ((), ()))
TN = (((0,), (0,)), ((), ()))


class Place:
    def __init__(self):
        self.c = lax.axis_index("ctx")
        self.e = lax.axis_index("expert")
        self.k = lax.rem(self.e, 2)
        self.z = lax.div(self.e, 2)
        self.cx = self.c + 1 - 2 * lax.rem(self.c, 2)
        self.cy = lax.rem(self.c + 2, 4)
        self.cd = lax.rem(self.cx + 2, 4)
        self.dx = (self.cx, self.e)
        self.dy = (self.cy, self.e)
        self.dd = (self.cd, self.e)
        self.pair = (self.c, self.e + 1 - 2 * self.k)
        self.up = (self.c, self.e + 2)
        self.down = (self.c, self.e - 2)


def greet(p, nz, line=True, pair=True, diagonal=False):
    barrier = pltpu.get_barrier_semaphore()

    def tell(device):
        pl.semaphore_signal(barrier, inc=1, device_id=device, device_id_type=MESH)

    friends = [p.dx, p.dy] + [p.pair] * pair + [p.dd] * diagonal
    for device in friends:
        tell(device)
    count = len(friends)
    if line:
        for there, device in ((p.z > 0, p.down), (p.z < nz - 1, p.up)):

            @pl.when(there)
            def _():
                tell(device)

            count = count + there.astype(jnp.int32)
    pl.semaphore_wait(barrier, count)


def remote(src, dst, send, recv, device):
    return pltpu.make_async_remote_copy(
        src_ref=src,
        dst_ref=dst,
        send_sem=send,
        recv_sem=recv,
        device_id=device,
        device_id_type=MESH,
    )


def far_first(nz, z):
    return sorted(range(nz), key=lambda to: (-abs(to - z), to))


def near_first(nz, z):
    return sorted(range(nz), key=lambda to: (abs(to - z), to))


def pick_order(p, nz, order=far_first):
    tables = [order(nz, z) for z in range(nz)]
    return [sum(jnp.where(p.z == z, tables[z][i], 0) for z in range(nz)) for i in range(nz)]


class Spread:
    def __init__(self, p, nz, mine, block, half, send, recv, line=True, side=True, pair=True):
        self.p, self.nz, self.mine, self.block, self.half = p, nz, mine, block, half
        self.send, self.recv = send, recv
        self.line, self.side, self.pair = line, side, pair
        self.order = pick_order(p, nz, near_first) if line else [p.z]

    def ref(self, c, z, k, h=None):
        whole = self.block(c, z, k)
        return whole if h is None else whole.at[pl.ds(h * self.half, self.half)]

    def copy(self, kind, z, own=False):
        p = self.p
        at = functools.partial(self.ref, z=z, k=p.k)
        src, i, j, device = {
            "x": lambda: (at(p.c), 0, 1, p.dx),
            "y": lambda: (at(p.c), 1, 2, p.dy),
            "up": lambda: (at(p.c), 2, 0, p.up),
            "down": lambda: (at(p.c), 3, 0, p.down),
            "via_y": lambda: (at(p.cx, h=0), 4, 3, p.dy),
            "via_x": lambda: (at(p.cy, h=1), 5, 4, p.dx),
            "pair0": lambda: (at(p.c), 6, 5, p.pair),
            "pair1": lambda: (at(p.cx), 7, 6, p.pair),
            "pair2": lambda: (at(p.cy), 8, 7, p.pair),
            "pair3": lambda: (at(p.cd, h=0), 9, 8, p.pair),
            "pair4": lambda: (at(p.cd, h=1), 10, 9, p.pair),
        }[kind]()
        return remote(
            self.mine if own else src, src, self.send.at[z, i], self.recv.at[z, j], device
        )

    def got(self, j, z):
        p = self.p
        k = p.k if j < 5 else 1 - p.k
        c, h = ((p.c, None), (p.cx, None), (p.cy, None), (p.cd, 0), (p.cd, 1))[j % 5]
        ref = self.ref(c, z, k, h)
        remote(ref, ref, self.send.at[z, 0], self.recv.at[z, j], p.pair).wait_recv()

    def each(self, far, act):
        if far == 0:
            act(self.p.z, 0)
            return
        for way in (-1, 1):
            z = self.p.z + way * far

            @pl.when((z >= 0) & (z < self.nz))
            def _():
                act(z, way)

    def onward(self, z, way, act):
        if self.line and way >= 0:

            @pl.when(self.p.z > 0)
            def _():
                act(self.copy("down", z, way == 0))

        if self.line and way <= 0:

            @pl.when(self.p.z < self.nz - 1)
            def _():
                act(self.copy("up", z, way == 0))

    def direct(self):
        return ["x", "y"] * self.side + ["pair0"] * self.pair

    def along(self, far):
        def act(z, way):
            if way:
                self.got(0, z)
            self.onward(z, way, lambda copy: copy.start())
            for kind in self.direct():
                self.copy(kind, z, way == 0).start()

        self.each(far, act)

    def beside(self, z):
        for j, kinds in ((1, ["via_y", "pair1"]), (2, ["via_x", "pair2"])):
            self.got(j, z)
            for kind in kinds[: 1 + self.pair]:
                self.copy(kind, z).start()

    def across(self, z):
        for j, kind in ((3, "pair3"), (4, "pair4")):
            self.got(j, z)
            if self.pair:
                self.copy(kind, z).start()

    def from_pair(self, z):
        if self.pair:
            for j in range(5, 10 if self.side else 6):
                self.got(j, z)

    def step(self, i):
        reach = self.nz if self.line else 1
        if i < reach:
            self.along(i)
        if self.side and 1 <= i <= reach:
            self.beside(self.order[i - 1])
        if self.side and 2 <= i <= reach + 1:
            self.across(self.order[i - 2])

    def finish(self, pair=True):
        def act(z, way):
            if pair:
                self.from_pair(z)
            self.onward(z, way, lambda copy: copy.wait_send())
            for kind in self.direct():
                self.copy(kind, z, way == 0).wait_send()
            if self.side:
                for kind in ["via_y", "via_x"] + ["pair1", "pair2", "pair3", "pair4"] * self.pair:
                    self.copy(kind, z).wait_send()

        for far in range(self.nz if self.line else 1):
            self.each(far, act)


class SpreadDeep:
    def __init__(self, p, nz, mine, block, send, recv, send_in, recv_in):
        self.p, self.nz, self.mine, self.block = p, nz, mine, block
        self.send, self.recv, self.send_in, self.recv_in = send, recv, send_in, recv_in
        self.places = (p.c, p.cx, p.cy, p.cd)
        self.half = mine.shape[0] // 2

    def ref(self, r, z, h=None, k=None):
        whole = self.block(self.places[r], z, self.p.k if k is None else k)
        return whole if h is None else whole.at[pl.ds(h * self.half, self.half)]

    def near(self, i):
        p, own = self.p, self.ref(0, self.p.z)
        src, dst, device = (
            lambda: (self.mine, own, p.dx),
            lambda: (self.mine, own, p.dy),
            lambda: (self.ref(1, p.z, 0), self.ref(1, p.z, 0), p.dy),
            lambda: (self.ref(2, p.z, 1), self.ref(2, p.z, 1), p.dx),
        )[i]()
        return remote(src, dst, self.send_in.at[i], self.recv_in.at[i], device)

    def hop(self, r, z, i, own=False):
        dst = self.ref(r, z)
        device = (self.p.up, self.p.down, self.p.pair)[i]
        src = self.mine if own else dst
        return remote(src, dst, self.send.at[z, r, i], self.recv.at[z, r, i // 2], device)

    def forward(self, r, z, way, act):
        p, own = self.p, r == 0 and way == 0
        if way <= 0:

            @pl.when(p.z < self.nz - 1)
            def _():
                act(self.hop(r, z, 0, own))

        if way >= 0:

            @pl.when(p.z > 0)
            def _():
                act(self.hop(r, z, 1, own))

        act(self.hop(r, z, 2, own))

    def each(self, far, act):
        for way in (-1, 1):
            z = self.p.z + way * far

            @pl.when((z >= 0) & (z < self.nz))
            def _():
                act(z, way)

    def step(self, i):
        start = lambda copy: copy.start()
        z = self.p.z
        if i == 0:
            self.near(0).start()
            self.near(1).start()
            self.forward(0, z, 0, start)
        elif i == 1:
            for n in (0, 1):
                ref = self.ref(1 + n, z)
                remote(ref, ref, self.send_in.at[n], self.recv_in.at[n], self.p.pair).wait_recv()
                self.near(2 + n).start()
                self.forward(1 + n, z, 0, start)
        elif i == 2:
            for n in (0, 1):
                ref = self.ref(3, z, n)
                remote(
                    ref, ref, self.send_in.at[n], self.recv_in.at[2 + n], self.p.pair
                ).wait_recv()
            self.forward(3, z, 0, start)
        elif i < self.nz + 2:

            def act(z, way):
                for r in range(4):
                    self.got(r, z, 0)
                    self.forward(r, z, way, start)

            self.each(i - 2, act)

    def got(self, r, z, i):
        ref = self.ref(r, z, None, self.p.k if i == 0 else 1 - self.p.k)
        remote(ref, ref, self.send.at[z, r, 0], self.recv.at[z, r, i], self.p.pair).wait_recv()

    def finish(self, pair=True):
        def act(z, way):
            for r in range(4):
                if pair:
                    self.got(r, z, 1)
                self.forward(r, z, way, lambda copy: copy.wait_send())

        for i in range(4):
            self.near(i).wait_send()
        act(self.p.z, 0)
        for far in range(1, self.nz):
            self.each(far, act)


def deep_sems(nz):
    dma = pltpu.SemaphoreType.DMA
    return [dma((nz, 4, 3)), dma((nz, 4, 2)), dma((4,)), dma((4,))]


def lines_of(ref, nz, first, count):
    return lambda c, z, k: ref.at[c * (2 * nz) + z * 2 + k, pl.ds(first, count)]


def by_device(ref, nz):
    return lambda c, z, k: ref.at[c * (2 * nz) + z * 2 + k]


def spread_sems(nz):
    return [pltpu.SemaphoreType.DMA((nz, 11)), pltpu.SemaphoreType.DMA((nz, 10))]


class Fold:
    def __init__(self, p, parts, sx, sy, h0, h1, bx, by, send, recv, far=None):
        far = parts if far is None else far
        half = bx.shape[0] // 2
        self.halves = low, high = pl.ds(0, half), pl.ds(half, half)
        self.p, self.parts, self.sx, self.sy = p, parts, sx, sy
        self.h0, self.h1, self.bx, self.by = h0, h1, bx, by
        copy = lambda i, src, dst, device: remote(src, dst, send.at[i], recv.at[i], device)
        self.to_x = copy(0, far.at[p.cd, low], h0, p.dx)
        self.to_y = copy(1, far.at[p.cd, high], h1, p.dy)
        self.x_low = copy(2, far.at[p.cx, low], bx.at[low], p.dx)
        self.y_high = copy(3, far.at[p.cy, high], by.at[high], p.dy)
        self.x_high = copy(4, sx, bx.at[high], p.dx)
        self.y_low = copy(5, sy, by.at[low], p.dy)

    def begin(self):
        for copy in (self.to_x, self.to_y, self.x_low, self.y_high):
            copy.start()

    def middle(self):
        p, (low, high), parts = self.p, self.halves, self.parts
        self.to_y.wait_recv()
        total = parts[p.cx, high].astype(f32) + self.h1[...].astype(f32)
        self.sx[...] = total.astype(self.sx.dtype)
        self.x_high.start()
        self.to_x.wait_recv()
        total = parts[p.cy, low].astype(f32) + self.h0[...].astype(f32)
        self.sy[...] = total.astype(self.sy.dtype)
        self.y_low.start()

    def end(self, store):
        p, parts = self.p, self.parts
        low, high = self.halves
        for rows, waits in ((low, (self.x_low, self.y_low)), (high, (self.y_high, self.x_high))):
            for copy in waits:
                copy.wait_recv()
            total = parts[p.c, rows].astype(f32) + self.bx[rows].astype(f32)
            store(rows, total + self.by[rows].astype(f32))
        for copy in (self.to_x, self.to_y, self.x_low, self.y_high, self.x_high, self.y_low):
            copy.wait_send()


def fold_scratch(seq, width):
    buf = lambda r: pltpu.VMEM((r, width), bf16)
    return (
        [buf(seq // 2)] * 4 + [buf(seq)] * 2 + [pltpu.SemaphoreType.DMA((6,))] * 2
    )


def front_kernel(nz, scale, *refs):
    pack, wo, tok, cot, meta, cosine, sine = refs[:7]
    packs, wos, toks, cots, metas = refs[7:12]
    results, held = refs[12:25], refs[25:38]
    xn, raw, q, k, v, ot, lse, hidden, hn, gain_out, head_out, slots, gates = held
    tok_v, w_v, wo_v, meta_v, vt, ob, part = refs[38:45]
    fold_refs, pair_sems = refs[45:53], refs[53:63]
    a_send, a_recv, local, load, out_sem = refs[63:68]

    def copy_out(*which):
        for i in which:
            pltpu.make_async_copy(held[i], results[i], out_sem.at[i]).start()

    p = Place()
    seq, width = tok.shape
    length = 4 * seq
    heads = q.shape[0]
    me = p.c * (2 * nz) + p.e
    greet(p, nz, diagonal=True)
    into = [
        pltpu.make_async_copy(src, dst, local.at[i])
        for i, (src, dst) in enumerate(
            (
                (pack.at[p.c], w_v.at[p.c, p.e]),
                (wo, wo_v.at[p.e]),
                (tok, tok_v.at[p.c]),
                (cot, part.at[0]),
            )
        )
    ]
    own = [
        pltpu.make_async_copy(src, dst, local.at[4 + i])
        for i, (src, dst) in enumerate(
            (
                (w_v.at[p.c, p.e], packs.at[p.c, p.e]),
                (wo_v.at[p.e], wos.at[p.e]),
                (meta, metas.at[me]),
                (part.at[0], cots.at[me]),
            )
        )
    ]
    loads = [
        pltpu.make_async_copy(src, dst, load.at[i])
        for i, (src, dst) in enumerate(
            [(packs, w_v), (wos, wo_v), (metas, meta_v)]
            + [(toks.at[c], tok_v.at[c]) for c in (p.cx, p.cy, p.cd)]
        )
    ]
    for copy in into:
        copy.start()
    own[2].start()
    swaps = [
        remote(pack.at[c], packs.at[p.c, p.e], a_send.at[i], a_recv.at[i], device)
        for i, (c, device) in enumerate(((p.cx, p.dx), (p.cy, p.dy), (p.cd, p.dd)))
    ]
    for copy in swaps:
        copy.start()

    def job(i, src, block, half, *ways):
        return Spread(p, nz, src, block, half, *pair_sems[2 * i : 2 * i + 2], *ways)

    j_tok = job(0, tok, lambda c, z, k: toks.at[c], seq // 2, False, True, False)
    j_meta = job(1, meta, by_device(metas, nz), meta.shape[0] // 2)
    most = seq - DEEP
    j_cot = job(2, cot.at[pl.ds(0, most)], lines_of(cots, nz, 0, most), most // 2)
    j_deep = SpreadDeep(
        p, nz, cot.at[pl.ds(most, DEEP)], lines_of(cots, nz, most, DEEP), *refs[68:]
    )
    j_wo = job(3, wo, lambda c, z, k: wos.at[z * 2 + k], 0, True, False, True)
    own_pack = packs.at[:, p.e]
    j_pack = job(4, own_pack, lambda c, z, k: packs.at[:, z * 2 + k], 0, True, False, True)
    j_meta.step(0)
    j_tok.step(0)
    for i in (0, 1, 3):
        into[i].wait()
        own[i].start()
    for i, c in enumerate((p.cx, p.cy, p.cd)):
        ref = packs.at[c, p.e]
        remote(ref, ref, a_send.at[i], a_recv.at[i], p.dx).wait_recv()
    own[0].wait()
    j_pack.step(0)
    j_meta.step(1)
    j_pack.step(1)
    j_tok.step(1)
    loads[3].start()
    loads[4].start()
    j_tok.step(2)
    loads[5].start()
    j_meta.step(2)
    j_pack.step(2)
    j_cot.step(0)
    j_deep.step(0)
    for i in range(3, nz + 2):
        j_meta.step(i)
        j_pack.step(i)
    own[2].wait()
    for z in j_meta.order:
        j_meta.from_pair(z)
    loads[2].start()
    j_wo.step(0)
    for z in j_pack.order:
        j_pack.from_pair(z)
    loads[0].start()

    loads[2].wait()
    n = meta_lines(q.shape[1], width, seq)
    per = 128 * 8 * nz // width

    def gain(line):
        found = [
            sum(meta_v[per * j + i, pl.ds(line, 1)] for i in range(per))
            for j in range(width // 128)
        ]
        return jnp.concatenate(found, axis=1)

    def head_gain(line):
        return sum(meta_v[b, pl.ds(line, 1)] for b in range(8 * nz))

    gain_out[0:1] = gain(n)
    gain_out[1:2] = gain(n + 1)
    head_out[0:1] = head_gain(n + 2)
    head_out[1:2] = head_gain(n + 3)

    def rms(x, g):
        return x * lax.rsqrt(jnp.mean(x * x, axis=-1, keepdims=True) + epsilon) * g

    into[2].wait()
    for copy in loads[3:]:
        copy.wait()

    @pl.loop(0, 8)
    def _(i):
        c, h = lax.div(i, 2), lax.rem(i, 2)
        half = seq // 2
        rows = tok_v[c, pl.ds(pl.multiple_of(h * half, half), half)].astype(f32)
        here = pl.ds(pl.multiple_of(i * half, half), half)
        xn[here] = rms(rows, gain_out[0:1]).astype(bf16)

    loads[0].wait()

    @pl.loop(0, raw.shape[1] // 256)
    def _(t):
        cols = pl.ds(pl.multiple_of(t * 256, 256), 256)
        w = w_v[:, :, :, cols].reshape(width, 256)
        raw[:, cols] = jnp.dot(xn[...], w, preferred_element_type=f32)

    copy_out(0, 1, 9, 10)
    j_cot.step(1)
    j_deep.step(1)
    j_wo.step(1)

    def prep(x, g):
        y = rms(x, g)
        return (y * cosine[...] + pltpu.roll(y, HD // 2, 1) * sine[...]).astype(bf16)

    k[...] = prep(raw[:, pl.ds(heads * HD, HD)], head_out[1:2])
    values = raw[:, pl.ds((heads + 1) * HD, HD)]
    v[...] = values.astype(bf16)
    vt[...] = values.T.astype(bf16)
    copy_out(3, 4)

    def attend(h):
        cols = pl.ds(pl.multiple_of(h * HD, HD), HD)
        q[h] = prep(raw[:, cols], head_out[0:1])
        for i in range(length // seq):
            keys = (i + 1) * seq
            here = pl.ds(i * seq, seq)
            s = lax.dot_general(k[pl.ds(0, keys)], q[h, here], NT, preferred_element_type=f32)
            s = s * scale
            key_pos = lax.broadcasted_iota(jnp.int32, s.shape, 0)
            query_pos = lax.broadcasted_iota(jnp.int32, s.shape, 1) + i * seq
            s = jnp.where(key_pos <= query_pos, s, masked_value)
            largest = jnp.max(s, axis=0, keepdims=True)
            weights = jnp.exp(s - largest)
            total = jnp.sum(weights, axis=0, keepdims=True)
            o = jnp.dot(vt[:, pl.ds(0, keys)], weights.astype(bf16), preferred_element_type=f32)
            o = o / total
            ot[h, :, here] = o.astype(bf16)
            ob[here, cols] = o.T.astype(bf16)
            lse[h, :, here] = largest + jnp.log(total)

    pl.loop(0, heads // 2)(attend)
    j_wo.step(2)
    j_cot.step(2)
    j_deep.step(2)
    pl.loop(heads // 2, heads)(attend)
    copy_out(2, 5, 6)
    for i in range(3, nz + 2):
        j_wo.step(i)
    own[1].wait()
    for z in j_wo.order:
        j_wo.from_pair(z)
    loads[1].start()
    own[3].wait()

    upto = lax.broadcasted_iota(jnp.int32, (seq, seq), 0) <= lax.broadcasted_iota(
        jnp.int32, (seq, seq), 1
    )
    upto = upto.astype(f32).astype(bf16)
    lines = seq // 128
    topk = n // lines // 2
    for j, expert in enumerate((me, me + 1 - 2 * p.k)):
        expert = expert.astype(f32)
        member, weight = [], []
        for line in range(lines):
            named = [meta_v[:, i * lines + line] == expert for i in range(topk)]
            gate = [meta_v[:, (topk + i) * lines + line] for i in range(topk)]
            member.append(sum(x.astype(f32) for x in named))
            weight.append(sum(jnp.where(x, y, 0.0) for x, y in zip(named, gate)))
        member = jnp.concatenate(member, axis=1)
        rank = jnp.dot(member.astype(bf16), upto, preferred_element_type=f32)
        slots[j] = jnp.where(member > 0.5, rank.astype(jnp.int32) - 1, -1)
        gates[j] = jnp.concatenate(weight, axis=1)

    copy_out(11, 12)
    loads[1].wait()
    tile = 512

    @pl.loop(0, width // tile)
    def _(t):
        cols = pl.ds(pl.multiple_of(t * tile, tile), tile)
        w = wo_v[:, :, cols].reshape(heads * HD, tile)
        out = jnp.dot(ob[...], w, preferred_element_type=f32)
        part[:, :, cols] = out.astype(bf16).reshape(4, seq, tile)

    fold = Fold(p, part, *fold_refs)
    fold.begin()
    j_cot.step(3)
    j_deep.step(3)
    fold.middle()

    def store(rows, total):
        h = tok_v[p.c, rows].astype(f32) + total
        hidden[rows] = h
        hn[rows] = rms(h, gain_out[1:2]).astype(bf16)

    fold.end(store)
    copy_out(7, 8)
    for i in range(4, nz + 2):
        j_cot.step(i)
        j_deep.step(i)
    for copy in swaps:
        copy.wait_send()
    for spread in (j_tok, j_meta, j_cot, j_wo, j_pack):
        spread.finish(pair=spread is j_cot)
    j_deep.finish()
    for i in range(len(held)):
        pltpu.make_async_copy(held[i], results[i], out_sem.at[i]).wait()


def meta_lines(length, width, seq):
    return 2 * 8 * seq // 128


def front(nz, scale, pack, wo, tok, cot, meta, cosine, sine):
    blocks = 8 * nz
    seq, width = tok.shape
    length = 4 * seq
    wide = pack.shape[2]
    heads = wide // HD - 2
    hbm = lambda n, a: jax.ShapeDtypeStruct(n + a.shape, a.dtype)
    out = lambda *n: jax.ShapeDtypeStruct(n[:-1], n[-1])
    vmem = lambda *n: pltpu.VMEM(n, bf16)
    dma = pltpu.SemaphoreType.DMA
    held = [
        out(length, width, bf16),
        out(length, wide, f32),
        out(heads, length, HD, bf16),
        out(length, HD, bf16),
        out(length, HD, bf16),
        out(heads, HD, length, bf16),
        out(heads, 1, length, f32),
        out(seq, width, f32),
        out(seq, width, bf16),
        out(2, width, f32),
        out(2, HD, f32),
        out(2, blocks, seq, jnp.int32),
        out(2, blocks, seq, f32),
    ]
    return pl.pallas_call(
        functools.partial(front_kernel, nz, scale),
        out_shape=[
            jax.ShapeDtypeStruct((4, 2 * nz) + pack.shape[1:], bf16),
            hbm((2 * nz,), wo),
            hbm((4,), tok),
            hbm((blocks,), cot),
            hbm((blocks,), meta),
        ]
        + held,
        in_specs=[ANY] * 5 + [IN_VMEM] * 2,
        out_specs=[ANY] * 18,
        scratch_shapes=[pltpu.VMEM(a.shape, a.dtype) for a in held]
        + [
            vmem(4, seq, width),
            vmem(4, 2 * nz, pack.shape[1], wide),
            vmem(2 * nz, wo.shape[0], width),
            pltpu.VMEM((blocks,) + meta.shape, f32),
            vmem(HD, length),
            vmem(length, heads * HD),
            vmem(4, seq, width),
        ]
        + fold_scratch(seq, width)
        + spread_sems(nz) * 5
        + [dma((n,)) for n in (3, 3, 8, 6, len(held))]
        + deep_sems(nz),
        compiler_params=pltpu.CompilerParams(
            collective_id=1, has_side_effects=True, vmem_limit_bytes=VMEM_BYTES
        ),
    )(pack, wo, tok, cot, meta, cosine, sine)


def spread_kernel(nz, everywhere, mine, out, send, recv, local):
    p = Place()
    greet(p, nz, line=everywhere, pair=everywhere)
    block = by_device(out, nz) if everywhere else (lambda c, z, k: out.at[c])
    keep = pltpu.make_async_copy(mine, block(p.c, p.z, p.k), local)
    keep.start()
    job = Spread(
        p, nz, mine, block, mine.shape[0] // 2, send, recv, everywhere, True, everywhere
    )
    for far in range(nz + 2 if everywhere else 3):
        job.step(far)
    keep.wait()
    job.finish()


def gather_rows(nz, everywhere, mine, collective_id):
    blocks = 8 * nz if everywhere else 4
    return pl.pallas_call(
        functools.partial(spread_kernel, nz, everywhere),
        out_shape=jax.ShapeDtypeStruct((blocks,) + mine.shape, mine.dtype),
        in_specs=[IN_VMEM],
        out_specs=ANY,
        scratch_shapes=spread_sems(nz) + [pltpu.SemaphoreType.DMA],
        compiler_params=pltpu.CompilerParams(collective_id=collective_id, has_side_effects=True),
    )(mine)


class Combine:
    def __init__(self, p, nz, cap, col, deep, rows, slots, gates, out, *scratch):
        self.p, self.nz, self.cap, self.rows, self.slots, self.gates = p, nz, cap, rows, slots, gates
        self.out = out
        self.rbuf, self.sd, self.sx, self.sy = scratch[:4]
        self.h0, self.h1, self.bx, self.by, self.bz = scratch[4:9]
        self.pair_send, self.pair_recv, self.load = scratch[9:12]
        self.s_h0, self.s_h1, self.s_x, self.s_y, self.s_z = scratch[12:17]
        self.r_h0, self.r_h1, self.r_x, self.r_y, self.r_z = scratch[17:22]
        self.order = pick_order(p, nz)
        self.most, self.width = self.sx.shape[1:]
        self.seq = self.most + deep
        self.half = self.most // 2
        self.cols = pl.ds(col, self.width)
        self.deep = deep
        self.tile = max(t for t in range(128, 1025, 128) if self.width % t == 0)
        if deep:
            self.s_d, self.b_d, self.send_d, self.recv_d = scratch[22:26]
            self.fold = Fold(p, self.s_d.at[p.z], *scratch[26:])

    def clear(self):
        bz, nz = self.bz, self.nz

        @pl.when(self.p.z == 0)
        def _():
            for ref in [bz] + ([self.b_d] if self.deep else []):
                ref[pl.ds(0, nz)] = jnp.zeros((nz,) + ref.shape[1:], ref.dtype)

        @pl.when(self.p.z == nz - 1)
        def _():
            for ref in [bz] + ([self.b_d] if self.deep else []):
                ref[pl.ds(0, nz - 1)] = jnp.zeros((nz - 1,) + ref.shape[1:], ref.dtype)
                ref[nz] = jnp.zeros(ref.shape[1:], ref.dtype)

    def pair_copy(self, c, z):
        p = self.p
        return remote(
            self.rows.at[c * (2 * self.nz) + z * 2 + 1 - p.k, :, self.cols],
            self.rbuf.at[c, z, pl.ds(self.cap, self.cap)],
            self.pair_send.at[c, z],
            self.pair_recv.at[c, z],
            p.pair,
        )

    def load_copy(self, c, z):
        return pltpu.make_async_copy(
            self.rows.at[c * (2 * self.nz) + z * 2 + self.p.k, :, self.cols],
            self.rbuf.at[c, z, pl.ds(0, self.cap)],
            self.load.at[c, z],
        )

    def begin(self):
        p = self.p
        for z in self.order:
            for c in (p.cd, p.cx, p.cy, p.c):
                self.load_copy(c, z).start()
                self.pair_copy(c, z).start()

    def places(self, c, z):
        b = pl.ds(c * (2 * self.nz) + z * 2 + self.p.k, 1)
        names = lax.broadcasted_iota(jnp.int32, (self.cap, self.seq), 0)
        both = [jnp.where(names == self.slots[n, b], self.gates[n, b], 0.0) for n in (0, 1)]
        return jnp.concatenate(both, axis=0).T.astype(bf16)

    def arrived(self, c, z):
        self.load_copy(c, z).wait()
        self.pair_copy(c, z).wait_recv()

    def copy_deep(self, z, up):
        p = self.p
        slot = z if up else jnp.where(z == p.z - 1, self.nz, z)
        return remote(
            self.s_d.at[z],
            self.b_d.at[slot],
            self.send_d.at[z],
            self.recv_d.at[slot],
            p.up if up else p.down,
        )

    def deep_send(self, z):
        @pl.when(z > self.p.z)
        def _():
            self.copy_deep(z, True).start()

        @pl.when(z < self.p.z)
        def _():
            self.copy_deep(z, False).start()

    def deep_recv(self, slot):
        ref = self.b_d.at[slot]
        remote(ref, ref, self.send_d.at[0], self.recv_d.at[slot], self.p.pair).wait_recv()

    def deep_first(self, i):
        p, nz, z = self.p, self.nz, self.order[i]
        for c in range(4):
            self.arrived(c, z)
            w = self.places(c, z)[self.most :]
            for t in range(self.width // self.tile):
                cols = pl.ds(t * self.tile, self.tile)
                total = jnp.dot(w, self.rbuf[c, z, :, cols], preferred_element_type=f32)
                self.s_d[z, c, :, cols] = total.astype(bf16)
        if i < nz - 1:

            @pl.when((p.z == 0) | (p.z == nz - 1))
            def _():
                self.deep_send(z)

    def deep_add(self, z, *slots):
        for c in range(4):
            total = self.s_d[z, c].astype(f32)
            for slot in slots:
                total = total + self.b_d[slot, c].astype(f32)
            self.s_d[z, c] = total.astype(bf16)

    def deep_next(self, i):
        p, nz, z = self.p, self.nz, self.order[i]
        if i < nz - 1:

            @pl.when((p.z > 0) & (p.z < nz - 1))
            def _():
                self.deep_recv(z)
                self.deep_add(z, z)
                self.deep_send(z)

            return

        @pl.when(p.z > 0)
        def _():
            self.deep_recv(z)

        @pl.when(p.z < nz - 1)
        def _():
            self.deep_recv(nz)

        self.deep_add(z, z, nz)
        self.fold.begin()

    def deep_end(self, i):
        if i == 0:
            self.fold.middle()
            return

        def store(lines, total):
            self.out[pl.ds(self.most + lines.start, lines.size)] = total

        self.fold.end(store)

    def fill(self, c, z, low, high, store):
        half, tile = self.half, self.tile
        w = self.places(c, z)[: self.most]
        if not self.deep:
            self.arrived(c, z)
        for t in range(self.width // tile):
            cols = pl.ds(t * tile, tile)
            total = jnp.dot(w, self.rbuf[c, z, :, cols], preferred_element_type=f32)
            for first, adds in ((0, low), (half, high)):
                part = total[first : first + half]
                for ref, start in adds:
                    part = part + ref[pl.ds(start, half), cols].astype(f32)
                store(pl.ds(first, half), cols, part)

    def into(self, buf, z):
        def store(lines, cols, total):
            buf[z, lines, cols] = total.astype(buf.dtype)

        return store

    def copy_h0(self, z):
        src = self.sd.at[z, pl.ds(0, self.half)]
        return remote(src, self.h0.at[z], self.s_h0.at[z], self.r_h0.at[z], self.p.dx)

    def copy_h1(self, z):
        src = self.sd.at[z, pl.ds(self.half, self.half)]
        return remote(src, self.h1.at[z], self.s_h1.at[z], self.r_h1.at[z], self.p.dy)

    def copy_x(self, z):
        return remote(self.sx.at[z], self.bx.at[z], self.s_x.at[z], self.r_x.at[z], self.p.dx)

    def copy_y(self, z):
        return remote(self.sy.at[z], self.by.at[z], self.s_y.at[z], self.r_y.at[z], self.p.dy)

    def copy_up(self, z):
        return remote(self.sx.at[z], self.bz.at[z], self.s_z.at[z], self.r_z.at[z], self.p.up)

    def copy_down(self, z):
        slot = jnp.where(z == self.p.z - 1, self.nz, z)
        return remote(
            self.sx.at[z], self.bz.at[slot], self.s_z.at[z], self.r_z.at[slot], self.p.down
        )

    def line_recv(self, slot):
        ref = self.bz.at[slot]
        remote(ref, ref, self.s_z.at[0], self.r_z.at[slot], self.p.pair).wait_recv()

    def diagonal(self, i):
        z = self.order[i]
        self.fill(self.p.cd, z, [], [], self.into(self.sd, z))
        self.copy_h0(z).start()
        self.copy_h1(z).start()

    def sides(self, i):
        z = self.order[i]
        self.copy_h1(z).wait_recv()
        self.fill(self.p.cx, z, [], [(self.h1.at[z], 0)], self.into(self.sx, z))
        self.copy_x(z).start()
        self.copy_h0(z).wait_recv()
        self.fill(self.p.cy, z, [(self.h0.at[z], 0)], [], self.into(self.sy, z))
        self.copy_y(z).start()

    def mine(self, i):
        p, nz, z, last = self.p, self.nz, self.order[i], i == self.nz - 1
        self.copy_x(z).wait_recv()
        self.copy_y(z).wait_recv()
        self.copy_x(z).wait_send()
        arrived = [self.bx.at[z], self.by.at[z], self.bz.at[z]]
        if last:

            @pl.when(p.z > 0)
            def _():
                self.line_recv(z)

            @pl.when(p.z < nz - 1)
            def _():
                self.line_recv(nz)

            def store(lines, cols, total):
                self.out[lines, cols] = total

            arrived.append(self.bz.at[nz])
        else:

            @pl.when(((z > p.z) & (p.z > 0)) | ((z < p.z) & (p.z < nz - 1)))
            def _():
                self.line_recv(z)

            store = self.into(self.sx, z)
        lower, upper = [(ref, 0) for ref in arrived], [(ref, self.half) for ref in arrived]
        self.fill(p.c, z, lower, upper, store)
        if not last:

            @pl.when(z > p.z)
            def _():
                self.copy_up(z).start()

            @pl.when(z < p.z)
            def _():
                self.copy_down(z).start()

    def steps(self):
        nz = self.nz
        found = [(self.diagonal, 0)] + [(self.diagonal, 1)] * (nz > 1)
        for i in range(nz):
            found.append((self.sides, i))
            if i + 2 < nz:
                found.append((self.diagonal, i + 2))
            if i > 0:
                found.append((self.mine, i - 1))
        found.append((self.mine, nz - 1))
        if self.deep:
            first = [(self.deep_first, i) for i in range(nz)]
            late = [(self.deep_next, i) for i in range(nz)]
            plan = first[:1]
            for act in found:
                if act[0] == self.diagonal and act[1] > 0:
                    plan.append(first[act[1]])
                if act == (self.mine, nz - 1):
                    plan.append(late[nz - 1])
                plan.append(act)
                if act[0] == self.sides and 1 <= act[1] < nz:
                    plan.append(late[act[1] - 1])
            found = plan + [(self.deep_end, 0), (self.deep_end, 1)]
        return [functools.partial(act, i) for act, i in found]

    def finish(self):
        p = self.p
        for i, z in enumerate(self.order):
            for c in (p.cd, p.cx, p.cy, p.c):
                self.pair_copy(c, z).wait_send()
            for copy in (self.copy_h0(z), self.copy_h1(z), self.copy_y(z)):
                copy.wait_send()
            if i < self.nz - 1:
                self.copy_up(z).wait_send()
                if self.deep:
                    self.copy_deep(z, True).wait_send()


def combine_scratch(nz, cap, seq, width, deep):
    dma = pltpu.SemaphoreType.DMA
    buf = lambda n, r: pltpu.VMEM((n, r, width), bf16)
    seq = seq - deep
    last = []
    if deep:
        last = [pltpu.VMEM((n, 4, deep, width), bf16) for n in (nz, nz + 1)]
        last += [dma((nz,)), dma((nz + 1,))] + fold_scratch(deep, width)
    return (
        [pltpu.VMEM((4, nz, 2 * cap, width), bf16)]
        + [buf(nz, seq)] * 3
        + [buf(nz, seq // 2)] * 2
        + [buf(nz, seq)] * 2
        + [buf(nz + 1, seq)]
        + [dma((4, nz))] * 3
        + [dma((nz,))] * 9
        + [dma((nz + 1,))]
        + last
    )


def combine_kernel(nz, cap, deep, rows, slots, gates, out, *scratch):
    p = Place()
    job = Combine(p, nz, cap, 0, deep, rows, slots, gates, out, *scratch)
    job.clear()
    greet(p, nz)
    job.begin()
    for step in job.steps():
        step()
    job.finish()


def combine(nz, deep, rows, slots, gates, collective_id):
    _, cap, width = rows.shape
    seq = slots.shape[2]
    return pl.pallas_call(
        functools.partial(combine_kernel, nz, cap, deep),
        out_shape=jax.ShapeDtypeStruct((seq, width), f32),
        in_specs=[ANY, IN_VMEM, IN_VMEM],
        out_specs=IN_VMEM,
        scratch_shapes=combine_scratch(nz, cap, seq, width, deep),
        compiler_params=pltpu.CompilerParams(
            collective_id=collective_id, has_side_effects=True, vmem_limit_bytes=VMEM_BYTES
        ),
    )(rows, slots, gates)


class LineSum:
    def __init__(self, p, nz, part, own, sib, b, pair_s, pair_r, line_s, line_r):
        self.p, self.nz, self.part, self.own, self.sib, self.b = p, nz, part, own, sib, b
        self.pair_s, self.pair_r, self.line_s, self.line_r = pair_s, pair_r, line_s, line_r
        self.order = pick_order(p, nz)

    def clear(self):
        b, nz = self.b, self.nz

        @pl.when(self.p.z == 0)
        def _():
            b[pl.ds(0, nz)] = jnp.zeros((nz,) + b.shape[1:], b.dtype)

        @pl.when(self.p.z == nz - 1)
        def _():
            b[pl.ds(0, nz - 1)] = jnp.zeros((nz - 1,) + b.shape[1:], b.dtype)
            b[nz] = jnp.zeros(b.shape[1:], b.dtype)

    def pair_copy(self, z):
        p = self.p
        src = self.part(z, 1 - p.k)
        return remote(src, self.sib.at[z], self.pair_s.at[z], self.pair_r.at[z], p.pair)

    def begin(self):
        for z in self.order:
            self.pair_copy(z).start()

    def copy_up(self, z):
        p = self.p
        return remote(self.own(z), self.b.at[z], self.line_s.at[z], self.line_r.at[z], p.up)

    def copy_down(self, z):
        p = self.p
        slot = jnp.where(z == p.z - 1, self.nz, z)
        return remote(self.own(z), self.b.at[slot], self.line_s.at[z], self.line_r.at[slot], p.down)

    def line_recv(self, slot):
        ref = self.b.at[slot]
        remote(ref, ref, self.line_s.at[0], self.line_r.at[slot], self.p.pair).wait_recv()

    def reduce(self, n, store=None):
        p, nz, z = self.p, self.nz, self.order[n]
        own, b = self.own(z), self.b
        self.pair_copy(z).wait_recv()
        if n == nz - 1:

            @pl.when(p.z > 0)
            def _():
                self.line_recv(z)

            @pl.when(p.z < nz - 1)
            def _():
                self.line_recv(nz)

            total = own[...].astype(f32) + self.sib[z].astype(f32) + b[z].astype(f32)
            store(total + b[nz].astype(f32))
            return

        @pl.when(((z > p.z) & (p.z > 0)) | ((z < p.z) & (p.z < nz - 1)))
        def _():
            self.line_recv(z)

        total = own[...].astype(f32) + self.sib[z].astype(f32) + b[z].astype(f32)
        own[...] = total.astype(own.dtype)

        @pl.when(z > p.z)
        def _():
            self.copy_up(z).start()

        @pl.when(z < p.z)
        def _():
            self.copy_down(z).start()

    def finish(self):
        for n, z in enumerate(self.order):
            self.pair_copy(z).wait_send()
            if n < self.nz - 1:
                self.copy_up(z).wait_send()


def line_sems(nz):
    dma = pltpu.SemaphoreType.DMA
    return [dma((nz,))] * 3 + [dma((nz + 1,))]


def rms_back(x, gain, grad):
    r = lax.rsqrt(jnp.mean(x * x, axis=-1, keepdims=True) + epsilon)
    scaled = gain * grad
    mean = jnp.mean(x * scaled, axis=-1, keepdims=True)
    by_gain = jnp.sum(x * r * grad, axis=0, keepdims=True)
    return r * scaled - x * (r * r * r * mean), by_gain


def back_kernel(nz, cap, scale, *refs):
    branch, wos, packs, xn, raw, q, ot, rows = refs[:8]
    k, v, lse, cosine, sine, head_gain, slots, gates = refs[8:16]
    sum_o, gw, part, head_grad, mixed = refs[16:21]
    rows_v, wo_v, w_v, raw_v, q_v, ot_v, do, kt, low, dq, dk, dv, w_stage, sib, line_b = refs[21:36]
    load, w_sem, ot_sem = refs[36:39]
    p = Place()
    line = LineSum(
        p,
        nz,
        lambda z, k: wo_v.at[z * 2 + k],
        lambda z: wo_v.at[z * 2 + p.k],
        sib,
        line_b,
        *refs[39:43],
    )
    combine = Combine(p, nz, cap, 0, 0, rows, slots, gates, mixed, *refs[43:])
    length, wide = raw.shape
    heads = q.shape[0]
    seq = length // 4
    width = xn.shape[2]
    loads = [
        pltpu.make_async_copy(src, dst, load.at[i])
        for i, (src, dst) in enumerate(
            ((branch, rows_v), (wos, wo_v), (q, q_v), (packs, w_v))
        )
    ]
    load_ot = [
        pltpu.make_async_copy(ot.at[pl.ds(2 * t, 2)], ot_v.at[t % 2], ot_sem.at[t % 2])
        for t in range(heads // 2)
    ]
    load_xn = pltpu.make_async_copy(xn, rows_v, load.at[5])

    def load_raw(cols):
        return pltpu.make_async_copy(raw.at[:, cols], raw_v, load.at[6])

    for copy in loads + load_ot[:2]:
        copy.start()
    combine.clear()
    line.clear()
    greet(p, nz)
    combine.begin()
    steps = combine.steps()
    run = lambda n: [steps.pop(0)() for _ in range(min(n, len(steps)))]
    kt[...] = k[...].astype(f32).T.astype(bf16)
    run(2)
    loads[0].wait()
    loads[1].wait()

    @pl.loop(0, heads * HD // 256)
    def _(t):
        cols = pl.ds(pl.multiple_of(t * 256, 256), 256)
        w = wo_v[pl.ds(t * (256 // wo_v.shape[1]), 256 // wo_v.shape[1])].reshape(256, width)
        out = lax.dot_general(rows_v[...].reshape(length, width), w, NT, preferred_element_type=f32)
        do[:, cols] = out.astype(bf16)

    run(1)

    for t in range(heads // 2):
        load_ot[t].wait()
        here = 2 * HD // wo_v.shape[1]

        @pl.loop(0, width // 512)
        def _(i):
            cols = pl.ds(pl.multiple_of(i * 512, 512), 512)
            out = jnp.dot(
                ot_v[t % 2].reshape(2 * HD, length),
                rows_v[:, :, cols].reshape(length, 512),
                preferred_element_type=f32,
            )
            wo_v[pl.ds(t * here, here), :, cols] = out.astype(bf16).reshape(
                here, wo_v.shape[1], 512
            )

        if t + 2 < heads // 2:
            load_ot[t + 2].start()

    line.begin()
    load_xn.start()
    run(1)
    loads[2].wait()
    dk[...] = jnp.zeros(dk.shape, f32)
    dv[...] = jnp.zeros(dv.shape, f32)
    head_grad[...] = jnp.zeros(head_grad.shape, f32)

    def unprep(gain, grad, cols):
        by_gain = jnp.zeros((1, HD), f32)
        for i in range(length // seq):
            here = pl.ds(i * seq, seq)
            g = grad[here]
            g = g * cosine[here] + pltpu.roll(g * sine[here], HD // 2, 1)
            by_x, more = rms_back(raw_v[here], gain, g)
            low[here, cols] = by_x.astype(bf16)
            by_gain = by_gain + more
        return by_gain

    def attend(h):
        cols = pl.ds(pl.multiple_of(h * HD, HD), HD)
        load_raw(cols).start()
        for i in range(length // seq):
            keys = pl.ds(0, (i + 1) * seq)
            here = pl.ds(i * seq, seq)
            s = lax.dot_general(k[keys], q_v[h, here], NT, preferred_element_type=f32) * scale
            key_pos = lax.broadcasted_iota(jnp.int32, s.shape, 0)
            query_pos = lax.broadcasted_iota(jnp.int32, s.shape, 1) + i * seq
            probs = jnp.where(key_pos <= query_pos, jnp.exp(s - lse[h, :, here]), 0.0)
            dp = lax.dot_general(v[keys], do[here, cols], NT, preferred_element_type=f32)
            delta = jnp.sum(probs * dp, axis=0, keepdims=True)
            ds = (probs * (dp - delta)).astype(bf16)
            dk[keys] += jnp.dot(ds, q_v[h, here], preferred_element_type=f32) * scale
            dv[keys] += jnp.dot(probs.astype(bf16), do[here, cols], preferred_element_type=f32)
            dq[here] = (jnp.dot(kt[:, keys], ds, preferred_element_type=f32) * scale).T
        load_raw(cols).wait()
        head_grad[0:1] += unprep(head_gain[0:1], dq, cols)

    def store(total):
        sum_o[...] = total

    for n, first in enumerate(range(0, heads, 2)):
        pl.loop(first, first + 2)(attend)
        run(1)
        if n < nz - 1:
            line.reduce(n)
    load_raw(pl.ds(heads * HD, HD)).start()
    load_raw(pl.ds(heads * HD, HD)).wait()
    head_grad[1:2] = unprep(head_gain[1:2], dk, pl.ds(heads * HD, HD))
    low[:, pl.ds((heads + 1) * HD, HD)] = dv[...].astype(bf16)

    load_xn.wait()
    lines = w_stage.shape[1] * w_stage.shape[2]

    def w_out(t):
        first = t * w_stage.shape[1]
        c, e = first // (2 * nz), first % (2 * nz)
        return pltpu.make_async_copy(
            w_stage.at[t % 2], gw.at[c, pl.ds(e, w_stage.shape[1])], w_sem.at[t % 2]
        )

    for t in range(width // lines):
        if t >= 2:
            w_out(t - 2).wait()
        x = rows_v[:, :, pl.ds(t * lines, lines)].reshape(length, lines)
        out = lax.dot_general(x, low[...], TN, preferred_element_type=f32)
        w_stage[t % 2] = out.astype(bf16).reshape(w_stage.shape[1:])
        w_out(t).start()
        if t % 3 == 2:
            run(1)
    loads[3].wait()
    for c in range(4):

        @pl.loop(0, 2)
        def _(i):
            here = nz * w_v.shape[2]
            w = w_v[c, pl.ds(i * nz, nz)].reshape(here, wide)
            out = lax.dot_general(low[...], w, NT, preferred_element_type=f32)
            cols = pl.ds(pl.multiple_of((2 * c + i) * here, here), here)
            rows_v[:, :, cols] = out.astype(bf16).reshape(4, seq, here)

        if c % 2:
            run(1)
    part_out = pltpu.make_async_copy(rows_v, part, load.at[4])
    part_out.start()
    line.reduce(nz - 1, store)
    run(len(steps))
    part_out.wait()
    for t in range(2):
        w_out(width // lines - 2 + t).wait()
    combine.finish()
    line.finish()


def back(nz, scale, columns, branch, wos, packs, xn, raw, q, ot, rows, k, v, lse, cosine, sine, head_gain, slots, gates):
    length, wide = raw.shape
    heads = q.shape[0]
    seq = length // 4
    width = xn.shape[1]
    cap = rows.shape[1]
    shape = jax.ShapeDtypeStruct
    vmem = lambda *n: pltpu.VMEM(n, bf16)
    wide_f = lambda *n: pltpu.VMEM(n, f32)
    dma = pltpu.SemaphoreType.DMA
    return pl.pallas_call(
        functools.partial(back_kernel, nz, cap, scale),
        out_shape=[
            shape(wos.shape[1:], f32),
            shape(packs.shape, bf16),
            shape((4, seq, width), bf16),
            shape((2, HD), f32),
            shape((seq, columns), f32),
        ],
        in_specs=[ANY] * 8 + [IN_VMEM] * 8,
        out_specs=[IN_VMEM, ANY, ANY] + [IN_VMEM] * 2,
        scratch_shapes=[
            vmem(4, seq, width),
            vmem(*wos.shape),
            vmem(*packs.shape),
            wide_f(length, HD),
            vmem(*q.shape),
            vmem(2, 2, HD, length),
            vmem(length, heads * HD),
            vmem(HD, length),
            vmem(length, wide),
            wide_f(length, HD),
            wide_f(length, HD),
            wide_f(length, HD),
            vmem(2, 4, packs.shape[2], wide),
            vmem(nz, *wos.shape[1:]),
            vmem(nz + 1, *wos.shape[1:]),
            dma((7,)),
            dma((2,)),
            dma((2,)),
        ]
        + line_sems(nz)
        + combine_scratch(nz, cap, seq, columns, 0),
        compiler_params=pltpu.CompilerParams(
            collective_id=5, has_side_effects=True, vmem_limit_bytes=VMEM_BYTES
        ),
    )(branch, wos, packs, xn.reshape(4, seq, width), raw, q, ot, rows, k, v, lse, cosine, sine, head_gain, slots, gates)


def last_kernel(nz, cap, col, *refs):
    gq, rows, part, tok_in, dh_in, gains, mlp_grad, head_grad, slots, gates = refs[:10]
    oq, ok, ov, all_gains, grad_tokens, mixed = refs[10:16]
    own, sib, line_b, swap_s, swap_r, gain_v, part_v, tok, dh = refs[16:25]
    load, a_send, a_recv, g_send, g_recv, local, in_sem = refs[25:32]
    p = Place()
    fold = Fold(p, part_v, *refs[32:40], far=part)
    line = LineSum(
        p, nz, lambda z, k: gq.at[:, z * 2 + k], lambda z: own.at[z], sib, line_b, *refs[40:44]
    )
    combine = Combine(p, nz, cap, col, LAST_DEEP, rows, slots, gates, mixed, *refs[44:])
    combine.clear()
    line.clear()
    inputs = [
        pltpu.make_async_copy(src, dst, in_sem.at[i])
        for i, (src, dst) in enumerate(((part, part_v), (tok_in, tok), (dh_in, dh)))
    ]
    for copy in inputs:
        copy.start()
    greet(p, nz, diagonal=True)

    def load_copy(z):
        return pltpu.make_async_copy(gq.at[:, z * 2 + p.k], own.at[z], load.at[z])

    def swaps():
        return [
            remote(swap_s.at[c], swap_r.at[p.c], a_send.at[n], a_recv.at[n], device)
            for n, (c, device) in enumerate(((p.cx, p.dx), (p.cy, p.dy), (p.cd, p.dd)))
        ]

    def swap(total):
        swap_s[...] = total.astype(swap_s.dtype)
        for copy in swaps():
            copy.start()
        swap_r[p.c] = swap_s[p.c]

    fold.begin()
    line.begin()
    for z in line.order:
        load_copy(z).start()
    combine.begin()
    steps = combine.steps()
    run = lambda n: [steps.pop(0)() for _ in range(min(n, len(steps)))]

    def reduce(n):
        load_copy(line.order[n]).wait()
        line.reduce(n, swap)

    reduce(0)
    run(1)
    inputs[0].wait()
    fold.middle()
    reduce(1)
    run(2)

    gain_v[...] = jnp.zeros(gain_v.shape, f32)
    width = tok.shape[1]
    for copy in inputs[1:]:
        copy.wait()

    def store(lines, total):
        by_x, by_gain = rms_back(tok[lines].astype(f32), gains[0:1], total)
        grad_tokens[lines] = (dh[lines] + by_x).astype(bf16)
        for j in range(width // 128):
            gain_v[pl.ds(j, 1)] += by_gain[:, j * 128 : (j + 1) * 128]

    fold.end(store)
    for j in range(width // 128):
        gain_v[pl.ds(width // 128 + j, 1)] = mlp_grad[:, pl.ds(j * 128, 128)]
    gain_v[pl.ds(2 * width // 128, 2)] = head_grad[...]
    block = by_device(all_gains, nz)
    keep = pltpu.make_async_copy(gain_v, block(p.c, p.z, p.k), local)
    keep.start()
    job = Spread(p, nz, gain_v, block, gain_v.shape[0] // 2, g_send, g_recv)
    job.step(0)
    run(1)
    job.step(1)
    for n in range(2, nz):
        reduce(n)
        run(2)
        job.step(n)
    for i in range(nz, nz + 2):
        job.step(i)
        run(1)
    for n, c in enumerate((p.cx, p.cy, p.cd)):
        ref = swap_r.at[c]
        remote(ref, ref, a_send.at[n], a_recv.at[n], p.dx).wait_recv()
    heads = oq.shape[1] // 4
    kv = ok.shape[1] // 4
    for c in range(4):
        oq[:, pl.ds(c * heads, heads)] = swap_r[c, :, pl.ds(0, heads)].astype(f32)
        ok[:, pl.ds(c * kv, kv)] = swap_r[c, :, pl.ds(heads, kv)].astype(f32)
        ov[:, pl.ds(c * kv, kv)] = swap_r[c, :, pl.ds(heads + kv, kv)].astype(f32)
    run(len(steps))
    for copy in swaps():
        copy.wait_send()
    keep.wait()
    job.finish()
    combine.finish()
    line.finish()


def reduce_last(nz, col, gq, rows, part, tok, dh, gains, mlp_grad, head_grad, slots, gates):
    _, _, rows_q, wide = gq.shape
    seq, width = tok.shape
    cap = rows.shape[1]
    kv = HD
    heads = wide - 2 * kv
    lines = -(-(2 * width // 128 + 2) // 16) * 16
    dma = pltpu.SemaphoreType.DMA
    shape = jax.ShapeDtypeStruct
    q = lambda *n: pltpu.VMEM(n + (4, rows_q, wide), bf16)
    return pl.pallas_call(
        functools.partial(last_kernel, nz, cap, col),
        out_shape=[
            shape((rows_q, 4 * heads), f32),
            shape((rows_q, 4 * kv), f32),
            shape((rows_q, 4 * kv), f32),
            shape((8 * nz, lines, 128), f32),
            shape((seq, width), bf16),
            shape((seq, width - col), f32),
        ],
        in_specs=[ANY] * 5 + [IN_VMEM] * 5,
        out_specs=[IN_VMEM] * 3 + [ANY] + [IN_VMEM] * 2,
        scratch_shapes=[q(nz), q(nz), q(nz + 1), q(), q()]
        + [pltpu.VMEM((lines, 128), f32)]
        + [pltpu.VMEM((4, seq, width), bf16), pltpu.VMEM((seq, width), bf16)]
        + [pltpu.VMEM((seq, width), f32)]
        + [dma((nz,))]
        + [dma((3,))] * 2
        + spread_sems(nz)
        + [dma, dma((3,))]
        + fold_scratch(seq, width)
        + line_sems(nz)
        + combine_scratch(nz, cap, seq, width - col, LAST_DEEP),
        compiler_params=pltpu.CompilerParams(
            collective_id=9, has_side_effects=True, vmem_limit_bytes=VMEM_BYTES
        ),
    )(gq, rows, part, tok, dh, gains, mlp_grad, head_grad, slots, gates)


def experts_kernel(
    nz,
    cap,
    mine,
    cots,
    slots,
    gates,
    wg_hbm,
    wu_hbm,
    wd_hbm,
    all_rows,
    produced,
    grad_inputs,
    x_out,
    dr_out,
    a_out,
    dg_out,
    du_out,
    stage_x,
    stage_d,
    x,
    dr,
    r,
    dx,
    a,
    dg,
    du,
    send,
    recv,
    load,
    out_sem,
    back_sem,
    wg,
    wu,
    wd,
    w_sem,
):
    p = Place()
    weights = [
        pltpu.make_async_copy(src, dst, w_sem.at[i])
        for i, (src, dst) in enumerate(((wg_hbm, wg), (wu_hbm, wu), (wd_hbm, wd)))
    ]
    for copy in weights:
        copy.start()
    greet(p, nz)
    job = Spread(p, nz, mine, by_device(all_rows, nz), mine.shape[0] // 2, send, recv)
    seq, width = mine.shape
    ff = a.shape[2]
    wide = min(512, width)
    narrow = min(256, ff)
    lines = [(p.c, 0), (p.cx, 0), (p.c, 1), (p.cx, 1)], [(p.cy, 0), (p.cd, 0), (p.cy, 1), (p.cd, 1)]
    turns = [(i - j, j) for i in range(1, nz + 2) for j in (1, 2) if 0 <= i - j < nz]
    turns = [(i, j - 1) for i, j in turns]

    def index(h, i, z):
        c, other = lines[h][i]
        return c * (2 * nz) + z * 2 + lax.rem(p.k + other, 2)

    def load_x(n, i):
        at, h = turns[n]
        src = mine if n == i == 0 else all_rows.at[index(h, i, job.order[at])]
        return pltpu.make_async_copy(src, stage_x.at[i], load.at[0, i])

    def load_d(n, i):
        at, h = turns[n]
        src = cots.at[index(h, i, job.order[at])]
        return pltpu.make_async_copy(src, stage_d.at[n % 2, i], load.at[1 + n % 2, i])

    def outs(h, z):
        whole = ((x, x_out), (dr, dr_out), (a, a_out), (dg, dg_out), (du, du_out))
        found = [
            pltpu.make_async_copy(src.at[h], dst.at[z, h], out_sem.at[h, n])
            for n, (src, dst) in enumerate(whole)
        ]
        for n, (src, dst) in enumerate(((r, produced), (dx, grad_inputs))):
            for i in range(4):
                found.append(
                    pltpu.make_async_copy(
                        src.at[h, pl.ds(i * cap, cap)], dst.at[index(h, i, z)], back_sem.at[h, n, i]
                    )
                )
        return found

    def group(n):
        at, h = turns[n]
        z = job.order[at]
        for i in range(4):
            load_x(n, i).start()
        if n + 1 < len(turns):
            for i in range(4):
                load_d(n + 1, i).start()
        if at:
            for copy in outs(h, job.order[at - 1]):
                copy.wait()
        for i in range(4):
            at_b = pl.ds(index(h, i, z), 1)
            names = lax.broadcasted_iota(jnp.int32, (cap, seq), 0) == slots[0, at_b]
            chosen = names.astype(f32).astype(bf16)
            row_gate = jnp.where(names, gates[0, at_b], 0.0)
            row_gate = jnp.sum(row_gate, axis=1, keepdims=True)
            here = pl.ds(i * cap, cap)
            load_d(n, i).wait()
            picked = jnp.dot(chosen, stage_d[n % 2, i], preferred_element_type=f32)
            dr[h, here] = (row_gate * picked).astype(bf16)
            load_x(n, i).wait()
            picked = jnp.dot(chosen, stage_x[i], preferred_element_type=f32)
            x[h, here] = picked.astype(bf16)

        if n == 0:
            for copy in weights:
                copy.wait()

        @pl.loop(0, ff // narrow)
        def _(t):
            cols = pl.ds(pl.multiple_of(t * narrow, narrow), narrow)
            g = jnp.dot(x[h], wg[:, cols], preferred_element_type=f32)
            u = jnp.dot(x[h], wu[:, cols], preferred_element_type=f32)
            da = lax.dot_general(dr[h], wd[cols, :], NT, preferred_element_type=f32)
            s = jax.nn.sigmoid(g)
            swish = g * s
            a[h, :, cols] = (swish * u).astype(bf16)
            du[h, :, cols] = (da * swish).astype(bf16)
            dg[h, :, cols] = (da * u * s * (1.0 + g * (1.0 - s))).astype(bf16)

        @pl.loop(0, width // wide)
        def _(t):
            cols = pl.ds(pl.multiple_of(t * wide, wide), wide)
            r[h, :, cols] = jnp.dot(a[h], wd[:, cols], preferred_element_type=f32).astype(bf16)
            back = lax.dot_general(dg[h], wg[cols, :], NT, preferred_element_type=f32)
            back = back + lax.dot_general(du[h], wu[cols, :], NT, preferred_element_type=f32)
            dx[h, :, cols] = back.astype(bf16)

        for copy in outs(h, z):
            copy.start()

    for i in range(4):
        load_d(0, i).start()
    done = 0
    for i in range(nz + 2):
        if i < nz:
            job.along(i)
        if 1 <= i <= nz:
            z = job.order[i - 1]
            job.beside(z)
            for j in (5, 6):
                job.got(j, z)
            group(done)
            done += 1
        if i >= 2:
            z = job.order[i - 2]
            job.across(z)
            for j in (7, 8, 9):
                job.got(j, z)
            group(done)
            done += 1
    for h in (0, 1):
        for copy in outs(h, job.order[nz - 1]):
            copy.wait()
    job.finish(pair=False)


def run_experts(nz, cap, mine, cots, slots, gates, wg, wu, wd):
    seq, width = mine.shape
    ff = wg.shape[1]
    rows = 4 * cap
    blocks = 8 * nz
    shape = lambda *n: jax.ShapeDtypeStruct(n, bf16)
    vmem = lambda *n: pltpu.VMEM(n, bf16)
    dma = pltpu.SemaphoreType.DMA
    return pl.pallas_call(
        functools.partial(experts_kernel, nz, cap),
        out_shape=[shape(blocks, seq, width)]
        + [shape(blocks, cap, width)] * 2
        + [shape(nz, 2, rows, width)] * 2
        + [shape(nz, 2, rows, ff)] * 3,
        in_specs=[ANY] * 2 + [IN_VMEM] * 2 + [ANY] * 3,
        out_specs=[ANY] * 8,
        scratch_shapes=[vmem(4, seq, width), vmem(2, 4, seq, width)]
        + [vmem(2, rows, width)] * 4
        + [vmem(2, rows, ff)] * 3
        + spread_sems(nz)
        + [dma((3, 4)), dma((2, 5)), dma((2, 2, 4))]
        + [vmem(*wg.shape), vmem(*wu.shape), vmem(*wd.shape), dma((3,))],
        compiler_params=pltpu.CompilerParams(
            collective_id=3, has_side_effects=True, vmem_limit_bytes=VMEM_BYTES
        ),
    )(mine, cots, slots, gates, wg, wu, wd)[1:]


def mm(a, b, contract, kind=f32):
    return lax.dot_general(a, b, ((contract[:1], contract[1:]), ((), ())), preferred_element_type=f32).astype(kind)


def fast_body(
    tokens,
    query_weight,
    key_weight,
    value_weight,
    output_weight,
    norm_gains,
    head_gains,
    expert_gate,
    expert_up,
    expert_down,
    routes,
    route_gates,
    cotangent,
):
    seq, width = tokens.shape[1:]
    nz = lax.axis_size("expert") // 2
    devices = lax.axis_size(("ctx", "expert"))
    length = 4 * seq
    topk = routes.shape[2]
    cap = max(2, 5 * seq * topk // (4 * devices))
    heads = HQ // 4
    wq = heads * HD
    scale = HD ** (-0.5)
    c = lax.axis_index("ctx")
    e = lax.axis_index("expert")
    k = lax.rem(e, 2)
    me = c * (2 * nz) + e
    rows_q = query_weight.shape[0]

    def cols(weight):
        return weight.reshape(rows_q, 4, -1).transpose(1, 0, 2)

    pack = jnp.concatenate([cols(query_weight), cols(key_weight), cols(value_weight)], axis=2)
    share = norm_gains.shape[1]
    head_share = head_gains.shape[1]
    lane = jnp.arange(128)

    def placed(part, size):
        spread = jnp.tile(part.astype(f32), (1, 128 // size))
        return jnp.where(lane[None, :] // size == lax.rem(me, 128 // size), spread, 0.0)

    meta = jnp.concatenate(
        [
            routes.reshape(seq, topk).T.astype(f32).reshape(-1, 128),
            route_gates.reshape(seq, topk).T.reshape(-1, 128),
            placed(norm_gains, share),
            placed(head_gains, head_share),
        ]
    )
    meta = jnp.pad(meta, ((0, -meta.shape[0] % 16), (0, 0)))
    half = HD // 2
    angles = jnp.arange(length, dtype=jnp.int32).astype(f32)[:, None] * (
        rope_base ** (-jnp.arange(half, dtype=f32) / half)
    )
    cosine, sine = jnp.cos(angles), jnp.sin(angles)
    tables = (
        jnp.concatenate([cosine, cosine], axis=1),
        jnp.concatenate([-sine, sine], axis=1),
    )
    found = front(
        nz,
        scale,
        pack,
        output_weight,
        tokens.reshape(seq, width),
        cotangent.reshape(seq, width),
        meta,
        *tables,
    )
    weight, wo, _, cots, _, normed, raw, queries, keys, values, attended, lse = found[:12]
    hidden, normed_mlp, gains, head_gain, slots2, gates2 = found[12:]
    produced, grad_inputs, arrived, grad_arrived, activated, grad_gate_pre, grad_up_pre = run_experts(
        nz, cap, normed_mlp, cots, slots2, gates2, expert_gate[0], expert_up[0], expert_down[0]
    )
    grad_normed_mlp = combine(nz, 32, grad_inputs, slots2, jnp.ones_like(gates2), 4)
    arrived, grad_arrived, activated, grad_gate_pre, grad_up_pre = (
        a.reshape(devices * cap, -1)
        for a in (arrived, grad_arrived, activated, grad_gate_pre, grad_up_pre)
    )
    grad_down = mm(activated, grad_arrived, (0, 0))
    grad_gate = mm(arrived, grad_gate_pre, (0, 0))
    grad_up = mm(arrived, grad_up_pre, (0, 0))

    grad_out = cotangent.reshape(seq, width).astype(f32)
    _, norm_pull = jax.vjp(rms_scale, hidden, gains[1])
    grad_hidden_norm, grad_gain_mlp = norm_pull(grad_normed_mlp)
    grad_hidden = grad_out + grad_hidden_norm
    branch = gather_rows(nz, False, grad_hidden.astype(bf16), 6)
    columns = width // 2
    sum_o, grad_weight, part, grad_head, mixed_low = back(
        nz,
        scale,
        columns,
        branch,
        wo,
        weight,
        normed,
        raw,
        queries,
        attended,
        produced,
        keys,
        values,
        lse,
        *tables,
        head_gain,
        slots2,
        gates2,
    )
    sum_q, sum_k, sum_v, all_gain_parts, grad_input, mixed_high = reduce_last(
        nz,
        columns,
        grad_weight,
        produced,
        part,
        tokens.reshape(seq, width),
        grad_hidden,
        gains,
        grad_gain_mlp.reshape(1, width),
        grad_head,
        slots2,
        gates2,
    )
    mixed = hidden + jnp.concatenate([mixed_low, mixed_high], axis=1)
    gain_sums = jnp.sum(all_gain_parts, axis=0).reshape(-1)
    norm_sums = gain_sums[: 2 * width].reshape(2, width)
    head_sums = gain_sums[2 * width : 2 * width + 2 * HD].reshape(2, HD)
    return (
        mixed.astype(bf16).reshape(tokens.shape),
        grad_input.reshape(tokens.shape),
        sum_q,
        sum_k,
        sum_v,
        sum_o,
        lax.dynamic_slice_in_dim(norm_sums, me * share, share, 1),
        lax.dynamic_slice_in_dim(head_sums, me * head_share, head_share, 1),
        grad_gate[None],
        grad_up[None],
        grad_down[None],
    )


def solution(mesh):
    small = mesh.shape["ctx"] == HK and mesh.size == 32
    return jax.shard_map(
        fast_body if small else body,
        mesh=mesh,
        in_specs=(
            P("expert", "ctx", None),
            P(("ctx", "expert"), None),
            P(("ctx", "expert"), None),
            P(("ctx", "expert"), None),
            P(("ctx", "expert"), None),
            P(None, ("ctx", "expert")),
            P(None, ("ctx", "expert")),
            P(("ctx", "expert"), None, None),
            P(("ctx", "expert"), None, None),
            P(("ctx", "expert"), None, None),
            P("expert", "ctx", None),
            P("expert", "ctx", None),
            P("expert", "ctx", None),
        ),
        out_specs=(
            P("expert", "ctx", None),
            P("expert", "ctx", None),
            P(("ctx", "expert"), None),
            P(("ctx", "expert"), None),
            P(("ctx", "expert"), None),
            P(("ctx", "expert"), None),
            P(None, ("ctx", "expert")),
            P(None, ("ctx", "expert")),
            P(("ctx", "expert"), None, None),
            P(("ctx", "expert"), None, None),
            P(("ctx", "expert"), None, None),
        ),
        check_vma=False,
    )
```

```python
import functools

import jax
import jax.numpy as jnp
from jax import lax
from jax.experimental import pallas as pl
from jax.experimental.pallas import tpu as pltpu
from jax.sharding import PartitionSpec as P

HQ = 32
HK = 4
HD = 128


epsilon = 1e-06
rope_base = 1000000.0
masked_value = -1e30


def rms_scale(values, scale_gain):
    return (
        values * lax.rsqrt(jnp.mean(values * values, axis=-1, keepdims=True) + epsilon) * scale_gain
    )


def rotate(values, positions):
    half_size = values.shape[-1] // 2
    frequency = rope_base ** (-jnp.arange(half_size, dtype=jnp.float32) / half_size)
    angles = positions.astype(jnp.float32)[:, None] * frequency[None, :]
    cosine = jnp.cos(angles)[:, None, :]
    sine_part = jnp.sin(angles)[:, None, :]
    first_half = values[..., :half_size]
    second_half = values[..., half_size:]
    return jnp.concatenate(
        [
            first_half * cosine - second_half * sine_part,
            second_half * cosine + first_half * sine_part,
        ],
        axis=-1,
    )


def body(
    tokens,
    query_weight,
    key_weight,
    value_weight,
    output_weight,
    norm_gains,
    head_gains,
    expert_gate,
    expert_up,
    expert_down,
    routes,
    route_gates,
    cotangent,
):
    seq_rows = tokens.shape[1]
    width = tokens.shape[2]
    groups = HQ // HK
    kv_width = HK * HD
    scale = HD ** (-0.5)
    positions = lax.axis_index("ctx") * seq_rows + jnp.arange(seq_rows, dtype=jnp.int32)
    last_pos = lax.axis_index("ctx") * seq_rows + seq_rows - 1
    rows_in = tokens.reshape(seq_rows, width).astype(jnp.float32)
    full_q, full_k, full_v, full_o, gains, head_gain = (
        lax.all_gather(query_weight, ("ctx", "expert"), axis=0, tiled=True),
        lax.all_gather(key_weight, ("ctx", "expert"), axis=0, tiled=True),
        lax.all_gather(value_weight, ("ctx", "expert"), axis=0, tiled=True),
        lax.all_gather(output_weight, ("ctx", "expert"), axis=0, tiled=True),
        lax.all_gather(norm_gains, ("ctx", "expert"), axis=1, tiled=True),
        lax.all_gather(head_gains, ("ctx", "expert"), axis=1, tiled=True),
    )

    def head_prep(raw_heads, gain_vec):
        return rotate(rms_scale(raw_heads, gain_vec), positions)

    normed = rms_scale(rows_in, gains[0].astype(jnp.float32)).astype(jnp.bfloat16)
    query_raw = jnp.dot(normed, full_q, preferred_element_type=jnp.float32).reshape(
        seq_rows, HQ, HD
    )
    key_raw = jnp.dot(normed, full_k, preferred_element_type=jnp.float32).reshape(seq_rows, HK, HD)
    value_rows = jnp.dot(normed, full_v, preferred_element_type=jnp.float32).astype(jnp.bfloat16)
    query_gain = head_gain[0].astype(jnp.float32)
    key_gain = head_gain[1].astype(jnp.float32)
    queries = head_prep(query_raw, query_gain).astype(jnp.bfloat16)
    keys_rot = head_prep(key_raw, key_gain).astype(jnp.bfloat16)
    kv_rows = jnp.concatenate([keys_rot.reshape(seq_rows, kv_width), value_rows], axis=1)
    grouped = queries.reshape(seq_rows, HK, groups, HD)

    def scores_for(key_block, base_row):
        scores = (
            jnp.einsum("qhgd,khd->hgqk", grouped, key_block, preferred_element_type=jnp.float32)
            * scale
        )
        key_pos = base_row + jnp.arange(key_block.shape[0], dtype=jnp.int32)
        allowed = key_pos[None, :] <= positions[:, None]
        return (scores, allowed)

    start_state = (
        jnp.full((HK, groups, seq_rows), masked_value, jnp.float32),
        jnp.zeros((HK, groups, seq_rows), jnp.float32),
        jnp.zeros((HK, groups, seq_rows, HD), jnp.float32),
    )
    shard_rows = lax.all_gather(kv_rows, "ctx", axis=0, tiled=True)
    blocks = shard_rows.reshape(shard_rows.shape[0] // seq_rows, seq_rows, 2 * kv_width)

    def step(state_now, element):
        block_index, block_rows = element
        base_row = block_index * seq_rows

        def step_visit(state_in):
            largest, total_sum, accum = state_in
            key_block = block_rows[:, :kv_width].reshape(seq_rows, HK, HD)
            value_block = block_rows[:, kv_width:].reshape(seq_rows, HK, HD)
            scores, allowed = scores_for(key_block, base_row)
            scores = jnp.where(allowed, scores, masked_value)
            new_largest = jnp.maximum(largest, jnp.max(scores, axis=-1))
            weights = jnp.where(allowed, jnp.exp(scores - new_largest[..., None]), 0.0)
            factor = jnp.exp(largest - new_largest)
            total_sum = total_sum * factor + jnp.sum(weights, axis=-1)
            accum = accum * factor[..., None] + jnp.einsum(
                "hgqk,khd->hgqd",
                weights.astype(jnp.bfloat16),
                value_block,
                preferred_element_type=jnp.float32,
            )
            return (new_largest, total_sum, accum)

        def step_skip(state_in):
            return state_in

        return (lax.cond(base_row <= last_pos, step_visit, step_skip, state_now), None)

    final_state, unused = lax.scan(
        step, start_state, (jnp.arange(blocks.shape[0], dtype=jnp.int32), blocks)
    )
    largest, total_sum, accum = final_state
    attended = (accum / total_sum[..., None]).transpose(2, 0, 1, 3).reshape(seq_rows, HQ * HD)
    log_total = largest + jnp.log(total_sum)
    attended_low = attended.astype(jnp.bfloat16)
    hidden = rows_in + jnp.dot(attended_low, full_o, preferred_element_type=jnp.float32)
    normed_mlp = rms_scale(hidden, gains[1].astype(jnp.float32)).astype(jnp.bfloat16)
    devices = lax.axis_size(("ctx", "expert"))
    local_experts = expert_gate.shape[0]
    experts = local_experts * devices
    topk = routes.shape[2]
    capacity = max(2, 5 * seq_rows * topk // (4 * experts))
    route_ids = routes.reshape(seq_rows * topk)
    onehot = (route_ids[:, None] == jnp.arange(experts, dtype=jnp.int32)[None, :]).astype(jnp.int32)
    slots = jnp.sum((jnp.cumsum(onehot, axis=0) - 1) * onehot, axis=1)
    target = route_ids * capacity + slots
    owner_row = jnp.arange(seq_rows * topk, dtype=jnp.int32) // topk
    gate_rows = route_gates.reshape(seq_rows, topk)

    def to_slots(row_block):
        buffer = (
            jnp.zeros((experts * capacity, row_block.shape[1]), row_block.dtype)
            .at[target]
            .set(row_block)
        )
        return buffer.reshape(devices, local_experts * capacity, row_block.shape[1])

    def to_experts(arrived):
        return (
            arrived.reshape(devices, local_experts, capacity, -1)
            .transpose(1, 0, 2, 3)
            .reshape(local_experts, devices * capacity, -1)
        )

    def from_experts(expert_rows):
        return (
            expert_rows.reshape(local_experts, devices, capacity, -1)
            .transpose(1, 0, 2, 3)
            .reshape(devices, local_experts * capacity, -1)
        )

    arrived = to_experts(
        lax.all_to_all(
            to_slots(normed_mlp[owner_row]),
            ("ctx", "expert"),
            split_axis=0,
            concat_axis=0,
            tiled=True,
        )
    )
    gate_pre = jnp.einsum("erd,edf->erf", arrived, expert_gate, preferred_element_type=jnp.float32)
    up_pre = jnp.einsum("erd,edf->erf", arrived, expert_up, preferred_element_type=jnp.float32)
    sigmoid_gate = jax.nn.sigmoid(gate_pre)
    swish_gate = gate_pre * sigmoid_gate
    activated = (swish_gate * up_pre).astype(jnp.bfloat16)
    produced = jnp.einsum(
        "erf,efd->erd", activated, expert_down, preferred_element_type=jnp.float32
    ).astype(jnp.bfloat16)
    returned = lax.all_to_all(
        from_experts(produced), ("ctx", "expert"), split_axis=0, concat_axis=0, tiled=True
    ).reshape(experts * capacity, width)
    expert_out = returned[target].astype(jnp.float32).reshape(seq_rows, topk, width)
    mixed = hidden + jnp.sum(gate_rows[:, :, None] * expert_out, axis=1)
    full_q, full_k, full_v, full_o, gains, head_gain = (
        lax.all_gather(query_weight, ("ctx", "expert"), axis=0, tiled=True),
        lax.all_gather(key_weight, ("ctx", "expert"), axis=0, tiled=True),
        lax.all_gather(value_weight, ("ctx", "expert"), axis=0, tiled=True),
        lax.all_gather(output_weight, ("ctx", "expert"), axis=0, tiled=True),
        lax.all_gather(norm_gains, ("ctx", "expert"), axis=1, tiled=True),
        lax.all_gather(head_gains, ("ctx", "expert"), axis=1, tiled=True),
    )
    grad_out = cotangent.reshape(seq_rows, width).astype(jnp.float32)
    grad_rows = (
        (gate_rows[:, :, None] * grad_out[:, None, :])
        .astype(jnp.bfloat16)
        .reshape(seq_rows * topk, width)
    )
    grad_arrived = to_experts(
        lax.all_to_all(
            to_slots(grad_rows), ("ctx", "expert"), split_axis=0, concat_axis=0, tiled=True
        )
    )
    grad_down = jnp.einsum(
        "erf,erd->efd", activated, grad_arrived, preferred_element_type=jnp.float32
    )
    grad_act = jnp.einsum(
        "erd,efd->erf", grad_arrived, expert_down, preferred_element_type=jnp.float32
    )
    grad_up_pre = (grad_act * swish_gate).astype(jnp.bfloat16)
    grad_gate_pre = (
        grad_act * up_pre * sigmoid_gate * (1.0 + gate_pre * (1.0 - sigmoid_gate))
    ).astype(jnp.bfloat16)
    grad_gate = jnp.einsum(
        "erd,erf->edf", arrived, grad_gate_pre, preferred_element_type=jnp.float32
    )
    grad_up = jnp.einsum("erd,erf->edf", arrived, grad_up_pre, preferred_element_type=jnp.float32)
    grad_inputs = jnp.einsum(
        "erf,edf->erd", grad_gate_pre, expert_gate, preferred_element_type=jnp.float32
    )
    grad_inputs = (
        grad_inputs
        + jnp.einsum("erf,edf->erd", grad_up_pre, expert_up, preferred_element_type=jnp.float32)
    ).astype(jnp.bfloat16)
    grad_back = lax.all_to_all(
        from_experts(grad_inputs), ("ctx", "expert"), split_axis=0, concat_axis=0, tiled=True
    ).reshape(experts * capacity, width)
    grad_normed_mlp = jnp.sum(
        grad_back[target].astype(jnp.float32).reshape(seq_rows, topk, width), axis=1
    )
    unused_norm, norm_pull = jax.vjp(rms_scale, hidden, gains[1].astype(jnp.float32))
    grad_hidden_norm, grad_gain_mlp = norm_pull(grad_normed_mlp)
    grad_hidden = grad_out + grad_hidden_norm
    grad_branch = grad_hidden.astype(jnp.bfloat16)
    grad_wo = jnp.einsum("qa,qd->ad", attended_low, grad_branch, preferred_element_type=jnp.float32)
    grad_attended = jnp.einsum(
        "qd,ad->qa", grad_branch, full_o, preferred_element_type=jnp.float32
    ).astype(jnp.bfloat16)
    all_kv = lax.all_gather(kv_rows, "ctx", axis=0, tiled=True)
    grad_grouped = grad_attended.reshape(seq_rows, HK, groups, HD)
    delta = jnp.einsum(
        "qhgd,qhgd->hgq",
        grad_grouped.astype(jnp.float32),
        attended.reshape(seq_rows, HK, groups, HD),
    )
    kv_blocks = all_kv.reshape(-1, seq_rows, 2 * kv_width)

    def back_step(grad_query, element):
        block_index, block_rows = element
        base_row = block_index * seq_rows

        def back_visit(grad_in):
            key_block = block_rows[:, :kv_width].reshape(seq_rows, HK, HD)
            value_block = block_rows[:, kv_width:].reshape(seq_rows, HK, HD)
            scores, allowed = scores_for(key_block, base_row)
            probs = jnp.where(allowed, jnp.exp(scores - log_total[..., None]), 0.0)
            grad_probs = jnp.einsum(
                "qhgd,khd->hgqk", grad_grouped, value_block, preferred_element_type=jnp.float32
            )
            grad_scores = (probs * (grad_probs - delta[..., None])).astype(jnp.bfloat16)
            grad_next = grad_in + jnp.einsum(
                "hgqk,khd->qhgd", grad_scores, key_block, preferred_element_type=jnp.float32
            )
            grad_keys = (
                jnp.einsum(
                    "hgqk,qhgd->khd", grad_scores, grouped, preferred_element_type=jnp.float32
                )
                * scale
            )
            grad_values = jnp.einsum(
                "hgqk,qhgd->khd",
                probs.astype(jnp.bfloat16),
                grad_grouped,
                preferred_element_type=jnp.float32,
            )
            joined = jnp.concatenate(
                [grad_keys.reshape(seq_rows, kv_width), grad_values.reshape(seq_rows, kv_width)],
                axis=1,
            )
            return (grad_next, joined)

        def back_skip(grad_in):
            return (grad_in, jnp.zeros((seq_rows, 2 * kv_width), jnp.float32))

        return lax.cond(base_row <= last_pos, back_visit, back_skip, grad_query)

    grad_query, grad_kv_terms = lax.scan(
        back_step,
        jnp.zeros((seq_rows, HK, groups, HD), jnp.float32),
        (jnp.arange(kv_blocks.shape[0], dtype=jnp.int32), kv_blocks),
    )
    grad_query = grad_query * scale
    grad_kv = lax.psum_scatter(
        grad_kv_terms.reshape(-1, 2 * kv_width).astype(jnp.bfloat16),
        "ctx",
        scatter_dimension=0,
        tiled=True,
    ).astype(jnp.float32)
    unused_query, pull_query = jax.vjp(head_prep, query_raw, query_gain)
    grad_query_raw, grad_query_gain = pull_query(grad_query.reshape(seq_rows, HQ, HD))
    unused_key, pull_key = jax.vjp(head_prep, key_raw, key_gain)
    grad_key_raw, grad_key_gain = pull_key(grad_kv[:, :kv_width].reshape(seq_rows, HK, HD))
    grad_q_low = grad_query_raw.reshape(seq_rows, HQ * HD).astype(jnp.bfloat16)
    grad_k_low = grad_key_raw.reshape(seq_rows, kv_width).astype(jnp.bfloat16)
    grad_v_low = grad_kv[:, kv_width:].astype(jnp.bfloat16)
    grad_wq = jnp.einsum("qd,qa->da", normed, grad_q_low, preferred_element_type=jnp.float32)
    grad_wk = jnp.einsum("qd,qa->da", normed, grad_k_low, preferred_element_type=jnp.float32)
    grad_wv = jnp.einsum("qd,qa->da", normed, grad_v_low, preferred_element_type=jnp.float32)
    grad_normed = jnp.einsum("qa,da->qd", grad_q_low, full_q, preferred_element_type=jnp.float32)
    grad_normed = grad_normed + jnp.einsum(
        "qa,da->qd", grad_k_low, full_k, preferred_element_type=jnp.float32
    )
    grad_normed = grad_normed + jnp.einsum(
        "qa,da->qd", grad_v_low, full_v, preferred_element_type=jnp.float32
    )
    unused_attn, pull_attn = jax.vjp(rms_scale, rows_in, gains[0].astype(jnp.float32))
    grad_rows_norm, grad_gain_attn = pull_attn(grad_normed)
    grad_input = grad_hidden + grad_rows_norm
    gain_grads = jnp.stack([grad_gain_attn, grad_gain_mlp])
    head_grads = jnp.stack([grad_query_gain, grad_key_gain])
    sum_q, sum_k, sum_v, sum_o, sum_gain, sum_head = (
        lax.psum_scatter(grad_wq, ("ctx", "expert"), scatter_dimension=0, tiled=True),
        lax.psum_scatter(grad_wk, ("ctx", "expert"), scatter_dimension=0, tiled=True),
        lax.psum_scatter(grad_wv, ("ctx", "expert"), scatter_dimension=0, tiled=True),
        lax.psum_scatter(grad_wo, ("ctx", "expert"), scatter_dimension=0, tiled=True),
        lax.psum_scatter(gain_grads, ("ctx", "expert"), scatter_dimension=1, tiled=True),
        lax.psum_scatter(head_grads, ("ctx", "expert"), scatter_dimension=1, tiled=True),
    )
    return (
        mixed.astype(jnp.bfloat16).reshape(tokens.shape),
        grad_input.astype(jnp.bfloat16).reshape(tokens.shape),
        sum_q,
        sum_k,
        sum_v,
        sum_o,
        sum_gain,
        sum_head,
        grad_gate,
        grad_up,
        grad_down,
    )


MESH = pl.DeviceIdType.MESH
VMEM_BYTES = 58 * 2**20
LAST_DEEP = 0
DEEP = 32
ANY = pl.BlockSpec(memory_space=pl.ANY)
IN_VMEM = pl.BlockSpec(memory_space=pltpu.VMEM)
f32, bf16 = jnp.float32, jnp.bfloat16
NT = (((1,), (1,)), ((), ()))
TN = (((0,), (0,)), ((), ()))


class Place:
    def __init__(self):
        self.c = lax.axis_index("ctx")
        self.e = lax.axis_index("expert")
        self.k = lax.rem(self.e, 2)
        self.z = lax.div(self.e, 2)
        self.cx = self.c + 1 - 2 * lax.rem(self.c, 2)
        self.cy = lax.rem(self.c + 2, 4)
        self.cd = lax.rem(self.cx + 2, 4)
        self.dx = (self.cx, self.e)
        self.dy = (self.cy, self.e)
        self.dd = (self.cd, self.e)
        self.pair = (self.c, self.e + 1 - 2 * self.k)
        self.up = (self.c, self.e + 2)
        self.down = (self.c, self.e - 2)


def greet(p, nz, line=True, pair=True, diagonal=False):
    barrier = pltpu.get_barrier_semaphore()

    def tell(device):
        pl.semaphore_signal(barrier, inc=1, device_id=device, device_id_type=MESH)

    friends = [p.dx, p.dy] + [p.pair] * pair + [p.dd] * diagonal
    for device in friends:
        tell(device)
    count = len(friends)
    if line:
        for there, device in ((p.z > 0, p.down), (p.z < nz - 1, p.up)):

            @pl.when(there)
            def _():
                tell(device)

            count = count + there.astype(jnp.int32)
    pl.semaphore_wait(barrier, count)


def remote(src, dst, send, recv, device):
    return pltpu.make_async_remote_copy(
        src_ref=src,
        dst_ref=dst,
        send_sem=send,
        recv_sem=recv,
        device_id=device,
        device_id_type=MESH,
    )


def far_first(nz, z):
    return sorted(range(nz), key=lambda to: (-abs(to - z), to))


def near_first(nz, z):
    return sorted(range(nz), key=lambda to: (abs(to - z), to))


def pick_order(p, nz, order=far_first):
    tables = [order(nz, z) for z in range(nz)]
    return [sum(jnp.where(p.z == z, tables[z][i], 0) for z in range(nz)) for i in range(nz)]


class Spread:
    def __init__(self, p, nz, mine, block, half, send, recv, line=True, side=True, pair=True):
        self.p, self.nz, self.mine, self.block, self.half = p, nz, mine, block, half
        self.send, self.recv = send, recv
        self.line, self.side, self.pair = line, side, pair
        self.order = pick_order(p, nz, near_first) if line else [p.z]

    def ref(self, c, z, k, h=None):
        whole = self.block(c, z, k)
        return whole if h is None else whole.at[pl.ds(h * self.half, self.half)]

    def copy(self, kind, z, own=False):
        p = self.p
        at = functools.partial(self.ref, z=z, k=p.k)
        src, i, j, device = {
            "x": lambda: (at(p.c), 0, 1, p.dx),
            "y": lambda: (at(p.c), 1, 2, p.dy),
            "up": lambda: (at(p.c), 2, 0, p.up),
            "down": lambda: (at(p.c), 3, 0, p.down),
            "via_y": lambda: (at(p.cx, h=0), 4, 3, p.dy),
            "via_x": lambda: (at(p.cy, h=1), 5, 4, p.dx),
            "pair0": lambda: (at(p.c), 6, 5, p.pair),
            "pair1": lambda: (at(p.cx), 7, 6, p.pair),
            "pair2": lambda: (at(p.cy), 8, 7, p.pair),
            "pair3": lambda: (at(p.cd, h=0), 9, 8, p.pair),
            "pair4": lambda: (at(p.cd, h=1), 10, 9, p.pair),
        }[kind]()
        return remote(
            self.mine if own else src, src, self.send.at[z, i], self.recv.at[z, j], device
        )

    def got(self, j, z):
        p = self.p
        k = p.k if j < 5 else 1 - p.k
        c, h = ((p.c, None), (p.cx, None), (p.cy, None), (p.cd, 0), (p.cd, 1))[j % 5]
        ref = self.ref(c, z, k, h)
        remote(ref, ref, self.send.at[z, 0], self.recv.at[z, j], p.pair).wait_recv()

    def each(self, far, act):
        if far == 0:
            act(self.p.z, 0)
            return
        for way in (-1, 1):
            z = self.p.z + way * far

            @pl.when((z >= 0) & (z < self.nz))
            def _():
                act(z, way)

    def onward(self, z, way, act):
        if self.line and way >= 0:

            @pl.when(self.p.z > 0)
            def _():
                act(self.copy("down", z, way == 0))

        if self.line and way <= 0:

            @pl.when(self.p.z < self.nz - 1)
            def _():
                act(self.copy("up", z, way == 0))

    def direct(self):
        return ["x", "y"] * self.side + ["pair0"] * self.pair

    def along(self, far):
        def act(z, way):
            if way:
                self.got(0, z)
            self.onward(z, way, lambda copy: copy.start())
            for kind in self.direct():
                self.copy(kind, z, way == 0).start()

        self.each(far, act)

    def beside(self, z):
        for j, kinds in ((1, ["via_y", "pair1"]), (2, ["via_x", "pair2"])):
            self.got(j, z)
            for kind in kinds[: 1 + self.pair]:
                self.copy(kind, z).start()

    def across(self, z):
        for j, kind in ((3, "pair3"), (4, "pair4")):
            self.got(j, z)
            if self.pair:
                self.copy(kind, z).start()

    def from_pair(self, z):
        if self.pair:
            for j in range(5, 10 if self.side else 6):
                self.got(j, z)

    def step(self, i):
        reach = self.nz if self.line else 1
        if i < reach:
            self.along(i)
        if self.side and 1 <= i <= reach:
            self.beside(self.order[i - 1])
        if self.side and 2 <= i <= reach + 1:
            self.across(self.order[i - 2])

    def finish(self, pair=True):
        def act(z, way):
            if pair:
                self.from_pair(z)
            self.onward(z, way, lambda copy: copy.wait_send())
            for kind in self.direct():
                self.copy(kind, z, way == 0).wait_send()
            if self.side:
                for kind in ["via_y", "via_x"] + ["pair1", "pair2", "pair3", "pair4"] * self.pair:
                    self.copy(kind, z).wait_send()

        for far in range(self.nz if self.line else 1):
            self.each(far, act)


class SpreadDeep:
    def __init__(self, p, nz, mine, block, send, recv, send_in, recv_in):
        self.p, self.nz, self.mine, self.block = p, nz, mine, block
        self.send, self.recv, self.send_in, self.recv_in = send, recv, send_in, recv_in
        self.places = (p.c, p.cx, p.cy, p.cd)
        self.half = mine.shape[0] // 2

    def ref(self, r, z, h=None, k=None):
        whole = self.block(self.places[r], z, self.p.k if k is None else k)
        return whole if h is None else whole.at[pl.ds(h * self.half, self.half)]

    def near(self, i):
        p, own = self.p, self.ref(0, self.p.z)
        src, dst, device = (
            lambda: (self.mine, own, p.dx),
            lambda: (self.mine, own, p.dy),
            lambda: (self.ref(1, p.z, 0), self.ref(1, p.z, 0), p.dy),
            lambda: (self.ref(2, p.z, 1), self.ref(2, p.z, 1), p.dx),
        )[i]()
        return remote(src, dst, self.send_in.at[i], self.recv_in.at[i], device)

    def hop(self, r, z, i, own=False):
        dst = self.ref(r, z)
        device = (self.p.up, self.p.down, self.p.pair)[i]
        src = self.mine if own else dst
        return remote(src, dst, self.send.at[z, r, i], self.recv.at[z, r, i // 2], device)

    def forward(self, r, z, way, act):
        p, own = self.p, r == 0 and way == 0
        if way <= 0:

            @pl.when(p.z < self.nz - 1)
            def _():
                act(self.hop(r, z, 0, own))

        if way >= 0:

            @pl.when(p.z > 0)
            def _():
                act(self.hop(r, z, 1, own))

        act(self.hop(r, z, 2, own))

    def each(self, far, act):
        for way in (-1, 1):
            z = self.p.z + way * far

            @pl.when((z >= 0) & (z < self.nz))
            def _():
                act(z, way)

    def step(self, i):
        start = lambda copy: copy.start()
        z = self.p.z
        if i == 0:
            self.near(0).start()
            self.near(1).start()
            self.forward(0, z, 0, start)
        elif i == 1:
            for n in (0, 1):
                ref = self.ref(1 + n, z)
                remote(ref, ref, self.send_in.at[n], self.recv_in.at[n], self.p.pair).wait_recv()
                self.near(2 + n).start()
                self.forward(1 + n, z, 0, start)
        elif i == 2:
            for n in (0, 1):
                ref = self.ref(3, z, n)
                remote(
                    ref, ref, self.send_in.at[n], self.recv_in.at[2 + n], self.p.pair
                ).wait_recv()
            self.forward(3, z, 0, start)
        elif i < self.nz + 2:

            def act(z, way):
                for r in range(4):
                    self.got(r, z, 0)
                    self.forward(r, z, way, start)

            self.each(i - 2, act)

    def got(self, r, z, i):
        ref = self.ref(r, z, None, self.p.k if i == 0 else 1 - self.p.k)
        remote(ref, ref, self.send.at[z, r, 0], self.recv.at[z, r, i], self.p.pair).wait_recv()

    def finish(self, pair=True):
        def act(z, way):
            for r in range(4):
                if pair:
                    self.got(r, z, 1)
                self.forward(r, z, way, lambda copy: copy.wait_send())

        for i in range(4):
            self.near(i).wait_send()
        act(self.p.z, 0)
        for far in range(1, self.nz):
            self.each(far, act)


def deep_sems(nz):
    dma = pltpu.SemaphoreType.DMA
    return [dma((nz, 4, 3)), dma((nz, 4, 2)), dma((4,)), dma((4,))]


def lines_of(ref, nz, first, count):
    return lambda c, z, k: ref.at[c * (2 * nz) + z * 2 + k, pl.ds(first, count)]


def by_device(ref, nz):
    return lambda c, z, k: ref.at[c * (2 * nz) + z * 2 + k]


def spread_sems(nz):
    return [pltpu.SemaphoreType.DMA((nz, 11)), pltpu.SemaphoreType.DMA((nz, 10))]


class Fold:
    def __init__(self, p, parts, sx, sy, h0, h1, bx, by, send, recv, far=None):
        far = parts if far is None else far
        half = bx.shape[0] // 2
        self.halves = low, high = pl.ds(0, half), pl.ds(half, half)
        self.p, self.parts, self.sx, self.sy = p, parts, sx, sy
        self.h0, self.h1, self.bx, self.by = h0, h1, bx, by
        copy = lambda i, src, dst, device: remote(src, dst, send.at[i], recv.at[i], device)
        self.to_x = copy(0, far.at[p.cd, low], h0, p.dx)
        self.to_y = copy(1, far.at[p.cd, high], h1, p.dy)
        self.x_low = copy(2, far.at[p.cx, low], bx.at[low], p.dx)
        self.y_high = copy(3, far.at[p.cy, high], by.at[high], p.dy)
        self.x_high = copy(4, sx, bx.at[high], p.dx)
        self.y_low = copy(5, sy, by.at[low], p.dy)

    def begin(self):
        for copy in (self.to_x, self.to_y, self.x_low, self.y_high):
            copy.start()

    def middle(self):
        p, (low, high), parts = self.p, self.halves, self.parts
        self.to_y.wait_recv()
        total = parts[p.cx, high].astype(f32) + self.h1[...].astype(f32)
        self.sx[...] = total.astype(self.sx.dtype)
        self.x_high.start()
        self.to_x.wait_recv()
        total = parts[p.cy, low].astype(f32) + self.h0[...].astype(f32)
        self.sy[...] = total.astype(self.sy.dtype)
        self.y_low.start()

    def end(self, store):
        p, parts = self.p, self.parts
        low, high = self.halves
        for rows, waits in ((low, (self.x_low, self.y_low)), (high, (self.y_high, self.x_high))):
            for copy in waits:
                copy.wait_recv()
            total = parts[p.c, rows].astype(f32) + self.bx[rows].astype(f32)
            store(rows, total + self.by[rows].astype(f32))
        for copy in (self.to_x, self.to_y, self.x_low, self.y_high, self.x_high, self.y_low):
            copy.wait_send()


def fold_scratch(seq, width):
    buf = lambda r: pltpu.VMEM((r, width), bf16)
    return (
        [buf(seq // 2)] * 4 + [buf(seq)] * 2 + [pltpu.SemaphoreType.DMA((6,))] * 2
    )


def front_kernel(nz, scale, *refs):
    pack, wo, tok, cot, meta, cosine, sine = refs[:7]
    packs, wos, toks, cots, metas = refs[7:12]
    results, held = refs[12:25], refs[25:38]
    xn, raw, q, k, v, ot, lse, hidden, hn, gain_out, head_out, slots, gates = held
    tok_v, w_v, wo_v, meta_v, vt, ob, part = refs[38:45]
    fold_refs, pair_sems = refs[45:53], refs[53:63]
    a_send, a_recv, local, load, out_sem = refs[63:68]

    def copy_out(*which):
        for i in which:
            pltpu.make_async_copy(held[i], results[i], out_sem.at[i]).start()

    p = Place()
    seq, width = tok.shape
    length = 4 * seq
    heads = q.shape[0]
    me = p.c * (2 * nz) + p.e
    greet(p, nz, diagonal=True)
    into = [
        pltpu.make_async_copy(src, dst, local.at[i])
        for i, (src, dst) in enumerate(
            (
                (pack.at[p.c], w_v.at[p.c, p.e]),
                (wo, wo_v.at[p.e]),
                (tok, tok_v.at[p.c]),
                (cot, part.at[0]),
            )
        )
    ]
    own = [
        pltpu.make_async_copy(src, dst, local.at[4 + i])
        for i, (src, dst) in enumerate(
            (
                (w_v.at[p.c, p.e], packs.at[p.c, p.e]),
                (wo_v.at[p.e], wos.at[p.e]),
                (meta, metas.at[me]),
                (part.at[0], cots.at[me]),
            )
        )
    ]
    loads = [
        pltpu.make_async_copy(src, dst, load.at[i])
        for i, (src, dst) in enumerate(
            [(packs, w_v), (wos, wo_v), (metas, meta_v)]
            + [(toks.at[c], tok_v.at[c]) for c in (p.cx, p.cy, p.cd)]
        )
    ]
    for copy in into:
        copy.start()
    own[2].start()
    swaps = [
        remote(pack.at[c], packs.at[p.c, p.e], a_send.at[i], a_recv.at[i], device)
        for i, (c, device) in enumerate(((p.cx, p.dx), (p.cy, p.dy), (p.cd, p.dd)))
    ]
    for copy in swaps:
        copy.start()

    def job(i, src, block, half, *ways):
        return Spread(p, nz, src, block, half, *pair_sems[2 * i : 2 * i + 2], *ways)

    j_tok = job(0, tok, lambda c, z, k: toks.at[c], seq // 2, False, True, False)
    j_meta = job(1, meta, by_device(metas, nz), meta.shape[0] // 2)
    most = seq - DEEP
    j_cot = job(2, cot.at[pl.ds(0, most)], lines_of(cots, nz, 0, most), most // 2)
    j_deep = SpreadDeep(
        p, nz, cot.at[pl.ds(most, DEEP)], lines_of(cots, nz, most, DEEP), *refs[68:]
    )
    j_wo = job(3, wo, lambda c, z, k: wos.at[z * 2 + k], 0, True, False, True)
    own_pack = packs.at[:, p.e]
    j_pack = job(4, own_pack, lambda c, z, k: packs.at[:, z * 2 + k], 0, True, False, True)
    j_meta.step(0)
    j_tok.step(0)
    for i in (0, 1, 3):
        into[i].wait()
        own[i].start()
    for i, c in enumerate((p.cx, p.cy, p.cd)):
        ref = packs.at[c, p.e]
        remote(ref, ref, a_send.at[i], a_recv.at[i], p.dx).wait_recv()
    own[0].wait()
    j_pack.step(0)
    j_meta.step(1)
    j_pack.step(1)
    j_tok.step(1)
    loads[3].start()
    loads[4].start()
    j_tok.step(2)
    loads[5].start()
    j_meta.step(2)
    j_pack.step(2)
    j_cot.step(0)
    j_deep.step(0)
    for i in range(3, nz + 2):
        j_meta.step(i)
        j_pack.step(i)
    own[2].wait()
    for z in j_meta.order:
        j_meta.from_pair(z)
    loads[2].start()
    j_wo.step(0)
    for z in j_pack.order:
        j_pack.from_pair(z)
    loads[0].start()

    loads[2].wait()
    n = meta_lines(q.shape[1], width, seq)
    per = 128 * 8 * nz // width

    def gain(line):
        found = [
            sum(meta_v[per * j + i, pl.ds(line, 1)] for i in range(per))
            for j in range(width // 128)
        ]
        return jnp.concatenate(found, axis=1)

    def head_gain(line):
        return sum(meta_v[b, pl.ds(line, 1)] for b in range(8 * nz))

    gain_out[0:1] = gain(n)
    gain_out[1:2] = gain(n + 1)
    head_out[0:1] = head_gain(n + 2)
    head_out[1:2] = head_gain(n + 3)

    def rms(x, g):
        return x * lax.rsqrt(jnp.mean(x * x, axis=-1, keepdims=True) + epsilon) * g

    into[2].wait()
    for copy in loads[3:]:
        copy.wait()

    @pl.loop(0, 8)
    def _(i):
        c, h = lax.div(i, 2), lax.rem(i, 2)
        half = seq // 2
        rows = tok_v[c, pl.ds(pl.multiple_of(h * half, half), half)].astype(f32)
        here = pl.ds(pl.multiple_of(i * half, half), half)
        xn[here] = rms(rows, gain_out[0:1]).astype(bf16)

    j_cot.step(1)
    loads[0].wait()

    @pl.loop(0, raw.shape[1] // 256)
    def _(t):
        cols = pl.ds(pl.multiple_of(t * 256, 256), 256)
        w = w_v[:, :, :, cols].reshape(width, 256)
        raw[:, cols] = jnp.dot(xn[...], w, preferred_element_type=f32)

    copy_out(0, 1, 9, 10)
    j_wo.step(1)
    j_cot.step(2)
    j_deep.step(1)

    def prep(x, g):
        y = rms(x, g)
        return (y * cosine[...] + pltpu.roll(y, HD // 2, 1) * sine[...]).astype(bf16)

    k[...] = prep(raw[:, pl.ds(heads * HD, HD)], head_out[1:2])
    values = raw[:, pl.ds((heads + 1) * HD, HD)]
    v[...] = values.astype(bf16)
    vt[...] = values.T.astype(bf16)
    copy_out(3, 4)

    def attend(h):
        cols = pl.ds(pl.multiple_of(h * HD, HD), HD)
        q[h] = prep(raw[:, cols], head_out[0:1])
        for i in range(length // seq):
            keys = (i + 1) * seq
            here = pl.ds(i * seq, seq)
            s = lax.dot_general(k[pl.ds(0, keys)], q[h, here], NT, preferred_element_type=f32)
            s = s * scale
            key_pos = lax.broadcasted_iota(jnp.int32, s.shape, 0)
            query_pos = lax.broadcasted_iota(jnp.int32, s.shape, 1) + i * seq
            s = jnp.where(key_pos <= query_pos, s, masked_value)
            largest = jnp.max(s, axis=0, keepdims=True)
            weights = jnp.exp(s - largest)
            total = jnp.sum(weights, axis=0, keepdims=True)
            o = jnp.dot(vt[:, pl.ds(0, keys)], weights.astype(bf16), preferred_element_type=f32)
            o = o / total
            ot[h, :, here] = o.astype(bf16)
            ob[here, cols] = o.T.astype(bf16)
            lse[h, :, here] = largest + jnp.log(total)

    pl.loop(0, heads // 2)(attend)
    j_cot.step(3)
    j_wo.step(2)
    j_deep.step(2)
    pl.loop(heads // 2, heads)(attend)
    copy_out(2, 5, 6)
    j_wo.step(3)
    j_cot.step(4)
    j_deep.step(3)
    own[1].wait()
    for z in j_wo.order:
        j_wo.from_pair(z)
    loads[1].start()
    own[3].wait()

    upto = lax.broadcasted_iota(jnp.int32, (seq, seq), 0) <= lax.broadcasted_iota(
        jnp.int32, (seq, seq), 1
    )
    upto = upto.astype(f32).astype(bf16)
    lines = seq // 128
    topk = n // lines // 2
    for j, expert in enumerate((me, me + 1 - 2 * p.k)):
        expert = expert.astype(f32)
        member, weight = [], []
        for line in range(lines):
            named = [meta_v[:, i * lines + line] == expert for i in range(topk)]
            gate = [meta_v[:, (topk + i) * lines + line] for i in range(topk)]
            member.append(sum(x.astype(f32) for x in named))
            weight.append(sum(jnp.where(x, y, 0.0) for x, y in zip(named, gate)))
        member = jnp.concatenate(member, axis=1)
        rank = jnp.dot(member.astype(bf16), upto, preferred_element_type=f32)
        slots[j] = jnp.where(member > 0.5, rank.astype(jnp.int32) - 1, -1)
        gates[j] = jnp.concatenate(weight, axis=1)

    copy_out(11, 12)
    loads[1].wait()
    tile = 512

    @pl.loop(0, width // tile)
    def _(t):
        cols = pl.ds(pl.multiple_of(t * tile, tile), tile)
        w = wo_v[:, :, cols].reshape(heads * HD, tile)
        out = jnp.dot(ob[...], w, preferred_element_type=f32)
        part[:, :, cols] = out.astype(bf16).reshape(4, seq, tile)

    fold = Fold(p, part, *fold_refs)
    fold.begin()
    j_cot.step(5)
    j_deep.step(4)
    fold.middle()

    def store(rows, total):
        h = tok_v[p.c, rows].astype(f32) + total
        hidden[rows] = h
        hn[rows] = rms(h, gain_out[1:2]).astype(bf16)

    fold.end(store)
    copy_out(7, 8)
    j_deep.step(5)
    for copy in swaps:
        copy.wait_send()
    for spread in (j_tok, j_meta, j_cot, j_wo, j_pack):
        spread.finish(pair=spread is j_cot)
    j_deep.finish()
    for i in range(len(held)):
        pltpu.make_async_copy(held[i], results[i], out_sem.at[i]).wait()


def meta_lines(length, width, seq):
    return 2 * 8 * seq // 128


def front(nz, scale, pack, wo, tok, cot, meta, cosine, sine):
    blocks = 8 * nz
    seq, width = tok.shape
    length = 4 * seq
    wide = pack.shape[2]
    heads = wide // HD - 2
    hbm = lambda n, a: jax.ShapeDtypeStruct(n + a.shape, a.dtype)
    out = lambda *n: jax.ShapeDtypeStruct(n[:-1], n[-1])
    vmem = lambda *n: pltpu.VMEM(n, bf16)
    dma = pltpu.SemaphoreType.DMA
    held = [
        out(length, width, bf16),
        out(length, wide, f32),
        out(heads, length, HD, bf16),
        out(length, HD, bf16),
        out(length, HD, bf16),
        out(heads, HD, length, bf16),
        out(heads, 1, length, f32),
        out(seq, width, f32),
        out(seq, width, bf16),
        out(2, width, f32),
        out(2, HD, f32),
        out(2, blocks, seq, jnp.int32),
        out(2, blocks, seq, f32),
    ]
    return pl.pallas_call(
        functools.partial(front_kernel, nz, scale),
        out_shape=[
            jax.ShapeDtypeStruct((4, 2 * nz) + pack.shape[1:], bf16),
            hbm((2 * nz,), wo),
            hbm((4,), tok),
            hbm((blocks,), cot),
            hbm((blocks,), meta),
        ]
        + held,
        in_specs=[ANY] * 5 + [IN_VMEM] * 2,
        out_specs=[ANY] * 18,
        scratch_shapes=[pltpu.VMEM(a.shape, a.dtype) for a in held]
        + [
            vmem(4, seq, width),
            vmem(4, 2 * nz, pack.shape[1], wide),
            vmem(2 * nz, wo.shape[0], width),
            pltpu.VMEM((blocks,) + meta.shape, f32),
            vmem(HD, length),
            vmem(length, heads * HD),
            vmem(4, seq, width),
        ]
        + fold_scratch(seq, width)
        + spread_sems(nz) * 5
        + [dma((n,)) for n in (3, 3, 8, 6, len(held))]
        + deep_sems(nz),
        compiler_params=pltpu.CompilerParams(
            collective_id=1, has_side_effects=True, vmem_limit_bytes=VMEM_BYTES
        ),
    )(pack, wo, tok, cot, meta, cosine, sine)


class Combine:
    def __init__(self, p, nz, cap, col, deep, rows, slots, gates, out, *scratch):
        self.p, self.nz, self.cap, self.rows, self.slots, self.gates = p, nz, cap, rows, slots, gates
        self.out = out
        self.rbuf, self.sd, self.sx, self.sy = scratch[:4]
        self.h0, self.h1, self.bx, self.by, self.bz = scratch[4:9]
        self.pair_send, self.pair_recv, self.load = scratch[9:12]
        self.s_h0, self.s_h1, self.s_x, self.s_y, self.s_z = scratch[12:17]
        self.r_h0, self.r_h1, self.r_x, self.r_y, self.r_z = scratch[17:22]
        self.order = pick_order(p, nz)
        self.most, self.width = self.sx.shape[1:]
        self.seq = self.most + deep
        self.half = self.most // 2
        self.cols = pl.ds(col, self.width)
        self.deep = deep
        self.tile = max(t for t in range(128, 1025, 128) if self.width % t == 0)
        if deep:
            self.s_d, self.b_d, self.send_d, self.recv_d = scratch[22:26]
            self.fold = Fold(p, self.s_d.at[p.z], *scratch[26:])

    def clear(self):
        bz, nz = self.bz, self.nz

        @pl.when(self.p.z == 0)
        def _():
            for ref in [bz] + ([self.b_d] if self.deep else []):
                ref[pl.ds(0, nz)] = jnp.zeros((nz,) + ref.shape[1:], ref.dtype)

        @pl.when(self.p.z == nz - 1)
        def _():
            for ref in [bz] + ([self.b_d] if self.deep else []):
                ref[pl.ds(0, nz - 1)] = jnp.zeros((nz - 1,) + ref.shape[1:], ref.dtype)
                ref[nz] = jnp.zeros(ref.shape[1:], ref.dtype)

    def pair_copy(self, c, z):
        p = self.p
        return remote(
            self.rows.at[c * (2 * self.nz) + z * 2 + 1 - p.k, :, self.cols],
            self.rbuf.at[c, z, pl.ds(self.cap, self.cap)],
            self.pair_send.at[c, z],
            self.pair_recv.at[c, z],
            p.pair,
        )

    def load_copy(self, c, z):
        return pltpu.make_async_copy(
            self.rows.at[c * (2 * self.nz) + z * 2 + self.p.k, :, self.cols],
            self.rbuf.at[c, z, pl.ds(0, self.cap)],
            self.load.at[c, z],
        )

    def begin(self):
        p = self.p
        for z in self.order:
            for c in (p.cd, p.cx, p.cy, p.c):
                self.load_copy(c, z).start()
                self.pair_copy(c, z).start()

    def places(self, c, z):
        b = pl.ds(c * (2 * self.nz) + z * 2 + self.p.k, 1)
        names = lax.broadcasted_iota(jnp.int32, (self.cap, self.seq), 0)
        both = [jnp.where(names == self.slots[n, b], self.gates[n, b], 0.0) for n in (0, 1)]
        return jnp.concatenate(both, axis=0).T.astype(bf16)

    def arrived(self, c, z):
        self.load_copy(c, z).wait()
        self.pair_copy(c, z).wait_recv()

    def copy_deep(self, z, up):
        p = self.p
        slot = z if up else jnp.where(z == p.z - 1, self.nz, z)
        return remote(
            self.s_d.at[z],
            self.b_d.at[slot],
            self.send_d.at[z],
            self.recv_d.at[slot],
            p.up if up else p.down,
        )

    def deep_send(self, z):
        @pl.when(z > self.p.z)
        def _():
            self.copy_deep(z, True).start()

        @pl.when(z < self.p.z)
        def _():
            self.copy_deep(z, False).start()

    def deep_recv(self, slot):
        ref = self.b_d.at[slot]
        remote(ref, ref, self.send_d.at[0], self.recv_d.at[slot], self.p.pair).wait_recv()

    def deep_first(self, i):
        p, nz, z = self.p, self.nz, self.order[i]
        for c in range(4):
            self.arrived(c, z)
            w = self.places(c, z)[self.most :]
            for t in range(self.width // self.tile):
                cols = pl.ds(t * self.tile, self.tile)
                total = jnp.dot(w, self.rbuf[c, z, :, cols], preferred_element_type=f32)
                self.s_d[z, c, :, cols] = total.astype(bf16)
        if i < nz - 1:

            @pl.when((p.z == 0) | (p.z == nz - 1))
            def _():
                self.deep_send(z)

    def deep_add(self, z, *slots):
        for c in range(4):
            total = self.s_d[z, c].astype(f32)
            for slot in slots:
                total = total + self.b_d[slot, c].astype(f32)
            self.s_d[z, c] = total.astype(bf16)

    def deep_next(self, i):
        p, nz, z = self.p, self.nz, self.order[i]
        if i < nz - 1:

            @pl.when((p.z > 0) & (p.z < nz - 1))
            def _():
                self.deep_recv(z)
                self.deep_add(z, z)
                self.deep_send(z)

            return

        @pl.when(p.z > 0)
        def _():
            self.deep_recv(z)

        @pl.when(p.z < nz - 1)
        def _():
            self.deep_recv(nz)

        self.deep_add(z, z, nz)
        self.fold.begin()

    def deep_end(self, i):
        if i == 0:
            self.fold.middle()
            return

        def store(lines, total):
            self.out[pl.ds(self.most + lines.start, lines.size)] = total

        self.fold.end(store)

    def fill(self, c, z, low, high, store):
        half, tile = self.half, self.tile
        w = self.places(c, z)[: self.most]
        if not self.deep:
            self.arrived(c, z)
        for t in range(self.width // tile):
            cols = pl.ds(t * tile, tile)
            total = jnp.dot(w, self.rbuf[c, z, :, cols], preferred_element_type=f32)
            for first, adds in ((0, low), (half, high)):
                part = total[first : first + half]
                for ref, start in adds:
                    part = part + ref[pl.ds(start, half), cols].astype(f32)
                store(pl.ds(first, half), cols, part)

    def into(self, buf, z):
        def store(lines, cols, total):
            buf[z, lines, cols] = total.astype(buf.dtype)

        return store

    def copy_h0(self, z):
        src = self.sd.at[z, pl.ds(0, self.half)]
        return remote(src, self.h0.at[z], self.s_h0.at[z], self.r_h0.at[z], self.p.dx)

    def copy_h1(self, z):
        src = self.sd.at[z, pl.ds(self.half, self.half)]
        return remote(src, self.h1.at[z], self.s_h1.at[z], self.r_h1.at[z], self.p.dy)

    def copy_x(self, z):
        return remote(self.sx.at[z], self.bx.at[z], self.s_x.at[z], self.r_x.at[z], self.p.dx)

    def copy_y(self, z):
        return remote(self.sy.at[z], self.by.at[z], self.s_y.at[z], self.r_y.at[z], self.p.dy)

    def copy_up(self, z):
        return remote(self.sx.at[z], self.bz.at[z], self.s_z.at[z], self.r_z.at[z], self.p.up)

    def copy_down(self, z):
        slot = jnp.where(z == self.p.z - 1, self.nz, z)
        return remote(
            self.sx.at[z], self.bz.at[slot], self.s_z.at[z], self.r_z.at[slot], self.p.down
        )

    def line_recv(self, slot):
        ref = self.bz.at[slot]
        remote(ref, ref, self.s_z.at[0], self.r_z.at[slot], self.p.pair).wait_recv()

    def diagonal(self, i):
        z = self.order[i]
        self.fill(self.p.cd, z, [], [], self.into(self.sd, z))
        self.copy_h0(z).start()
        self.copy_h1(z).start()

    def sides(self, i):
        z = self.order[i]
        self.copy_h1(z).wait_recv()
        self.fill(self.p.cx, z, [], [(self.h1.at[z], 0)], self.into(self.sx, z))
        self.copy_x(z).start()
        self.copy_h0(z).wait_recv()
        self.fill(self.p.cy, z, [(self.h0.at[z], 0)], [], self.into(self.sy, z))
        self.copy_y(z).start()

    def mine(self, i):
        p, nz, z, last = self.p, self.nz, self.order[i], i == self.nz - 1
        self.copy_x(z).wait_recv()
        self.copy_y(z).wait_recv()
        self.copy_x(z).wait_send()
        arrived = [self.bx.at[z], self.by.at[z], self.bz.at[z]]
        if last:

            @pl.when(p.z > 0)
            def _():
                self.line_recv(z)

            @pl.when(p.z < nz - 1)
            def _():
                self.line_recv(nz)

            def store(lines, cols, total):
                self.out[lines, cols] = total

            arrived.append(self.bz.at[nz])
        else:

            @pl.when(((z > p.z) & (p.z > 0)) | ((z < p.z) & (p.z < nz - 1)))
            def _():
                self.line_recv(z)

            store = self.into(self.sx, z)
        lower, upper = [(ref, 0) for ref in arrived], [(ref, self.half) for ref in arrived]
        self.fill(p.c, z, lower, upper, store)
        if not last:

            @pl.when(z > p.z)
            def _():
                self.copy_up(z).start()

            @pl.when(z < p.z)
            def _():
                self.copy_down(z).start()

    def steps(self):
        nz = self.nz
        found = [(self.diagonal, 0)] + [(self.diagonal, 1)] * (nz > 1)
        for i in range(nz):
            found.append((self.sides, i))
            if i + 2 < nz:
                found.append((self.diagonal, i + 2))
            if i > 0:
                found.append((self.mine, i - 1))
        found.append((self.mine, nz - 1))
        if self.deep:
            first = [(self.deep_first, i) for i in range(nz)]
            late = [(self.deep_next, i) for i in range(nz)]
            plan = first[:1]
            for act in found:
                if act[0] == self.diagonal and act[1] > 0:
                    plan.append(first[act[1]])
                if act == (self.mine, nz - 1):
                    plan.append(late[nz - 1])
                plan.append(act)
                if act[0] == self.sides and 1 <= act[1] < nz:
                    plan.append(late[act[1] - 1])
            found = plan + [(self.deep_end, 0), (self.deep_end, 1)]
        return [functools.partial(act, i) for act, i in found]

    def finish(self):
        p = self.p
        for i, z in enumerate(self.order):
            for c in (p.cd, p.cx, p.cy, p.c):
                self.pair_copy(c, z).wait_send()
            for copy in (self.copy_h0(z), self.copy_h1(z), self.copy_y(z)):
                copy.wait_send()
            if i < self.nz - 1:
                self.copy_up(z).wait_send()
                if self.deep:
                    self.copy_deep(z, True).wait_send()


def combine_scratch(nz, cap, seq, width, deep):
    dma = pltpu.SemaphoreType.DMA
    buf = lambda n, r: pltpu.VMEM((n, r, width), bf16)
    seq = seq - deep
    last = []
    if deep:
        last = [pltpu.VMEM((n, 4, deep, width), bf16) for n in (nz, nz + 1)]
        last += [dma((nz,)), dma((nz + 1,))] + fold_scratch(deep, width)
    return (
        [pltpu.VMEM((4, nz, 2 * cap, width), bf16)]
        + [buf(nz, seq)] * 3
        + [buf(nz, seq // 2)] * 2
        + [buf(nz, seq)] * 2
        + [buf(nz + 1, seq)]
        + [dma((4, nz))] * 3
        + [dma((nz,))] * 9
        + [dma((nz + 1,))]
        + last
    )


class WeightGrads:
    def __init__(self, pairs, outs, held, tiles, stage, stage_t, load, load_held, out_sem):
        self.pairs, self.outs, self.held, self.tiles = pairs, outs, held, tiles
        self.stage, self.stage_t = stage, stage_t
        self.load, self.load_held, self.out_sem = load, load_held, out_sem
        self.wide = tiles.shape[2]
        self.per = pairs[0][0].shape[1] // self.wide
        self.count = self.per * len(pairs)
        self.next = 0

    def columns(self, u):
        return pl.ds(u % self.per * self.wide, self.wide)

    def tile_copy(self, u):
        src = self.pairs[u // self.per][0].at[:, self.columns(u)]
        return pltpu.make_async_copy(src, self.tiles.at[u % 2], self.load.at[u % 2])

    def held_copy(self, n):
        return pltpu.make_async_copy(self.pairs[n][1], self.held, self.load_held)

    def out_copy(self, u):
        n = u // self.per
        if n < 2:
            return pltpu.make_async_copy(self.stage, self.outs[n].at[self.columns(u)], self.out_sem)
        out = self.outs[n].at[:, self.columns(u)]
        return pltpu.make_async_copy(self.stage_t, out, self.out_sem)

    def begin(self):
        self.held_copy(0).start()
        self.tile_copy(0).start()
        self.tile_copy(1).start()

    def unit(self):
        u = self.next
        if u == self.count:
            return
        self.next = u + 1
        n = u // self.per
        if u % self.per == 0:
            self.held_copy(n).wait()
        self.tile_copy(u).wait()
        total = lax.dot_general(
            self.tiles[u % 2], self.held[...], TN, preferred_element_type=f32
        )
        if u:
            self.out_copy(u - 1).wait()
        if n < 2:
            self.stage[...] = total
        else:
            self.stage_t[...] = total.T
        self.out_copy(u).start()
        if u + 2 < self.count:
            self.tile_copy(u + 2).start()
        if u + 1 < self.count and (u + 1) % self.per == 0:
            self.held_copy(n + 1).start()

    def finish(self):
        while self.next < self.count:
            self.unit()
        self.out_copy(self.count - 1).wait()


def middle_kernel(nz, cap, deep, *refs):
    rows, x, dr, a, dg, du, slots, gates, hidden, cot, gains = refs[:11]
    grad_hidden, mlp_grad, branch, out_gate, out_up, out_down = refs[11:17]
    low, local, send, recv = refs[17:21]
    p = Place()
    work = WeightGrads(((x, dg), (x, du), (dr, a)), (out_gate, out_up, out_down), *refs[21:28])
    job = Combine(p, nz, cap, 0, deep, rows, slots, gates, grad_hidden, *refs[28:])
    job.clear()
    greet(p, nz)
    job.begin()
    work.begin()
    for i, step in enumerate(job.steps()):
        step()
        if i >= 4 and i % 2:
            work.unit()
    seq = cot.shape[0]
    mlp_grad[...] = jnp.zeros(mlp_grad.shape, f32)
    for first in range(0, seq, seq // 4):
        lines = pl.ds(first, seq // 4)
        by_x, by_gain = rms_back(hidden[lines], gains[1:2], grad_hidden[lines])
        total = cot[lines].astype(f32) + by_x
        grad_hidden[lines] = total
        low[lines] = total.astype(bf16)
        mlp_grad[...] += by_gain
    keep = pltpu.make_async_copy(low, branch.at[p.c], local)
    keep.start()
    gather = Spread(
        p, nz, low, lambda c, z, k: branch.at[c], seq // 2, send, recv, False, True, False
    )
    gather.step(0)
    for i in range(8):
        work.unit()
    gather.step(1)
    work.finish()
    gather.step(2)
    keep.wait()
    gather.finish()
    job.finish()


def middle(nz, deep, rows, x, dr, a, dg, du, slots, gates, hidden, cot, gains):
    _, cap, width = rows.shape
    seq = slots.shape[2]
    ff = a.shape[1]
    shape = jax.ShapeDtypeStruct
    dma = pltpu.SemaphoreType.DMA
    vmem = lambda *n: pltpu.VMEM(n, bf16)
    tile = min(256, ff)
    return pl.pallas_call(
        functools.partial(middle_kernel, nz, cap, deep),
        out_shape=[
            shape((seq, width), f32),
            shape((1, width), f32),
            shape((4, seq, width), bf16),
            shape((width, ff), f32),
            shape((width, ff), f32),
            shape((ff, width), f32),
        ],
        in_specs=[ANY] * 6 + [IN_VMEM] * 5,
        out_specs=[IN_VMEM] * 2 + [ANY] * 4,
        scratch_shapes=[vmem(seq, width), dma]
        + spread_sems(nz)
        + [vmem(*a.shape), vmem(2, x.shape[0], tile)]
        + [pltpu.VMEM((tile, ff), f32), pltpu.VMEM((ff, tile), f32)]
        + [dma((2,)), dma, dma]
        + combine_scratch(nz, cap, seq, width, deep),
        compiler_params=pltpu.CompilerParams(
            collective_id=4, has_side_effects=True, vmem_limit_bytes=VMEM_BYTES
        ),
    )(rows, x, dr, a, dg, du, slots, gates, hidden, cot, gains)


class LineSum:
    def __init__(self, p, nz, part, own, sib, b, pair_s, pair_r, line_s, line_r):
        self.p, self.nz, self.part, self.own, self.sib, self.b = p, nz, part, own, sib, b
        self.pair_s, self.pair_r, self.line_s, self.line_r = pair_s, pair_r, line_s, line_r
        self.order = pick_order(p, nz)

    def clear(self):
        b, nz = self.b, self.nz

        @pl.when(self.p.z == 0)
        def _():
            b[pl.ds(0, nz)] = jnp.zeros((nz,) + b.shape[1:], b.dtype)

        @pl.when(self.p.z == nz - 1)
        def _():
            b[pl.ds(0, nz - 1)] = jnp.zeros((nz - 1,) + b.shape[1:], b.dtype)
            b[nz] = jnp.zeros(b.shape[1:], b.dtype)

    def pair_copy(self, z):
        p = self.p
        src = self.part(z, 1 - p.k)
        return remote(src, self.sib.at[z], self.pair_s.at[z], self.pair_r.at[z], p.pair)

    def begin(self):
        for z in self.order:
            self.pair_copy(z).start()

    def copy_up(self, z):
        p = self.p
        return remote(self.own(z), self.b.at[z], self.line_s.at[z], self.line_r.at[z], p.up)

    def copy_down(self, z):
        p = self.p
        slot = jnp.where(z == p.z - 1, self.nz, z)
        return remote(self.own(z), self.b.at[slot], self.line_s.at[z], self.line_r.at[slot], p.down)

    def line_recv(self, slot):
        ref = self.b.at[slot]
        remote(ref, ref, self.line_s.at[0], self.line_r.at[slot], self.p.pair).wait_recv()

    def reduce(self, n, store=None):
        p, nz, z = self.p, self.nz, self.order[n]
        own, b = self.own(z), self.b
        self.pair_copy(z).wait_recv()
        if n == nz - 1:

            @pl.when(p.z > 0)
            def _():
                self.line_recv(z)

            @pl.when(p.z < nz - 1)
            def _():
                self.line_recv(nz)

            total = own[...].astype(f32) + self.sib[z].astype(f32) + b[z].astype(f32)
            store(total + b[nz].astype(f32))
            return

        @pl.when(((z > p.z) & (p.z > 0)) | ((z < p.z) & (p.z < nz - 1)))
        def _():
            self.line_recv(z)

        total = own[...].astype(f32) + self.sib[z].astype(f32) + b[z].astype(f32)
        own[...] = total.astype(own.dtype)

        @pl.when(z > p.z)
        def _():
            self.copy_up(z).start()

        @pl.when(z < p.z)
        def _():
            self.copy_down(z).start()

    def finish(self):
        for n, z in enumerate(self.order):
            self.pair_copy(z).wait_send()
            if n < self.nz - 1:
                self.copy_up(z).wait_send()


def line_sems(nz):
    dma = pltpu.SemaphoreType.DMA
    return [dma((nz,))] * 3 + [dma((nz + 1,))]


def rms_back(x, gain, grad):
    r = lax.rsqrt(jnp.mean(x * x, axis=-1, keepdims=True) + epsilon)
    scaled = gain * grad
    mean = jnp.mean(x * scaled, axis=-1, keepdims=True)
    by_gain = jnp.sum(x * r * grad, axis=0, keepdims=True)
    return r * scaled - x * (r * r * r * mean), by_gain


def back_kernel(nz, cap, scale, *refs):
    branch, wos, packs, xn, raw, q, ot, rows = refs[:8]
    k, v, lse, cosine, sine, head_gain, slots, gates = refs[8:16]
    sum_o, gw, part, head_grad, mixed = refs[16:21]
    rows_v, wo_v, w_v, raw_v, q_v, ot_v, do, kt, low, dq, dk, dv, w_stage, sib, line_b = refs[21:36]
    load, w_sem, ot_sem = refs[36:39]
    p = Place()
    line = LineSum(
        p,
        nz,
        lambda z, k: wo_v.at[z * 2 + k],
        lambda z: wo_v.at[z * 2 + p.k],
        sib,
        line_b,
        *refs[39:43],
    )
    combine = Combine(p, nz, cap, 0, 0, rows, slots, gates, mixed, *refs[43:])
    length, wide = raw.shape
    heads = q.shape[0]
    seq = length // 4
    width = xn.shape[2]
    loads = [
        pltpu.make_async_copy(src, dst, load.at[i])
        for i, (src, dst) in enumerate(
            ((branch, rows_v), (wos, wo_v), (q, q_v), (packs, w_v))
        )
    ]
    load_ot = [
        pltpu.make_async_copy(ot.at[pl.ds(2 * t, 2)], ot_v.at[t % 2], ot_sem.at[t % 2])
        for t in range(heads // 2)
    ]
    load_xn = pltpu.make_async_copy(xn, rows_v, load.at[5])

    def load_raw(cols):
        return pltpu.make_async_copy(raw.at[:, cols], raw_v, load.at[6])

    for copy in loads + load_ot[:2]:
        copy.start()
    combine.clear()
    line.clear()
    greet(p, nz)
    combine.begin()
    steps = combine.steps()
    run = lambda n: [steps.pop(0)() for _ in range(min(n, len(steps)))]
    kt[...] = k[...].astype(f32).T.astype(bf16)
    run(2)
    loads[0].wait()
    loads[1].wait()

    @pl.loop(0, heads * HD // 256)
    def _(t):
        cols = pl.ds(pl.multiple_of(t * 256, 256), 256)
        w = wo_v[pl.ds(t * (256 // wo_v.shape[1]), 256 // wo_v.shape[1])].reshape(256, width)
        out = lax.dot_general(rows_v[...].reshape(length, width), w, NT, preferred_element_type=f32)
        do[:, cols] = out.astype(bf16)

    run(1)

    for t in range(heads // 2):
        load_ot[t].wait()
        here = 2 * HD // wo_v.shape[1]

        @pl.loop(0, width // 512)
        def _(i):
            cols = pl.ds(pl.multiple_of(i * 512, 512), 512)
            out = jnp.dot(
                ot_v[t % 2].reshape(2 * HD, length),
                rows_v[:, :, cols].reshape(length, 512),
                preferred_element_type=f32,
            )
            wo_v[pl.ds(t * here, here), :, cols] = out.astype(bf16).reshape(
                here, wo_v.shape[1], 512
            )

        if t + 2 < heads // 2:
            load_ot[t + 2].start()

    line.begin()
    load_xn.start()
    run(1)
    loads[2].wait()
    dk[...] = jnp.zeros(dk.shape, f32)
    dv[...] = jnp.zeros(dv.shape, f32)
    head_grad[...] = jnp.zeros(head_grad.shape, f32)

    def unprep(gain, grad, cols):
        by_gain = jnp.zeros((1, HD), f32)
        for i in range(length // seq):
            here = pl.ds(i * seq, seq)
            g = grad[here]
            g = g * cosine[here] + pltpu.roll(g * sine[here], HD // 2, 1)
            by_x, more = rms_back(raw_v[here], gain, g)
            low[here, cols] = by_x.astype(bf16)
            by_gain = by_gain + more
        return by_gain

    def attend(h):
        cols = pl.ds(pl.multiple_of(h * HD, HD), HD)
        load_raw(cols).start()
        for i in range(length // seq):
            keys = pl.ds(0, (i + 1) * seq)
            here = pl.ds(i * seq, seq)
            s = lax.dot_general(k[keys], q_v[h, here], NT, preferred_element_type=f32) * scale
            key_pos = lax.broadcasted_iota(jnp.int32, s.shape, 0)
            query_pos = lax.broadcasted_iota(jnp.int32, s.shape, 1) + i * seq
            probs = jnp.where(key_pos <= query_pos, jnp.exp(s - lse[h, :, here]), 0.0)
            dp = lax.dot_general(v[keys], do[here, cols], NT, preferred_element_type=f32)
            delta = jnp.sum(probs * dp, axis=0, keepdims=True)
            ds = (probs * (dp - delta)).astype(bf16)
            dk[keys] += jnp.dot(ds, q_v[h, here], preferred_element_type=f32) * scale
            dv[keys] += jnp.dot(probs.astype(bf16), do[here, cols], preferred_element_type=f32)
            dq[here] = (jnp.dot(kt[:, keys], ds, preferred_element_type=f32) * scale).T
        load_raw(cols).wait()
        head_grad[0:1] += unprep(head_gain[0:1], dq, cols)

    def store(total):
        sum_o[...] = total

    for n, first in enumerate(range(0, heads, 2)):
        pl.loop(first, first + 2)(attend)
        run(1)
        if n < nz - 1:
            line.reduce(n)
    load_raw(pl.ds(heads * HD, HD)).start()
    load_raw(pl.ds(heads * HD, HD)).wait()
    head_grad[1:2] = unprep(head_gain[1:2], dk, pl.ds(heads * HD, HD))
    low[:, pl.ds((heads + 1) * HD, HD)] = dv[...].astype(bf16)

    load_xn.wait()
    lines = w_stage.shape[1] * w_stage.shape[2]

    def w_out(t):
        first = t * w_stage.shape[1]
        c, e = first // (2 * nz), first % (2 * nz)
        return pltpu.make_async_copy(
            w_stage.at[t % 2], gw.at[c, pl.ds(e, w_stage.shape[1])], w_sem.at[t % 2]
        )

    for t in range(width // lines):
        if t >= 2:
            w_out(t - 2).wait()
        x = rows_v[:, :, pl.ds(t * lines, lines)].reshape(length, lines)
        out = lax.dot_general(x, low[...], TN, preferred_element_type=f32)
        w_stage[t % 2] = out.astype(bf16).reshape(w_stage.shape[1:])
        w_out(t).start()
        if t % 3 == 2:
            run(1)
    loads[3].wait()
    for c in range(4):

        @pl.loop(0, 2)
        def _(i):
            here = nz * w_v.shape[2]
            w = w_v[c, pl.ds(i * nz, nz)].reshape(here, wide)
            out = lax.dot_general(low[...], w, NT, preferred_element_type=f32)
            cols = pl.ds(pl.multiple_of((2 * c + i) * here, here), here)
            rows_v[:, :, cols] = out.astype(bf16).reshape(4, seq, here)

        if c % 2:
            run(1)
    part_out = pltpu.make_async_copy(rows_v, part, load.at[4])
    part_out.start()
    line.reduce(nz - 1, store)
    run(len(steps))
    part_out.wait()
    for t in range(2):
        w_out(width // lines - 2 + t).wait()
    combine.finish()
    line.finish()


def back(nz, scale, columns, branch, wos, packs, xn, raw, q, ot, rows, k, v, lse, cosine, sine, head_gain, slots, gates):
    length, wide = raw.shape
    heads = q.shape[0]
    seq = length // 4
    width = xn.shape[1]
    cap = rows.shape[1]
    shape = jax.ShapeDtypeStruct
    vmem = lambda *n: pltpu.VMEM(n, bf16)
    wide_f = lambda *n: pltpu.VMEM(n, f32)
    dma = pltpu.SemaphoreType.DMA
    return pl.pallas_call(
        functools.partial(back_kernel, nz, cap, scale),
        out_shape=[
            shape(wos.shape[1:], f32),
            shape(packs.shape, bf16),
            shape((4, seq, width), bf16),
            shape((2, HD), f32),
            shape((seq, columns), f32),
        ],
        in_specs=[ANY] * 8 + [IN_VMEM] * 8,
        out_specs=[IN_VMEM, ANY, ANY] + [IN_VMEM] * 2,
        scratch_shapes=[
            vmem(4, seq, width),
            vmem(*wos.shape),
            vmem(*packs.shape),
            wide_f(length, HD),
            vmem(*q.shape),
            vmem(2, 2, HD, length),
            vmem(length, heads * HD),
            vmem(HD, length),
            vmem(length, wide),
            wide_f(length, HD),
            wide_f(length, HD),
            wide_f(length, HD),
            vmem(2, 4, packs.shape[2], wide),
            vmem(nz, *wos.shape[1:]),
            vmem(nz + 1, *wos.shape[1:]),
            dma((7,)),
            dma((2,)),
            dma((2,)),
        ]
        + line_sems(nz)
        + combine_scratch(nz, cap, seq, columns, 0),
        compiler_params=pltpu.CompilerParams(
            collective_id=5, has_side_effects=True, vmem_limit_bytes=VMEM_BYTES
        ),
    )(branch, wos, packs, xn.reshape(4, seq, width), raw, q, ot, rows, k, v, lse, cosine, sine, head_gain, slots, gates)


def last_kernel(nz, cap, col, *refs):
    gq, rows, part, tok_in, dh_in, gains, mlp_grad, head_grad, slots, gates = refs[:10]
    oq, ok, ov, all_gains, grad_tokens, mixed = refs[10:16]
    own, sib, line_b, swap_s, swap_r, gain_v, part_v, tok, dh = refs[16:25]
    load, a_send, a_recv, g_send, g_recv, local, in_sem = refs[25:32]
    p = Place()
    fold = Fold(p, part_v, *refs[32:40], far=part)
    line = LineSum(
        p, nz, lambda z, k: gq.at[:, z * 2 + k], lambda z: own.at[z], sib, line_b, *refs[40:44]
    )
    combine = Combine(p, nz, cap, col, LAST_DEEP, rows, slots, gates, mixed, *refs[44:])
    combine.clear()
    line.clear()
    inputs = [
        pltpu.make_async_copy(src, dst, in_sem.at[i])
        for i, (src, dst) in enumerate(((part, part_v), (tok_in, tok), (dh_in, dh)))
    ]
    for copy in inputs:
        copy.start()
    greet(p, nz, diagonal=True)

    def load_copy(z):
        return pltpu.make_async_copy(gq.at[:, z * 2 + p.k], own.at[z], load.at[z])

    def swaps():
        return [
            remote(swap_s.at[c], swap_r.at[p.c], a_send.at[n], a_recv.at[n], device)
            for n, (c, device) in enumerate(((p.cx, p.dx), (p.cy, p.dy), (p.cd, p.dd)))
        ]

    def swap(total):
        swap_s[...] = total.astype(swap_s.dtype)
        for copy in swaps():
            copy.start()
        swap_r[p.c] = swap_s[p.c]

    fold.begin()
    line.begin()
    for z in line.order:
        load_copy(z).start()
    combine.begin()
    steps = combine.steps()
    run = lambda n: [steps.pop(0)() for _ in range(min(n, len(steps)))]

    def reduce(n):
        load_copy(line.order[n]).wait()
        line.reduce(n, swap)

    reduce(0)
    run(1)
    inputs[0].wait()
    fold.middle()
    reduce(1)
    run(2)

    gain_v[...] = jnp.zeros(gain_v.shape, f32)
    width = tok.shape[1]
    for copy in inputs[1:]:
        copy.wait()

    def store(lines, total):
        by_x, by_gain = rms_back(tok[lines].astype(f32), gains[0:1], total)
        grad_tokens[lines] = (dh[lines] + by_x).astype(bf16)
        for j in range(width // 128):
            gain_v[pl.ds(j, 1)] += by_gain[:, j * 128 : (j + 1) * 128]

    fold.end(store)
    for j in range(width // 128):
        gain_v[pl.ds(width // 128 + j, 1)] = mlp_grad[:, pl.ds(j * 128, 128)]
    gain_v[pl.ds(2 * width // 128, 2)] = head_grad[...]
    block = by_device(all_gains, nz)
    keep = pltpu.make_async_copy(gain_v, block(p.c, p.z, p.k), local)
    keep.start()
    job = Spread(p, nz, gain_v, block, gain_v.shape[0] // 2, g_send, g_recv)
    run(2)
    reduce(2)
    job.step(0)
    run(2)
    job.step(1)
    reduce(3)
    run(1)
    for n in range(2, nz + 2):
        job.step(n)
        run(1)
    for n, c in enumerate((p.cx, p.cy, p.cd)):
        ref = swap_r.at[c]
        remote(ref, ref, a_send.at[n], a_recv.at[n], p.dx).wait_recv()
    heads = oq.shape[1] // 4
    kv = ok.shape[1] // 4
    for c in range(4):
        oq[:, pl.ds(c * heads, heads)] = swap_r[c, :, pl.ds(0, heads)].astype(f32)
        ok[:, pl.ds(c * kv, kv)] = swap_r[c, :, pl.ds(heads, kv)].astype(f32)
        ov[:, pl.ds(c * kv, kv)] = swap_r[c, :, pl.ds(heads + kv, kv)].astype(f32)
    run(len(steps))
    for copy in swaps():
        copy.wait_send()
    keep.wait()
    job.finish()
    combine.finish()
    line.finish()


def reduce_last(nz, col, gq, rows, part, tok, dh, gains, mlp_grad, head_grad, slots, gates):
    _, _, rows_q, wide = gq.shape
    seq, width = tok.shape
    cap = rows.shape[1]
    kv = HD
    heads = wide - 2 * kv
    lines = -(-(2 * width // 128 + 2) // 16) * 16
    dma = pltpu.SemaphoreType.DMA
    shape = jax.ShapeDtypeStruct
    q = lambda *n: pltpu.VMEM(n + (4, rows_q, wide), bf16)
    return pl.pallas_call(
        functools.partial(last_kernel, nz, cap, col),
        out_shape=[
            shape((rows_q, 4 * heads), f32),
            shape((rows_q, 4 * kv), f32),
            shape((rows_q, 4 * kv), f32),
            shape((8 * nz, lines, 128), f32),
            shape((seq, width), bf16),
            shape((seq, width - col), f32),
        ],
        in_specs=[ANY] * 5 + [IN_VMEM] * 5,
        out_specs=[IN_VMEM] * 3 + [ANY] + [IN_VMEM] * 2,
        scratch_shapes=[q(nz), q(nz), q(nz + 1), q(), q()]
        + [pltpu.VMEM((lines, 128), f32)]
        + [pltpu.VMEM((4, seq, width), bf16), pltpu.VMEM((seq, width), bf16)]
        + [pltpu.VMEM((seq, width), f32)]
        + [dma((nz,))]
        + [dma((3,))] * 2
        + spread_sems(nz)
        + [dma, dma((3,))]
        + fold_scratch(seq, width)
        + line_sems(nz)
        + combine_scratch(nz, cap, seq, width - col, LAST_DEEP),
        compiler_params=pltpu.CompilerParams(
            collective_id=9, has_side_effects=True, vmem_limit_bytes=VMEM_BYTES
        ),
    )(gq, rows, part, tok, dh, gains, mlp_grad, head_grad, slots, gates)


def experts_kernel(
    nz,
    cap,
    mine,
    cots,
    slots,
    gates,
    wg_hbm,
    wu_hbm,
    wd_hbm,
    all_rows,
    produced,
    grad_inputs,
    x_out,
    dr_out,
    a_out,
    dg_out,
    du_out,
    stage_x,
    stage_d,
    x,
    dr,
    r,
    dx,
    a,
    dg,
    du,
    send,
    recv,
    load,
    out_sem,
    back_sem,
    wg,
    wu,
    wd,
    w_sem,
):
    p = Place()
    weights = [
        pltpu.make_async_copy(src, dst, w_sem.at[i])
        for i, (src, dst) in enumerate(((wg_hbm, wg), (wu_hbm, wu), (wd_hbm, wd)))
    ]
    for copy in weights:
        copy.start()
    greet(p, nz)
    job = Spread(p, nz, mine, by_device(all_rows, nz), mine.shape[0] // 2, send, recv)
    seq, width = mine.shape
    ff = a.shape[2]
    wide = min(512, width)
    narrow = min(256, ff)
    lines = [(p.c, 0), (p.cx, 0), (p.c, 1), (p.cx, 1)], [(p.cy, 0), (p.cd, 0), (p.cy, 1), (p.cd, 1)]
    turns = [(i - j, j) for i in range(1, nz + 2) for j in (1, 2) if 0 <= i - j < nz]
    turns = [(i, j - 1) for i, j in turns]

    def index(h, i, z):
        c, other = lines[h][i]
        return c * (2 * nz) + z * 2 + lax.rem(p.k + other, 2)

    def load_x(n, i):
        at, h = turns[n]
        src = mine if n == i == 0 else all_rows.at[index(h, i, job.order[at])]
        return pltpu.make_async_copy(src, stage_x.at[i], load.at[0, i])

    def load_d(n, i):
        at, h = turns[n]
        src = cots.at[index(h, i, job.order[at])]
        return pltpu.make_async_copy(src, stage_d.at[n % 2, i], load.at[1 + n % 2, i])

    def outs(h, z):
        whole = ((x, x_out), (dr, dr_out), (a, a_out), (dg, dg_out), (du, du_out))
        found = [
            pltpu.make_async_copy(src.at[h], dst.at[z, h], out_sem.at[h, n])
            for n, (src, dst) in enumerate(whole)
        ]
        for n, (src, dst) in enumerate(((r, produced), (dx, grad_inputs))):
            for i in range(4):
                found.append(
                    pltpu.make_async_copy(
                        src.at[h, pl.ds(i * cap, cap)], dst.at[index(h, i, z)], back_sem.at[h, n, i]
                    )
                )
        return found

    def group(n):
        at, h = turns[n]
        z = job.order[at]
        for i in range(4):
            load_x(n, i).start()
        if n + 1 < len(turns):
            for i in range(4):
                load_d(n + 1, i).start()
        if at:
            for copy in outs(h, job.order[at - 1]):
                copy.wait()
        for i in range(4):
            at_b = pl.ds(index(h, i, z), 1)
            names = lax.broadcasted_iota(jnp.int32, (cap, seq), 0) == slots[0, at_b]
            chosen = names.astype(f32).astype(bf16)
            row_gate = jnp.where(names, gates[0, at_b], 0.0)
            row_gate = jnp.sum(row_gate, axis=1, keepdims=True)
            here = pl.ds(i * cap, cap)
            load_d(n, i).wait()
            picked = jnp.dot(chosen, stage_d[n % 2, i], preferred_element_type=f32)
            dr[h, here] = (row_gate * picked).astype(bf16)
            load_x(n, i).wait()
            picked = jnp.dot(chosen, stage_x[i], preferred_element_type=f32)
            x[h, here] = picked.astype(bf16)

        if n == 0:
            for copy in weights:
                copy.wait()

        @pl.loop(0, ff // narrow)
        def _(t):
            cols = pl.ds(pl.multiple_of(t * narrow, narrow), narrow)
            g = jnp.dot(x[h], wg[:, cols], preferred_element_type=f32)
            u = jnp.dot(x[h], wu[:, cols], preferred_element_type=f32)
            da = lax.dot_general(dr[h], wd[cols, :], NT, preferred_element_type=f32)
            s = jax.nn.sigmoid(g)
            swish = g * s
            a[h, :, cols] = (swish * u).astype(bf16)
            du[h, :, cols] = (da * swish).astype(bf16)
            dg[h, :, cols] = (da * u * s * (1.0 + g * (1.0 - s))).astype(bf16)

        @pl.loop(0, width // wide)
        def _(t):
            cols = pl.ds(pl.multiple_of(t * wide, wide), wide)
            r[h, :, cols] = jnp.dot(a[h], wd[:, cols], preferred_element_type=f32).astype(bf16)
            back = lax.dot_general(dg[h], wg[cols, :], NT, preferred_element_type=f32)
            back = back + lax.dot_general(du[h], wu[cols, :], NT, preferred_element_type=f32)
            dx[h, :, cols] = back.astype(bf16)

        for copy in outs(h, z):
            copy.start()

    for i in range(4):
        load_d(0, i).start()
    done = 0
    for i in range(nz + 2):
        if i < nz:
            job.along(i)
        if 1 <= i <= nz:
            z = job.order[i - 1]
            job.beside(z)
            for j in (5, 6):
                job.got(j, z)
            group(done)
            done += 1
        if i >= 2:
            z = job.order[i - 2]
            job.across(z)
            for j in (7, 8, 9):
                job.got(j, z)
            group(done)
            done += 1
    for h in (0, 1):
        for copy in outs(h, job.order[nz - 1]):
            copy.wait()
    job.finish(pair=False)


def run_experts(nz, cap, mine, cots, slots, gates, wg, wu, wd):
    seq, width = mine.shape
    ff = wg.shape[1]
    rows = 4 * cap
    blocks = 8 * nz
    shape = lambda *n: jax.ShapeDtypeStruct(n, bf16)
    vmem = lambda *n: pltpu.VMEM(n, bf16)
    dma = pltpu.SemaphoreType.DMA
    return pl.pallas_call(
        functools.partial(experts_kernel, nz, cap),
        out_shape=[shape(blocks, seq, width)]
        + [shape(blocks, cap, width)] * 2
        + [shape(nz, 2, rows, width)] * 2
        + [shape(nz, 2, rows, ff)] * 3,
        in_specs=[ANY] * 2 + [IN_VMEM] * 2 + [ANY] * 3,
        out_specs=[ANY] * 8,
        scratch_shapes=[vmem(4, seq, width), vmem(2, 4, seq, width)]
        + [vmem(2, rows, width)] * 4
        + [vmem(2, rows, ff)] * 3
        + spread_sems(nz)
        + [dma((3, 4)), dma((2, 5)), dma((2, 2, 4))]
        + [vmem(*wg.shape), vmem(*wu.shape), vmem(*wd.shape), dma((3,))],
        compiler_params=pltpu.CompilerParams(
            collective_id=3, has_side_effects=True, vmem_limit_bytes=VMEM_BYTES
        ),
    )(mine, cots, slots, gates, wg, wu, wd)[1:]


def mm(a, b, contract, kind=f32):
    return lax.dot_general(a, b, ((contract[:1], contract[1:]), ((), ())), preferred_element_type=f32).astype(kind)


def fast_body(
    tokens,
    query_weight,
    key_weight,
    value_weight,
    output_weight,
    norm_gains,
    head_gains,
    expert_gate,
    expert_up,
    expert_down,
    routes,
    route_gates,
    cotangent,
):
    seq, width = tokens.shape[1:]
    nz = lax.axis_size("expert") // 2
    devices = lax.axis_size(("ctx", "expert"))
    length = 4 * seq
    topk = routes.shape[2]
    cap = max(2, 5 * seq * topk // (4 * devices))
    heads = HQ // 4
    wq = heads * HD
    scale = HD ** (-0.5)
    c = lax.axis_index("ctx")
    e = lax.axis_index("expert")
    k = lax.rem(e, 2)
    me = c * (2 * nz) + e
    rows_q = query_weight.shape[0]

    def cols(weight):
        return weight.reshape(rows_q, 4, -1).transpose(1, 0, 2)

    pack = jnp.concatenate([cols(query_weight), cols(key_weight), cols(value_weight)], axis=2)
    share = norm_gains.shape[1]
    head_share = head_gains.shape[1]
    lane = jnp.arange(128)

    def placed(part, size):
        spread = jnp.tile(part.astype(f32), (1, 128 // size))
        return jnp.where(lane[None, :] // size == lax.rem(me, 128 // size), spread, 0.0)

    meta = jnp.concatenate(
        [
            routes.reshape(seq, topk).T.astype(f32).reshape(-1, 128),
            route_gates.reshape(seq, topk).T.reshape(-1, 128),
            placed(norm_gains, share),
            placed(head_gains, head_share),
        ]
    )
    meta = jnp.pad(meta, ((0, -meta.shape[0] % 16), (0, 0)))
    half = HD // 2
    angles = jnp.arange(length, dtype=jnp.int32).astype(f32)[:, None] * (
        rope_base ** (-jnp.arange(half, dtype=f32) / half)
    )
    cosine, sine = jnp.cos(angles), jnp.sin(angles)
    tables = (
        jnp.concatenate([cosine, cosine], axis=1),
        jnp.concatenate([-sine, sine], axis=1),
    )
    found = front(
        nz,
        scale,
        pack,
        output_weight,
        tokens.reshape(seq, width),
        cotangent.reshape(seq, width),
        meta,
        *tables,
    )
    weight, wo, _, cots, _, normed, raw, queries, keys, values, attended, lse = found[:12]
    hidden, normed_mlp, gains, head_gain, slots2, gates2 = found[12:]
    produced, grad_inputs, arrived, grad_arrived, activated, grad_gate_pre, grad_up_pre = run_experts(
        nz, cap, normed_mlp, cots, slots2, gates2, expert_gate[0], expert_up[0], expert_down[0]
    )
    grad_hidden, grad_gain_mlp, branch, grad_gate, grad_up, grad_down = middle(
        nz,
        DEEP,
        grad_inputs,
        *(
            a.reshape(devices * cap, -1)
            for a in (arrived, grad_arrived, activated, grad_gate_pre, grad_up_pre)
        ),
        slots2,
        jnp.ones_like(gates2),
        hidden,
        cotangent.reshape(seq, width),
        gains,
    )
    columns = width // 2
    sum_o, grad_weight, part, grad_head, mixed_low = back(
        nz,
        scale,
        columns,
        branch,
        wo,
        weight,
        normed,
        raw,
        queries,
        attended,
        produced,
        keys,
        values,
        lse,
        *tables,
        head_gain,
        slots2,
        gates2,
    )
    sum_q, sum_k, sum_v, all_gain_parts, grad_input, mixed_high = reduce_last(
        nz,
        columns,
        grad_weight,
        produced,
        part,
        tokens.reshape(seq, width),
        grad_hidden,
        gains,
        grad_gain_mlp,
        grad_head,
        slots2,
        gates2,
    )
    mixed = hidden + jnp.concatenate([mixed_low, mixed_high], axis=1)
    gain_sums = jnp.sum(all_gain_parts, axis=0).reshape(-1)
    norm_sums = gain_sums[: 2 * width].reshape(2, width)
    head_sums = gain_sums[2 * width : 2 * width + 2 * HD].reshape(2, HD)
    return (
        mixed.astype(bf16).reshape(tokens.shape),
        grad_input.reshape(tokens.shape),
        sum_q,
        sum_k,
        sum_v,
        sum_o,
        lax.dynamic_slice_in_dim(norm_sums, me * share, share, 1),
        lax.dynamic_slice_in_dim(head_sums, me * head_share, head_share, 1),
        grad_gate[None],
        grad_up[None],
        grad_down[None],
    )


def solution(mesh):
    small = mesh.shape["ctx"] == HK and mesh.size == 32
    return jax.shard_map(
        fast_body if small else body,
        mesh=mesh,
        in_specs=(
            P("expert", "ctx", None),
            P(("ctx", "expert"), None),
            P(("ctx", "expert"), None),
            P(("ctx", "expert"), None),
            P(("ctx", "expert"), None),
            P(None, ("ctx", "expert")),
            P(None, ("ctx", "expert")),
            P(("ctx", "expert"), None, None),
            P(("ctx", "expert"), None, None),
            P(("ctx", "expert"), None, None),
            P("expert", "ctx", None),
            P("expert", "ctx", None),
            P("expert", "ctx", None),
        ),
        out_specs=(
            P("expert", "ctx", None),
            P("expert", "ctx", None),
            P(("ctx", "expert"), None),
            P(("ctx", "expert"), None),
            P(("ctx", "expert"), None),
            P(("ctx", "expert"), None),
            P(None, ("ctx", "expert")),
            P(None, ("ctx", "expert")),
            P(("ctx", "expert"), None, None),
            P(("ctx", "expert"), None, None),
            P(("ctx", "expert"), None, None),
        ),
        check_vma=False,
    )
```

```python
import functools

import jax
import jax.numpy as jnp
from jax import lax
from jax.experimental import pallas as pl
from jax.experimental.pallas import tpu as pltpu
from jax.sharding import PartitionSpec as P

HQ = 32
HK = 4
HD = 128


epsilon = 1e-06
rope_base = 1000000.0
masked_value = -1e30


def rms_scale(values, scale_gain):
    return (
        values * lax.rsqrt(jnp.mean(values * values, axis=-1, keepdims=True) + epsilon) * scale_gain
    )


def rotate(values, positions):
    half_size = values.shape[-1] // 2
    frequency = rope_base ** (-jnp.arange(half_size, dtype=jnp.float32) / half_size)
    angles = positions.astype(jnp.float32)[:, None] * frequency[None, :]
    cosine = jnp.cos(angles)[:, None, :]
    sine_part = jnp.sin(angles)[:, None, :]
    first_half = values[..., :half_size]
    second_half = values[..., half_size:]
    return jnp.concatenate(
        [
            first_half * cosine - second_half * sine_part,
            second_half * cosine + first_half * sine_part,
        ],
        axis=-1,
    )


def body(
    tokens,
    query_weight,
    key_weight,
    value_weight,
    output_weight,
    norm_gains,
    head_gains,
    expert_gate,
    expert_up,
    expert_down,
    routes,
    route_gates,
    cotangent,
):
    seq_rows = tokens.shape[1]
    width = tokens.shape[2]
    groups = HQ // HK
    kv_width = HK * HD
    scale = HD ** (-0.5)
    positions = lax.axis_index("ctx") * seq_rows + jnp.arange(seq_rows, dtype=jnp.int32)
    last_pos = lax.axis_index("ctx") * seq_rows + seq_rows - 1
    rows_in = tokens.reshape(seq_rows, width).astype(jnp.float32)
    full_q, full_k, full_v, full_o, gains, head_gain = (
        lax.all_gather(query_weight, ("ctx", "expert"), axis=0, tiled=True),
        lax.all_gather(key_weight, ("ctx", "expert"), axis=0, tiled=True),
        lax.all_gather(value_weight, ("ctx", "expert"), axis=0, tiled=True),
        lax.all_gather(output_weight, ("ctx", "expert"), axis=0, tiled=True),
        lax.all_gather(norm_gains, ("ctx", "expert"), axis=1, tiled=True),
        lax.all_gather(head_gains, ("ctx", "expert"), axis=1, tiled=True),
    )

    def head_prep(raw_heads, gain_vec):
        return rotate(rms_scale(raw_heads, gain_vec), positions)

    normed = rms_scale(rows_in, gains[0].astype(jnp.float32)).astype(jnp.bfloat16)
    query_raw = jnp.dot(normed, full_q, preferred_element_type=jnp.float32).reshape(
        seq_rows, HQ, HD
    )
    key_raw = jnp.dot(normed, full_k, preferred_element_type=jnp.float32).reshape(seq_rows, HK, HD)
    value_rows = jnp.dot(normed, full_v, preferred_element_type=jnp.float32).astype(jnp.bfloat16)
    query_gain = head_gain[0].astype(jnp.float32)
    key_gain = head_gain[1].astype(jnp.float32)
    queries = head_prep(query_raw, query_gain).astype(jnp.bfloat16)
    keys_rot = head_prep(key_raw, key_gain).astype(jnp.bfloat16)
    kv_rows = jnp.concatenate([keys_rot.reshape(seq_rows, kv_width), value_rows], axis=1)
    grouped = queries.reshape(seq_rows, HK, groups, HD)

    def scores_for(key_block, base_row):
        scores = (
            jnp.einsum("qhgd,khd->hgqk", grouped, key_block, preferred_element_type=jnp.float32)
            * scale
        )
        key_pos = base_row + jnp.arange(key_block.shape[0], dtype=jnp.int32)
        allowed = key_pos[None, :] <= positions[:, None]
        return (scores, allowed)

    start_state = (
        jnp.full((HK, groups, seq_rows), masked_value, jnp.float32),
        jnp.zeros((HK, groups, seq_rows), jnp.float32),
        jnp.zeros((HK, groups, seq_rows, HD), jnp.float32),
    )
    shard_rows = lax.all_gather(kv_rows, "ctx", axis=0, tiled=True)
    blocks = shard_rows.reshape(shard_rows.shape[0] // seq_rows, seq_rows, 2 * kv_width)

    def step(state_now, element):
        block_index, block_rows = element
        base_row = block_index * seq_rows

        def step_visit(state_in):
            largest, total_sum, accum = state_in
            key_block = block_rows[:, :kv_width].reshape(seq_rows, HK, HD)
            value_block = block_rows[:, kv_width:].reshape(seq_rows, HK, HD)
            scores, allowed = scores_for(key_block, base_row)
            scores = jnp.where(allowed, scores, masked_value)
            new_largest = jnp.maximum(largest, jnp.max(scores, axis=-1))
            weights = jnp.where(allowed, jnp.exp(scores - new_largest[..., None]), 0.0)
            factor = jnp.exp(largest - new_largest)
            total_sum = total_sum * factor + jnp.sum(weights, axis=-1)
            accum = accum * factor[..., None] + jnp.einsum(
                "hgqk,khd->hgqd",
                weights.astype(jnp.bfloat16),
                value_block,
                preferred_element_type=jnp.float32,
            )
            return (new_largest, total_sum, accum)

        def step_skip(state_in):
            return state_in

        return (lax.cond(base_row <= last_pos, step_visit, step_skip, state_now), None)

    final_state, unused = lax.scan(
        step, start_state, (jnp.arange(blocks.shape[0], dtype=jnp.int32), blocks)
    )
    largest, total_sum, accum = final_state
    attended = (accum / total_sum[..., None]).transpose(2, 0, 1, 3).reshape(seq_rows, HQ * HD)
    log_total = largest + jnp.log(total_sum)
    attended_low = attended.astype(jnp.bfloat16)
    hidden = rows_in + jnp.dot(attended_low, full_o, preferred_element_type=jnp.float32)
    normed_mlp = rms_scale(hidden, gains[1].astype(jnp.float32)).astype(jnp.bfloat16)
    devices = lax.axis_size(("ctx", "expert"))
    local_experts = expert_gate.shape[0]
    experts = local_experts * devices
    topk = routes.shape[2]
    capacity = max(2, 5 * seq_rows * topk // (4 * experts))
    route_ids = routes.reshape(seq_rows * topk)
    onehot = (route_ids[:, None] == jnp.arange(experts, dtype=jnp.int32)[None, :]).astype(jnp.int32)
    slots = jnp.sum((jnp.cumsum(onehot, axis=0) - 1) * onehot, axis=1)
    target = route_ids * capacity + slots
    owner_row = jnp.arange(seq_rows * topk, dtype=jnp.int32) // topk
    gate_rows = route_gates.reshape(seq_rows, topk)

    def to_slots(row_block):
        buffer = (
            jnp.zeros((experts * capacity, row_block.shape[1]), row_block.dtype)
            .at[target]
            .set(row_block)
        )
        return buffer.reshape(devices, local_experts * capacity, row_block.shape[1])

    def to_experts(arrived):
        return (
            arrived.reshape(devices, local_experts, capacity, -1)
            .transpose(1, 0, 2, 3)
            .reshape(local_experts, devices * capacity, -1)
        )

    def from_experts(expert_rows):
        return (
            expert_rows.reshape(local_experts, devices, capacity, -1)
            .transpose(1, 0, 2, 3)
            .reshape(devices, local_experts * capacity, -1)
        )

    arrived = to_experts(
        lax.all_to_all(
            to_slots(normed_mlp[owner_row]),
            ("ctx", "expert"),
            split_axis=0,
            concat_axis=0,
            tiled=True,
        )
    )
    gate_pre = jnp.einsum("erd,edf->erf", arrived, expert_gate, preferred_element_type=jnp.float32)
    up_pre = jnp.einsum("erd,edf->erf", arrived, expert_up, preferred_element_type=jnp.float32)
    sigmoid_gate = jax.nn.sigmoid(gate_pre)
    swish_gate = gate_pre * sigmoid_gate
    activated = (swish_gate * up_pre).astype(jnp.bfloat16)
    produced = jnp.einsum(
        "erf,efd->erd", activated, expert_down, preferred_element_type=jnp.float32
    ).astype(jnp.bfloat16)
    returned = lax.all_to_all(
        from_experts(produced), ("ctx", "expert"), split_axis=0, concat_axis=0, tiled=True
    ).reshape(experts * capacity, width)
    expert_out = returned[target].astype(jnp.float32).reshape(seq_rows, topk, width)
    mixed = hidden + jnp.sum(gate_rows[:, :, None] * expert_out, axis=1)
    full_q, full_k, full_v, full_o, gains, head_gain = (
        lax.all_gather(query_weight, ("ctx", "expert"), axis=0, tiled=True),
        lax.all_gather(key_weight, ("ctx", "expert"), axis=0, tiled=True),
        lax.all_gather(value_weight, ("ctx", "expert"), axis=0, tiled=True),
        lax.all_gather(output_weight, ("ctx", "expert"), axis=0, tiled=True),
        lax.all_gather(norm_gains, ("ctx", "expert"), axis=1, tiled=True),
        lax.all_gather(head_gains, ("ctx", "expert"), axis=1, tiled=True),
    )
    grad_out = cotangent.reshape(seq_rows, width).astype(jnp.float32)
    grad_rows = (
        (gate_rows[:, :, None] * grad_out[:, None, :])
        .astype(jnp.bfloat16)
        .reshape(seq_rows * topk, width)
    )
    grad_arrived = to_experts(
        lax.all_to_all(
            to_slots(grad_rows), ("ctx", "expert"), split_axis=0, concat_axis=0, tiled=True
        )
    )
    grad_down = jnp.einsum(
        "erf,erd->efd", activated, grad_arrived, preferred_element_type=jnp.float32
    )
    grad_act = jnp.einsum(
        "erd,efd->erf", grad_arrived, expert_down, preferred_element_type=jnp.float32
    )
    grad_up_pre = (grad_act * swish_gate).astype(jnp.bfloat16)
    grad_gate_pre = (
        grad_act * up_pre * sigmoid_gate * (1.0 + gate_pre * (1.0 - sigmoid_gate))
    ).astype(jnp.bfloat16)
    grad_gate = jnp.einsum(
        "erd,erf->edf", arrived, grad_gate_pre, preferred_element_type=jnp.float32
    )
    grad_up = jnp.einsum("erd,erf->edf", arrived, grad_up_pre, preferred_element_type=jnp.float32)
    grad_inputs = jnp.einsum(
        "erf,edf->erd", grad_gate_pre, expert_gate, preferred_element_type=jnp.float32
    )
    grad_inputs = (
        grad_inputs
        + jnp.einsum("erf,edf->erd", grad_up_pre, expert_up, preferred_element_type=jnp.float32)
    ).astype(jnp.bfloat16)
    grad_back = lax.all_to_all(
        from_experts(grad_inputs), ("ctx", "expert"), split_axis=0, concat_axis=0, tiled=True
    ).reshape(experts * capacity, width)
    grad_normed_mlp = jnp.sum(
        grad_back[target].astype(jnp.float32).reshape(seq_rows, topk, width), axis=1
    )
    unused_norm, norm_pull = jax.vjp(rms_scale, hidden, gains[1].astype(jnp.float32))
    grad_hidden_norm, grad_gain_mlp = norm_pull(grad_normed_mlp)
    grad_hidden = grad_out + grad_hidden_norm
    grad_branch = grad_hidden.astype(jnp.bfloat16)
    grad_wo = jnp.einsum("qa,qd->ad", attended_low, grad_branch, preferred_element_type=jnp.float32)
    grad_attended = jnp.einsum(
        "qd,ad->qa", grad_branch, full_o, preferred_element_type=jnp.float32
    ).astype(jnp.bfloat16)
    all_kv = lax.all_gather(kv_rows, "ctx", axis=0, tiled=True)
    grad_grouped = grad_attended.reshape(seq_rows, HK, groups, HD)
    delta = jnp.einsum(
        "qhgd,qhgd->hgq",
        grad_grouped.astype(jnp.float32),
        attended.reshape(seq_rows, HK, groups, HD),
    )
    kv_blocks = all_kv.reshape(-1, seq_rows, 2 * kv_width)

    def back_step(grad_query, element):
        block_index, block_rows = element
        base_row = block_index * seq_rows

        def back_visit(grad_in):
            key_block = block_rows[:, :kv_width].reshape(seq_rows, HK, HD)
            value_block = block_rows[:, kv_width:].reshape(seq_rows, HK, HD)
            scores, allowed = scores_for(key_block, base_row)
            probs = jnp.where(allowed, jnp.exp(scores - log_total[..., None]), 0.0)
            grad_probs = jnp.einsum(
                "qhgd,khd->hgqk", grad_grouped, value_block, preferred_element_type=jnp.float32
            )
            grad_scores = (probs * (grad_probs - delta[..., None])).astype(jnp.bfloat16)
            grad_next = grad_in + jnp.einsum(
                "hgqk,khd->qhgd", grad_scores, key_block, preferred_element_type=jnp.float32
            )
            grad_keys = (
                jnp.einsum(
                    "hgqk,qhgd->khd", grad_scores, grouped, preferred_element_type=jnp.float32
                )
                * scale
            )
            grad_values = jnp.einsum(
                "hgqk,qhgd->khd",
                probs.astype(jnp.bfloat16),
                grad_grouped,
                preferred_element_type=jnp.float32,
            )
            joined = jnp.concatenate(
                [grad_keys.reshape(seq_rows, kv_width), grad_values.reshape(seq_rows, kv_width)],
                axis=1,
            )
            return (grad_next, joined)

        def back_skip(grad_in):
            return (grad_in, jnp.zeros((seq_rows, 2 * kv_width), jnp.float32))

        return lax.cond(base_row <= last_pos, back_visit, back_skip, grad_query)

    grad_query, grad_kv_terms = lax.scan(
        back_step,
        jnp.zeros((seq_rows, HK, groups, HD), jnp.float32),
        (jnp.arange(kv_blocks.shape[0], dtype=jnp.int32), kv_blocks),
    )
    grad_query = grad_query * scale
    grad_kv = lax.psum_scatter(
        grad_kv_terms.reshape(-1, 2 * kv_width).astype(jnp.bfloat16),
        "ctx",
        scatter_dimension=0,
        tiled=True,
    ).astype(jnp.float32)
    unused_query, pull_query = jax.vjp(head_prep, query_raw, query_gain)
    grad_query_raw, grad_query_gain = pull_query(grad_query.reshape(seq_rows, HQ, HD))
    unused_key, pull_key = jax.vjp(head_prep, key_raw, key_gain)
    grad_key_raw, grad_key_gain = pull_key(grad_kv[:, :kv_width].reshape(seq_rows, HK, HD))
    grad_q_low = grad_query_raw.reshape(seq_rows, HQ * HD).astype(jnp.bfloat16)
    grad_k_low = grad_key_raw.reshape(seq_rows, kv_width).astype(jnp.bfloat16)
    grad_v_low = grad_kv[:, kv_width:].astype(jnp.bfloat16)
    grad_wq = jnp.einsum("qd,qa->da", normed, grad_q_low, preferred_element_type=jnp.float32)
    grad_wk = jnp.einsum("qd,qa->da", normed, grad_k_low, preferred_element_type=jnp.float32)
    grad_wv = jnp.einsum("qd,qa->da", normed, grad_v_low, preferred_element_type=jnp.float32)
    grad_normed = jnp.einsum("qa,da->qd", grad_q_low, full_q, preferred_element_type=jnp.float32)
    grad_normed = grad_normed + jnp.einsum(
        "qa,da->qd", grad_k_low, full_k, preferred_element_type=jnp.float32
    )
    grad_normed = grad_normed + jnp.einsum(
        "qa,da->qd", grad_v_low, full_v, preferred_element_type=jnp.float32
    )
    unused_attn, pull_attn = jax.vjp(rms_scale, rows_in, gains[0].astype(jnp.float32))
    grad_rows_norm, grad_gain_attn = pull_attn(grad_normed)
    grad_input = grad_hidden + grad_rows_norm
    gain_grads = jnp.stack([grad_gain_attn, grad_gain_mlp])
    head_grads = jnp.stack([grad_query_gain, grad_key_gain])
    sum_q, sum_k, sum_v, sum_o, sum_gain, sum_head = (
        lax.psum_scatter(grad_wq, ("ctx", "expert"), scatter_dimension=0, tiled=True),
        lax.psum_scatter(grad_wk, ("ctx", "expert"), scatter_dimension=0, tiled=True),
        lax.psum_scatter(grad_wv, ("ctx", "expert"), scatter_dimension=0, tiled=True),
        lax.psum_scatter(grad_wo, ("ctx", "expert"), scatter_dimension=0, tiled=True),
        lax.psum_scatter(gain_grads, ("ctx", "expert"), scatter_dimension=1, tiled=True),
        lax.psum_scatter(head_grads, ("ctx", "expert"), scatter_dimension=1, tiled=True),
    )
    return (
        mixed.astype(jnp.bfloat16).reshape(tokens.shape),
        grad_input.astype(jnp.bfloat16).reshape(tokens.shape),
        sum_q,
        sum_k,
        sum_v,
        sum_o,
        sum_gain,
        sum_head,
        grad_gate,
        grad_up,
        grad_down,
    )


MESH = pl.DeviceIdType.MESH
VMEM_BYTES = 58 * 2**20
LAST_DEEP = 0
DEEP = 32
ANY = pl.BlockSpec(memory_space=pl.ANY)
IN_VMEM = pl.BlockSpec(memory_space=pltpu.VMEM)
f32, bf16 = jnp.float32, jnp.bfloat16
NT = (((1,), (1,)), ((), ()))
TN = (((0,), (0,)), ((), ()))


class Place:
    def __init__(self):
        self.c = lax.axis_index("ctx")
        self.e = lax.axis_index("expert")
        self.k = lax.rem(self.e, 2)
        self.z = lax.div(self.e, 2)
        self.cx = self.c + 1 - 2 * lax.rem(self.c, 2)
        self.cy = lax.rem(self.c + 2, 4)
        self.cd = lax.rem(self.cx + 2, 4)
        self.dx = (self.cx, self.e)
        self.dy = (self.cy, self.e)
        self.dd = (self.cd, self.e)
        self.pair = (self.c, self.e + 1 - 2 * self.k)
        self.up = (self.c, self.e + 2)
        self.down = (self.c, self.e - 2)


def greet(p, nz, line=True, pair=True, diagonal=False):
    barrier = pltpu.get_barrier_semaphore()

    def tell(device):
        pl.semaphore_signal(barrier, inc=1, device_id=device, device_id_type=MESH)

    friends = [p.dx, p.dy] + [p.pair] * pair + [p.dd] * diagonal
    for device in friends:
        tell(device)
    count = len(friends)
    if line:
        for there, device in ((p.z > 0, p.down), (p.z < nz - 1, p.up)):

            @pl.when(there)
            def _():
                tell(device)

            count = count + there.astype(jnp.int32)
    pl.semaphore_wait(barrier, count)


def remote(src, dst, send, recv, device):
    return pltpu.make_async_remote_copy(
        src_ref=src,
        dst_ref=dst,
        send_sem=send,
        recv_sem=recv,
        device_id=device,
        device_id_type=MESH,
    )


def far_first(nz, z):
    return sorted(range(nz), key=lambda to: (-abs(to - z), to))


def near_first(nz, z):
    return sorted(range(nz), key=lambda to: (abs(to - z), to))


def pick_order(p, nz, order=far_first):
    tables = [order(nz, z) for z in range(nz)]
    return [sum(jnp.where(p.z == z, tables[z][i], 0) for z in range(nz)) for i in range(nz)]


class Spread:
    def __init__(self, p, nz, mine, block, half, send, recv, line=True, side=True, pair=True):
        self.p, self.nz, self.mine, self.block, self.half = p, nz, mine, block, half
        self.send, self.recv = send, recv
        self.line, self.side, self.pair = line, side, pair
        self.order = pick_order(p, nz, near_first) if line else [p.z]

    def ref(self, c, z, k, h=None):
        whole = self.block(c, z, k)
        return whole if h is None else whole.at[pl.ds(h * self.half, self.half)]

    def copy(self, kind, z, own=False):
        p = self.p
        at = functools.partial(self.ref, z=z, k=p.k)
        src, i, j, device = {
            "x": lambda: (at(p.c), 0, 1, p.dx),
            "y": lambda: (at(p.c), 1, 2, p.dy),
            "up": lambda: (at(p.c), 2, 0, p.up),
            "down": lambda: (at(p.c), 3, 0, p.down),
            "via_y": lambda: (at(p.cx, h=0), 4, 3, p.dy),
            "via_x": lambda: (at(p.cy, h=1), 5, 4, p.dx),
            "pair0": lambda: (at(p.c), 6, 5, p.pair),
            "pair1": lambda: (at(p.cx), 7, 6, p.pair),
            "pair2": lambda: (at(p.cy), 8, 7, p.pair),
            "pair3": lambda: (at(p.cd, h=0), 9, 8, p.pair),
            "pair4": lambda: (at(p.cd, h=1), 10, 9, p.pair),
        }[kind]()
        return remote(
            self.mine if own else src, src, self.send.at[z, i], self.recv.at[z, j], device
        )

    def got(self, j, z):
        p = self.p
        k = p.k if j < 5 else 1 - p.k
        c, h = ((p.c, None), (p.cx, None), (p.cy, None), (p.cd, 0), (p.cd, 1))[j % 5]
        ref = self.ref(c, z, k, h)
        remote(ref, ref, self.send.at[z, 0], self.recv.at[z, j], p.pair).wait_recv()

    def each(self, far, act):
        if far == 0:
            act(self.p.z, 0)
            return
        for way in (-1, 1):
            z = self.p.z + way * far

            @pl.when((z >= 0) & (z < self.nz))
            def _():
                act(z, way)

    def onward(self, z, way, act):
        if self.line and way >= 0:

            @pl.when(self.p.z > 0)
            def _():
                act(self.copy("down", z, way == 0))

        if self.line and way <= 0:

            @pl.when(self.p.z < self.nz - 1)
            def _():
                act(self.copy("up", z, way == 0))

    def direct(self):
        return ["x", "y"] * self.side + ["pair0"] * self.pair

    def along(self, far):
        def act(z, way):
            if way:
                self.got(0, z)
            self.onward(z, way, lambda copy: copy.start())
            for kind in self.direct():
                self.copy(kind, z, way == 0).start()

        self.each(far, act)

    def beside(self, z):
        for j, kinds in ((1, ["via_y", "pair1"]), (2, ["via_x", "pair2"])):
            self.got(j, z)
            for kind in kinds[: 1 + self.pair]:
                self.copy(kind, z).start()

    def across(self, z):
        for j, kind in ((3, "pair3"), (4, "pair4")):
            self.got(j, z)
            if self.pair:
                self.copy(kind, z).start()

    def from_pair(self, z):
        if self.pair:
            for j in range(5, 10 if self.side else 6):
                self.got(j, z)

    def step(self, i):
        reach = self.nz if self.line else 1
        if i < reach:
            self.along(i)
        if self.side and 1 <= i <= reach:
            self.beside(self.order[i - 1])
        if self.side and 2 <= i <= reach + 1:
            self.across(self.order[i - 2])

    def finish(self, pair=True):
        def act(z, way):
            if pair:
                self.from_pair(z)
            self.onward(z, way, lambda copy: copy.wait_send())
            for kind in self.direct():
                self.copy(kind, z, way == 0).wait_send()
            if self.side:
                for kind in ["via_y", "via_x"] + ["pair1", "pair2", "pair3", "pair4"] * self.pair:
                    self.copy(kind, z).wait_send()

        for far in range(self.nz if self.line else 1):
            self.each(far, act)


class SpreadDeep:
    def __init__(self, p, nz, mine, block, send, recv, send_in, recv_in):
        self.p, self.nz, self.mine, self.block = p, nz, mine, block
        self.send, self.recv, self.send_in, self.recv_in = send, recv, send_in, recv_in
        self.places = (p.c, p.cx, p.cy, p.cd)
        self.half = mine.shape[0] // 2

    def ref(self, r, z, h=None, k=None):
        whole = self.block(self.places[r], z, self.p.k if k is None else k)
        return whole if h is None else whole.at[pl.ds(h * self.half, self.half)]

    def near(self, i):
        p, own = self.p, self.ref(0, self.p.z)
        src, dst, device = (
            lambda: (self.mine, own, p.dx),
            lambda: (self.mine, own, p.dy),
            lambda: (self.ref(1, p.z, 0), self.ref(1, p.z, 0), p.dy),
            lambda: (self.ref(2, p.z, 1), self.ref(2, p.z, 1), p.dx),
        )[i]()
        return remote(src, dst, self.send_in.at[i], self.recv_in.at[i], device)

    def hop(self, r, z, i, own=False):
        dst = self.ref(r, z)
        device = (self.p.up, self.p.down, self.p.pair)[i]
        src = self.mine if own else dst
        return remote(src, dst, self.send.at[z, r, i], self.recv.at[z, r, i // 2], device)

    def forward(self, r, z, way, act):
        p, own = self.p, r == 0 and way == 0
        if way <= 0:

            @pl.when(p.z < self.nz - 1)
            def _():
                act(self.hop(r, z, 0, own))

        if way >= 0:

            @pl.when(p.z > 0)
            def _():
                act(self.hop(r, z, 1, own))

        act(self.hop(r, z, 2, own))

    def each(self, far, act):
        for way in (-1, 1):
            z = self.p.z + way * far

            @pl.when((z >= 0) & (z < self.nz))
            def _():
                act(z, way)

    def step(self, i):
        start = lambda copy: copy.start()
        z = self.p.z
        if i == 0:
            self.near(0).start()
            self.near(1).start()
            self.forward(0, z, 0, start)
        elif i == 1:
            for n in (0, 1):
                ref = self.ref(1 + n, z)
                remote(ref, ref, self.send_in.at[n], self.recv_in.at[n], self.p.pair).wait_recv()
                self.near(2 + n).start()
                self.forward(1 + n, z, 0, start)
        elif i == 2:
            for n in (0, 1):
                ref = self.ref(3, z, n)
                remote(
                    ref, ref, self.send_in.at[n], self.recv_in.at[2 + n], self.p.pair
                ).wait_recv()
            self.forward(3, z, 0, start)
        elif i < self.nz + 2:

            def act(z, way):
                for r in range(4):
                    self.got(r, z, 0)
                    self.forward(r, z, way, start)

            self.each(i - 2, act)

    def got(self, r, z, i):
        ref = self.ref(r, z, None, self.p.k if i == 0 else 1 - self.p.k)
        remote(ref, ref, self.send.at[z, r, 0], self.recv.at[z, r, i], self.p.pair).wait_recv()

    def finish(self, pair=True):
        def act(z, way):
            for r in range(4):
                if pair:
                    self.got(r, z, 1)
                self.forward(r, z, way, lambda copy: copy.wait_send())

        for i in range(4):
            self.near(i).wait_send()
        act(self.p.z, 0)
        for far in range(1, self.nz):
            self.each(far, act)


def deep_sems(nz):
    dma = pltpu.SemaphoreType.DMA
    return [dma((nz, 4, 3)), dma((nz, 4, 2)), dma((4,)), dma((4,))]


def lines_of(ref, nz, first, count):
    return lambda c, z, k: ref.at[c * (2 * nz) + z * 2 + k, pl.ds(first, count)]


def by_device(ref, nz):
    return lambda c, z, k: ref.at[c * (2 * nz) + z * 2 + k]


def spread_sems(nz):
    return [pltpu.SemaphoreType.DMA((nz, 11)), pltpu.SemaphoreType.DMA((nz, 10))]


class Fold:
    def __init__(self, p, parts, sx, sy, h0, h1, bx, by, send, recv, far=None):
        far = parts if far is None else far
        half = bx.shape[0] // 2
        self.halves = low, high = pl.ds(0, half), pl.ds(half, half)
        self.p, self.parts, self.sx, self.sy = p, parts, sx, sy
        self.h0, self.h1, self.bx, self.by = h0, h1, bx, by
        copy = lambda i, src, dst, device: remote(src, dst, send.at[i], recv.at[i], device)
        self.to_x = copy(0, far.at[p.cd, low], h0, p.dx)
        self.to_y = copy(1, far.at[p.cd, high], h1, p.dy)
        self.x_low = copy(2, far.at[p.cx, low], bx.at[low], p.dx)
        self.y_high = copy(3, far.at[p.cy, high], by.at[high], p.dy)
        self.x_high = copy(4, sx, bx.at[high], p.dx)
        self.y_low = copy(5, sy, by.at[low], p.dy)

    def begin(self):
        for copy in (self.to_x, self.to_y, self.x_low, self.y_high):
            copy.start()

    def middle(self):
        p, (low, high), parts = self.p, self.halves, self.parts
        self.to_y.wait_recv()
        total = parts[p.cx, high].astype(f32) + self.h1[...].astype(f32)
        self.sx[...] = total.astype(self.sx.dtype)
        self.x_high.start()
        self.to_x.wait_recv()
        total = parts[p.cy, low].astype(f32) + self.h0[...].astype(f32)
        self.sy[...] = total.astype(self.sy.dtype)
        self.y_low.start()

    def end(self, store):
        p, parts = self.p, self.parts
        low, high = self.halves
        for rows, waits in ((low, (self.x_low, self.y_low)), (high, (self.y_high, self.x_high))):
            for copy in waits:
                copy.wait_recv()
            total = parts[p.c, rows].astype(f32) + self.bx[rows].astype(f32)
            store(rows, total + self.by[rows].astype(f32))
        for copy in (self.to_x, self.to_y, self.x_low, self.y_high, self.x_high, self.y_low):
            copy.wait_send()


def fold_scratch(seq, width):
    buf = lambda r: pltpu.VMEM((r, width), bf16)
    return (
        [buf(seq // 2)] * 4 + [buf(seq)] * 2 + [pltpu.SemaphoreType.DMA((6,))] * 2
    )


def front_kernel(nz, scale, *refs):
    pack, wo, tok, cot, meta, cosine, sine = refs[:7]
    packs, wos, toks, cots, metas = refs[7:12]
    results, held = refs[12:25], refs[25:38]
    xn, raw, q, k, v, ot, lse, hidden, hn, gain_out, head_out, slots, gates = held
    tok_v, w_v, wo_v, meta_v, vt, ob, part = refs[38:45]
    fold_refs, pair_sems = refs[45:53], refs[53:63]
    a_send, a_recv, local, load, out_sem = refs[63:68]

    def copy_out(*which):
        for i in which:
            pltpu.make_async_copy(held[i], results[i], out_sem.at[i]).start()

    p = Place()
    seq, width = tok.shape
    length = 4 * seq
    heads = q.shape[0]
    me = p.c * (2 * nz) + p.e
    greet(p, nz, diagonal=True)
    into = [
        pltpu.make_async_copy(src, dst, local.at[i])
        for i, (src, dst) in enumerate(
            (
                (pack.at[p.c], w_v.at[p.c, p.e]),
                (wo, wo_v.at[p.e]),
                (tok, tok_v.at[p.c]),
                (cot, part.at[0]),
            )
        )
    ]
    own = [
        pltpu.make_async_copy(src, dst, local.at[4 + i])
        for i, (src, dst) in enumerate(
            (
                (w_v.at[p.c, p.e], packs.at[p.c, p.e]),
                (wo_v.at[p.e], wos.at[p.e]),
                (meta, metas.at[me]),
                (part.at[0], cots.at[me]),
            )
        )
    ]
    loads = [
        pltpu.make_async_copy(src, dst, load.at[i])
        for i, (src, dst) in enumerate(
            [(packs, w_v), (wos, wo_v), (metas, meta_v)]
            + [(toks.at[c], tok_v.at[c]) for c in (p.cx, p.cy, p.cd)]
        )
    ]
    for copy in into:
        copy.start()
    own[2].start()
    swaps = [
        remote(pack.at[c], packs.at[p.c, p.e], a_send.at[i], a_recv.at[i], device)
        for i, (c, device) in enumerate(((p.cx, p.dx), (p.cy, p.dy), (p.cd, p.dd)))
    ]
    for copy in swaps:
        copy.start()

    def job(i, src, block, half, *ways):
        return Spread(p, nz, src, block, half, *pair_sems[2 * i : 2 * i + 2], *ways)

    j_tok = job(0, tok, lambda c, z, k: toks.at[c], seq // 2, False, True, False)
    j_meta = job(1, meta, by_device(metas, nz), meta.shape[0] // 2)
    most = seq - DEEP
    j_cot = job(2, cot.at[pl.ds(0, most)], lines_of(cots, nz, 0, most), most // 2)
    j_deep = SpreadDeep(
        p, nz, cot.at[pl.ds(most, DEEP)], lines_of(cots, nz, most, DEEP), *refs[68:]
    )
    j_wo = job(3, wo, lambda c, z, k: wos.at[z * 2 + k], 0, True, False, True)
    own_pack = packs.at[:, p.e]
    j_pack = job(4, own_pack, lambda c, z, k: packs.at[:, z * 2 + k], 0, True, False, True)
    j_meta.step(0)
    j_tok.step(0)
    for i in (0, 1, 3):
        into[i].wait()
        own[i].start()
    for i, c in enumerate((p.cx, p.cy, p.cd)):
        ref = packs.at[c, p.e]
        remote(ref, ref, a_send.at[i], a_recv.at[i], p.dx).wait_recv()
    own[0].wait()
    j_pack.step(0)
    j_meta.step(1)
    j_pack.step(1)
    j_tok.step(1)
    loads[3].start()
    loads[4].start()
    j_tok.step(2)
    loads[5].start()
    j_meta.step(2)
    j_pack.step(2)
    j_cot.step(0)
    j_deep.step(0)
    for i in range(3, nz + 2):
        j_meta.step(i)
        j_pack.step(i)
    own[2].wait()
    for z in j_meta.order:
        j_meta.from_pair(z)
    loads[2].start()
    j_wo.step(0)
    for z in j_pack.order:
        j_pack.from_pair(z)
    loads[0].start()

    loads[2].wait()
    n = meta_lines(q.shape[1], width, seq)
    per = 128 * 8 * nz // width

    def gain(line):
        found = [
            sum(meta_v[per * j + i, pl.ds(line, 1)] for i in range(per))
            for j in range(width // 128)
        ]
        return jnp.concatenate(found, axis=1)

    def head_gain(line):
        return sum(meta_v[b, pl.ds(line, 1)] for b in range(8 * nz))

    gain_out[0:1] = gain(n)
    gain_out[1:2] = gain(n + 1)
    head_out[0:1] = head_gain(n + 2)
    head_out[1:2] = head_gain(n + 3)

    def rms(x, g):
        return x * lax.rsqrt(jnp.mean(x * x, axis=-1, keepdims=True) + epsilon) * g

    into[2].wait()
    for copy in loads[3:]:
        copy.wait()

    @pl.loop(0, 8)
    def _(i):
        c, h = lax.div(i, 2), lax.rem(i, 2)
        half = seq // 2
        rows = tok_v[c, pl.ds(pl.multiple_of(h * half, half), half)].astype(f32)
        here = pl.ds(pl.multiple_of(i * half, half), half)
        xn[here] = rms(rows, gain_out[0:1]).astype(bf16)

    j_cot.step(1)
    loads[0].wait()

    @pl.loop(0, raw.shape[1] // 256)
    def _(t):
        cols = pl.ds(pl.multiple_of(t * 256, 256), 256)
        w = w_v[:, :, :, cols].reshape(width, 256)
        raw[:, cols] = jnp.dot(xn[...], w, preferred_element_type=f32)

    copy_out(0, 1, 9, 10)
    j_wo.step(1)
    j_cot.step(2)
    j_deep.step(1)

    def prep(x, g):
        y = rms(x, g)
        return (y * cosine[...] + pltpu.roll(y, HD // 2, 1) * sine[...]).astype(bf16)

    k[...] = prep(raw[:, pl.ds(heads * HD, HD)], head_out[1:2])
    values = raw[:, pl.ds((heads + 1) * HD, HD)]
    v[...] = values.astype(bf16)
    vt[...] = values.T.astype(bf16)
    copy_out(3, 4)

    def attend(h):
        cols = pl.ds(pl.multiple_of(h * HD, HD), HD)
        q[h] = prep(raw[:, cols], head_out[0:1])
        for i in range(length // seq):
            keys = (i + 1) * seq
            here = pl.ds(i * seq, seq)
            s = lax.dot_general(k[pl.ds(0, keys)], q[h, here], NT, preferred_element_type=f32)
            s = s * scale
            key_pos = lax.broadcasted_iota(jnp.int32, s.shape, 0)
            query_pos = lax.broadcasted_iota(jnp.int32, s.shape, 1) + i * seq
            s = jnp.where(key_pos <= query_pos, s, masked_value)
            largest = jnp.max(s, axis=0, keepdims=True)
            weights = jnp.exp(s - largest)
            total = jnp.sum(weights, axis=0, keepdims=True)
            o = jnp.dot(vt[:, pl.ds(0, keys)], weights.astype(bf16), preferred_element_type=f32)
            o = o / total
            ot[h, :, here] = o.astype(bf16)
            ob[here, cols] = o.T.astype(bf16)
            lse[h, :, here] = largest + jnp.log(total)

    pl.loop(0, heads // 2)(attend)
    j_cot.step(3)
    j_wo.step(2)
    j_deep.step(2)
    pl.loop(heads // 2, heads)(attend)
    copy_out(2, 5, 6)
    j_wo.step(3)
    j_cot.step(4)
    j_deep.step(3)
    own[1].wait()
    for z in j_wo.order:
        j_wo.from_pair(z)
    loads[1].start()
    own[3].wait()

    upto = lax.broadcasted_iota(jnp.int32, (seq, seq), 0) <= lax.broadcasted_iota(
        jnp.int32, (seq, seq), 1
    )
    upto = upto.astype(f32).astype(bf16)
    lines = seq // 128
    topk = n // lines // 2
    for j, expert in enumerate((me, me + 1 - 2 * p.k)):
        expert = expert.astype(f32)
        member, weight = [], []
        for line in range(lines):
            named = [meta_v[:, i * lines + line] == expert for i in range(topk)]
            gate = [meta_v[:, (topk + i) * lines + line] for i in range(topk)]
            member.append(sum(x.astype(f32) for x in named))
            weight.append(sum(jnp.where(x, y, 0.0) for x, y in zip(named, gate)))
        member = jnp.concatenate(member, axis=1)
        rank = jnp.dot(member.astype(bf16), upto, preferred_element_type=f32)
        slots[j] = jnp.where(member > 0.5, rank.astype(jnp.int32) - 1, -1)
        gates[j] = jnp.concatenate(weight, axis=1)

    copy_out(11, 12)
    loads[1].wait()
    tile = 512

    @pl.loop(0, width // tile)
    def _(t):
        cols = pl.ds(pl.multiple_of(t * tile, tile), tile)
        w = wo_v[:, :, cols].reshape(heads * HD, tile)
        out = jnp.dot(ob[...], w, preferred_element_type=f32)
        part[:, :, cols] = out.astype(bf16).reshape(4, seq, tile)

    fold = Fold(p, part, *fold_refs)
    fold.begin()
    j_cot.step(5)
    j_deep.step(4)
    fold.middle()

    def store(rows, total):
        h = tok_v[p.c, rows].astype(f32) + total
        hidden[rows] = h
        hn[rows] = rms(h, gain_out[1:2]).astype(bf16)

    fold.end(store)
    copy_out(7, 8)
    j_deep.step(5)
    for copy in swaps:
        copy.wait_send()
    for spread in (j_tok, j_meta, j_cot, j_wo, j_pack):
        spread.finish(pair=spread is j_cot)
    j_deep.finish()
    for i in range(len(held)):
        pltpu.make_async_copy(held[i], results[i], out_sem.at[i]).wait()


def meta_lines(length, width, seq):
    return 2 * 8 * seq // 128


def front(nz, scale, pack, wo, tok, cot, meta, cosine, sine):
    blocks = 8 * nz
    seq, width = tok.shape
    length = 4 * seq
    wide = pack.shape[2]
    heads = wide // HD - 2
    hbm = lambda n, a: jax.ShapeDtypeStruct(n + a.shape, a.dtype)
    out = lambda *n: jax.ShapeDtypeStruct(n[:-1], n[-1])
    vmem = lambda *n: pltpu.VMEM(n, bf16)
    dma = pltpu.SemaphoreType.DMA
    held = [
        out(length, width, bf16),
        out(length, wide, f32),
        out(heads, length, HD, bf16),
        out(length, HD, bf16),
        out(length, HD, bf16),
        out(heads, HD, length, bf16),
        out(heads, 1, length, f32),
        out(seq, width, f32),
        out(seq, width, bf16),
        out(2, width, f32),
        out(2, HD, f32),
        out(2, blocks, seq, jnp.int32),
        out(2, blocks, seq, f32),
    ]
    return pl.pallas_call(
        functools.partial(front_kernel, nz, scale),
        out_shape=[
            jax.ShapeDtypeStruct((4, 2 * nz) + pack.shape[1:], bf16),
            hbm((2 * nz,), wo),
            hbm((4,), tok),
            hbm((blocks,), cot),
            hbm((blocks,), meta),
        ]
        + held,
        in_specs=[ANY] * 5 + [IN_VMEM] * 2,
        out_specs=[ANY] * 18,
        scratch_shapes=[pltpu.VMEM(a.shape, a.dtype) for a in held]
        + [
            vmem(4, seq, width),
            vmem(4, 2 * nz, pack.shape[1], wide),
            vmem(2 * nz, wo.shape[0], width),
            pltpu.VMEM((blocks,) + meta.shape, f32),
            vmem(HD, length),
            vmem(length, heads * HD),
            vmem(4, seq, width),
        ]
        + fold_scratch(seq, width)
        + spread_sems(nz) * 5
        + [dma((n,)) for n in (3, 3, 8, 6, len(held))]
        + deep_sems(nz),
        compiler_params=pltpu.CompilerParams(
            collective_id=1, has_side_effects=True, vmem_limit_bytes=VMEM_BYTES
        ),
    )(pack, wo, tok, cot, meta, cosine, sine)


class Combine:
    def __init__(self, p, nz, cap, col, deep, rows, slots, gates, out, *scratch):
        self.p, self.nz, self.cap, self.rows, self.slots, self.gates = p, nz, cap, rows, slots, gates
        self.out = out
        self.rbuf, self.sd, self.sx, self.sy = scratch[:4]
        self.h0, self.h1, self.bx, self.by, self.bz = scratch[4:9]
        self.pair_send, self.pair_recv, self.load = scratch[9:12]
        self.s_h0, self.s_h1, self.s_x, self.s_y, self.s_z = scratch[12:17]
        self.r_h0, self.r_h1, self.r_x, self.r_y, self.r_z = scratch[17:22]
        self.order = pick_order(p, nz)
        self.most, self.width = self.sx.shape[1:]
        self.seq = self.most + deep
        self.half = self.most // 2
        self.cols = pl.ds(col, self.width)
        self.deep = deep
        self.tile = max(t for t in range(128, 1025, 128) if self.width % t == 0)
        if deep:
            self.s_d, self.b_d, self.send_d, self.recv_d = scratch[22:26]
            self.fold = Fold(p, self.s_d.at[p.z], *scratch[26:])

    def clear(self):
        bz, nz = self.bz, self.nz

        @pl.when(self.p.z == 0)
        def _():
            for ref in [bz] + ([self.b_d] if self.deep else []):
                ref[pl.ds(0, nz)] = jnp.zeros((nz,) + ref.shape[1:], ref.dtype)

        @pl.when(self.p.z == nz - 1)
        def _():
            for ref in [bz] + ([self.b_d] if self.deep else []):
                ref[pl.ds(0, nz - 1)] = jnp.zeros((nz - 1,) + ref.shape[1:], ref.dtype)
                ref[nz] = jnp.zeros(ref.shape[1:], ref.dtype)

    def pair_copy(self, c, z):
        p = self.p
        return remote(
            self.rows.at[c * (2 * self.nz) + z * 2 + 1 - p.k, :, self.cols],
            self.rbuf.at[c, z, pl.ds(self.cap, self.cap)],
            self.pair_send.at[c, z],
            self.pair_recv.at[c, z],
            p.pair,
        )

    def load_copy(self, c, z):
        return pltpu.make_async_copy(
            self.rows.at[c * (2 * self.nz) + z * 2 + self.p.k, :, self.cols],
            self.rbuf.at[c, z, pl.ds(0, self.cap)],
            self.load.at[c, z],
        )

    def begin(self):
        p = self.p
        for z in self.order:
            for c in (p.cd, p.cx, p.cy, p.c):
                self.load_copy(c, z).start()
                self.pair_copy(c, z).start()

    def places(self, c, z):
        b = pl.ds(c * (2 * self.nz) + z * 2 + self.p.k, 1)
        names = lax.broadcasted_iota(jnp.int32, (self.cap, self.seq), 0)
        both = [jnp.where(names == self.slots[n, b], self.gates[n, b], 0.0) for n in (0, 1)]
        return jnp.concatenate(both, axis=0).T.astype(bf16)

    def arrived(self, c, z):
        self.load_copy(c, z).wait()
        self.pair_copy(c, z).wait_recv()

    def copy_deep(self, z, up):
        p = self.p
        slot = z if up else jnp.where(z == p.z - 1, self.nz, z)
        return remote(
            self.s_d.at[z],
            self.b_d.at[slot],
            self.send_d.at[z],
            self.recv_d.at[slot],
            p.up if up else p.down,
        )

    def deep_send(self, z):
        @pl.when(z > self.p.z)
        def _():
            self.copy_deep(z, True).start()

        @pl.when(z < self.p.z)
        def _():
            self.copy_deep(z, False).start()

    def deep_recv(self, slot):
        ref = self.b_d.at[slot]
        remote(ref, ref, self.send_d.at[0], self.recv_d.at[slot], self.p.pair).wait_recv()

    def deep_first(self, i):
        p, nz, z = self.p, self.nz, self.order[i]
        for c in range(4):
            self.arrived(c, z)
            w = self.places(c, z)[self.most :]
            for t in range(self.width // self.tile):
                cols = pl.ds(t * self.tile, self.tile)
                total = jnp.dot(w, self.rbuf[c, z, :, cols], preferred_element_type=f32)
                self.s_d[z, c, :, cols] = total.astype(bf16)
        if i < nz - 1:

            @pl.when((p.z == 0) | (p.z == nz - 1))
            def _():
                self.deep_send(z)

    def deep_add(self, z, *slots):
        for c in range(4):
            total = self.s_d[z, c].astype(f32)
            for slot in slots:
                total = total + self.b_d[slot, c].astype(f32)
            self.s_d[z, c] = total.astype(bf16)

    def deep_next(self, i):
        p, nz, z = self.p, self.nz, self.order[i]
        if i < nz - 1:

            @pl.when((p.z > 0) & (p.z < nz - 1))
            def _():
                self.deep_recv(z)
                self.deep_add(z, z)
                self.deep_send(z)

            return

        @pl.when(p.z > 0)
        def _():
            self.deep_recv(z)

        @pl.when(p.z < nz - 1)
        def _():
            self.deep_recv(nz)

        self.deep_add(z, z, nz)
        self.fold.begin()

    def deep_end(self, i):
        if i == 0:
            self.fold.middle()
            return

        def store(lines, total):
            self.out[pl.ds(self.most + lines.start, lines.size)] = total

        self.fold.end(store)

    def fill(self, c, z, low, high, store):
        half, tile = self.half, self.tile
        w = self.places(c, z)[: self.most]
        if not self.deep:
            self.arrived(c, z)
        for t in range(self.width // tile):
            cols = pl.ds(t * tile, tile)
            total = jnp.dot(w, self.rbuf[c, z, :, cols], preferred_element_type=f32)
            for first, adds in ((0, low), (half, high)):
                part = total[first : first + half]
                for ref, start in adds:
                    part = part + ref[pl.ds(start, half), cols].astype(f32)
                store(pl.ds(first, half), cols, part)

    def into(self, buf, z):
        def store(lines, cols, total):
            buf[z, lines, cols] = total.astype(buf.dtype)

        return store

    def copy_h0(self, z):
        src = self.sd.at[z, pl.ds(0, self.half)]
        return remote(src, self.h0.at[z], self.s_h0.at[z], self.r_h0.at[z], self.p.dx)

    def copy_h1(self, z):
        src = self.sd.at[z, pl.ds(self.half, self.half)]
        return remote(src, self.h1.at[z], self.s_h1.at[z], self.r_h1.at[z], self.p.dy)

    def copy_x(self, z):
        return remote(self.sx.at[z], self.bx.at[z], self.s_x.at[z], self.r_x.at[z], self.p.dx)

    def copy_y(self, z):
        return remote(self.sy.at[z], self.by.at[z], self.s_y.at[z], self.r_y.at[z], self.p.dy)

    def copy_up(self, z):
        return remote(self.sx.at[z], self.bz.at[z], self.s_z.at[z], self.r_z.at[z], self.p.up)

    def copy_down(self, z):
        slot = jnp.where(z == self.p.z - 1, self.nz, z)
        return remote(
            self.sx.at[z], self.bz.at[slot], self.s_z.at[z], self.r_z.at[slot], self.p.down
        )

    def line_recv(self, slot):
        ref = self.bz.at[slot]
        remote(ref, ref, self.s_z.at[0], self.r_z.at[slot], self.p.pair).wait_recv()

    def diagonal(self, i):
        z = self.order[i]
        self.fill(self.p.cd, z, [], [], self.into(self.sd, z))
        self.copy_h0(z).start()
        self.copy_h1(z).start()

    def sides(self, i):
        z = self.order[i]
        self.copy_h1(z).wait_recv()
        self.fill(self.p.cx, z, [], [(self.h1.at[z], 0)], self.into(self.sx, z))
        self.copy_x(z).start()
        self.copy_h0(z).wait_recv()
        self.fill(self.p.cy, z, [(self.h0.at[z], 0)], [], self.into(self.sy, z))
        self.copy_y(z).start()

    def mine(self, i):
        p, nz, z, last = self.p, self.nz, self.order[i], i == self.nz - 1
        self.copy_x(z).wait_recv()
        self.copy_y(z).wait_recv()
        self.copy_x(z).wait_send()
        arrived = [self.bx.at[z], self.by.at[z], self.bz.at[z]]
        if last:

            @pl.when(p.z > 0)
            def _():
                self.line_recv(z)

            @pl.when(p.z < nz - 1)
            def _():
                self.line_recv(nz)

            def store(lines, cols, total):
                self.out[lines, cols] = total

            arrived.append(self.bz.at[nz])
        else:

            @pl.when(((z > p.z) & (p.z > 0)) | ((z < p.z) & (p.z < nz - 1)))
            def _():
                self.line_recv(z)

            store = self.into(self.sx, z)
        lower, upper = [(ref, 0) for ref in arrived], [(ref, self.half) for ref in arrived]
        self.fill(p.c, z, lower, upper, store)
        if not last:

            @pl.when(z > p.z)
            def _():
                self.copy_up(z).start()

            @pl.when(z < p.z)
            def _():
                self.copy_down(z).start()

    def steps(self):
        nz = self.nz
        found = [(self.diagonal, 0)] + [(self.diagonal, 1)] * (nz > 1)
        for i in range(nz):
            found.append((self.sides, i))
            if i + 2 < nz:
                found.append((self.diagonal, i + 2))
            if i > 0:
                found.append((self.mine, i - 1))
        found.append((self.mine, nz - 1))
        if self.deep:
            first = [(self.deep_first, i) for i in range(nz)]
            late = [(self.deep_next, i) for i in range(nz)]
            plan = first[:1]
            for act in found:
                if act[0] == self.diagonal and act[1] > 0:
                    plan.append(first[act[1]])
                if act == (self.mine, nz - 1):
                    plan.append(late[nz - 1])
                plan.append(act)
                if act[0] == self.sides and 1 <= act[1] < nz:
                    plan.append(late[act[1] - 1])
            found = plan + [(self.deep_end, 0), (self.deep_end, 1)]
        return [functools.partial(act, i) for act, i in found]

    def finish(self):
        p = self.p
        for i, z in enumerate(self.order):
            for c in (p.cd, p.cx, p.cy, p.c):
                self.pair_copy(c, z).wait_send()
            for copy in (self.copy_h0(z), self.copy_h1(z), self.copy_y(z)):
                copy.wait_send()
            if i < self.nz - 1:
                self.copy_up(z).wait_send()
                if self.deep:
                    self.copy_deep(z, True).wait_send()


def combine_scratch(nz, cap, seq, width, deep):
    dma = pltpu.SemaphoreType.DMA
    buf = lambda n, r: pltpu.VMEM((n, r, width), bf16)
    seq = seq - deep
    last = []
    if deep:
        last = [pltpu.VMEM((n, 4, deep, width), bf16) for n in (nz, nz + 1)]
        last += [dma((nz,)), dma((nz + 1,))] + fold_scratch(deep, width)
    return (
        [pltpu.VMEM((4, nz, 2 * cap, width), bf16)]
        + [buf(nz, seq)] * 3
        + [buf(nz, seq // 2)] * 2
        + [buf(nz, seq)] * 2
        + [buf(nz + 1, seq)]
        + [dma((4, nz))] * 3
        + [dma((nz,))] * 9
        + [dma((nz + 1,))]
        + last
    )


class WeightGrads:
    def __init__(self, pairs, outs, held, tiles, stage, stage_t, load, load_held, out_sem):
        self.pairs, self.outs, self.held, self.tiles = pairs, outs, held, tiles
        self.stage, self.stage_t = stage, stage_t
        self.load, self.load_held, self.out_sem = load, load_held, out_sem
        self.wide = tiles.shape[2]
        self.per = pairs[0][0].shape[1] // self.wide
        self.count = self.per * len(pairs)
        self.next = 0

    def columns(self, u):
        return pl.ds(u % self.per * self.wide, self.wide)

    def tile_copy(self, u):
        src = self.pairs[u // self.per][0].at[:, self.columns(u)]
        return pltpu.make_async_copy(src, self.tiles.at[u % 2], self.load.at[u % 2])

    def held_copy(self, n):
        return pltpu.make_async_copy(self.pairs[n][1], self.held, self.load_held)

    def out_copy(self, u):
        n = u // self.per
        if n < 2:
            return pltpu.make_async_copy(self.stage, self.outs[n].at[self.columns(u)], self.out_sem)
        out = self.outs[n].at[:, self.columns(u)]
        return pltpu.make_async_copy(self.stage_t, out, self.out_sem)

    def begin(self):
        self.held_copy(0).start()
        self.tile_copy(0).start()
        self.tile_copy(1).start()

    def unit(self):
        u = self.next
        if u == self.count:
            return
        self.next = u + 1
        n = u // self.per
        if u % self.per == 0:
            self.held_copy(n).wait()
        self.tile_copy(u).wait()
        total = lax.dot_general(
            self.tiles[u % 2], self.held[...], TN, preferred_element_type=f32
        )
        if u:
            self.out_copy(u - 1).wait()
        if n < 2:
            self.stage[...] = total
        else:
            self.stage_t[...] = total.T
        self.out_copy(u).start()
        if u + 2 < self.count:
            self.tile_copy(u + 2).start()
        if u + 1 < self.count and (u + 1) % self.per == 0:
            self.held_copy(n + 1).start()

    def finish(self):
        while self.next < self.count:
            self.unit()
        self.out_copy(self.count - 1).wait()


def middle_kernel(nz, cap, deep, *refs):
    rows, x, dr, a, dg, du, slots, gates, hidden, cot, gains = refs[:11]
    grad_hidden, mlp_grad, branch, out_gate, out_up, out_down = refs[11:17]
    low, local, send, recv = refs[17:21]
    p = Place()
    work = WeightGrads(((x, dg), (x, du), (dr, a)), (out_gate, out_up, out_down), *refs[21:28])
    job = Combine(p, nz, cap, 0, deep, rows, slots, gates, grad_hidden, *refs[28:])
    job.clear()
    greet(p, nz)
    job.begin()
    work.begin()
    for i, step in enumerate(job.steps()):
        step()
        if 1 <= i < 10:
            work.unit()
        if 1 <= i < 5:
            work.unit()
    seq = cot.shape[0]
    mlp_grad[...] = jnp.zeros(mlp_grad.shape, f32)
    for first in range(0, seq, seq // 4):
        lines = pl.ds(first, seq // 4)
        by_x, by_gain = rms_back(hidden[lines], gains[1:2], grad_hidden[lines])
        total = cot[lines].astype(f32) + by_x
        grad_hidden[lines] = total
        low[lines] = total.astype(bf16)
        mlp_grad[...] += by_gain
    keep = pltpu.make_async_copy(low, branch.at[p.c], local)
    keep.start()
    gather = Spread(
        p, nz, low, lambda c, z, k: branch.at[c], seq // 2, send, recv, False, True, False
    )
    gather.step(0)
    for i in range(8):
        work.unit()
    gather.step(1)
    work.finish()
    gather.step(2)
    keep.wait()
    gather.finish()
    job.finish()


def middle(nz, deep, rows, x, dr, a, dg, du, slots, gates, hidden, cot, gains):
    _, cap, width = rows.shape
    seq = slots.shape[2]
    ff = a.shape[1]
    shape = jax.ShapeDtypeStruct
    dma = pltpu.SemaphoreType.DMA
    vmem = lambda *n: pltpu.VMEM(n, bf16)
    tile = min(256, ff)
    return pl.pallas_call(
        functools.partial(middle_kernel, nz, cap, deep),
        out_shape=[
            shape((seq, width), f32),
            shape((1, width), f32),
            shape((4, seq, width), bf16),
            shape((width, ff), f32),
            shape((width, ff), f32),
            shape((ff, width), f32),
        ],
        in_specs=[ANY] * 6 + [IN_VMEM] * 5,
        out_specs=[IN_VMEM] * 2 + [ANY] * 4,
        scratch_shapes=[vmem(seq, width), dma]
        + spread_sems(nz)
        + [vmem(*a.shape), vmem(2, x.shape[0], tile)]
        + [pltpu.VMEM((tile, ff), f32), pltpu.VMEM((ff, tile), f32)]
        + [dma((2,)), dma, dma]
        + combine_scratch(nz, cap, seq, width, deep),
        compiler_params=pltpu.CompilerParams(
            collective_id=4, has_side_effects=True, vmem_limit_bytes=VMEM_BYTES
        ),
    )(rows, x, dr, a, dg, du, slots, gates, hidden, cot, gains)


class LineSum:
    def __init__(self, p, nz, part, own, sib, b, pair_s, pair_r, line_s, line_r):
        self.p, self.nz, self.part, self.own, self.sib, self.b = p, nz, part, own, sib, b
        self.pair_s, self.pair_r, self.line_s, self.line_r = pair_s, pair_r, line_s, line_r
        self.order = pick_order(p, nz)

    def clear(self):
        b, nz = self.b, self.nz

        @pl.when(self.p.z == 0)
        def _():
            b[pl.ds(0, nz)] = jnp.zeros((nz,) + b.shape[1:], b.dtype)

        @pl.when(self.p.z == nz - 1)
        def _():
            b[pl.ds(0, nz - 1)] = jnp.zeros((nz - 1,) + b.shape[1:], b.dtype)
            b[nz] = jnp.zeros(b.shape[1:], b.dtype)

    def pair_copy(self, z):
        p = self.p
        src = self.part(z, 1 - p.k)
        return remote(src, self.sib.at[z], self.pair_s.at[z], self.pair_r.at[z], p.pair)

    def begin(self):
        for z in self.order:
            self.pair_copy(z).start()

    def copy_up(self, z):
        p = self.p
        return remote(self.own(z), self.b.at[z], self.line_s.at[z], self.line_r.at[z], p.up)

    def copy_down(self, z):
        p = self.p
        slot = jnp.where(z == p.z - 1, self.nz, z)
        return remote(self.own(z), self.b.at[slot], self.line_s.at[z], self.line_r.at[slot], p.down)

    def line_recv(self, slot):
        ref = self.b.at[slot]
        remote(ref, ref, self.line_s.at[0], self.line_r.at[slot], self.p.pair).wait_recv()

    def reduce(self, n, store=None):
        p, nz, z = self.p, self.nz, self.order[n]
        own, b = self.own(z), self.b
        self.pair_copy(z).wait_recv()
        if n == nz - 1:

            @pl.when(p.z > 0)
            def _():
                self.line_recv(z)

            @pl.when(p.z < nz - 1)
            def _():
                self.line_recv(nz)

            total = own[...].astype(f32) + self.sib[z].astype(f32) + b[z].astype(f32)
            store(total + b[nz].astype(f32))
            return

        @pl.when(((z > p.z) & (p.z > 0)) | ((z < p.z) & (p.z < nz - 1)))
        def _():
            self.line_recv(z)

        total = own[...].astype(f32) + self.sib[z].astype(f32) + b[z].astype(f32)
        own[...] = total.astype(own.dtype)

        @pl.when(z > p.z)
        def _():
            self.copy_up(z).start()

        @pl.when(z < p.z)
        def _():
            self.copy_down(z).start()

    def finish(self):
        for n, z in enumerate(self.order):
            self.pair_copy(z).wait_send()
            if n < self.nz - 1:
                self.copy_up(z).wait_send()


def line_sems(nz):
    dma = pltpu.SemaphoreType.DMA
    return [dma((nz,))] * 3 + [dma((nz + 1,))]


def rms_back(x, gain, grad):
    r = lax.rsqrt(jnp.mean(x * x, axis=-1, keepdims=True) + epsilon)
    scaled = gain * grad
    mean = jnp.mean(x * scaled, axis=-1, keepdims=True)
    by_gain = jnp.sum(x * r * grad, axis=0, keepdims=True)
    return r * scaled - x * (r * r * r * mean), by_gain


def back_kernel(nz, cap, scale, *refs):
    branch, wos, packs, xn, raw, q, ot, rows = refs[:8]
    k, v, lse, cosine, sine, head_gain, slots, gates = refs[8:16]
    sum_o, gw, part, head_grad, mixed = refs[16:21]
    rows_v, wo_v, w_v, raw_v, q_v, ot_v, do, kt, low, dq, dk, dv, w_stage, sib, line_b = refs[21:36]
    load, w_sem, ot_sem = refs[36:39]
    p = Place()
    line = LineSum(
        p,
        nz,
        lambda z, k: wo_v.at[z * 2 + k],
        lambda z: wo_v.at[z * 2 + p.k],
        sib,
        line_b,
        *refs[39:43],
    )
    combine = Combine(p, nz, cap, 0, 0, rows, slots, gates, mixed, *refs[43:])
    length, wide = raw.shape
    heads = q.shape[0]
    seq = length // 4
    width = xn.shape[2]
    loads = [
        pltpu.make_async_copy(src, dst, load.at[i])
        for i, (src, dst) in enumerate(
            ((branch, rows_v), (wos, wo_v), (q, q_v), (packs, w_v))
        )
    ]
    load_ot = [
        pltpu.make_async_copy(ot.at[pl.ds(2 * t, 2)], ot_v.at[t % 2], ot_sem.at[t % 2])
        for t in range(heads // 2)
    ]
    load_xn = pltpu.make_async_copy(xn, rows_v, load.at[5])

    def load_raw(cols):
        return pltpu.make_async_copy(raw.at[:, cols], raw_v, load.at[6])

    for copy in loads + load_ot[:2]:
        copy.start()
    combine.clear()
    line.clear()
    greet(p, nz)
    combine.begin()
    steps = combine.steps()
    run = lambda n: [steps.pop(0)() for _ in range(min(n, len(steps)))]
    kt[...] = k[...].astype(f32).T.astype(bf16)
    run(2)
    loads[0].wait()
    loads[1].wait()

    @pl.loop(0, heads * HD // 256)
    def _(t):
        cols = pl.ds(pl.multiple_of(t * 256, 256), 256)
        w = wo_v[pl.ds(t * (256 // wo_v.shape[1]), 256 // wo_v.shape[1])].reshape(256, width)
        out = lax.dot_general(rows_v[...].reshape(length, width), w, NT, preferred_element_type=f32)
        do[:, cols] = out.astype(bf16)

    run(1)

    for t in range(heads // 2):
        load_ot[t].wait()
        here = 2 * HD // wo_v.shape[1]

        @pl.loop(0, width // 512)
        def _(i):
            cols = pl.ds(pl.multiple_of(i * 512, 512), 512)
            out = jnp.dot(
                ot_v[t % 2].reshape(2 * HD, length),
                rows_v[:, :, cols].reshape(length, 512),
                preferred_element_type=f32,
            )
            wo_v[pl.ds(t * here, here), :, cols] = out.astype(bf16).reshape(
                here, wo_v.shape[1], 512
            )

        if t + 2 < heads // 2:
            load_ot[t + 2].start()

    line.begin()
    load_xn.start()
    run(1)
    loads[2].wait()
    dk[...] = jnp.zeros(dk.shape, f32)
    dv[...] = jnp.zeros(dv.shape, f32)
    head_grad[...] = jnp.zeros(head_grad.shape, f32)

    def unprep(gain, grad, cols):
        by_gain = jnp.zeros((1, HD), f32)
        for i in range(length // seq):
            here = pl.ds(i * seq, seq)
            g = grad[here]
            g = g * cosine[here] + pltpu.roll(g * sine[here], HD // 2, 1)
            by_x, more = rms_back(raw_v[here], gain, g)
            low[here, cols] = by_x.astype(bf16)
            by_gain = by_gain + more
        return by_gain

    def attend(h):
        cols = pl.ds(pl.multiple_of(h * HD, HD), HD)
        load_raw(cols).start()
        for i in range(length // seq):
            keys = pl.ds(0, (i + 1) * seq)
            here = pl.ds(i * seq, seq)
            s = lax.dot_general(k[keys], q_v[h, here], NT, preferred_element_type=f32) * scale
            key_pos = lax.broadcasted_iota(jnp.int32, s.shape, 0)
            query_pos = lax.broadcasted_iota(jnp.int32, s.shape, 1) + i * seq
            probs = jnp.where(key_pos <= query_pos, jnp.exp(s - lse[h, :, here]), 0.0)
            dp = lax.dot_general(v[keys], do[here, cols], NT, preferred_element_type=f32)
            delta = jnp.sum(probs * dp, axis=0, keepdims=True)
            ds = (probs * (dp - delta)).astype(bf16)
            dk[keys] += jnp.dot(ds, q_v[h, here], preferred_element_type=f32) * scale
            dv[keys] += jnp.dot(probs.astype(bf16), do[here, cols], preferred_element_type=f32)
            dq[here] = (jnp.dot(kt[:, keys], ds, preferred_element_type=f32) * scale).T
        load_raw(cols).wait()
        head_grad[0:1] += unprep(head_gain[0:1], dq, cols)

    def store(total):
        sum_o[...] = total

    for n, first in enumerate(range(0, heads, 2)):
        pl.loop(first, first + 2)(attend)
        run(1)
        if n < nz - 1:
            line.reduce(n)
    load_raw(pl.ds(heads * HD, HD)).start()
    load_raw(pl.ds(heads * HD, HD)).wait()
    head_grad[1:2] = unprep(head_gain[1:2], dk, pl.ds(heads * HD, HD))
    low[:, pl.ds((heads + 1) * HD, HD)] = dv[...].astype(bf16)

    load_xn.wait()
    lines = w_stage.shape[1] * w_stage.shape[2]

    def w_out(t):
        first = t * w_stage.shape[1]
        c, e = first // (2 * nz), first % (2 * nz)
        return pltpu.make_async_copy(
            w_stage.at[t % 2], gw.at[c, pl.ds(e, w_stage.shape[1])], w_sem.at[t % 2]
        )

    for t in range(width // lines):
        if t >= 2:
            w_out(t - 2).wait()
        x = rows_v[:, :, pl.ds(t * lines, lines)].reshape(length, lines)
        out = lax.dot_general(x, low[...], TN, preferred_element_type=f32)
        w_stage[t % 2] = out.astype(bf16).reshape(w_stage.shape[1:])
        w_out(t).start()
        if t % 3 == 2:
            run(1)
    loads[3].wait()
    for c in range(4):

        @pl.loop(0, 2)
        def _(i):
            here = nz * w_v.shape[2]
            w = w_v[c, pl.ds(i * nz, nz)].reshape(here, wide)
            out = lax.dot_general(low[...], w, NT, preferred_element_type=f32)
            cols = pl.ds(pl.multiple_of((2 * c + i) * here, here), here)
            rows_v[:, :, cols] = out.astype(bf16).reshape(4, seq, here)

        if c % 2:
            run(1)
    part_out = pltpu.make_async_copy(rows_v, part, load.at[4])
    part_out.start()
    line.reduce(nz - 1, store)
    run(len(steps))
    part_out.wait()
    for t in range(2):
        w_out(width // lines - 2 + t).wait()
    combine.finish()
    line.finish()


def back(nz, scale, columns, branch, wos, packs, xn, raw, q, ot, rows, k, v, lse, cosine, sine, head_gain, slots, gates):
    length, wide = raw.shape
    heads = q.shape[0]
    seq = length // 4
    width = xn.shape[1]
    cap = rows.shape[1]
    shape = jax.ShapeDtypeStruct
    vmem = lambda *n: pltpu.VMEM(n, bf16)
    wide_f = lambda *n: pltpu.VMEM(n, f32)
    dma = pltpu.SemaphoreType.DMA
    return pl.pallas_call(
        functools.partial(back_kernel, nz, cap, scale),
        out_shape=[
            shape(wos.shape[1:], f32),
            shape(packs.shape, bf16),
            shape((4, seq, width), bf16),
            shape((2, HD), f32),
            shape((seq, columns), f32),
        ],
        in_specs=[ANY] * 8 + [IN_VMEM] * 8,
        out_specs=[IN_VMEM, ANY, ANY] + [IN_VMEM] * 2,
        scratch_shapes=[
            vmem(4, seq, width),
            vmem(*wos.shape),
            vmem(*packs.shape),
            wide_f(length, HD),
            vmem(*q.shape),
            vmem(2, 2, HD, length),
            vmem(length, heads * HD),
            vmem(HD, length),
            vmem(length, wide),
            wide_f(length, HD),
            wide_f(length, HD),
            wide_f(length, HD),
            vmem(2, 4, packs.shape[2], wide),
            vmem(nz, *wos.shape[1:]),
            vmem(nz + 1, *wos.shape[1:]),
            dma((7,)),
            dma((2,)),
            dma((2,)),
        ]
        + line_sems(nz)
        + combine_scratch(nz, cap, seq, columns, 0),
        compiler_params=pltpu.CompilerParams(
            collective_id=5, has_side_effects=True, vmem_limit_bytes=VMEM_BYTES
        ),
    )(branch, wos, packs, xn.reshape(4, seq, width), raw, q, ot, rows, k, v, lse, cosine, sine, head_gain, slots, gates)


def last_kernel(nz, cap, col, *refs):
    gq, rows, part, tok_in, dh_in, gains, mlp_grad, head_grad, slots, gates = refs[:10]
    oq, ok, ov, all_gains, grad_tokens, mixed = refs[10:16]
    own, sib, line_b, swap_s, swap_r, gain_v, part_v, tok, dh = refs[16:25]
    load, a_send, a_recv, g_send, g_recv, local, in_sem = refs[25:32]
    p = Place()
    fold = Fold(p, part_v, *refs[32:40], far=part)
    line = LineSum(
        p, nz, lambda z, k: gq.at[:, z * 2 + k], lambda z: own.at[z], sib, line_b, *refs[40:44]
    )
    combine = Combine(p, nz, cap, col, LAST_DEEP, rows, slots, gates, mixed, *refs[44:])
    combine.clear()
    line.clear()
    inputs = [
        pltpu.make_async_copy(src, dst, in_sem.at[i])
        for i, (src, dst) in enumerate(((part, part_v), (tok_in, tok), (dh_in, dh)))
    ]
    for copy in inputs:
        copy.start()
    greet(p, nz, diagonal=True)

    def load_copy(z):
        return pltpu.make_async_copy(gq.at[:, z * 2 + p.k], own.at[z], load.at[z])

    def swaps():
        return [
            remote(swap_s.at[c], swap_r.at[p.c], a_send.at[n], a_recv.at[n], device)
            for n, (c, device) in enumerate(((p.cx, p.dx), (p.cy, p.dy), (p.cd, p.dd)))
        ]

    def swap(total):
        swap_s[...] = total.astype(swap_s.dtype)
        for copy in swaps():
            copy.start()
        swap_r[p.c] = swap_s[p.c]

    fold.begin()
    line.begin()
    for z in line.order:
        load_copy(z).start()
    combine.begin()
    steps = combine.steps()
    run = lambda n: [steps.pop(0)() for _ in range(min(n, len(steps)))]

    def reduce(n):
        load_copy(line.order[n]).wait()
        line.reduce(n, swap)

    reduce(0)
    run(1)
    inputs[0].wait()
    fold.middle()
    reduce(1)
    run(2)

    gain_v[...] = jnp.zeros(gain_v.shape, f32)
    width = tok.shape[1]
    for copy in inputs[1:]:
        copy.wait()

    def store(lines, total):
        by_x, by_gain = rms_back(tok[lines].astype(f32), gains[0:1], total)
        grad_tokens[lines] = (dh[lines] + by_x).astype(bf16)
        for j in range(width // 128):
            gain_v[pl.ds(j, 1)] += by_gain[:, j * 128 : (j + 1) * 128]

    fold.end(store)
    for j in range(width // 128):
        gain_v[pl.ds(width // 128 + j, 1)] = mlp_grad[:, pl.ds(j * 128, 128)]
    gain_v[pl.ds(2 * width // 128, 2)] = head_grad[...]
    block = by_device(all_gains, nz)
    keep = pltpu.make_async_copy(gain_v, block(p.c, p.z, p.k), local)
    keep.start()
    job = Spread(p, nz, gain_v, block, gain_v.shape[0] // 2, g_send, g_recv)
    run(2)
    reduce(2)
    job.step(0)
    run(2)
    job.step(1)
    reduce(3)
    run(1)
    for n in range(2, nz + 2):
        job.step(n)
        run(1)
    for n, c in enumerate((p.cx, p.cy, p.cd)):
        ref = swap_r.at[c]
        remote(ref, ref, a_send.at[n], a_recv.at[n], p.dx).wait_recv()
    heads = oq.shape[1] // 4
    kv = ok.shape[1] // 4
    for c in range(4):
        oq[:, pl.ds(c * heads, heads)] = swap_r[c, :, pl.ds(0, heads)].astype(f32)
        ok[:, pl.ds(c * kv, kv)] = swap_r[c, :, pl.ds(heads, kv)].astype(f32)
        ov[:, pl.ds(c * kv, kv)] = swap_r[c, :, pl.ds(heads + kv, kv)].astype(f32)
    run(len(steps))
    for copy in swaps():
        copy.wait_send()
    keep.wait()
    job.finish()
    combine.finish()
    line.finish()


def reduce_last(nz, col, gq, rows, part, tok, dh, gains, mlp_grad, head_grad, slots, gates):
    _, _, rows_q, wide = gq.shape
    seq, width = tok.shape
    cap = rows.shape[1]
    kv = HD
    heads = wide - 2 * kv
    lines = -(-(2 * width // 128 + 2) // 16) * 16
    dma = pltpu.SemaphoreType.DMA
    shape = jax.ShapeDtypeStruct
    q = lambda *n: pltpu.VMEM(n + (4, rows_q, wide), bf16)
    return pl.pallas_call(
        functools.partial(last_kernel, nz, cap, col),
        out_shape=[
            shape((rows_q, 4 * heads), f32),
            shape((rows_q, 4 * kv), f32),
            shape((rows_q, 4 * kv), f32),
            shape((8 * nz, lines, 128), f32),
            shape((seq, width), bf16),
            shape((seq, width - col), f32),
        ],
        in_specs=[ANY] * 5 + [IN_VMEM] * 5,
        out_specs=[IN_VMEM] * 3 + [ANY] + [IN_VMEM] * 2,
        scratch_shapes=[q(nz), q(nz), q(nz + 1), q(), q()]
        + [pltpu.VMEM((lines, 128), f32)]
        + [pltpu.VMEM((4, seq, width), bf16), pltpu.VMEM((seq, width), bf16)]
        + [pltpu.VMEM((seq, width), f32)]
        + [dma((nz,))]
        + [dma((3,))] * 2
        + spread_sems(nz)
        + [dma, dma((3,))]
        + fold_scratch(seq, width)
        + line_sems(nz)
        + combine_scratch(nz, cap, seq, width - col, LAST_DEEP),
        compiler_params=pltpu.CompilerParams(
            collective_id=9, has_side_effects=True, vmem_limit_bytes=VMEM_BYTES
        ),
    )(gq, rows, part, tok, dh, gains, mlp_grad, head_grad, slots, gates)


def experts_kernel(
    nz,
    cap,
    mine,
    cots,
    slots,
    gates,
    wg_hbm,
    wu_hbm,
    wd_hbm,
    all_rows,
    produced,
    grad_inputs,
    x_out,
    dr_out,
    a_out,
    dg_out,
    du_out,
    stage_x,
    stage_d,
    x,
    dr,
    r,
    dx,
    a,
    dg,
    du,
    send,
    recv,
    load,
    out_sem,
    back_sem,
    wg,
    wu,
    wd,
    w_sem,
):
    p = Place()
    weights = [
        pltpu.make_async_copy(src, dst, w_sem.at[i])
        for i, (src, dst) in enumerate(((wg_hbm, wg), (wu_hbm, wu), (wd_hbm, wd)))
    ]
    for copy in weights:
        copy.start()
    greet(p, nz)
    job = Spread(p, nz, mine, by_device(all_rows, nz), mine.shape[0] // 2, send, recv)
    seq, width = mine.shape
    ff = a.shape[2]
    wide = min(512, width)
    narrow = min(256, ff)
    lines = [(p.c, 0), (p.cx, 0), (p.c, 1), (p.cx, 1)], [(p.cy, 0), (p.cd, 0), (p.cy, 1), (p.cd, 1)]
    turns = [(i - j, j) for i in range(1, nz + 2) for j in (1, 2) if 0 <= i - j < nz]
    turns = [(i, j - 1) for i, j in turns]

    def index(h, i, z):
        c, other = lines[h][i]
        return c * (2 * nz) + z * 2 + lax.rem(p.k + other, 2)

    def load_x(n, i):
        at, h = turns[n]
        src = mine if n == i == 0 else all_rows.at[index(h, i, job.order[at])]
        return pltpu.make_async_copy(src, stage_x.at[i], load.at[0, i])

    def load_d(n, i):
        at, h = turns[n]
        src = cots.at[index(h, i, job.order[at])]
        return pltpu.make_async_copy(src, stage_d.at[n % 2, i], load.at[1 + n % 2, i])

    def outs(h, z):
        whole = ((x, x_out), (dr, dr_out), (a, a_out), (dg, dg_out), (du, du_out))
        found = [
            pltpu.make_async_copy(src.at[h], dst.at[z, h], out_sem.at[h, n])
            for n, (src, dst) in enumerate(whole)
        ]
        for n, (src, dst) in enumerate(((r, produced), (dx, grad_inputs))):
            for i in range(4):
                found.append(
                    pltpu.make_async_copy(
                        src.at[h, pl.ds(i * cap, cap)], dst.at[index(h, i, z)], back_sem.at[h, n, i]
                    )
                )
        return found

    def group(n):
        at, h = turns[n]
        z = job.order[at]
        for i in range(4):
            load_x(n, i).start()
        if n + 1 < len(turns):
            for i in range(4):
                load_d(n + 1, i).start()
        if at:
            for copy in outs(h, job.order[at - 1]):
                copy.wait()
        for i in range(4):
            at_b = pl.ds(index(h, i, z), 1)
            names = lax.broadcasted_iota(jnp.int32, (cap, seq), 0) == slots[0, at_b]
            chosen = names.astype(f32).astype(bf16)
            row_gate = jnp.where(names, gates[0, at_b], 0.0)
            row_gate = jnp.sum(row_gate, axis=1, keepdims=True)
            here = pl.ds(i * cap, cap)
            load_d(n, i).wait()
            picked = jnp.dot(chosen, stage_d[n % 2, i], preferred_element_type=f32)
            dr[h, here] = (row_gate * picked).astype(bf16)
            load_x(n, i).wait()
            picked = jnp.dot(chosen, stage_x[i], preferred_element_type=f32)
            x[h, here] = picked.astype(bf16)

        if n == 0:
            for copy in weights:
                copy.wait()

        @pl.loop(0, ff // narrow)
        def _(t):
            cols = pl.ds(pl.multiple_of(t * narrow, narrow), narrow)
            g = jnp.dot(x[h], wg[:, cols], preferred_element_type=f32)
            u = jnp.dot(x[h], wu[:, cols], preferred_element_type=f32)
            da = lax.dot_general(dr[h], wd[cols, :], NT, preferred_element_type=f32)
            s = jax.nn.sigmoid(g)
            swish = g * s
            a[h, :, cols] = (swish * u).astype(bf16)
            du[h, :, cols] = (da * swish).astype(bf16)
            dg[h, :, cols] = (da * u * s * (1.0 + g * (1.0 - s))).astype(bf16)

        @pl.loop(0, width // wide)
        def _(t):
            cols = pl.ds(pl.multiple_of(t * wide, wide), wide)
            r[h, :, cols] = jnp.dot(a[h], wd[:, cols], preferred_element_type=f32).astype(bf16)
            back = lax.dot_general(dg[h], wg[cols, :], NT, preferred_element_type=f32)
            back = back + lax.dot_general(du[h], wu[cols, :], NT, preferred_element_type=f32)
            dx[h, :, cols] = back.astype(bf16)

        for copy in outs(h, z):
            copy.start()

    for i in range(4):
        load_d(0, i).start()
    done = 0
    for i in range(nz + 2):
        if i < nz:
            job.along(i)
        if 1 <= i <= nz:
            z = job.order[i - 1]
            job.beside(z)
            for j in (5, 6):
                job.got(j, z)
            group(done)
            done += 1
        if i >= 2:
            z = job.order[i - 2]
            job.across(z)
            for j in (7, 8, 9):
                job.got(j, z)
            group(done)
            done += 1
    for h in (0, 1):
        for copy in outs(h, job.order[nz - 1]):
            copy.wait()
    job.finish(pair=False)


def run_experts(nz, cap, mine, cots, slots, gates, wg, wu, wd):
    seq, width = mine.shape
    ff = wg.shape[1]
    rows = 4 * cap
    blocks = 8 * nz
    shape = lambda *n: jax.ShapeDtypeStruct(n, bf16)
    vmem = lambda *n: pltpu.VMEM(n, bf16)
    dma = pltpu.SemaphoreType.DMA
    return pl.pallas_call(
        functools.partial(experts_kernel, nz, cap),
        out_shape=[shape(blocks, seq, width)]
        + [shape(blocks, cap, width)] * 2
        + [shape(nz, 2, rows, width)] * 2
        + [shape(nz, 2, rows, ff)] * 3,
        in_specs=[ANY] * 2 + [IN_VMEM] * 2 + [ANY] * 3,
        out_specs=[ANY] * 8,
        scratch_shapes=[vmem(4, seq, width), vmem(2, 4, seq, width)]
        + [vmem(2, rows, width)] * 4
        + [vmem(2, rows, ff)] * 3
        + spread_sems(nz)
        + [dma((3, 4)), dma((2, 5)), dma((2, 2, 4))]
        + [vmem(*wg.shape), vmem(*wu.shape), vmem(*wd.shape), dma((3,))],
        compiler_params=pltpu.CompilerParams(
            collective_id=3, has_side_effects=True, vmem_limit_bytes=VMEM_BYTES
        ),
    )(mine, cots, slots, gates, wg, wu, wd)[1:]


def mm(a, b, contract, kind=f32):
    return lax.dot_general(a, b, ((contract[:1], contract[1:]), ((), ())), preferred_element_type=f32).astype(kind)


def fast_body(
    tokens,
    query_weight,
    key_weight,
    value_weight,
    output_weight,
    norm_gains,
    head_gains,
    expert_gate,
    expert_up,
    expert_down,
    routes,
    route_gates,
    cotangent,
):
    seq, width = tokens.shape[1:]
    nz = lax.axis_size("expert") // 2
    devices = lax.axis_size(("ctx", "expert"))
    length = 4 * seq
    topk = routes.shape[2]
    cap = max(2, 5 * seq * topk // (4 * devices))
    heads = HQ // 4
    wq = heads * HD
    scale = HD ** (-0.5)
    c = lax.axis_index("ctx")
    e = lax.axis_index("expert")
    k = lax.rem(e, 2)
    me = c * (2 * nz) + e
    rows_q = query_weight.shape[0]

    def cols(weight):
        return weight.reshape(rows_q, 4, -1).transpose(1, 0, 2)

    pack = jnp.concatenate([cols(query_weight), cols(key_weight), cols(value_weight)], axis=2)
    share = norm_gains.shape[1]
    head_share = head_gains.shape[1]
    lane = jnp.arange(128)

    def placed(part, size):
        spread = jnp.tile(part.astype(f32), (1, 128 // size))
        return jnp.where(lane[None, :] // size == lax.rem(me, 128 // size), spread, 0.0)

    meta = jnp.concatenate(
        [
            routes.reshape(seq, topk).T.astype(f32).reshape(-1, 128),
            route_gates.reshape(seq, topk).T.reshape(-1, 128),
            placed(norm_gains, share),
            placed(head_gains, head_share),
        ]
    )
    meta = jnp.pad(meta, ((0, -meta.shape[0] % 16), (0, 0)))
    half = HD // 2
    angles = jnp.arange(length, dtype=jnp.int32).astype(f32)[:, None] * (
        rope_base ** (-jnp.arange(half, dtype=f32) / half)
    )
    cosine, sine = jnp.cos(angles), jnp.sin(angles)
    tables = (
        jnp.concatenate([cosine, cosine], axis=1),
        jnp.concatenate([-sine, sine], axis=1),
    )
    found = front(
        nz,
        scale,
        pack,
        output_weight,
        tokens.reshape(seq, width),
        cotangent.reshape(seq, width),
        meta,
        *tables,
    )
    weight, wo, _, cots, _, normed, raw, queries, keys, values, attended, lse = found[:12]
    hidden, normed_mlp, gains, head_gain, slots2, gates2 = found[12:]
    produced, grad_inputs, arrived, grad_arrived, activated, grad_gate_pre, grad_up_pre = run_experts(
        nz, cap, normed_mlp, cots, slots2, gates2, expert_gate[0], expert_up[0], expert_down[0]
    )
    grad_hidden, grad_gain_mlp, branch, grad_gate, grad_up, grad_down = middle(
        nz,
        DEEP,
        grad_inputs,
        *(
            a.reshape(devices * cap, -1)
            for a in (arrived, grad_arrived, activated, grad_gate_pre, grad_up_pre)
        ),
        slots2,
        jnp.ones_like(gates2),
        hidden,
        cotangent.reshape(seq, width),
        gains,
    )
    columns = width // 2
    sum_o, grad_weight, part, grad_head, mixed_low = back(
        nz,
        scale,
        columns,
        branch,
        wo,
        weight,
        normed,
        raw,
        queries,
        attended,
        produced,
        keys,
        values,
        lse,
        *tables,
        head_gain,
        slots2,
        gates2,
    )
    sum_q, sum_k, sum_v, all_gain_parts, grad_input, mixed_high = reduce_last(
        nz,
        columns,
        grad_weight,
        produced,
        part,
        tokens.reshape(seq, width),
        grad_hidden,
        gains,
        grad_gain_mlp,
        grad_head,
        slots2,
        gates2,
    )
    mixed = hidden + jnp.concatenate([mixed_low, mixed_high], axis=1)
    gain_sums = jnp.sum(all_gain_parts, axis=0).reshape(-1)
    norm_sums = gain_sums[: 2 * width].reshape(2, width)
    head_sums = gain_sums[2 * width : 2 * width + 2 * HD].reshape(2, HD)
    return (
        mixed.astype(bf16).reshape(tokens.shape),
        grad_input.reshape(tokens.shape),
        sum_q,
        sum_k,
        sum_v,
        sum_o,
        lax.dynamic_slice_in_dim(norm_sums, me * share, share, 1),
        lax.dynamic_slice_in_dim(head_sums, me * head_share, head_share, 1),
        grad_gate[None],
        grad_up[None],
        grad_down[None],
    )


def solution(mesh):
    small = mesh.shape["ctx"] == HK and mesh.size == 32
    return jax.shard_map(
        fast_body if small else body,
        mesh=mesh,
        in_specs=(
            P("expert", "ctx", None),
            P(("ctx", "expert"), None),
            P(("ctx", "expert"), None),
            P(("ctx", "expert"), None),
            P(("ctx", "expert"), None),
            P(None, ("ctx", "expert")),
            P(None, ("ctx", "expert")),
            P(("ctx", "expert"), None, None),
            P(("ctx", "expert"), None, None),
            P(("ctx", "expert"), None, None),
            P("expert", "ctx", None),
            P("expert", "ctx", None),
            P("expert", "ctx", None),
        ),
        out_specs=(
            P("expert", "ctx", None),
            P("expert", "ctx", None),
            P(("ctx", "expert"), None),
            P(("ctx", "expert"), None),
            P(("ctx", "expert"), None),
            P(("ctx", "expert"), None),
            P(None, ("ctx", "expert")),
            P(None, ("ctx", "expert")),
            P(("ctx", "expert"), None, None),
            P(("ctx", "expert"), None, None),
            P(("ctx", "expert"), None, None),
        ),
        check_vma=False,
    )
```
